32 devices in a mesh: row: 8 (over z, x), col: 4 (over y, core).
Axes of the slice: x: 2, y: 2, z: 4, core: 2. Of those that a mesh axis runs over, the one named last changes fastest.
Arguments:
- stem_map: bfloat16 [384, 128, 128], P('row', 'col'), may hold values from -6 to 6
- layout: int32 [5, 192, 64], P(None, 'row', 'col'), may hold values from 0 to 192, as said below
- labels: int32 [52], replicated, may hold values from 0 to 999
- live: int32 [52], replicated, may hold values 0 or 1
- conv_weight: float32 [1152, 256], P(None, 'row'), may hold values from -0.1875 to 0.1875
- input_proj: float32 [2, 256, 768], P(None, 'row'), may hold values from -0.375 to 0.375
- output_proj: float32 [2, 256, 256], P(None, 'row'), may hold values from -2.5 to 2.5
- expand_weight: float32 [2, 256, 768], P(None, 'row'), may hold values from -0.375 to 0.375
- reduce_weight: float32 [2, 768, 256], P(None, 'row'), may hold values from -0.21875 to 0.21875
- head_weight: float32 [256, 1000], P('row'), may hold values from -0.375 to 0.375
- small_params: float32 [8312], replicated
- first_conv: float32 [1152, 256], P(None, 'row'), may hold values from -0.0007324219 to 0.0007324219
- first_input: float32 [2, 256, 768], P(None, 'row'), may hold values from -0.0007324219 to 0.0007324219
- first_output: float32 [2, 256, 256], P(None, 'row'), may hold values from -0.0007324219 to 0.0007324219
- first_expand: float32 [2, 256, 768], P(None, 'row'), may hold values from -0.0007324219 to 0.0007324219
- first_reduce: float32 [2, 768, 256], P(None, 'row'), may hold values from -0.0007324219 to 0.0007324219
- first_head: float32 [256, 1000], P('row'), may hold values from -0.0007324219 to 0.0007324219
- first_small: float32 [8312], replicated, may hold values from -0.005859375 to 0.005859375
- second_conv: float32 [1152, 256], P(None, 'row'), may hold values from 6.3476563e-10 to 1.0172526e-08
- second_input: float32 [2, 256, 768], P(None, 'row'), may hold values from 6.3476563e-10 to 1.0172526e-08
- second_output: float32 [2, 256, 256], P(None, 'row'), may hold values from 6.3476563e-10 to 1.0172526e-08
- second_expand: float32 [2, 256, 768], P(None, 'row'), may hold values from 6.3476563e-10 to 1.0172526e-08
- second_reduce: float32 [2, 768, 256], P(None, 'row'), may hold values from 6.3476563e-10 to 1.0172526e-08
- second_head: float32 [256, 1000], P('row'), may hold values from 6.3476563e-10 to 1.0172526e-08
- second_small: float32 [8312], replicated, may hold values from 4.0690104e-08 to 6.5104166e-07
Outputs:
- loss: float32 [], replicated
- conv_first_new: float32 [1152, 256], P(None, 'row')
- conv_second_new: float32 [1152, 256], P(None, 'row')
- conv_weight_new: float32 [1152, 256], P(None, 'row')
- input_first_new: float32 [2, 256, 768], P(None, 'row')
- input_second_new: float32 [2, 256, 768], P(None, 'row')
- input_weight_new: float32 [2, 256, 768], P(None, 'row')
- output_first_new: float32 [2, 256, 256], P(None, 'row')
- output_second_new: float32 [2, 256, 256], P(None, 'row')
- output_weight_new: float32 [2, 256, 256], P(None, 'row')
- expand_first_new: float32 [2, 256, 768], P(None, 'row')
- expand_second_new: float32 [2, 256, 768], P(None, 'row')
- expand_weight_new: float32 [2, 256, 768], P(None, 'row')
- reduce_first_new: float32 [2, 768, 256], P(None, 'row')
- reduce_second_new: float32 [2, 768, 256], P(None, 'row')
- reduce_weight_new: float32 [2, 768, 256], P(None, 'row')
- head_first_new: float32 [256, 1000], P('row')
- head_second_new: float32 [256, 1000], P('row')
- head_weight_new: float32 [256, 1000], P('row')
- small_first_new: float32 [8312], replicated
- small_second_new: float32 [8312], replicated
- small_params_new: float32 [8312], replicated
The draws below stay inside these ranges and needn't reach their ends.
Inputs may be any that keep to these rules, and one draw needn't show every extreme that they name: The canvas is cut into bands of rows; most bands are 14, 18 or 24 rows high, the last one 14 to 37 and ending at row 192. Each band is cut into images as wide as the band's bucket side, the last one in a band taking the remaining columns up to 64; every image is 14 or more positions high and wide. layout gives each position its image's top row, bottom row (exclusive), left column, right column (exclusive) and slot; slots are unique to an image and numbered in order of bands and columns, the canvas's last image having slot 51; the lowest slots hold no positions. Images cross tile borders.
All inputs are finite; a program needn't handle non-finite values.
Results may differ from the reference program's by a relative error of at most 0.019.
Values may be sent and summed in bfloat16 or wider, within the bound.
No kernel may reach another device: no remote copies, remote signals or barrier semaphores. Data moves between devices by JAX's collectives and lax.ppermute only.
A program may use at most 448 MiB of HBM per device.

```python
import math
import jax
import jax.numpy as jnp
from jax import lax

D = 256
HEADS = 8
FF = 768
STEM = 128
CLASSES = 1000
LAYERS = 2
STEP = 5
TH = 24
TW = 16
ROWS = 192
COLS = 64
IMAGES = 52
SMALL = 8312
N_ROW = 8
N_COL = 4


def draw_small_params(key, part):
    keys = jax.random.split(jax.random.fold_in(key, 11), 4)
    norms = 0.1 * jax.random.normal(keys[0], (2 + 2 * LAYERS, 2, D), jnp.float32)
    norms = norms.at[:, 0].add(1.0)
    exp_bias = 0.1 * jax.random.normal(keys[1], (LAYERS * FF,), jnp.float32)
    head_bias = 0.5 * jax.random.normal(keys[2], (CLASSES,), jnp.float32)
    pos_bias = jax.random.normal(keys[3], (LAYERS * HEADS * 169,), jnp.float32)
    return jnp.concatenate([norms.reshape(-1), exp_bias, head_bias, pos_bias])


def draw_layout(key, part):
    most = ROWS // 14 + 1
    table = jnp.array([14, 18, 24], jnp.int32)
    sides = table[jax.random.randint(jax.random.fold_in(key, 5), (most,), 0, 3)]
    ends = jnp.cumsum(sides).astype(jnp.int32)
    kept = ends <= ROWS
    last_end = jnp.max(jnp.where(kept, ends, 0))
    rest = ROWS - last_end
    bound = jnp.where(kept & ((ends < last_end) | (rest >= 14)), ends, ROWS)
    row_ids = jnp.arange(ROWS, dtype=jnp.int32)[:, None]
    starts = jnp.max(jnp.where(bound[None, :] <= row_ids, bound[None, :], 0), 1)
    stops = jnp.min(jnp.where(bound[None, :] > row_ids, bound[None, :], ROWS), 1)
    height = stops - starts
    side_row = jnp.where(height <= 24, height, height - rest)
    number_row = COLS // side_row
    row_line = jnp.arange(ROWS, dtype=jnp.int32)
    first_mark = (row_line == starts).astype(jnp.int32)
    band_count = first_mark * number_row
    total = jnp.sum(band_count)
    prior = jnp.sum(jnp.where(row_line[None, :] < starts[:, None], band_count[None, :], 0), 1)
    side = side_row[:, None]
    col_ids = jnp.arange(COLS, dtype=jnp.int32)[None, :]
    number = number_row[:, None]
    index = jnp.minimum(col_ids // side, number - 1)
    left = index * side
    right = jnp.where(index == number - 1, COLS, left + side)
    slot = IMAGES - total + prior[:, None] + index
    shape = (ROWS, COLS)
    return jnp.stack([jnp.broadcast_to(starts[:, None], shape), jnp.broadcast_to(stops[:, None], shape), left, right, slot]).astype(jnp.int32)


def with_ends(entries, key, low, top_value):
    shape = entries.shape
    spot = [jax.random.randint(jax.random.fold_in(key, axis), (), 0, shape[axis]) for axis in range(len(shape))]
    entries = entries.at[tuple(spot)].set(low)
    longest = shape.index(max(shape))
    spot[longest] = (spot[longest] + 1) % shape[longest]
    return entries.at[tuple(spot)].set(top_value)


def levels(key, dims, shards, least, largest):
    def one(dim, shards_of):
        draws = jax.random.uniform(jax.random.fold_in(jax.random.fold_in(key, 6), dim), (shards_of,), jnp.float32, least / len(shards), largest / len(shards))
        return jnp.repeat(jnp.exp(draws), dims[dim] // shards_of).reshape((-1,) + (1,) * (len(dims) - dim - 1))

    factor_of = one(*shards[0])
    for cut in shards[1:]:
        factor_of = factor_of * one(*cut)
    return factor_of


def noise(stream_key, shape, width, most, cuts=(), kind=jnp.bfloat16):
    drawn = width * jax.random.normal(stream_key, shape, jnp.float32)
    if cuts:
        drawn = drawn * levels(stream_key, shape, cuts, -0.22, 0.18)
    return jnp.clip(drawn, -most, most).astype(kind)


def setup_inputs(seed: int = 0) -> dict:
    splits = jax.random.split(jax.random.key(seed), 26)
    return {
        "stem_map": noise(splits[0], (2 * ROWS, 2 * COLS, STEM), 1.0, 6.0, ((0, 8), (1, 4))),
        "layout": draw_layout(jax.random.fold_in(splits[25], 71), 0),
        "labels": with_ends(jax.random.randint(splits[2], (IMAGES,), 0, CLASSES), jax.random.fold_in(splits[2], 1), 0, CLASSES - 1).astype(jnp.int32),
        "live": with_ends((jax.random.randint(splits[3], (IMAGES,), 0, 4) < 3).astype(jnp.int32), jax.random.fold_in(splits[3], 1), 0, 1),
        "conv_weight": noise(splits[4], (9 * STEM, D), (9 * STEM) ** -0.5, 0.1875, ((1, 8),), jnp.float32),
        "input_proj": noise(splits[5], (LAYERS, D, 3 * D), D ** -0.5, 0.375, ((1, 8),), jnp.float32),
        "output_proj": noise(splits[6], (LAYERS, D, D), (D // 49) ** -0.5, 2.5, ((1, 8),), jnp.float32),
        "expand_weight": noise(splits[7], (LAYERS, D, FF), D ** -0.5, 0.375, ((1, 8),), jnp.float32),
        "reduce_weight": noise(splits[8], (LAYERS, FF, D), FF ** -0.5, 0.21875, ((1, 8),), jnp.float32),
        "head_weight": noise(splits[9], (D, CLASSES), D ** -0.5, 0.375, ((0, 8),), jnp.float32),
        "small_params": draw_small_params(jax.random.fold_in(splits[25], 71), 0),
        "first_conv": noise(splits[11], (9 * STEM, D), (0.014 * (N_ROW * N_COL * TH * TW) ** -0.5), 0.0007324219, ((1, 8),), jnp.float32),
        "first_input": noise(splits[12], (LAYERS, D, 3 * D), (0.014 * (N_ROW * N_COL * TH * TW) ** -0.5), 0.0007324219, ((1, 8),), jnp.float32),
        "first_output": noise(splits[13], (LAYERS, D, D), (0.014 * (N_ROW * N_COL * TH * TW) ** -0.5), 0.0007324219, ((1, 8),), jnp.float32),
        "first_expand": noise(splits[14], (LAYERS, D, FF), (0.014 * (N_ROW * N_COL * TH * TW) ** -0.5), 0.0007324219, ((1, 8),), jnp.float32),
        "first_reduce": noise(splits[15], (LAYERS, FF, D), (0.014 * (N_ROW * N_COL * TH * TW) ** -0.5), 0.0007324219, ((1, 8),), jnp.float32),
        "first_head": noise(splits[16], (D, CLASSES), (0.014 * (N_ROW * N_COL * TH * TW) ** -0.5), 0.0007324219, ((0, 8),), jnp.float32),
        "first_small": noise(splits[17], (SMALL,), (0.11 * (N_ROW * N_COL * TH * TW) ** -0.5), 0.005859375, (), jnp.float32),
        "second_conv": jnp.clip(jnp.exp(math.log(1.017252593271678e-08) - 2.77419 * jax.random.uniform(splits[18], (9 * STEM, D), jnp.float32) ** levels(splits[18], (9 * STEM, D), ((1, 8),), -0.2, 0.2)), 6.34765628948486e-10, 1.017252593271678e-08),
        "second_input": jnp.clip(jnp.exp(math.log(1.017252593271678e-08) - 2.77419 * jax.random.uniform(splits[19], (LAYERS, D, 3 * D), jnp.float32) ** levels(splits[19], (LAYERS, D, 3 * D), ((1, 8),), -0.2, 0.2)), 6.34765628948486e-10, 1.017252593271678e-08),
        "second_output": jnp.clip(jnp.exp(math.log(1.017252593271678e-08) - 2.77419 * jax.random.uniform(splits[20], (LAYERS, D, D), jnp.float32) ** levels(splits[20], (LAYERS, D, D), ((1, 8),), -0.2, 0.2)), 6.34765628948486e-10, 1.017252593271678e-08),
        "second_expand": jnp.clip(jnp.exp(math.log(1.017252593271678e-08) - 2.77419 * jax.random.uniform(splits[21], (LAYERS, D, FF), jnp.float32) ** levels(splits[21], (LAYERS, D, FF), ((1, 8),), -0.2, 0.2)), 6.34765628948486e-10, 1.017252593271678e-08),
        "second_reduce": jnp.clip(jnp.exp(math.log(1.017252593271678e-08) - 2.77419 * jax.random.uniform(splits[22], (LAYERS, FF, D), jnp.float32) ** levels(splits[22], (LAYERS, FF, D), ((1, 8),), -0.2, 0.2)), 6.34765628948486e-10, 1.017252593271678e-08),
        "second_head": jnp.clip(jnp.exp(math.log(1.017252593271678e-08) - 2.77419 * jax.random.uniform(splits[23], (D, CLASSES), jnp.float32) ** levels(splits[23], (D, CLASSES), ((0, 8),), -0.2, 0.2)), 6.34765628948486e-10, 1.017252593271678e-08),
        "second_small": jnp.clip(jnp.exp(jax.random.uniform(splits[24], (SMALL,), jnp.float32, math.log(4.069010373086712e-08), math.log(6.51041659693874e-07))), 4.069010373086712e-08, 6.51041659693874e-07),
    }


eps_norm = 1e-05
beta_one = 0.9
beta_two = 0.999
learn_rate = 0.2
decay_rate = 0.05
eps_adam = 1e-08

@jax.custom_vjp
def low(v):
    return lax.optimization_barrier(v.astype(jnp.bfloat16)).astype(jnp.float32)

@jax.custom_vjp
def low_back(v):
    return v

def low_keep(v):
    return (low(v), None)

def low_pass(kept, grad):
    return (grad,)

def back_keep(v):
    return (v, None)

def back_low(kept, grad):
    return (low(grad),)
low.defvjp(low_keep, low_pass)
low_back.defvjp(back_keep, back_low)

def matmul(left, right):
    return jnp.dot(left, right, precision=lax.Precision.HIGHEST, preferred_element_type=jnp.float32)

def layer_norm(values, gain, bias):
    centre = values - lax.optimization_barrier(jnp.mean(values, -1, keepdims=True))
    spread = lax.optimization_barrier(jnp.mean(centre * centre, -1, keepdims=True))
    return centre * lax.rsqrt(spread + eps_norm) * gain + bias

def unpack(small):
    count_norm = (2 + 2 * LAYERS) * 2 * D
    norms = small[:count_norm].reshape(2 + 2 * LAYERS, 2, D)
    exp_bias = small[count_norm:count_norm + LAYERS * FF].reshape(LAYERS, FF)
    start = count_norm + LAYERS * FF
    head_bias = small[start:start + CLASSES]
    pos_bias = small[start + CLASSES:].reshape(LAYERS, HEADS, 169)
    return (norms, exp_bias, head_bias, pos_bias)

def make_patches(framed, layout, row_first, col_first):
    rows, cols = (layout.shape[1], layout.shape[2])
    row_pos = row_first + jnp.arange(rows, dtype=jnp.int32)[:, None]
    col_pos = col_first + jnp.arange(cols, dtype=jnp.int32)[None, :]
    first_row = (row_pos == layout[0])[..., None]
    first_col = (col_pos == layout[2])[..., None]
    taps = []
    for a in range(3):
        for b in range(3):
            tap = framed[a:a + 2 * rows:2, b:b + 2 * cols:2]
            if a == 0:
                tap = jnp.where(first_row, jnp.zeros_like(tap), tap)
            if b == 0:
                tap = jnp.where(first_col, jnp.zeros_like(tap), tap)
            taps.append(tap)
    return jnp.concatenate(taps, -1).reshape(rows * cols, -1)

def offsets(layout, dilation, row_first, col_first):
    rows, cols = (layout.shape[1], layout.shape[2])
    row_pos = row_first + jnp.arange(rows, dtype=jnp.int32)[:, None] + jnp.zeros((rows, cols), jnp.int32)
    col_pos = col_first + jnp.arange(cols, dtype=jnp.int32)[None, :] + jnp.zeros((rows, cols), jnp.int32)

    def begin(place, first, extent):
        local = place - first
        group = local % dilation
        index = local // dilation
        length = (extent - group + dilation - 1) // dilation
        return jnp.clip(index - 3, 0, length - 7) - index
    return (begin(row_pos, layout[0], layout[1] - layout[0]), begin(col_pos, layout[2], layout[3] - layout[2]))

def window_index(lo_row, lo_col, dilation, reach, pad_cols):
    rows, cols = lo_row.shape
    steps = jnp.arange(7, dtype=jnp.int32)
    row_key = jnp.arange(rows, dtype=jnp.int32)[:, None, None, None] + reach + dilation * (lo_row[:, :, None, None] + steps[:, None])
    col_key = jnp.arange(cols, dtype=jnp.int32)[None, :, None, None] + reach + dilation * (lo_col[:, :, None, None] + steps[None, :])
    keys = (row_key * pad_cols + col_key).reshape(rows * cols, 49)
    table = ((lo_row[:, :, None, None] + steps[:, None] + 6) * 13 + lo_col[:, :, None, None] + steps[None, :] + 6).reshape(rows * cols, 49)
    return (keys, table)

def attend_block(query, flat, keys, table, bias):
    near = jnp.take(flat, keys, axis=0)
    count = query.shape[0]
    query4 = query.reshape(count, HEADS, -1)
    size = query4.shape[-1]
    key4 = near[..., :D].reshape(count, 49, HEADS, size)
    value4 = near[..., D:].reshape(count, 49, HEADS, size)
    score = jnp.einsum('nhc,nkhc->nhk', query4, key4, precision=lax.Precision.HIGHEST) * size ** (-0.5)
    score = score + jnp.take(bias, table, axis=1).transpose(1, 0, 2)
    probs = low(jax.nn.softmax(score, -1))
    return jnp.einsum('nhk,nkhc->nhc', probs, value4, precision=lax.Precision.HIGHEST).reshape(count, D)

def attend_all(query, flat, keys, table, bias):
    count = query.shape[0]
    block = math.gcd(count, 1024)

    def one_block(pieces):
        return attend_block(pieces[0], flat, pieces[1], pieces[2], bias)
    outs = lax.map(jax.checkpoint(one_block), (query.reshape(-1, block, D), keys.reshape(-1, block, 49), table.reshape(-1, block, 49)))
    return outs.reshape(count, D)

def adamw(weight, grad, first, second):
    first = beta_one * first + (1.0 - beta_one) * grad
    second = beta_two * second + (1.0 - beta_two) * grad * grad
    fix_one = 1.0 - beta_one ** STEP
    fix_two = 1.0 - beta_two ** STEP
    new = weight - learn_rate * (first / fix_one / (jnp.sqrt(second / fix_two) + eps_adam) + decay_rate * weight)
    return (first, second, new)

def reference(stem_map, layout, labels, live, conv_weight, input_proj, output_proj, expand_weight, reduce_weight, head_weight, small_params, first_conv, first_input, first_output, first_expand, first_reduce, first_head, first_small, second_conv, second_input, second_output, second_expand, second_reduce, second_head, second_small):
    rows_all = TH * N_ROW
    cols_all = TW * N_COL
    image = stem_map.astype(jnp.float32)
    framed = jnp.pad(image, ((1, 0), (1, 0), (0, 0)))
    patches = make_patches(framed, layout, 0, 0)
    slot = layout[4].reshape(-1)
    area = jax.ops.segment_sum(jnp.ones((rows_all * cols_all,), jnp.float32), slot, IMAGES)
    weight_item = live.astype(jnp.float32) * (area > 0.5).astype(jnp.float32)
    onehot = (labels[:, None] == jnp.arange(CLASSES, dtype=jnp.int32)[None, :]).astype(jnp.float32)
    indices = []
    for layer in range(LAYERS):
        dilation = layer + 1
        lo_row, lo_col = offsets(layout, dilation, 0, 0)
        indices.append(window_index(lo_row, lo_col, dilation, 6 * dilation, cols_all + 12 * dilation))

    def forward(wconv, wqkv, wproj, wexp, wred, whead, small):
        norms, exp_bias, head_bias, pos_bias = unpack(small)
        hidden = layer_norm(low_back(matmul(patches, low(wconv))), norms[0, 0], norms[0, 1])
        for layer in range(LAYERS):
            reach = 6 * (layer + 1)
            normed = low(layer_norm(hidden, norms[1 + 2 * layer, 0], norms[1 + 2 * layer, 1]))
            mixed = low_back(matmul(normed, low(wqkv[layer])))
            query = low(mixed[:, :D])
            keyval = low(mixed[:, D:]).reshape(rows_all, cols_all, 2 * D)
            flat = jnp.pad(keyval, ((reach, reach), (reach, reach), (0, 0))).reshape(-1, 2 * D)
            mixed_out = low(attend_all(query, flat, indices[layer][0], indices[layer][1], pos_bias[layer]))
            hidden = hidden + low_back(matmul(mixed_out, low(wproj[layer])))
            normed2 = low(layer_norm(hidden, norms[2 + 2 * layer, 0], norms[2 + 2 * layer, 1]))
            upper = low_back(matmul(normed2, low(wexp[layer])) + exp_bias[layer])
            gelu_low = low(jax.nn.gelu(upper, approximate=False))
            hidden = hidden + low_back(matmul(gelu_low, low(wred[layer])))
        final = layer_norm(hidden, norms[-1, 0], norms[-1, 1])
        sums = jax.ops.segment_sum(final, slot, IMAGES)
        pooled = low(sums / jnp.maximum(area, 1.0)[:, None])
        logits = low_back(matmul(pooled, low(whead)) + head_bias)
        logsum = jax.nn.logsumexp(logits, -1)
        cross = logsum - lax.optimization_barrier(jnp.sum(onehot * logits, -1))
        return jnp.sum(weight_item * cross) / jnp.maximum(jnp.sum(weight_item), 1.0)
    params = (conv_weight, input_proj, output_proj, expand_weight, reduce_weight, head_weight, small_params)
    loss, back = jax.vjp(forward, *params)
    grads = back(jnp.ones((), jnp.float32))
    firsts = (first_conv, first_input, first_output, first_expand, first_reduce, first_head, first_small)
    seconds = (second_conv, second_input, second_output, second_expand, second_reduce, second_head, second_small)
    res = [adamw(w, g, m, v) for w, g, m, v in zip(params, grads, firsts, seconds)]
    return (loss, res[0][0], res[0][1], res[0][2], res[1][0], res[1][1], res[1][2], res[2][0], res[2][1], res[2][2], res[3][0], res[3][1], res[3][2], res[4][0], res[4][1], res[4][2], res[5][0], res[5][1], res[5][2], res[6][0], res[6][1], res[6][2])
```

```python
import functools

import jax
import jax.numpy as jnp
from jax import lax
from jax.experimental import pallas as pl
from jax.experimental.pallas import tpu as pltpu
from jax.sharding import PartitionSpec as P

D = 256
HEADS = 8
FF = 768
CLASSES = 1000
LAYERS = 2
STEP = 5
WIN = 176

eps_norm = 1e-05
beta_one = 0.9
beta_two = 0.999
learn_rate = 0.2
decay_rate = 0.05
eps_adam = 1e-08
scale = (D // HEADS) ** -0.5

bf16 = jnp.bfloat16
f32 = jnp.float32
i32 = jnp.int32
MASKED = -1e30
VMEM = 56 * 1024 * 1024


def nn(a, b):
    return lax.dot_general(a, b, (((1,), (0,)), ((), ())), preferred_element_type=f32)


def nt(a, b):
    return lax.dot_general(a, b, (((1,), (1,)), ((), ())), preferred_element_type=f32)


def tn(a, b):
    return lax.dot_general(a, b, (((0,), (0,)), ((), ())), preferred_element_type=f32)


def two_parts(x):
    high = x.astype(bf16)
    return high, (x - high.astype(f32)).astype(bf16)


def norm_parts(x):
    centre = x - jnp.mean(x, -1, keepdims=True)
    rstd = lax.rsqrt(jnp.mean(centre * centre, -1, keepdims=True) + eps_norm)
    return centre * rstd, rstd


def norm(x, gain_bias):
    return norm_parts(x)[0] * gain_bias[0:1] + gain_bias[1:2]


def norm_back(x, gain_bias, dy):
    xhat, rstd = norm_parts(x)
    dxhat = dy * gain_bias[0:1]
    dx = rstd * (
        dxhat
        - jnp.mean(dxhat, -1, keepdims=True)
        - xhat * jnp.mean(dxhat * xhat, -1, keepdims=True)
    )
    return dx, jnp.sum(dy * xhat, 0, keepdims=True), jnp.sum(dy, 0, keepdims=True)


def normal_cdf(u):
    return 0.5 * (1.0 + lax.erf(u * 0.7071067811865476))


def join(ref, first, count):
    rows = ref.shape[1] // 3
    wide = [
        ref[:, k * rows : (k + 1) * rows, :].reshape(D, ref.shape[2])
        for k in range(first, first + count)
    ]
    return wide[0] if count == 1 else jnp.concatenate(wide, 1)


class One:
    dilation, queries, across, pieces, steps = 1, 64, 16, 4, 6
    keys = pieces * 128

    @staticmethod
    def key_col(piece, c8):
        two = 2 * (c8 & 3) + (c8 >> 2)
        return jnp.where(
            piece == 0,
            2 * c8,
            jnp.where(piece == 1, 2 * c8 + 1, jnp.where(piece == 2, two - 8, two + 16)),
        )

    @staticmethod
    def query_col(index):
        return 2 * (index & 7) + (index >> 3)


class Two:
    dilation, queries, across, pieces, steps = 2, 32, 8, 3, 12
    keys = pieces * 128

    @staticmethod
    def key_col(piece, c8):
        return jnp.where(piece == 0, c8, jnp.where(piece == 1, c8 - 8, c8 + 8))

    @staticmethod
    def query_col(index):
        return index


def key_place(geo):
    lane = lax.broadcasted_iota(i32, (1, geo.keys), 1)
    return (lane >> 3) & 15, geo.key_col(lane >> 7, lane & 7)


def window_mask(geo, lay, step, row_first, col_first):
    token = lax.broadcasted_iota(i32, (geo.queries, 1), 0)
    if geo.dilation == 1:
        block = step
        row = block * 4 + (token >> 4)
        col = geo.query_col(token & 15)
        row_pos, col_pos = row_first + row, col_first + col
    else:
        group = step // 3
        block = step - 3 * group
        row = block * 4 + (token >> 3)
        col = token & 7
        row_pos = row_first + 2 * row + (group >> 1)
        col_pos = col_first + 2 * col + (group & 1)

    def begin(place, first, end):
        local = place - first
        extent = end - first
        if geo.dilation == 1:
            index, length = local, extent
        else:
            index, length = local >> 1, (extent - (local & 1) + 1) >> 1
        return jnp.minimum(jnp.maximum(index - 3, 0), length - 7) - index

    row_start = row + begin(row_pos, lay[:, 0:1], lay[:, 1:2])
    col_start = col + begin(col_pos, lay[:, 2:3], lay[:, 3:4])
    key_row, key_col = key_place(geo)
    down = key_row + (block * 4 - 6) - row_start
    right = key_col - col_start
    inside = (down >= 0) & (down <= 6) & (right >= 0) & (right <= 6)
    return jnp.where(inside, 0.0, MASKED).astype(f32)


def position_onehot(geo, across):
    key_row, key_col = key_place(geo)
    right = key_col - geo.query_col(across) + 6
    index = jnp.where((right >= 0) & (right <= 12) & (key_row <= 12), key_row * 13 + right, -1)
    entry = lax.broadcasted_iota(i32, (WIN, geo.keys), 0)
    return jnp.where(entry == index, 1.0, 0.0).astype(bf16)


def position_table(geo, bias, first_ref):
    high = bias.astype(bf16)
    rest = bias - high.astype(f32)
    mid = rest.astype(bf16)
    low = (rest - mid.astype(f32)).astype(bf16)
    for across in range(geo.across):
        onehot = position_onehot(geo, across)
        row = nn(high, onehot) + nn(mid, onehot) + nn(low, onehot)
        for piece in range(geo.pieces):
            lanes = slice(piece * 128, piece * 128 + 128)
            first_ref[piece, pl.ds(across, HEADS, stride=geo.across), :] = row[:, lanes]


def spread_table(geo, first_ref, table_ref):
    for head in range(HEADS):
        for row in range(4):
            for piece in range(geo.pieces):
                lanes = slice(piece * 128, piece * 128 + 128)
                value = first_ref[piece, head * geo.across : (head + 1) * geo.across, :]
                if row:
                    value = pltpu.roll(value, 8 * row, 1)
                begin = head * geo.queries + row * geo.across
                table_ref[begin : begin + geo.across, lanes] = value


def gather_table(geo, table_ref, first_ref):
    for head in range(HEADS):
        for piece in range(geo.pieces):
            lanes = slice(piece * 128, piece * 128 + 128)
            total = None
            for row in range(4):
                begin = head * geo.queries + row * geo.across
                value = table_ref[begin : begin + geo.across, lanes]
                if row:
                    value = pltpu.roll(value, 128 - 8 * row, 1)
                total = value if total is None else total + value
            first_ref[piece, head * geo.across : (head + 1) * geo.across, :] = total
    grad = jnp.zeros((HEADS, WIN), f32)
    for across in range(geo.across):
        onehot = position_onehot(geo, across)
        rows = pl.ds(across, HEADS, stride=geo.across)
        first = [first_ref[piece, rows, :] for piece in range(geo.pieces)]
        high, low = two_parts(jnp.concatenate(first, 1))
        grad = grad + nt(high, onehot) + nt(low, onehot)
    return grad


def head_lanes(head):
    lane = lax.broadcasted_iota(i32, (1, D), 1)
    return jnp.where((lane >> 5) == head, 1.0, 0.0)


def by_head(x):
    return jnp.concatenate([x * head_lanes(h).astype(x.dtype) for h in range(HEADS)], 0)


def from_heads(x):
    count = x.shape[0] // HEADS
    total = None
    for h in range(HEADS):
        part = x[h * count : (h + 1) * count] * head_lanes(h)
        total = part if total is None else total + part
    return total


def key_rows(geo, step):
    if geo.dilation == 1:
        return None, pl.multiple_of(step * 32, 32)
    group = step // 3
    return group, pl.multiple_of((step - 3 * group) * 32, 32)


def load_keys(geo, pieces, step, lanes):
    group, first = key_rows(geo, step)
    if geo.dilation == 1:
        parts = [pieces[p, pl.ds(first, 128), lanes] for p in range(4)]
    else:
        parts = [pieces[p, group, pl.ds(first, 128), lanes] for p in range(3)]
    return jnp.concatenate(parts, 0)


def add_keys(geo, pieces, step, lanes, value):
    group, first = key_rows(geo, step)
    for p in range(geo.pieces):
        part = value[p * 128 : (p + 1) * 128]
        if geo.dilation == 1:
            pieces[p, pl.ds(first, 128), lanes] += part
        else:
            pieces[p, group, pl.ds(first, 128), lanes] += part


KEY = slice(0, D)
VALUE = slice(D, 2 * D)


def softmax_rows(score, table, mask):
    score = score * scale + (table + mask)
    top = jnp.max(score, -1, keepdims=True)
    weight = jnp.exp(score - top)
    return weight * (1.0 / jnp.sum(weight, -1, keepdims=True))


def attend(geo, place, lay_ref, query_ref, pieces, table_ref, out_ref, score_ref, prob_ref):
    count = geo.queries

    def step_of(step, carry):
        rows = pl.ds(pl.multiple_of(step * count, count), count)
        mask = window_mask(geo, lay_ref[rows, :], step, place[0], place[1])
        wide = by_head(query_ref[rows, :])
        score_ref[...] = nt(wide, load_keys(geo, pieces, step, KEY))
        for h in range(HEADS):
            span = slice(h * count, (h + 1) * count)
            prob = softmax_rows(score_ref[span, :], table_ref[span, :], mask)
            prob_ref[span, :] = prob.astype(bf16)
        out = nn(prob_ref[...], load_keys(geo, pieces, step, VALUE))
        out_ref[rows, :] = from_heads(out).astype(out_ref.dtype)
        return carry

    lax.fori_loop(0, geo.steps, step_of, 0)


def attend_back(
    geo, place, lay_ref, query_ref, dout_ref, pieces, table_ref, dquery_ref, dpieces, dtable_ref,
    score_ref, dprob_ref, prob_ref, dscore_ref,
):
    count = geo.queries
    dtable_ref[...] = jnp.zeros_like(dtable_ref)
    dpieces[...] = jnp.zeros_like(dpieces)

    def step_of(step, carry):
        rows = pl.ds(pl.multiple_of(step * count, count), count)
        mask = window_mask(geo, lay_ref[rows, :], step, place[0], place[1])
        wide = by_head(query_ref[rows, :])
        dwide = by_head(dout_ref[rows, :])
        keys = load_keys(geo, pieces, step, KEY)
        score_ref[...] = nt(wide, keys)
        dprob_ref[...] = nt(dwide, load_keys(geo, pieces, step, VALUE))
        for h in range(HEADS):
            span = slice(h * count, (h + 1) * count)
            prob = softmax_rows(score_ref[span, :], table_ref[span, :], mask)
            prob_ref[span, :] = prob.astype(bf16)
            dprob = dprob_ref[span, :]
            dscore = prob * (dprob - jnp.sum(prob * dprob, -1, keepdims=True))
            dtable_ref[span, :] += dscore
            dscore_ref[span, :] = dscore.astype(bf16)
        dscore = dscore_ref[...]
        add_keys(geo, dpieces, step, VALUE, tn(prob_ref[...], dwide))
        add_keys(geo, dpieces, step, KEY, tn(dscore, wide) * scale)
        dquery_ref[rows, :] = from_heads(nn(dscore, keys)) * scale
        return carry

    lax.fori_loop(0, geo.steps, step_of, 0)


def grouped(x):
    parts = x.reshape(12, 2, 2, 8, x.shape[-1])
    return [parts[:, g >> 1, g & 1].reshape(96, x.shape[-1]) for g in range(4)]


def run(kernel, outs, ins, scratch=(), specs=None, flops=0):
    in_specs = [pl.BlockSpec(memory_space=pltpu.VMEM)] * len(ins)
    for index, spec in (specs or {}).items():
        in_specs[index] = spec
    return pl.pallas_call(
        kernel,
        out_shape=outs,
        in_specs=in_specs,
        out_specs=[pl.BlockSpec(memory_space=pltpu.VMEM)] * len(outs),
        scratch_shapes=list(scratch),
        compiler_params=pltpu.CompilerParams(vmem_limit_bytes=VMEM),
        cost_estimate=pl.CostEstimate(flops=flops, bytes_accessed=4 << 20, transcendentals=0),
    )(*ins)


SMEM = pl.BlockSpec(memory_space=pltpu.SMEM)


def out(shape, dtype=f32):
    return jax.ShapeDtypeStruct(shape, dtype)


def pack_kernel(conv, qkv, proj, exp, red, head, early, late):
    sh = qkv.shape[1]
    for tap in range(9):
        early[tap * sh : (tap + 1) * sh, :] = conv[tap * 128 : (tap + 1) * 128, :].T.astype(bf16)
    for k in range(6):
        begin = (9 + k) * sh
        early[begin : begin + sh, :] = qkv[0, :, k * 128 : (k + 1) * 128].astype(bf16)

    def put(slot, value):
        late[slot * sh : slot * sh + value.shape[0], :] = value.astype(bf16)

    for k in range(3):
        cols = slice(k * D, (k + 1) * D)
        put(k, qkv[1, :, cols])
        put(3 + k, exp[0, :, cols])
        put(6 + k, exp[1, :, cols])
    put(9, red[0])
    put(12, red[1])
    put(15, proj[0])
    put(16, proj[1])
    for k in range(3):
        put(17 + k, head[:, k * D : (k + 1) * D])
    tail = head[:, 3 * D :]
    put(20, jnp.concatenate([tail, jnp.zeros((sh, 4 * D - CLASSES), f32)], 1))


def table_kernel(bias, first_one, first_two):
    position_table(One, bias[0:8, :], first_one)
    position_table(Two, bias[8:16, :], first_two)


def front_kernel(
    place, stem, above, left, lay, early, norms,
    patches, conv_out, hidden, query, keyval, edges,
    stem_f, above_f,
):
    nr, sh = early.shape[0], early.shape[1] // 15
    stem_f[...] = stem[...].astype(f32)
    above_f[...] = above[...].astype(f32)
    left_f = left[...].astype(f32)
    tiles = left_f[:384].reshape(24, 2, 8, 128)
    left_odd = tiles[:, 0]
    beside = [left_odd, tiles[:, 1], jnp.concatenate([left_odd[1:], left_f[384:392][None]], 0)]
    phases = []
    for m in range(4):
        part = stem_f[pl.ds(m, 384, stride=4), :].reshape(24, 2, 8, 128)
        even, odd = part[:, 0], part[:, 1]
        top = above_f[pl.ds(m, 8, stride=4), :]
        phases.append([jnp.concatenate([top[None], odd[:-1]], 0), even, odd])
    token = lax.broadcasted_iota(i32, (384, 1), 0)
    row_pos = place[0] + (token >> 4)
    col_pos = place[1] + One.query_col(token & 15)
    inner_row = jnp.where(row_pos == lay[:, 0:1], 0.0, 1.0)
    inner_col = jnp.where(col_pos == lay[:, 2:3], 0.0, 1.0)
    half = lax.broadcasted_iota(i32, (24, 8, 128), 1)
    for a in range(3):
        last = phases[3][a].reshape(192, 128)
        shifted = pltpu.roll(last.reshape(24, 8, 128), 1, 1)
        shifted = jnp.where(half == 0, beside[a], shifted)
        taps = (
            (shifted, phases[1][a]),
            (phases[0][a], phases[2][a]),
            (phases[1][a], phases[3][a]),
        )
        for b in range(3):
            value = jnp.stack(taps[b], 1).reshape(384, 128)
            if a == 0:
                value = value * inner_row
            if b == 0:
                value = value * inner_col
            lanes = slice((3 * a + b) * 128, (3 * a + b + 1) * 128)
            patches[:, lanes] = value.astype(bf16)
    wide = [early[:, k * sh : (k + 1) * sh, :].reshape(D, 128) for k in range(15)]
    conv = nt(patches[...], jnp.concatenate(wide[:9], 1))
    conv_out[...] = conv
    h = norm(conv, norms[0:2, :])
    hidden[...] = h
    low = norm(h, norms[2:4, :]).astype(bf16)
    mixed = nn(low, jnp.concatenate(wide[9:], 1))
    query[...] = mixed[:, :D].astype(bf16)
    both = mixed[:, D:].reshape(24, 2, 8, 2 * D)
    zero, one = both[:, 0], both[:, 1]
    keyval[0] = zero.reshape(192, 2 * D).astype(bf16)
    keyval[1] = one.reshape(192, 2 * D).astype(bf16)
    sub = lax.broadcasted_iota(i32, zero.shape, 1)
    edge_left = jnp.where(sub < 4, zero, pltpu.roll(one, 4, 1))
    edge_right = jnp.where(sub < 4, pltpu.roll(zero, 4, 1), one)
    edges[0] = edge_left.reshape(192, 2 * D).astype(bf16)
    edges[1] = edge_right.reshape(192, 2 * D).astype(bf16)


def gather_keys_one(keyval, left, right, above, below, pieces):
    for p in range(4):
        own = keyval[p] if p < 2 else (left, right)[p - 2][...]
        pieces[p, 0:48, :] = above[p]
        pieces[p, 48:240, :] = own
        pieces[p, 240:288, :] = below[p]


def feed_forward(hidden, norms, w_exp, w_red, bias):
    low = norm(hidden, norms).astype(bf16)
    upper = nn(low, w_exp) + bias
    gelu = upper * normal_cdf(upper)
    return hidden + nn(gelu.astype(bf16), w_red)


def fetch(late, slots, buffers, sems):
    rows = buffers.shape[2]
    takers = []
    for n, slot in enumerate(slots):
        copy = pltpu.make_async_copy(
            late.at[:, pl.ds(slot * rows, rows), :], buffers.at[n], sems.at[n]
        )
        copy.start()

        def take(copy=copy, n=n):
            copy.wait()
            return buffers.at[n]

        takers.append(take)
    return takers


QKV_TWO, EXP_ONE, EXP_TWO, RED_ONE, RED_TWO, PROJ, HEAD = range(7)


def first_block_kernel(
    place, lay, hidden, query, keyval, left, right, above, below, first_table, late, norms, ebias,
    att, middle, last, query2, keyval2,
    pieces, table, score, prob, buffers, sems,
):
    w_proj, w_exp, w_red, w_qkv = fetch(late, (PROJ, EXP_ONE, RED_ONE, QKV_TWO), buffers, sems)
    gather_keys_one(keyval, left, right, above, below, pieces)
    spread_table(One, first_table, table)
    attend(One, place, lay, query, pieces, table, att, score, prob)
    mid = hidden[...] + nn(att[...], join(w_proj(), 0, 1))
    middle[...] = mid
    end = feed_forward(mid, norms[4:6, :], join(w_exp(), 0, 3), red_of(w_red()), ebias[0:1, :])
    last[...] = end
    low = norm(end, norms[6:8, :]).astype(bf16)
    mixed = nn(low, join(w_qkv(), 0, 3))
    for g, part in enumerate(grouped(mixed)):
        query2[g * 96 : (g + 1) * 96, :] = part[:, :D].astype(bf16)
        keyval2[g] = part[:, D:].astype(bf16)


def red_of(ref):
    return ref[...].reshape(FF, D)


def slot_onehot(slots, images):
    entry = lax.broadcasted_iota(i32, (384, images), 1)
    return jnp.where(slots[:, 4:5] == entry, 1.0, 0.0).astype(bf16)


def ungroup(value, ref):
    for g in range(4):
        ref[:, g >> 1, g & 1] = value[g * 96 : (g + 1) * 96].reshape(12, 8, value.shape[-1])


def second_block_kernel(
    place, lay, slots, hidden, query, own, left, right, first_table, late, norms, ebias,
    att, middle, last, sums,
    pieces, table, score, prob, att_group, att_token, buffers, sems,
):
    w_proj, w_exp, w_red = fetch(late, (PROJ, EXP_TWO, RED_TWO), buffers, sems)
    pieces[0] = own[...]
    pieces[1] = left[...]
    pieces[2] = right[...]
    spread_table(Two, first_table, table)
    attend(Two, place, lay, query, pieces, table, att_group, score, prob)
    ungroup(att_group[...], att_token)
    low = att_token[...].reshape(384, D).astype(bf16)
    att[...] = low
    mid = hidden[...] + nn(low, join(w_proj(), 1, 1))
    middle[...] = mid
    end = feed_forward(mid, norms[8:10, :], join(w_exp(), 0, 3), red_of(w_red()), ebias[1:2, :])
    last[...] = end
    final = norm(end, norms[10:12, :])
    where = slot_onehot(slots, sums.shape[0])
    high, low = two_parts(final)
    sums[:, :D] = tn(where, high) + tn(where, low)
    sums[:, D:] = tn(where, jnp.ones((384, 128), bf16))


def feed_forward_back(dhid, mid, gain_bias, w_exp, w_red, bias):
    low = norm(mid, gain_bias).astype(bf16)
    upper = nn(low, w_exp) + bias
    cdf = normal_cdf(upper)
    dz = dhid.astype(bf16)
    grad_red = tn((upper * cdf).astype(bf16), dz)
    slope = cdf + upper * (jnp.exp(-0.5 * upper * upper) * 0.3989422804014327)
    dupper = (nt(dz, w_red) * slope).astype(bf16)
    grad_bias = jnp.sum(dupper.astype(f32), 0, keepdims=True)
    grad_exp = tn(low, dupper)
    dx, dgain, dbias = norm_back(mid, gain_bias, nt(dupper, w_exp))
    return dhid + dx, grad_red, grad_exp, grad_bias, dgain, dbias


def put_cols(grads, first, value):
    devices, width = grads.shape[0], grads.shape[2]
    share = D // devices
    for k in range(value.shape[1] // width):
        part = value[:, k * width : (k + 1) * width].reshape(devices, share, width)
        grads[:, (first + k) * share : (first + k + 1) * share, :] = part.astype(bf16)


def put_red(grads, first, value):
    devices = grads.shape[0]
    share = D // devices
    part = value.reshape(devices, 3 * share, D)
    grads[:, first * share : (first + 3) * share, :] = part.astype(bf16)


def second_back_kernel(
    place, lay, slots, sums, labels, live, hbias, hidden, middle, att, query, own, left, right,
    first_table, late, norms, ebias,
    loss, grad_head, grad_hbias, dhidden, grads, dnorms, debias, dpos, dquery, down, dleft, dright,
    pieces, table, dtable, score, dscore_f, prob, dscore, dpieces, datt, dq_group, dfirst, dq_token, buffers, sems,
):
    w_p, w_h, w_red, w_exp = fetch(late, (PROJ, HEAD, RED_TWO, EXP_TWO), buffers, sems)
    pieces[0] = own[...]
    pieces[1] = left[...]
    pieces[2] = right[...]
    spread_table(Two, first_table, table)
    total, area = sums[:, :D], sums[:, D : D + 1]
    spread_area = jnp.maximum(area, 1.0)
    pooled = (total / spread_area).astype(bf16)
    proj_ref, head_ref = w_p(), w_h()
    w_head = jnp.concatenate([join(proj_ref, 2, 1), join(head_ref, 0, 3)], 1)
    logits = nn(pooled, w_head) + hbias[...]
    weight = live[...] * jnp.where(area > 0.5, 1.0, 0.0)
    count = jnp.maximum(jnp.sum(weight, 0, keepdims=True), 1.0)
    cls = lax.broadcasted_iota(i32, logits.shape, 1)
    onehot = jnp.where(cls == labels[...], 1.0, 0.0)
    top = jnp.max(logits, -1, keepdims=True)
    logsum = jnp.log(jnp.sum(jnp.exp(logits - top), -1, keepdims=True)) + top
    cross = logsum - jnp.sum(onehot * logits, -1, keepdims=True)
    loss[...] = jnp.broadcast_to(jnp.sum(weight * cross, 0, keepdims=True) / count, loss.shape)
    dlogit = ((weight / count) * (jnp.exp(logits - logsum) - onehot)).astype(bf16)
    grad_hbias[...] = jnp.sum(dlogit.astype(f32), 0, keepdims=True)
    share = grad_head.shape[0]
    channel = lax.broadcasted_iota(i32, (D, share), 0)
    mine = lax.broadcasted_iota(i32, (D, share), 1) + place[2]
    own_pooled = nn(pooled, jnp.where(channel == mine, 1.0, 0.0).astype(bf16)).astype(bf16)
    grad_head[...] = tn(own_pooled, dlogit)
    high, low = two_parts(nt(dlogit, w_head) / spread_area)
    where = slot_onehot(slots, sums.shape[0])
    dfinal = nn(where, high) + nn(where, low)
    dhid, dgain, dbias = norm_back(hidden[...], norms[10:12, :], dfinal)
    dnorms[2:3, :] = dgain
    dnorms[3:4, :] = dbias
    dhid, grad_red, grad_exp, grad_bias, dgain, dbias = feed_forward_back(
        dhid, middle[...], norms[8:10, :], join(w_exp(), 0, 3), red_of(w_red()), ebias[1:2, :]
    )
    put_cols(grads, 0, grad_exp)
    put_red(grads, 3, grad_red)
    debias[...] = grad_bias
    dnorms[0:1, :] = dgain
    dnorms[1:2, :] = dbias
    dhidden[...] = dhid
    dy = dhid.astype(bf16)
    put_cols(grads, 6, tn(att[...], dy))
    back = nt(dy, join(proj_ref, 1, 1))
    for g, part in enumerate(grouped(back)):
        datt[g * 96 : (g + 1) * 96, :] = part.astype(bf16)
    attend_back(
        Two, place, lay, query, datt, pieces, table, dq_group, dpieces, dtable,
        score, dscore_f, prob, dscore,
    )
    ungroup(dq_group[...], dq_token)
    dquery[...] = dq_token[...].reshape(384, D).astype(bf16)
    down[...] = dpieces[0]
    dleft[...] = dpieces[1].astype(bf16)
    dright[...] = dpieces[2].astype(bf16)
    dpos[...] = gather_table(Two, dtable, dfirst)


def first_back_kernel(
    place, lay, dhid_in, dquery2, dkv, from_above, from_below, hidden, middle, att, query, keyval,
    left, right, above, below, first_table, late, norms, ebias,
    dhidden, grads, dnorms, debias, dpos, dquery, inner, up, down,
    pieces, table, dtable, score, dscore_f, prob, dscore, dpieces, datt, dq, dfirst, dkv_token, buffers, sems,
):
    w_qkv, w_red, w_exp, w_proj = fetch(late, (QKV_TWO, RED_ONE, EXP_ONE, PROJ), buffers, sems)
    gather_keys_one(keyval, left, right, above, below, pieces)
    spread_table(One, first_table, table)
    for g in range(4):
        top = dkv[g, 0:48, :] + from_above[g].astype(f32)
        bottom = dkv[g, 48:96, :] + from_below[g].astype(f32)
        dkv_token[:, g >> 1, g & 1] = jnp.concatenate([top, bottom], 0).reshape(12, 8, 2 * D)
    dmixed = jnp.concatenate(
        [dquery2[...], dkv_token[...].reshape(384, 2 * D).astype(bf16)], 1
    )
    low = norm(hidden[...], norms[6:8, :]).astype(bf16)
    put_cols(grads, 0, tn(low, dmixed))
    dx, dgain, dbias = norm_back(
        hidden[...], norms[6:8, :], nt(dmixed, join(w_qkv(), 0, 3))
    )
    dnorms[2:3, :] = dgain
    dnorms[3:4, :] = dbias
    dhid, grad_red, grad_exp, grad_bias, dgain, dbias = feed_forward_back(
        dhid_in[...] + dx, middle[...], norms[4:6, :], join(w_exp(), 0, 3), red_of(w_red()), ebias[0:1, :]
    )
    put_cols(grads, 3, grad_exp)
    put_red(grads, 6, grad_red)
    debias[...] = grad_bias
    dnorms[0:1, :] = dgain
    dnorms[1:2, :] = dbias
    dhidden[...] = dhid
    dy = dhid.astype(bf16)
    put_cols(grads, 9, tn(att[...], dy))
    datt[...] = nt(dy, join(w_proj(), 0, 1)).astype(bf16)
    attend_back(
        One, place, lay, query, datt, pieces, table, dq, dpieces, dtable,
        score, dscore_f, prob, dscore,
    )
    dquery[...] = dq[...].astype(bf16)
    up[...] = dpieces[:, 0:48, :].astype(bf16)
    inner[...] = dpieces[:, 48:240, :]
    down[...] = dpieces[:, 240:288, :].astype(bf16)
    dpos[...] = gather_table(One, dtable, dfirst)


def front_back_kernel(
    dhid_in, dquery, inner, from_above, from_below, edge_left, edge_right, hidden, conv, patches,
    early, norms,
    grads, dnorms,
):
    sh = early.shape[1] // 15
    left = edge_left[...].astype(f32).reshape(24, 8, 2 * D)
    right = edge_right[...].astype(f32).reshape(24, 8, 2 * D)
    sub = lax.broadcasted_iota(i32, left.shape, 1)

    def whole(p):
        top = inner[p, 0:48, :] + from_above[p].astype(f32)
        bottom = inner[p, 144:192, :] + from_below[p].astype(f32)
        return jnp.concatenate([top, inner[p, 48:144, :], bottom], 0).reshape(24, 8, 2 * D)

    zero = whole(0) + jnp.where(sub < 4, left, pltpu.roll(right, 4, 1))
    one = whole(1) + jnp.where(sub < 4, pltpu.roll(left, 4, 1), right)
    dkv = jnp.stack([zero, one], 1).reshape(384, 2 * D).astype(bf16)
    dmixed = jnp.concatenate([dquery[...], dkv], 1)
    h = hidden[...]
    low = norm(h, norms[2:4, :]).astype(bf16)
    put_cols(grads, 9, tn(low, dmixed))
    w_qkv = jnp.concatenate(
        [early[:, k * sh : (k + 1) * sh, :].reshape(D, 128) for k in range(9, 15)], 1
    )
    dx, dgain, dbias = norm_back(h, norms[2:4, :], nt(dmixed, w_qkv))
    dnorms[2:3, :] = dgain
    dnorms[3:4, :] = dbias
    dconv, dgain, dbias = norm_back(conv[...], norms[0:2, :], dhid_in[...] + dx)
    dnorms[0:1, :] = dgain
    dnorms[1:2, :] = dbias
    put_cols(grads, 0, tn(dconv.astype(bf16), patches[...]))


def passed_along(value, axis, steps):
    count = lax.axis_size(axis)
    leading, last = (max(0, -steps), min(count, count - steps))
    return lax.ppermute(value, axis, [(source, source + steps) for source in range(leading, last)])


def sum_all(value):
    for axis in ("col", "row"):
        count = lax.axis_size(axis)
        step = 1
        while step < count:
            value = value + lax.ppermute(value, axis, [(i, i ^ step) for i in range(count)])
            step *= 2
    return value


def split_small(value):
    high = lax.reduce_precision(value, 8, 7)
    return jnp.concatenate([high.astype(bf16), (value - high).astype(bf16)], 0)


def join_small(parts):
    rows = parts.shape[-2] // 2
    return parts[..., :rows, :] + parts[..., rows:, :]


def reduce_big(grads):
    part = lax.psum_scatter(grads, "row", scatter_dimension=0, tiled=False)
    return lax.psum(part, "col").astype(f32)


def reduce_last(grads, small):
    devices, count, lanes = grads.shape
    cols = lax.axis_size("col")
    part = count // cols
    extra = small.shape[0] * 2
    value = grads.reshape(devices, cols, part, lanes).transpose(1, 0, 2, 3)
    value = value.reshape(cols, devices * part, lanes)
    value = jnp.concatenate([value, jnp.broadcast_to(split_small(small), (cols, extra, lanes))], 1)
    value = lax.all_to_all(value, "col", 0, 0, tiled=True).astype(f32)
    total = jnp.sum(value, 0)
    small = join_small(total[devices * part :])
    value = total[: devices * part].astype(bf16).reshape(devices, part, lanes)
    value = jnp.concatenate(
        [value, jnp.broadcast_to(split_small(small), (devices, extra, lanes))], 1
    )
    value = lax.all_to_all(value, "row", 0, 0, tiled=True).astype(f32)
    total = jnp.sum(value, 0)
    small = join_small(total[part:])
    main = lax.all_gather(total[:part].astype(bf16), "col", axis=0, tiled=True)
    return main.astype(f32), small


def adamw(weight, grad, first, second):
    first = beta_one * first + (1.0 - beta_one) * grad
    second = beta_two * second + (1.0 - beta_two) * grad * grad
    fix_one = 1.0 - beta_one**STEP
    fix_two = 1.0 - beta_two**STEP
    new = weight - learn_rate * (
        first / fix_one / (jnp.sqrt(second / fix_two) + eps_adam) + decay_rate * weight
    )
    return (first, second, new)


def on_device(
    stem_map, layout, labels, live,
    conv_weight, input_proj, output_proj, expand_weight, reduce_weight, head_weight, small_params,
    first_conv, first_input, first_output, first_expand, first_reduce, first_head, first_small,
    second_conv, second_input, second_output, second_expand, second_reduce, second_head, second_small,
):
    nr = lax.axis_size("row")
    sh = D // nr
    images = labels.shape[0]
    padded = -(-images // 16) * 16
    early, late = run(
        pack_kernel,
        [out((15 * sh, 128), bf16), out((21 * sh, D), bf16)],
        [conv_weight, input_proj, output_proj, expand_weight, reduce_weight, head_weight],
    )
    early = lax.all_gather(early, "row", axis=0)
    late = lax.all_gather(late, "row", axis=0)
    norms = small_params[: 12 * D].reshape(12, D)
    start = 12 * D
    ebias = small_params[start : start + LAYERS * FF].reshape(LAYERS, FF)
    start += LAYERS * FF
    hbias = jnp.pad(small_params[start : start + CLASSES], (0, 24), constant_values=MASKED)[None]
    start += CLASSES
    pos_bias = small_params[start:].reshape(LAYERS * HEADS, 169)
    first_one, first_two = run(
        table_kernel,
        [out((geo.pieces, HEADS * geo.across, 128)) for geo in (One, Two)],
        [jnp.pad(pos_bias, ((0, 0), (0, WIN - 169)))],
    )
    row_first = lax.axis_index("row") * 24
    col_first = lax.axis_index("col") * 16
    place = jnp.stack([row_first, col_first, lax.axis_index("row") * sh]).astype(i32)
    lay_one = layout.reshape(5, 24, 8, 2).transpose(1, 3, 2, 0).reshape(384, 5)
    lay_two = layout.reshape(5, 12, 2, 8, 2).transpose(2, 4, 1, 3, 0).reshape(384, 5)
    above = passed_along(stem_map[-1:], "row", 1)
    rim = jnp.concatenate([above[:, -1:], stem_map[:, -1:]], 0)
    rim = jnp.broadcast_to(passed_along(rim, "col", 1), (49, 8, 128))
    patches, conv_out, hidden0, query1, keyval1, edges1 = run(
        front_kernel,
        [
            out((384, 1152), bf16), out((384, D)), out((384, D)), out((384, D), bf16),
            out((2, 192, 2 * D), bf16), out((2, 192, 2 * D), bf16),
        ],
        [place, stem_map.reshape(1536, 128), above.reshape(32, 128), rim.reshape(392, 128), lay_one, early, norms],
        [pltpu.VMEM((1536, 128), f32), pltpu.VMEM((32, 128), f32)],
        {0: SMEM},
    )
    left1 = passed_along(edges1[1], "col", 1)
    right1 = passed_along(edges1[0], "col", -1)
    ring = lambda rows: jnp.concatenate([keyval1[:, rows], left1[None, rows], right1[None, rows]], 0)
    below1 = passed_along(ring(slice(0, 48)), "row", -1)
    above1 = passed_along(ring(slice(144, 192)), "row", 1)
    anywhere = pl.BlockSpec(memory_space=pl.ANY)
    block = lambda count: [pltpu.VMEM((count, nr, 3 * sh, D), bf16), pltpu.SemaphoreType.DMA((count,))]

    def tiles(geo, back):
        rows, keys = HEADS * geo.queries, geo.keys
        shape = (4, 288, 2 * D) if geo is One else (3, 4, 192, 2 * D)
        square = (rows, keys)
        if not back:
            return [pltpu.VMEM(shape, bf16), pltpu.VMEM(square, f32), pltpu.VMEM(square, f32), pltpu.VMEM(square, bf16)]
        return [
            pltpu.VMEM(shape, bf16), pltpu.VMEM(square, f32), pltpu.VMEM(square, f32), pltpu.VMEM(square, f32),
            pltpu.VMEM(square, f32), pltpu.VMEM(square, bf16), pltpu.VMEM(square, bf16), pltpu.VMEM(shape, f32),
            pltpu.VMEM((384, D), bf16), pltpu.VMEM((384, D), f32),
            pltpu.VMEM((geo.pieces, HEADS * geo.across, 128), f32),
        ]

    near1 = [keyval1, left1, right1, above1, below1, first_one]
    att1, middle1, last1, query2, keyval2 = run(
        first_block_kernel,
        [
            out((384, D), bf16), out((384, D)), out((384, D)), out((384, D), bf16),
            out((4, 96, 2 * D), bf16),
        ],
        [place, lay_one, hidden0, query1, *near1, late, norms, ebias],
        tiles(One, False) + block(4),
        {0: SMEM, 10: anywhere},
    )
    below2 = passed_along(keyval2[:, :48], "row", -1)
    above2 = passed_along(keyval2[:, 48:], "row", 1)
    own2 = jnp.concatenate([above2, keyval2, below2], 1)
    left2 = passed_along(own2, "col", 1)
    right2 = passed_along(own2, "col", -1)
    token5 = lambda width: pltpu.VMEM((12, 2, 2, 8, width), f32)
    near2 = [own2, left2, right2, first_two]
    att2, middle2, last2, sums = run(
        second_block_kernel,
        [out((384, D), bf16), out((384, D)), out((384, D)), out((padded, D + 128))],
        [place, lay_two, lay_one, last1, query2, *near2, late, norms, ebias],
        tiles(Two, False) + [pltpu.VMEM((384, D), f32), token5(D)] + block(3),
        {0: SMEM, 9: anywhere},
    )
    sums = sum_all(sums)
    pad_images = lambda x: jnp.pad(x, (0, padded - images))[:, None]
    (
        loss, grad_head, grad_hbias, dhid, grads2, dnorms2, debias2, dpos2, dquery2, down2, dleft2, dright2,
    ) = run(
        second_back_kernel,
        [
            out((8, 128)), out((sh, 1024)), out((1, 1024)), out((384, D)), out((nr, 7 * sh, D), bf16),
            out((4, D)), out((1, FF)), out((HEADS, WIN)), out((384, D), bf16),
            out((4, 192, 2 * D)), out((4, 192, 2 * D), bf16), out((4, 192, 2 * D), bf16),
        ],
        [
            place, lay_two, lay_one, sums, pad_images(labels), pad_images(live.astype(f32)), hbias,
            last2, middle2, att2, query2, *near2, late, norms, ebias,
        ],
        tiles(Two, True) + [token5(D)] + block(4),
        {0: SMEM, 15: anywhere},
    )
    from_right = passed_along(dleft2, "col", -1)
    from_left = passed_along(dright2, "col", 1)
    whole2 = down2 + from_right.astype(f32) + from_left.astype(f32)
    lower2 = passed_along(whole2[:, :48].astype(bf16), "row", -1)
    upper2 = passed_along(whole2[:, 144:].astype(bf16), "row", 1)
    big2 = reduce_big(grads2)
    dhid, grads1, dnorms1, debias1, dpos1, dquery1, inner1, up1, down1 = run(
        first_back_kernel,
        [
            out((384, D)), out((nr, 10 * sh, D), bf16), out((4, D)), out((1, FF)), out((HEADS, WIN)),
            out((384, D), bf16), out((4, 192, 2 * D)), out((4, 48, 2 * D), bf16), out((4, 48, 2 * D), bf16),
        ],
        [
            place, lay_one, dhid, dquery2, whole2[:, 48:144], upper2, lower2, last1, middle1, att1, query1,
            *near1, late, norms, ebias,
        ],
        tiles(One, True) + [token5(2 * D)] + block(4),
        {0: SMEM, 17: anywhere},
    )
    big1 = reduce_big(grads1)
    lower1 = passed_along(up1, "row", -1)
    upper1 = passed_along(down1, "row", 1)
    sides = inner1[2:] + jnp.concatenate(
        [upper1[2:].astype(f32), jnp.zeros((2, 96, 2 * D), f32), lower1[2:].astype(f32)], 1
    )
    sides = sides.astype(bf16)
    edge_right = passed_along(sides[0], "col", -1)
    edge_left = passed_along(sides[1], "col", 1)
    grads0, dnorms0 = run(
        front_back_kernel,
        [out((nr, 15 * sh, 128), bf16), out((4, D))],
        [
            dhid, dquery1, inner1, upper1, lower1, edge_left, edge_right, hidden0, conv_out, patches,
            early, norms,
        ],
    )
    small = jnp.concatenate(
        [
            dnorms0.reshape(-1), dnorms1.reshape(-1), dnorms2.reshape(-1), debias1[0], debias2[0],
            dpos1[:, :169].reshape(-1), dpos2[:, :169].reshape(-1),
        ]
    )
    width = small.shape[0]
    small = jnp.pad(small, (0, 8192 - width)).reshape(64, 128)
    main, small = reduce_last(grads0, small)
    small = small.reshape(-1)[:width]
    front = 12 * D + LAYERS * FF
    grad_small = jnp.concatenate([small[:front], grad_hbias[0, :CLASSES], small[front:]])
    cols = lambda x, first, count: jnp.concatenate(
        [x[k * sh : (k + 1) * sh] for k in range(first, first + count)], 1
    )
    grads = (
        cols(main, 0, 9).T,
        jnp.stack([cols(main, 9, 6), cols(big1, 0, 3)]),
        jnp.stack([big1[9 * sh :], big2[6 * sh :]]),
        jnp.stack([cols(big1, 3, 3), cols(big2, 0, 3)]),
        jnp.stack([big1[6 * sh : 9 * sh], big2[3 * sh : 6 * sh]]),
        grad_head[:, :CLASSES],
        grad_small,
    )
    params = (
        conv_weight, input_proj, output_proj, expand_weight, reduce_weight, head_weight, small_params,
    )
    firsts = (first_conv, first_input, first_output, first_expand, first_reduce, first_head, first_small)
    seconds = (
        second_conv, second_input, second_output, second_expand, second_reduce, second_head, second_small,
    )
    res = [adamw(w, g, m, v) for w, g, m, v in zip(params, grads, firsts, seconds)]
    return (loss[0, 0], *[entry for triple in res for entry in triple])


def solution(mesh):
    return jax.shard_map(
        on_device,
        mesh=mesh,
        in_specs=(
            P("row", "col", None),
            P(None, "row", "col"),
            P(),
            P(),
            P(None, "row"),
            P(None, "row", None),
            P(None, "row", None),
            P(None, "row", None),
            P(None, "row", None),
            P("row", None),
            P(),
            P(None, "row"),
            P(None, "row", None),
            P(None, "row", None),
            P(None, "row", None),
            P(None, "row", None),
            P("row", None),
            P(),
            P(None, "row"),
            P(None, "row", None),
            P(None, "row", None),
            P(None, "row", None),
            P(None, "row", None),
            P("row", None),
            P(),
        ),
        out_specs=(
            P(),
            P(None, "row"),
            P(None, "row"),
            P(None, "row"),
            P(None, "row", None),
            P(None, "row", None),
            P(None, "row", None),
            P(None, "row", None),
            P(None, "row", None),
            P(None, "row", None),
            P(None, "row", None),
            P(None, "row", None),
            P(None, "row", None),
            P(None, "row", None),
            P(None, "row", None),
            P(None, "row", None),
            P("row", None),
            P("row", None),
            P("row", None),
            P(),
            P(),
            P(),
        ),
        check_vma=False,
    )
```

```python
import functools

import jax
import jax.numpy as jnp
from jax import lax
from jax.experimental import pallas as pl
from jax.experimental.pallas import tpu as pltpu
from jax.sharding import PartitionSpec as P

D = 256
HEADS = 8
FF = 768
CLASSES = 1000
LAYERS = 2
STEP = 5
WIN = 176

eps_norm = 1e-05
beta_one = 0.9
beta_two = 0.999
learn_rate = 0.2
decay_rate = 0.05
eps_adam = 1e-08
scale = (D // HEADS) ** -0.5

bf16 = jnp.bfloat16
f32 = jnp.float32
i32 = jnp.int32
MASKED = -1e30
VMEM = 56 * 1024 * 1024


def nn(a, b):
    return lax.dot_general(a, b, (((1,), (0,)), ((), ())), preferred_element_type=f32)


def nt(a, b):
    return lax.dot_general(a, b, (((1,), (1,)), ((), ())), preferred_element_type=f32)


def tn(a, b):
    return lax.dot_general(a, b, (((0,), (0,)), ((), ())), preferred_element_type=f32)


def two_parts(x):
    high = x.astype(bf16)
    return high, (x - high.astype(f32)).astype(bf16)


def norm_parts(x):
    centre = x - jnp.mean(x, -1, keepdims=True)
    rstd = lax.rsqrt(jnp.mean(centre * centre, -1, keepdims=True) + eps_norm)
    return centre * rstd, rstd


def norm(x, gain_bias):
    return norm_parts(x)[0] * gain_bias[0:1] + gain_bias[1:2]


def norm_back(x, gain_bias, dy):
    xhat, rstd = norm_parts(x)
    dxhat = dy * gain_bias[0:1]
    dx = rstd * (
        dxhat
        - jnp.mean(dxhat, -1, keepdims=True)
        - xhat * jnp.mean(dxhat * xhat, -1, keepdims=True)
    )
    return dx, jnp.sum(dy * xhat, 0, keepdims=True), jnp.sum(dy, 0, keepdims=True)


def normal_cdf(u):
    return 0.5 * (1.0 + lax.erf(u * 0.7071067811865476))


class One:
    dilation, queries, across, pieces, steps = 1, 64, 16, 4, 6
    keys = pieces * 128

    @staticmethod
    def key_col(piece, c8):
        two = 2 * (c8 & 3) + (c8 >> 2)
        return jnp.where(
            piece == 0,
            2 * c8,
            jnp.where(piece == 1, 2 * c8 + 1, jnp.where(piece == 2, two - 8, two + 16)),
        )

    @staticmethod
    def query_col(index):
        return 2 * (index & 7) + (index >> 3)


class Two:
    dilation, queries, across, pieces, steps = 2, 32, 8, 3, 12
    keys = pieces * 128

    @staticmethod
    def key_col(piece, c8):
        return jnp.where(piece == 0, c8, jnp.where(piece == 1, c8 - 8, c8 + 8))

    @staticmethod
    def query_col(index):
        return index


def key_place(geo):
    lane = lax.broadcasted_iota(i32, (1, geo.keys), 1)
    return (lane >> 3) & 15, geo.key_col(lane >> 7, lane & 7)


def window_mask(geo, lay, step, row_first, col_first):
    token = lax.broadcasted_iota(i32, (geo.queries, 1), 0)
    if geo.dilation == 1:
        block = step
        row = block * 4 + (token >> 4)
        col = geo.query_col(token & 15)
        row_pos, col_pos = row_first + row, col_first + col
    else:
        group = step // 3
        block = step - 3 * group
        row = block * 4 + (token >> 3)
        col = token & 7
        row_pos = row_first + 2 * row + (group >> 1)
        col_pos = col_first + 2 * col + (group & 1)

    def begin(place, first, end):
        local = place - first
        extent = end - first
        if geo.dilation == 1:
            index, length = local, extent
        else:
            index, length = local >> 1, (extent - (local & 1) + 1) >> 1
        return jnp.minimum(jnp.maximum(index - 3, 0), length - 7) - index

    row_start = row + begin(row_pos, lay[:, 0:1], lay[:, 1:2])
    col_start = col + begin(col_pos, lay[:, 2:3], lay[:, 3:4])
    key_row, key_col = key_place(geo)
    down = key_row + (block * 4 - 6) - row_start
    right = key_col - col_start
    inside = (down >= 0) & (down <= 6) & (right >= 0) & (right <= 6)
    return jnp.where(inside, 0.0, MASKED).astype(f32)


def position_onehot(geo, across):
    key_row, key_col = key_place(geo)
    right = key_col - geo.query_col(across) + 6
    index = jnp.where((right >= 0) & (right <= 12) & (key_row <= 12), key_row * 13 + right, -1)
    entry = lax.broadcasted_iota(i32, (WIN, geo.keys), 0)
    return jnp.where(entry == index, 1.0, 0.0).astype(bf16)


def position_table(geo, bias, first_ref):
    high = bias.astype(bf16)
    rest = bias - high.astype(f32)
    mid = rest.astype(bf16)
    low = (rest - mid.astype(f32)).astype(bf16)
    for across in range(geo.across):
        onehot = position_onehot(geo, across)
        row = nn(high, onehot) + nn(mid, onehot) + nn(low, onehot)
        for piece in range(geo.pieces):
            lanes = slice(piece * 128, piece * 128 + 128)
            first_ref[piece, pl.ds(across, HEADS, stride=geo.across), :] = row[:, lanes]


def spread_table(geo, first_ref, table_ref):
    for head in range(HEADS):
        for row in range(4):
            for piece in range(geo.pieces):
                lanes = slice(piece * 128, piece * 128 + 128)
                value = first_ref[piece, head * geo.across : (head + 1) * geo.across, :]
                if row:
                    value = pltpu.roll(value, 8 * row, 1)
                begin = head * geo.queries + row * geo.across
                table_ref[begin : begin + geo.across, lanes] = value


def gather_table(geo, table_ref, first_ref):
    for head in range(HEADS):
        for piece in range(geo.pieces):
            lanes = slice(piece * 128, piece * 128 + 128)
            total = None
            for row in range(4):
                begin = head * geo.queries + row * geo.across
                value = table_ref[begin : begin + geo.across, lanes]
                if row:
                    value = pltpu.roll(value, 128 - 8 * row, 1)
                total = value if total is None else total + value
            first_ref[piece, head * geo.across : (head + 1) * geo.across, :] = total
    grad = jnp.zeros((HEADS, WIN), f32)
    for across in range(geo.across):
        onehot = position_onehot(geo, across)
        rows = pl.ds(across, HEADS, stride=geo.across)
        first = [first_ref[piece, rows, :] for piece in range(geo.pieces)]
        high, low = two_parts(jnp.concatenate(first, 1))
        grad = grad + nt(high, onehot) + nt(low, onehot)
    return grad


def head_lanes(head):
    lane = lax.broadcasted_iota(i32, (1, D), 1)
    return jnp.where((lane >> 5) == head, 1.0, 0.0)


def by_head(x):
    return jnp.concatenate([x * head_lanes(h).astype(x.dtype) for h in range(HEADS)], 0)


def from_heads(x):
    count = x.shape[0] // HEADS
    total = None
    for h in range(HEADS):
        part = x[h * count : (h + 1) * count] * head_lanes(h)
        total = part if total is None else total + part
    return total


def key_rows(geo, step):
    if geo.dilation == 1:
        return None, pl.multiple_of(step * 32, 32)
    group = step // 3
    return group, pl.multiple_of((step - 3 * group) * 32, 32)


def load_keys(geo, pieces, step, lanes):
    group, first = key_rows(geo, step)
    if geo.dilation == 1:
        parts = [pieces[p, pl.ds(first, 128), lanes] for p in range(4)]
    else:
        parts = [pieces[p, group, pl.ds(first, 128), lanes] for p in range(3)]
    return jnp.concatenate(parts, 0)


def add_keys(geo, pieces, step, lanes, value):
    group, first = key_rows(geo, step)
    for p in range(geo.pieces):
        part = value[p * 128 : (p + 1) * 128]
        if geo.dilation == 1:
            pieces[p, pl.ds(first, 128), lanes] += part
        else:
            pieces[p, group, pl.ds(first, 128), lanes] += part


KEY = slice(0, D)
VALUE = slice(D, 2 * D)


def softmax_rows(score, table, mask):
    score = score * scale + (table + mask)
    top = jnp.max(score, -1, keepdims=True)
    weight = jnp.exp(score - top)
    return weight * (1.0 / jnp.sum(weight, -1, keepdims=True))


def attend(geo, place, lay_ref, query_ref, pieces, table_ref, out_ref, score_ref, prob_ref):
    count = geo.queries

    def step_of(step, carry):
        rows = pl.ds(pl.multiple_of(step * count, count), count)
        mask = window_mask(geo, lay_ref[rows, :], step, place[0], place[1])
        wide = by_head(query_ref[rows, :])
        score_ref[...] = nt(wide, load_keys(geo, pieces, step, KEY))
        for h in range(HEADS):
            span = slice(h * count, (h + 1) * count)
            prob = softmax_rows(score_ref[span, :], table_ref[span, :], mask)
            prob_ref[span, :] = prob.astype(bf16)
        out = nn(prob_ref[...], load_keys(geo, pieces, step, VALUE))
        out_ref[rows, :] = from_heads(out).astype(out_ref.dtype)
        return carry

    lax.fori_loop(0, geo.steps, step_of, 0)


def attend_back(
    geo, place, lay_ref, query_ref, dout_ref, pieces, table_ref, dquery_ref, dpieces, dtable_ref,
    score_ref, dprob_ref, prob_ref, dscore_ref,
):
    count = geo.queries
    dtable_ref[...] = jnp.zeros_like(dtable_ref)
    dpieces[...] = jnp.zeros_like(dpieces)

    def step_of(step, carry):
        rows = pl.ds(pl.multiple_of(step * count, count), count)
        mask = window_mask(geo, lay_ref[rows, :], step, place[0], place[1])
        wide = by_head(query_ref[rows, :])
        dwide = by_head(dout_ref[rows, :])
        keys = load_keys(geo, pieces, step, KEY)
        score_ref[...] = nt(wide, keys)
        dprob_ref[...] = nt(dwide, load_keys(geo, pieces, step, VALUE))
        for h in range(HEADS):
            span = slice(h * count, (h + 1) * count)
            prob = softmax_rows(score_ref[span, :], table_ref[span, :], mask)
            prob_ref[span, :] = prob.astype(bf16)
            dprob = dprob_ref[span, :]
            dscore = prob * (dprob - jnp.sum(prob * dprob, -1, keepdims=True))
            dtable_ref[span, :] += dscore
            dscore_ref[span, :] = dscore.astype(bf16)
        dscore = dscore_ref[...]
        add_keys(geo, dpieces, step, VALUE, tn(prob_ref[...], dwide))
        add_keys(geo, dpieces, step, KEY, tn(dscore, wide) * scale)
        dquery_ref[rows, :] = from_heads(nn(dscore, keys)) * scale
        return carry

    lax.fori_loop(0, geo.steps, step_of, 0)


def grouped(x):
    parts = x.reshape(12, 2, 2, 8, x.shape[-1])
    return [parts[:, g >> 1, g & 1].reshape(96, x.shape[-1]) for g in range(4)]


def run(kernel, outs, ins, scratch=(), specs=None, flops=0):
    in_specs = [pl.BlockSpec(memory_space=pltpu.VMEM)] * len(ins)
    for index, spec in (specs or {}).items():
        in_specs[index] = spec
    return pl.pallas_call(
        kernel,
        out_shape=outs,
        in_specs=in_specs,
        out_specs=[pl.BlockSpec(memory_space=pltpu.VMEM)] * len(outs),
        scratch_shapes=list(scratch),
        compiler_params=pltpu.CompilerParams(vmem_limit_bytes=VMEM),
        cost_estimate=pl.CostEstimate(flops=flops, bytes_accessed=4 << 20, transcendentals=0),
    )(*ins)


SMEM = pl.BlockSpec(memory_space=pltpu.SMEM)


def out(shape, dtype=f32):
    return jax.ShapeDtypeStruct(shape, dtype)


def pack_kernel(col, conv, qkv, proj, exp, red, head, *refs):
    sh = qkv.shape[1]
    outs, groups = refs[:3], refs[3:]

    def cols(x):
        return [x[:, k * 128 : (k + 1) * 128] for k in range(x.shape[1] // 128)]

    def reds(x):
        return [part for k in range(3) for part in cols(x[k * sh : (k + 1) * sh, :])]

    tail = jnp.concatenate([head[:, 896:], jnp.zeros((sh, 1024 - CLASSES), f32)], 1)
    blocks = (
        cols(conv[...]) + cols(qkv[0]),
        cols(proj[0]) + cols(exp[0]) + reds(red[0]) + cols(qkv[1]),
        cols(proj[1]) + cols(exp[1]) + reds(red[1]) + cols(head[:, :896]) + [tail],
    )
    for result, group, values in zip(outs, groups, blocks):
        for k, value in enumerate(values):
            group[k * sh : (k + 1) * sh, :] = value.astype(bf16)
        empty = group.shape[0] - len(values) * sh
        if empty:
            group[len(values) * sh :, :] = jnp.zeros((empty, 128), bf16)
        part = result.shape[1]
        mine = group[pl.ds(pl.multiple_of(col[0] * part, 16), part), :]
        for row in range(result.shape[0]):
            result[row] = mine


def weight_of(blocks, first, count):
    sh = D // blocks.shape[1]
    per = blocks.shape[2] // sh
    parts = [
        blocks[k // per, :, (k % per) * sh : (k % per + 1) * sh, :].reshape(D, 128)
        for k in range(first, first + count)
    ]
    return jnp.concatenate(parts, 1)


def weight_red(blocks, first):
    rows = blocks.shape[1]
    parts = [weight_of(blocks, first + 2 * k, 2).reshape(rows, 1, D // rows, D) for k in range(3)]
    return jnp.concatenate(parts, 1).reshape(FF, D)


def table_kernel(bias, first_one, first_two):
    position_table(One, bias[0:8, :], first_one)
    position_table(Two, bias[8:16, :], first_two)


def patch_kernel(place, stem, above, left, lay, patches, stem_f, above_f):
    stem_f[...] = stem[...].astype(f32)
    above_f[...] = above[...].astype(f32)
    left_f = left[...].astype(f32)
    tiles = left_f[:384].reshape(24, 2, 8, 128)
    left_odd = tiles[:, 0]
    beside = [left_odd, tiles[:, 1], jnp.concatenate([left_odd[1:], left_f[384:392][None]], 0)]
    phases = []
    for m in range(4):
        part = stem_f[pl.ds(m, 384, stride=4), :].reshape(24, 2, 8, 128)
        even, odd = part[:, 0], part[:, 1]
        top = above_f[pl.ds(m, 8, stride=4), :]
        phases.append([jnp.concatenate([top[None], odd[:-1]], 0), even, odd])
    token = lax.broadcasted_iota(i32, (384, 1), 0)
    row_pos = place[0] + (token >> 4)
    col_pos = place[1] + One.query_col(token & 15)
    inner_row = jnp.where(row_pos == lay[:, 0:1], 0.0, 1.0)
    inner_col = jnp.where(col_pos == lay[:, 2:3], 0.0, 1.0)
    half = lax.broadcasted_iota(i32, (24, 8, 128), 1)
    for a in range(3):
        shifted = jnp.where(half == 0, beside[a], pltpu.roll(phases[3][a], 1, 1))
        taps = (
            (shifted, phases[1][a]),
            (phases[0][a], phases[2][a]),
            (phases[1][a], phases[3][a]),
        )
        for b in range(3):
            value = jnp.stack(taps[b], 1).reshape(384, 128)
            if a == 0:
                value = value * inner_row
            if b == 0:
                value = value * inner_col
            lanes = slice((3 * a + b) * 128, (3 * a + b + 1) * 128)
            patches[:, lanes] = value.astype(bf16)


def front_kernel(patches, early, norms, conv_out, hidden, query, keyval, edge_left, edge_right):
    conv = nt(patches[...], weight_of(early, 0, 9))
    conv_out[...] = conv
    h = norm(conv, norms[0:2, :])
    hidden[...] = h
    low = norm(h, norms[2:4, :]).astype(bf16)
    mixed = nn(low, weight_of(early, 9, 6))
    query[...] = mixed[:, :D].astype(bf16)
    both = mixed[:, D:].reshape(24, 2, 8, 2 * D)
    zero, one = both[:, 0], both[:, 1]
    keyval[0] = zero.reshape(192, 2 * D).astype(bf16)
    keyval[1] = one.reshape(192, 2 * D).astype(bf16)
    sub = lax.broadcasted_iota(i32, zero.shape, 1)
    left = jnp.where(sub < 4, zero, pltpu.roll(one, 4, 1))
    right = jnp.where(sub < 4, pltpu.roll(zero, 4, 1), one)
    edge_left[...] = left.reshape(192, 2 * D).astype(bf16)
    edge_right[...] = right.reshape(192, 2 * D).astype(bf16)


def gather_keys_one(keyval, left, right, above, below, pieces):
    for p in range(4):
        own = keyval[p] if p < 2 else (left, right)[p - 2][...]
        pieces[p, 0:48, :] = above[p]
        pieces[p, 48:240, :] = own
        pieces[p, 240:288, :] = below[p]


def feed_forward(hidden, norms, w_exp, w_red, bias):
    low = norm(hidden, norms).astype(bf16)
    upper = nn(low, w_exp) + bias
    gelu = upper * normal_cdf(upper)
    return hidden + nn(gelu.astype(bf16), w_red)


PROJ, EXP, RED, QKV, HEAD = 0, 2, 8, 14, 14


def fetch(source, buffer, sem):
    copy = pltpu.make_async_copy(source, buffer, sem.at[0])
    copy.start()
    return copy.wait


def first_block_kernel(
    place, lay, hidden, query, keyval, left, right, above, below, first_table, late, norms, ebias,
    att, middle, last, query2, keyval2, up, down,
    pieces, table, score, prob, group, sem,
):
    arrived = fetch(late, group, sem)
    gather_keys_one(keyval, left, right, above, below, pieces)
    spread_table(One, first_table, table)
    attend(One, place, lay, query, pieces, table, att, score, prob)
    arrived()
    mid = hidden[...] + nn(att[...], weight_of(group, PROJ, 2))
    middle[...] = mid
    end = feed_forward(mid, norms[4:6, :], weight_of(group, EXP, 6), weight_red(group, RED), ebias[0:1, :])
    last[...] = end
    low = norm(end, norms[6:8, :]).astype(bf16)
    mixed = nn(low, weight_of(group, QKV, 6))
    for g, part in enumerate(grouped(mixed)):
        query2[g * 96 : (g + 1) * 96, :] = part[:, :D].astype(bf16)
        low = part[:, D:].astype(bf16)
        keyval2[g] = low
        up[g] = low[:48]
        down[g] = low[48:]


def slot_onehot(slots, images):
    entry = lax.broadcasted_iota(i32, (384, images), 1)
    return jnp.where(slots[:, 4:5] == entry, 1.0, 0.0).astype(bf16)


def ungroup(value, ref):
    for g in range(4):
        ref[:, g >> 1, g & 1] = value[g * 96 : (g + 1) * 96].reshape(12, 8, value.shape[-1])


def second_block_kernel(
    place, lay, slots, hidden, query, own, left, right, first_table, late, norms, ebias,
    att, middle, last, sums,
    pieces, table, score, prob, att_group, att_token, group, sem,
):
    arrived = fetch(late, group, sem)
    pieces[0] = own[...]
    pieces[1] = left[...]
    pieces[2] = right[...]
    spread_table(Two, first_table, table)
    attend(Two, place, lay, query, pieces, table, att_group, score, prob)
    ungroup(att_group[...], att_token)
    low = att_token[...].reshape(384, D).astype(bf16)
    att[...] = low
    arrived()
    mid = hidden[...] + nn(low, weight_of(group, PROJ, 2))
    middle[...] = mid
    end = feed_forward(mid, norms[8:10, :], weight_of(group, EXP, 6), weight_red(group, RED), ebias[1:2, :])
    last[...] = end
    final = norm(end, norms[10:12, :])
    images = sums.shape[0] - 8
    where = slot_onehot(slots, images)
    high, low = two_parts(final)
    sums[...] = jnp.zeros_like(sums)
    sums[:images, :D] = tn(where, high) + tn(where, low)
    sums[images:, :images] = tn(jnp.ones((384, 8), bf16), where)


def feed_forward_back(dhid, mid, gain_bias, w_exp, w_red, bias):
    low = norm(mid, gain_bias).astype(bf16)
    upper = nn(low, w_exp) + bias
    cdf = normal_cdf(upper)
    dz = dhid.astype(bf16)
    grad_red = tn((upper * cdf).astype(bf16), dz)
    slope = cdf + upper * (jnp.exp(-0.5 * upper * upper) * 0.3989422804014327)
    dupper = (nt(dz, w_red) * slope).astype(bf16)
    grad_bias = jnp.sum(dupper.astype(f32), 0, keepdims=True)
    grad_exp = tn(low, dupper)
    dx, dgain, dbias = norm_back(mid, gain_bias, nt(dupper, w_exp))
    return dhid + dx, grad_red, grad_exp, grad_bias, dgain, dbias


def put_block(grads, k, value):
    per = grads.shape[1] // D
    grads[k // per, (k % per) * D : (k % per + 1) * D, :] = value.astype(bf16)


def put_cols(grads, first, value):
    for k in range(value.shape[1] // 128):
        put_block(grads, first + k, value[:, k * 128 : (k + 1) * 128])


def put_red(grads, first, value, share):
    parts = value.reshape(D // share, 3, share, D)
    for k in range(3):
        put_cols(grads, first + 2 * k, parts[:, k].reshape(D, D))


def put_zeros(grads, first):
    per = grads.shape[1] // D
    for k in range(first, per * grads.shape[0]):
        put_block(grads, k, jnp.zeros((D, 128), f32))


def second_back_kernel(
    place, lay, slots, sums, labels, live, hbias, hidden, middle, att, query, own, left, right,
    first_table, late, norms, ebias,
    loss, grad_head, grad_hbias, dhidden, grads, dnorms, debias, dpos, dquery, down, dleft, dright,
    pieces, table, dtable, score, dscore_f, prob, dscore, dpieces, datt, dq_group, dfirst, dq_token, group, sem,
):
    arrived = fetch(late, group, sem)
    pieces[0] = own[...]
    pieces[1] = left[...]
    pieces[2] = right[...]
    spread_table(Two, first_table, table)
    images = sums.shape[0] - 8
    total = sums[:images, :D]
    diagonal = lax.broadcasted_iota(i32, (images, images), 0)
    diagonal = diagonal == lax.broadcasted_iota(i32, (images, images), 1)
    area = jnp.where(diagonal, sums[images : images + 1, :images], 0.0)
    area = jnp.sum(area, -1, keepdims=True)
    spread_area = jnp.maximum(area, 1.0)
    pooled = (total / spread_area).astype(bf16)
    arrived()
    w_head = weight_of(group, HEAD, 8)
    logits = nn(pooled, w_head) + hbias[...]
    weight = live[...] * jnp.where(area > 0.5, 1.0, 0.0)
    count = jnp.maximum(jnp.sum(weight, 0, keepdims=True), 1.0)
    cls = lax.broadcasted_iota(i32, logits.shape, 1)
    onehot = jnp.where(cls == labels[...], 1.0, 0.0)
    top = jnp.max(logits, -1, keepdims=True)
    logsum = jnp.log(jnp.sum(jnp.exp(logits - top), -1, keepdims=True)) + top
    cross = logsum - jnp.sum(onehot * logits, -1, keepdims=True)
    loss[...] = jnp.broadcast_to(jnp.sum(weight * cross, 0, keepdims=True) / count, loss.shape)
    dlogit = ((weight / count) * (jnp.exp(logits - logsum) - onehot)).astype(bf16)
    grad_hbias[...] = jnp.sum(dlogit.astype(f32), 0, keepdims=True)
    share = grad_head.shape[0]
    channel = lax.broadcasted_iota(i32, (D, share), 0)
    mine = lax.broadcasted_iota(i32, (D, share), 1) + place[2]
    own_pooled = nn(pooled, jnp.where(channel == mine, 1.0, 0.0).astype(bf16)).astype(bf16)
    grad_head[...] = tn(own_pooled, dlogit)
    high, low = two_parts(nt(dlogit, w_head) / spread_area)
    where = slot_onehot(slots, images)
    dfinal = nn(where, high) + nn(where, low)
    dhid, dgain, dbias = norm_back(hidden[...], norms[10:12, :], dfinal)
    dnorms[2:3, :] = dgain
    dnorms[3:4, :] = dbias
    dhid, grad_red, grad_exp, grad_bias, dgain, dbias = feed_forward_back(
        dhid, middle[...], norms[8:10, :], weight_of(group, EXP, 6), weight_red(group, RED), ebias[1:2, :]
    )
    put_cols(grads, 0, grad_exp)
    put_red(grads, 6, grad_red, share)
    debias[...] = grad_bias
    dnorms[0:1, :] = dgain
    dnorms[1:2, :] = dbias
    dhidden[...] = dhid
    dy = dhid.astype(bf16)
    put_cols(grads, 12, tn(att[...], dy))
    put_zeros(grads, 14)
    back = nt(dy, weight_of(group, PROJ, 2))
    for g, part in enumerate(grouped(back)):
        datt[g * 96 : (g + 1) * 96, :] = part.astype(bf16)
    attend_back(
        Two, place, lay, query, datt, pieces, table, dq_group, dpieces, dtable,
        score, dscore_f, prob, dscore,
    )
    ungroup(dq_group[...], dq_token)
    dquery[...] = dq_token[...].reshape(384, D).astype(bf16)
    down[...] = dpieces[0]
    dleft[...] = dpieces[1].astype(bf16)
    dright[...] = dpieces[2].astype(bf16)
    dpos[...] = gather_table(Two, dtable, dfirst)


def first_back_kernel(
    place, lay, dhid_in, dquery2, dkv, from_left, from_right, from_above, from_below, hidden, middle, att, query, keyval,
    left, right, above, below, first_table, late, norms, ebias,
    dhidden, grads, dnorms, debias, dpos, dquery, inner, up, down,
    pieces, table, dtable, score, dscore_f, prob, dscore, dpieces, datt, dq, dfirst, dkv_token, group, sem,
):
    arrived = fetch(late, group, sem)
    gather_keys_one(keyval, left, right, above, below, pieces)
    spread_table(One, first_table, table)
    for g in range(4):
        rows = slice(48, 144)
        total = dkv[g, rows, :] + from_left[g, rows, :].astype(f32) + from_right[g, rows, :].astype(f32)
        total += jnp.concatenate([from_above[g], from_below[g]], 0).astype(f32)
        dkv_token[:, g >> 1, g & 1] = total.reshape(12, 8, 2 * D)
    dmixed = jnp.concatenate(
        [dquery2[...], dkv_token[...].reshape(384, 2 * D).astype(bf16)], 1
    )
    low = norm(hidden[...], norms[6:8, :]).astype(bf16)
    put_cols(grads, 0, tn(low, dmixed))
    arrived()
    dx, dgain, dbias = norm_back(
        hidden[...], norms[6:8, :], nt(dmixed, weight_of(group, QKV, 6))
    )
    dnorms[2:3, :] = dgain
    dnorms[3:4, :] = dbias
    dhid, grad_red, grad_exp, grad_bias, dgain, dbias = feed_forward_back(
        dhid_in[...] + dx, middle[...], norms[4:6, :], weight_of(group, EXP, 6), weight_red(group, RED), ebias[0:1, :]
    )
    put_cols(grads, 6, grad_exp)
    put_red(grads, 12, grad_red, D // late.shape[1])
    debias[...] = grad_bias
    dnorms[0:1, :] = dgain
    dnorms[1:2, :] = dbias
    dhidden[...] = dhid
    dy = dhid.astype(bf16)
    put_cols(grads, 18, tn(att[...], dy))
    put_zeros(grads, 20)
    datt[...] = nt(dy, weight_of(group, PROJ, 2)).astype(bf16)
    attend_back(
        One, place, lay, query, datt, pieces, table, dq, dpieces, dtable,
        score, dscore_f, prob, dscore,
    )
    dquery[...] = dq[...].astype(bf16)
    up[...] = dpieces[:, 0:48, :].astype(bf16)
    inner[...] = dpieces[:, 48:240, :]
    down[...] = dpieces[:, 240:288, :].astype(bf16)
    dpos[...] = gather_table(One, dtable, dfirst)


SMALL_ROWS = 80


def front_back_kernel(
    dhid_in, dquery, inner, from_above, from_below, edge_left, edge_right, hidden, conv, patches,
    early, norms, dnorms1, dnorms2, debias1, debias2, dpos1, dpos2,
    grads, small,
):
    left = edge_left[...].astype(f32).reshape(24, 8, 2 * D)
    right = edge_right[...].astype(f32).reshape(24, 8, 2 * D)
    sub = lax.broadcasted_iota(i32, left.shape, 1)

    def whole(p):
        top = inner[p, 0:48, :] + from_above[p].astype(f32)
        bottom = inner[p, 144:192, :] + from_below[p].astype(f32)
        return jnp.concatenate([top, inner[p, 48:144, :], bottom], 0).reshape(24, 8, 2 * D)

    zero = whole(0) + jnp.where(sub < 4, left, pltpu.roll(right, 4, 1))
    one = whole(1) + jnp.where(sub < 4, pltpu.roll(left, 4, 1), right)
    dkv = jnp.stack([zero, one], 1).reshape(384, 2 * D).astype(bf16)
    dmixed = jnp.concatenate([dquery[...], dkv], 1)
    h = hidden[...]
    low = norm(h, norms[2:4, :]).astype(bf16)
    put_cols(grads, 9, tn(low, dmixed))
    w_qkv = weight_of(early, 9, 6)
    dx, dgain1, dbias1 = norm_back(h, norms[2:4, :], nt(dmixed, w_qkv))
    dconv, dgain0, dbias0 = norm_back(conv[...], norms[0:2, :], dhid_in[...] + dx)
    put_cols(grads, 0, tn(dconv.astype(bf16), patches[...]))
    put_zeros(grads, 15)

    def place_row(first, value):
        for k in range(value.shape[1] // 128):
            small[first + k : first + k + 1, :] = value[:, k * 128 : (k + 1) * 128]

    small[...] = jnp.zeros_like(small)
    for k, value in enumerate((dgain0, dbias0, dgain1, dbias1)):
        place_row(2 * k, value)
    for k in range(4):
        place_row(8 + 2 * k, dnorms1[k : k + 1, :])
        place_row(16 + 2 * k, dnorms2[k : k + 1, :])
    place_row(24, debias1[...])
    place_row(30, debias2[...])
    for first, value in ((40, dpos1), (56, dpos2)):
        small[first : first + 8, :] = value[:, :128]
        small[first + 8 : first + 16, : WIN - 128] = value[:, 128:]
    high, low = two_parts(small[...])
    begin = grads.shape[1] - 2 * SMALL_ROWS
    for col in range(grads.shape[0]):
        grads[col, begin : begin + SMALL_ROWS, :] = high
        grads[col, begin + SMALL_ROWS :, :] = low


def small_of(parts, index, begin):
    high = parts[index, begin : begin + SMALL_ROWS, :].astype(f32)
    return high + parts[index, begin + SMALL_ROWS : begin + 2 * SMALL_ROWS, :].astype(f32)


def add_up(parts, rows):
    total = parts[0, rows, :].astype(f32)
    for index in range(1, parts.shape[0]):
        total += parts[index, rows, :].astype(f32)
    return total


def between_kernel(second, first, parts, result):
    rows = result.shape[0]
    sh = D // rows
    begin = 0
    for group in (second, first):
        for k in range(group.shape[0] // D):
            result[:, begin : begin + sh, :] = group[k * D : (k + 1) * D, :].reshape(rows, sh, 128)
            begin += sh
    for k in range(parts.shape[1] // D):
        total = add_up(parts, slice(k * D, (k + 1) * D)).astype(bf16)
        result[:, begin : begin + sh, :] = total.reshape(rows, sh, 128)
        begin += sh
    low_rows = parts.shape[1] - 2 * SMALL_ROWS
    total = small_of(parts, 0, low_rows)
    for col in range(1, parts.shape[0]):
        total += small_of(parts, col, low_rows)
    high, low = two_parts(total)
    for row in range(rows):
        result[row, begin : begin + SMALL_ROWS, :] = high
        result[row, begin + SMALL_ROWS :, :] = low


def last_sum_kernel(parts, result, small):
    count = result.shape[0]
    result[...] = add_up(parts, slice(0, count)).astype(bf16)
    total = small_of(parts, 0, count)
    for row in range(1, parts.shape[0]):
        total += small_of(parts, row, count)
    small[...] = total


def adamw(weight, grad, first, second):
    first = beta_one * first + (1.0 - beta_one) * grad
    second = beta_two * second + (1.0 - beta_two) * grad * grad
    fix_one = 1.0 - beta_one**STEP
    fix_two = 1.0 - beta_two**STEP
    new = weight - learn_rate * (
        first / fix_one / (jnp.sqrt(second / fix_two) + eps_adam) + decay_rate * weight
    )
    return (first, second, new)


def adamw_kernel(grads, *refs, sh, per):
    ins = [refs[3 * n : 3 * n + 3] for n in range(5)]
    outs = [refs[15 + 3 * n : 18 + 3 * n] for n in range(5)]

    def update(n, group, k, *where):
        begin = (sum(per[:group]) + k % per[group]) * sh
        grad = grads[k // per[group], begin : begin + sh, :].astype(f32)
        weight, first, second = (ref[where] for ref in ins[n])
        for ref, value in zip(outs[n], adamw(weight, grad, first, second)):
            ref[where] = value

    every = slice(None)
    for k in range(9):
        update(0, 2, k, every, slice(k * 128, (k + 1) * 128))
    for k in range(6):
        lanes = slice(k * 128, (k + 1) * 128)
        update(1, 2, 9 + k, 0, every, lanes)
        update(1, 1, k, 1, every, lanes)
        update(3, 1, 6 + k, 0, every, lanes)
        update(3, 0, k, 1, every, lanes)
        rows, half = slice((k // 2) * sh, (k // 2 + 1) * sh), slice((k % 2) * 128, (k % 2 + 1) * 128)
        update(4, 1, 12 + k, 0, rows, half)
        update(4, 0, 6 + k, 1, rows, half)
    for k in range(2):
        lanes = slice(k * 128, (k + 1) * 128)
        update(2, 1, 18 + k, 0, every, lanes)
        update(2, 0, 12 + k, 1, every, lanes)


def passed_along(value, axis, steps):
    count = lax.axis_size(axis)
    leading, last = (max(0, -steps), min(count, count - steps))
    return lax.ppermute(value, axis, [(source, source + steps) for source in range(leading, last)])


def sum_all(value):
    for axis in ("col", "row"):
        count = lax.axis_size(axis)
        step = 1
        while step < count:
            value = value + lax.ppermute(value, axis, [(i, i ^ step) for i in range(count)])
            step *= 2
    return value


def on_device(
    stem_map, layout, labels, live,
    conv_weight, input_proj, output_proj, expand_weight, reduce_weight, head_weight, small_params,
    first_conv, first_input, first_output, first_expand, first_reduce, first_head, first_small,
    second_conv, second_input, second_output, second_expand, second_reduce, second_head, second_small,
):
    nr, nc = lax.axis_size("row"), lax.axis_size("col")
    sh = D // nr
    images = labels.shape[0]
    padded = -(-images // 8) * 8
    per = [-(-count // nc) for count in (14, 20, 15)]
    row_index, col_index = lax.axis_index("row"), lax.axis_index("col")
    parts = [-(-count // nc) * sh for count in (15, 20, 22)]
    early, late1, late2 = run(
        pack_kernel,
        [out((nr, part, 128), bf16) for part in parts],
        [
            col_index.astype(i32)[None], conv_weight.T, input_proj, output_proj, expand_weight, reduce_weight,
            head_weight,
        ],
        [pltpu.VMEM((part * nc, 128), bf16) for part in parts],
        {0: SMEM},
    )
    early = lax.all_to_all(early, "row", 0, 0, tiled=True)
    early, late = lax.optimization_barrier((early, jnp.concatenate([late1, late2], 1)))
    late = lax.all_to_all(late, "row", 0, 0, tiled=True)
    norms = small_params[: 12 * D].reshape(12, D)
    start = 12 * D
    ebias = small_params[start : start + LAYERS * FF].reshape(LAYERS, FF)
    start += LAYERS * FF
    hbias = jnp.pad(small_params[start : start + CLASSES], (0, 24), constant_values=MASKED)[None]
    start += CLASSES
    pos_bias = small_params[start:].reshape(LAYERS * HEADS, 169)
    first_one, first_two = run(
        table_kernel,
        [out((geo.pieces, HEADS * geo.across, 128)) for geo in (One, Two)],
        [jnp.pad(pos_bias, ((0, 0), (0, WIN - 169)))],
    )
    place = jnp.stack([row_index * 24, col_index * 16, row_index * sh]).astype(i32)
    lay_one = layout.reshape(5, 24, 8, 2).transpose(1, 3, 2, 0).reshape(384, 5)
    lay_two = layout.reshape(5, 12, 2, 8, 2).transpose(2, 4, 1, 3, 0).reshape(384, 5)
    above = passed_along(stem_map[-1:], "row", 1)
    rim = jnp.concatenate([above[:, -1:], stem_map[:, -1:]], 0)
    rim = jnp.broadcast_to(passed_along(rim, "col", 1), (49, 8, 128))
    patches = run(
        patch_kernel,
        [out((384, 1152), bf16)],
        [place, stem_map.reshape(1536, 128), above.reshape(32, 128), rim.reshape(392, 128), lay_one],
        [pltpu.VMEM((1536, 128), f32), pltpu.VMEM((32, 128), f32)],
        {0: SMEM},
    )[0]
    early = lax.all_gather(early, "col", axis=0)
    late, patches = lax.optimization_barrier((late, patches))
    late1 = lax.all_gather(late[:, : parts[1]], "col", axis=0)
    late2 = lax.all_gather(late[:, parts[1] :], "col", axis=0)
    conv_out, hidden0, query1, keyval1, edge_left, edge_right = run(
        front_kernel,
        [
            out((384, D)), out((384, D)), out((384, D), bf16), out((2, 192, 2 * D), bf16),
            out((192, 2 * D), bf16), out((192, 2 * D), bf16),
        ],
        [patches, early, norms],
    )
    left1 = passed_along(edge_right, "col", 1)
    right1 = passed_along(edge_left, "col", -1)
    ring = lambda rows: jnp.concatenate([keyval1[:, rows], left1[None, rows], right1[None, rows]], 0)
    below1 = passed_along(ring(slice(0, 48)), "row", -1)
    above1 = passed_along(ring(slice(144, 192)), "row", 1)
    anywhere = pl.BlockSpec(memory_space=pl.ANY)
    block = lambda group: [pltpu.VMEM(group.shape, bf16), pltpu.SemaphoreType.DMA((1,))]

    def tiles(geo, back):
        square = (HEADS * geo.queries, geo.keys)
        shape = (4, 288, 2 * D) if geo is One else (3, 4, 192, 2 * D)
        wide, narrow = pltpu.VMEM(square, f32), pltpu.VMEM(square, bf16)
        if not back:
            return [pltpu.VMEM(shape, bf16), wide, wide, narrow]
        return [
            pltpu.VMEM(shape, bf16), wide, wide, wide, wide, narrow, narrow, pltpu.VMEM(shape, f32),
            pltpu.VMEM((384, D), bf16), pltpu.VMEM((384, D), f32),
            pltpu.VMEM((geo.pieces, HEADS * geo.across, 128), f32),
        ]

    token5 = lambda width: pltpu.VMEM((12, 2, 2, 8, width), f32)
    tokens, rows48, ext = out((384, D)), out((4, 48, 2 * D), bf16), out((4, 192, 2 * D), bf16)
    tokens_low = out((384, D), bf16)
    near1 = [keyval1, left1, right1, above1, below1, first_one]
    att1, middle1, last1, query2, keyval2, up2, down2 = run(
        first_block_kernel,
        [tokens_low, tokens, tokens, tokens_low, out((4, 96, 2 * D), bf16), rows48, rows48],
        [place, lay_one, hidden0, query1, *near1, late1, norms, ebias],
        tiles(One, False) + block(late1),
        {0: SMEM, 10: anywhere},
    )
    below2 = passed_along(up2, "row", -1)
    above2 = passed_along(down2, "row", 1)
    own2 = jnp.concatenate([above2, keyval2, below2], 1)
    left2 = passed_along(own2, "col", 1)
    right2 = passed_along(own2, "col", -1)
    near2 = [own2, left2, right2, first_two]
    att2, middle2, last2, sums = run(
        second_block_kernel,
        [tokens_low, tokens, tokens, out((padded + 8, max(D, -(-padded // 128) * 128)))],
        [place, lay_two, lay_one, last1, query2, *near2, late2, norms, ebias],
        tiles(Two, False) + [pltpu.VMEM((384, D), f32), token5(D)] + block(late2),
        {0: SMEM, 9: anywhere},
    )
    sums = sum_all(sums)
    pad_images = lambda x: jnp.pad(x, (0, padded - images))[:, None]
    (
        loss, grad_head, grad_hbias, dhid, grads2, dnorms2, debias2, dpos2, dquery2, down2, dleft2, dright2,
    ) = run(
        second_back_kernel,
        [
            out((8, 128)), out((sh, 1024)), out((1, 1024)), tokens, out((nc, per[0] * D, 128), bf16),
            out((4, D)), out((1, FF)), out((HEADS, WIN)), tokens_low,
            out((4, 192, 2 * D)), ext, ext,
        ],
        [
            place, lay_two, lay_one, sums, pad_images(labels), pad_images(live.astype(f32)), hbias,
            last2, middle2, att2, query2, *near2, late2, norms, ebias,
        ],
        tiles(Two, True) + [token5(D)] + block(late2),
        {0: SMEM, 15: anywhere},
    )
    from_right = passed_along(dleft2, "col", -1)
    from_left = passed_along(dright2, "col", 1)
    rim2 = lambda rows: (
        down2[:, rows] + from_left[:, rows].astype(f32) + from_right[:, rows].astype(f32)
    ).astype(bf16)
    lower2 = passed_along(rim2(slice(0, 48)), "row", -1)
    upper2 = passed_along(rim2(slice(144, 192)), "row", 1)
    grads2 = lax.psum_scatter(grads2, "col", scatter_dimension=0, tiled=False)
    dhid, grads1, dnorms1, debias1, dpos1, dquery1, inner1, up1, down1 = run(
        first_back_kernel,
        [
            tokens, out((nc, per[1] * D, 128), bf16), out((4, D)), out((1, FF)), out((HEADS, WIN)),
            tokens_low, out((4, 192, 2 * D)), rows48, rows48,
        ],
        [
            place, lay_one, dhid, dquery2, down2, from_left, from_right, upper2, lower2, last1, middle1, att1, query1,
            *near1, late1, norms, ebias,
        ],
        tiles(One, True) + [token5(2 * D)] + block(late1),
        {0: SMEM, 19: anywhere},
    )
    lower1 = passed_along(up1, "row", -1)
    upper1 = passed_along(down1, "row", 1)
    grads1 = lax.psum_scatter(grads1, "col", scatter_dimension=0, tiled=False)
    sides = inner1[2:] + jnp.concatenate(
        [upper1[2:].astype(f32), jnp.zeros((2, 96, 2 * D), f32), lower1[2:].astype(f32)], 1
    )
    sides = sides.astype(bf16)
    edge_right = passed_along(sides[0], "col", -1)
    edge_left = passed_along(sides[1], "col", 1)
    grads0, _ = run(
        front_back_kernel,
        [out((nc, per[2] * D + 2 * SMALL_ROWS, 128), bf16), out((SMALL_ROWS, 128))],
        [
            dhid, dquery1, inner1, upper1, lower1, edge_left, edge_right, hidden0, conv_out, patches,
            early, norms, dnorms1, dnorms2, debias1, debias2, dpos1, dpos2,
        ],
    )
    grads0 = lax.all_to_all(grads0, "col", 0, 0, tiled=True)
    grads0 = run(
        between_kernel,
        [out((nr, sum(per) * sh + 2 * SMALL_ROWS, 128), bf16)],
        [grads2, grads1, grads0],
    )[0]
    grads0 = lax.all_to_all(grads0, "row", 0, 0, tiled=True)
    mine, small = run(
        last_sum_kernel,
        [out((sum(per) * sh, 128), bf16), out((SMALL_ROWS, 128))],
        [grads0],
    )
    grads = lax.all_gather(mine, "col", axis=0)
    wide = [
        conv_weight.T, first_conv.T, second_conv.T, input_proj, first_input, second_input,
        output_proj, first_output, second_output, expand_weight, first_expand, second_expand,
        reduce_weight, first_reduce, second_reduce,
    ]
    new = run(
        functools.partial(adamw_kernel, sh=sh, per=per), [out(x.shape) for x in wide], [grads, *wide]
    )
    new = [x.T for x in new[:3]] + list(new[3:])
    pos = [
        jnp.concatenate([small[k : k + 8], small[k + 8 : k + 16, : 169 - 128]], 1).reshape(-1)
        for k in (40, 56)
    ]
    grad_small = jnp.concatenate([small[:36].reshape(-1), grad_hbias[0, :CLASSES], *pos])
    head = adamw(head_weight, grad_head[:, :CLASSES], first_head, second_head)
    return (loss[0, 0], *new, *head, *adamw(small_params, grad_small, first_small, second_small))


def solution(mesh):
    return jax.shard_map(
        on_device,
        mesh=mesh,
        in_specs=(
            P("row", "col", None),
            P(None, "row", "col"),
            P(),
            P(),
            P(None, "row"),
            P(None, "row", None),
            P(None, "row", None),
            P(None, "row", None),
            P(None, "row", None),
            P("row", None),
            P(),
            P(None, "row"),
            P(None, "row", None),
            P(None, "row", None),
            P(None, "row", None),
            P(None, "row", None),
            P("row", None),
            P(),
            P(None, "row"),
            P(None, "row", None),
            P(None, "row", None),
            P(None, "row", None),
            P(None, "row", None),
            P("row", None),
            P(),
        ),
        out_specs=(
            P(),
            P(None, "row"),
            P(None, "row"),
            P(None, "row"),
            P(None, "row", None),
            P(None, "row", None),
            P(None, "row", None),
            P(None, "row", None),
            P(None, "row", None),
            P(None, "row", None),
            P(None, "row", None),
            P(None, "row", None),
            P(None, "row", None),
            P(None, "row", None),
            P(None, "row", None),
            P(None, "row", None),
            P("row", None),
            P("row", None),
            P("row", None),
            P(),
            P(),
            P(),
        ),
        check_vma=False,
    )
```

```python
import functools

import jax
import jax.numpy as jnp
from jax import lax
from jax.experimental import pallas as pl
from jax.experimental.pallas import tpu as pltpu
from jax.sharding import PartitionSpec as P

D = 256
HEADS = 8
FF = 768
CLASSES = 1000
LAYERS = 2
STEP = 5
WIN = 176

eps_norm = 1e-05
beta_one = 0.9
beta_two = 0.999
learn_rate = 0.2
decay_rate = 0.05
eps_adam = 1e-08
scale = (D // HEADS) ** -0.5

bf16 = jnp.bfloat16
f32 = jnp.float32
i32 = jnp.int32
MASKED = -1e30
MIB = 1024 * 1024


def nn(a, b):
    return lax.dot_general(a, b, (((1,), (0,)), ((), ())), preferred_element_type=f32)


def nt(a, b):
    return lax.dot_general(a, b, (((1,), (1,)), ((), ())), preferred_element_type=f32)


def tn(a, b):
    return lax.dot_general(a, b, (((0,), (0,)), ((), ())), preferred_element_type=f32)


def two_parts(x):
    high = x.astype(bf16)
    return high, (x - high.astype(f32)).astype(bf16)


def norm_parts(x):
    centre = x - jnp.mean(x, -1, keepdims=True)
    rstd = lax.rsqrt(jnp.mean(centre * centre, -1, keepdims=True) + eps_norm)
    return centre * rstd, rstd


def norm(x, gain_bias):
    return norm_parts(x)[0] * gain_bias[0:1] + gain_bias[1:2]


def norm_back(x, gain_bias, dy):
    xhat, rstd = norm_parts(x)
    dxhat = dy * gain_bias[0:1]
    dx = rstd * (
        dxhat
        - jnp.mean(dxhat, -1, keepdims=True)
        - xhat * jnp.mean(dxhat * xhat, -1, keepdims=True)
    )
    return dx, jnp.sum(dy * xhat, 0, keepdims=True), jnp.sum(dy, 0, keepdims=True)


def normal_cdf(u):
    return 0.5 * (1.0 + lax.erf(u * 0.7071067811865476))


class One:
    dilation, queries, across, pieces, steps = 1, 64, 16, 4, 6
    keys = pieces * 128

    @staticmethod
    def key_col(piece, c8):
        two = 2 * (c8 & 3) + (c8 >> 2)
        return jnp.where(
            piece == 0,
            2 * c8,
            jnp.where(piece == 1, 2 * c8 + 1, jnp.where(piece == 2, two - 8, two + 16)),
        )

    @staticmethod
    def query_col(index):
        return 2 * (index & 7) + (index >> 3)


class Two:
    dilation, queries, across, pieces, steps = 2, 32, 8, 3, 12
    keys = pieces * 128

    @staticmethod
    def key_col(piece, c8):
        return jnp.where(piece == 0, c8, jnp.where(piece == 1, c8 - 8, c8 + 8))

    @staticmethod
    def query_col(index):
        return index


def key_place(geo):
    lane = lax.broadcasted_iota(i32, (1, geo.keys), 1)
    return (lane >> 3) & 15, geo.key_col(lane >> 7, lane & 7)


def window_mask(geo, lay, step, row_first, col_first):
    token = lax.broadcasted_iota(i32, (geo.queries, 1), 0)
    if geo.dilation == 1:
        block = step
        row = block * 4 + (token >> 4)
        col = geo.query_col(token & 15)
        row_pos, col_pos = row_first + row, col_first + col
    else:
        group = step // 3
        block = step - 3 * group
        row = block * 4 + (token >> 3)
        col = token & 7
        row_pos = row_first + 2 * row + (group >> 1)
        col_pos = col_first + 2 * col + (group & 1)

    def begin(place, first, end):
        local = place - first
        extent = end - first
        if geo.dilation == 1:
            index, length = local, extent
        else:
            index, length = local >> 1, (extent - (local & 1) + 1) >> 1
        return jnp.minimum(jnp.maximum(index - 3, 0), length - 7) - index

    row_start = row + begin(row_pos, lay[:, 0:1], lay[:, 1:2])
    col_start = col + begin(col_pos, lay[:, 2:3], lay[:, 3:4])
    key_row, key_col = key_place(geo)
    down = key_row + (block * 4 - 6) - row_start
    right = key_col - col_start
    inside = (down >= 0) & (down <= 6) & (right >= 0) & (right <= 6)
    return jnp.where(inside, 0.0, MASKED).astype(f32)


def position_onehot(geo, across):
    key_row, key_col = key_place(geo)
    right = key_col - geo.query_col(across) + 6
    index = jnp.where((right >= 0) & (right <= 12) & (key_row <= 12), key_row * 13 + right, -1)
    entry = lax.broadcasted_iota(i32, (WIN, geo.keys), 0)
    return jnp.where(entry == index, 1.0, 0.0).astype(bf16)


def position_table(geo, bias, first_ref):
    high = bias.astype(bf16)
    rest = bias - high.astype(f32)
    mid = rest.astype(bf16)
    low = (rest - mid.astype(f32)).astype(bf16)
    for across in range(geo.across):
        onehot = position_onehot(geo, across)
        row = nn(high, onehot) + nn(mid, onehot) + nn(low, onehot)
        for piece in range(geo.pieces):
            lanes = slice(piece * 128, piece * 128 + 128)
            first_ref[piece, pl.ds(across, HEADS, stride=geo.across), :] = row[:, lanes]


def spread_table(geo, first_ref, table_ref):
    for head in range(HEADS):
        for row in range(4):
            for piece in range(geo.pieces):
                lanes = slice(piece * 128, piece * 128 + 128)
                value = first_ref[piece, head * geo.across : (head + 1) * geo.across, :]
                if row:
                    value = pltpu.roll(value, 8 * row, 1)
                begin = head * geo.queries + row * geo.across
                table_ref[begin : begin + geo.across, lanes] = value


def gather_table(geo, table_ref, first_ref):
    for head in range(HEADS):
        for piece in range(geo.pieces):
            lanes = slice(piece * 128, piece * 128 + 128)
            total = None
            for row in range(4):
                begin = head * geo.queries + row * geo.across
                value = table_ref[begin : begin + geo.across, lanes]
                if row:
                    value = pltpu.roll(value, 128 - 8 * row, 1)
                total = value if total is None else total + value
            first_ref[piece, head * geo.across : (head + 1) * geo.across, :] = total
    grad = jnp.zeros((HEADS, WIN), f32)
    for across in range(geo.across):
        onehot = position_onehot(geo, across)
        rows = pl.ds(across, HEADS, stride=geo.across)
        first = [first_ref[piece, rows, :] for piece in range(geo.pieces)]
        high, low = two_parts(jnp.concatenate(first, 1))
        grad = grad + nt(high, onehot) + nt(low, onehot)
    return grad


def head_lanes(head):
    lane = lax.broadcasted_iota(i32, (1, D), 1)
    return jnp.where((lane >> 5) == head, 1.0, 0.0)


def by_head(x):
    return jnp.concatenate([x * head_lanes(h).astype(x.dtype) for h in range(HEADS)], 0)


def from_heads(x):
    count = x.shape[0] // HEADS
    total = None
    for h in range(HEADS):
        part = x[h * count : (h + 1) * count] * head_lanes(h)
        total = part if total is None else total + part
    return total


def key_rows(geo, step):
    if geo.dilation == 1:
        return None, pl.multiple_of(step * 32, 32)
    group = step // 3
    return group, pl.multiple_of((step - 3 * group) * 32, 32)


def load_keys(geo, pieces, step, lanes):
    group, first = key_rows(geo, step)
    if geo.dilation == 1:
        parts = [pieces[p, pl.ds(first, 128), lanes] for p in range(4)]
    else:
        parts = [pieces[p, group, pl.ds(first, 128), lanes] for p in range(3)]
    return jnp.concatenate(parts, 0)


def add_keys(geo, pieces, step, lanes, value):
    group, first = key_rows(geo, step)
    for p in range(geo.pieces):
        part = value[p * 128 : (p + 1) * 128]
        if geo.dilation == 1:
            pieces[p, pl.ds(first, 128), lanes] += part
        else:
            pieces[p, group, pl.ds(first, 128), lanes] += part


KEY = slice(0, D)
VALUE = slice(D, 2 * D)


def softmax_rows(score, table, mask):
    score = score * scale + (table + mask)
    top = jnp.max(score, -1, keepdims=True)
    weight = jnp.exp(score - top)
    return weight * (1.0 / jnp.sum(weight, -1, keepdims=True))


def attend(geo, place, lay_ref, query_ref, pieces, table_ref, out_ref, score_ref, prob_ref):
    count = geo.queries

    def step_of(step, carry):
        rows = pl.ds(pl.multiple_of(step * count, count), count)
        mask = window_mask(geo, lay_ref[rows, :], step, place[0], place[1])
        wide = by_head(query_ref[rows, :])
        score_ref[...] = nt(wide, load_keys(geo, pieces, step, KEY))
        for h in range(HEADS):
            span = slice(h * count, (h + 1) * count)
            prob = softmax_rows(score_ref[span, :], table_ref[span, :], mask)
            prob_ref[span, :] = prob.astype(bf16)
        out = nn(prob_ref[...], load_keys(geo, pieces, step, VALUE))
        out_ref[rows, :] = from_heads(out).astype(out_ref.dtype)
        return carry

    lax.fori_loop(0, geo.steps, step_of, 0)


def attend_back(
    geo, place, lay_ref, query_ref, dout_ref, pieces, table_ref, dquery_ref, dpieces, dtable_ref,
    score_ref, dprob_ref, prob_ref, dscore_ref,
):
    count = geo.queries
    dtable_ref[...] = jnp.zeros_like(dtable_ref)
    dpieces[...] = jnp.zeros_like(dpieces)

    def step_of(step, carry):
        rows = pl.ds(pl.multiple_of(step * count, count), count)
        mask = window_mask(geo, lay_ref[rows, :], step, place[0], place[1])
        wide = by_head(query_ref[rows, :])
        dwide = by_head(dout_ref[rows, :])
        keys = load_keys(geo, pieces, step, KEY)
        score_ref[...] = nt(wide, keys)
        dprob_ref[...] = nt(dwide, load_keys(geo, pieces, step, VALUE))
        for h in range(HEADS):
            span = slice(h * count, (h + 1) * count)
            prob = softmax_rows(score_ref[span, :], table_ref[span, :], mask)
            prob_ref[span, :] = prob.astype(bf16)
            dprob = dprob_ref[span, :]
            dscore = prob * (dprob - jnp.sum(prob * dprob, -1, keepdims=True))
            dtable_ref[span, :] += dscore
            dscore_ref[span, :] = dscore.astype(bf16)
        dscore = dscore_ref[...]
        add_keys(geo, dpieces, step, VALUE, tn(prob_ref[...], dwide))
        add_keys(geo, dpieces, step, KEY, tn(dscore, wide) * scale)
        dquery_ref[rows, :] = from_heads(nn(dscore, keys)) * scale
        return carry

    lax.fori_loop(0, geo.steps, step_of, 0)


def grouped(x):
    parts = x.reshape(12, 2, 2, 8, x.shape[-1])
    return [parts[:, g >> 1, g & 1].reshape(96, x.shape[-1]) for g in range(4)]


EVEN_ROW, EVEN_COL = 3, 4


def send(place, even, first, second, after, before):
    for ref, when_even, when_odd in ((first, after, before), (second, before, after)):

        @pl.when(place[even] == 1)
        def _(ref=ref, value=when_even):
            ref[...] = value()

        @pl.when(place[even] == 0)
        def _(ref=ref, value=when_odd):
            ref[...] = value()


def received(place, even, first, second):
    flag = place[even].astype(f32)
    one, two = first.astype(f32), second.astype(f32)
    return two * flag + one * (1.0 - flag), one * flag + two * (1.0 - flag)


def store_received(place, even, first, second, before, after):
    @pl.when(place[even] == 1)
    def _():
        before(second)
        after(first)

    @pl.when(place[even] == 0)
    def _():
        before(first)
        after(second)


def run(kernel, outs, ins, scratch=(), specs=None, vmem=16):
    in_specs = [pl.BlockSpec(memory_space=pltpu.VMEM)] * len(ins)
    for index, spec in (specs or {}).items():
        in_specs[index] = spec
    return pl.pallas_call(
        kernel,
        out_shape=outs,
        in_specs=in_specs,
        out_specs=[pl.BlockSpec(memory_space=pltpu.VMEM)] * len(outs),
        scratch_shapes=list(scratch),
        compiler_params=pltpu.CompilerParams(vmem_limit_bytes=vmem * MIB),
        cost_estimate=pl.CostEstimate(flops=0, bytes_accessed=4 << 20, transcendentals=0),
    )(*ins)


SMEM = pl.BlockSpec(memory_space=pltpu.SMEM)


def out(shape, dtype=f32):
    return jax.ShapeDtypeStruct(shape, dtype)


def pack_kernel(col, conv, qkv, proj, exp, red, head, *refs, across):
    sh = qkv.shape[1]
    outs, groups = refs[:2], refs[2:]

    def cols(x):
        return [x[:, k * 128 : (k + 1) * 128] for k in range(x.shape[1] // 128)]

    def reds(x):
        return [part for k in range(3) for part in cols(x[k * sh : (k + 1) * sh, :])]

    tail = jnp.concatenate([head[:, 896:], jnp.zeros((sh, 1024 - CLASSES), f32)], 1)
    blocks = (
        cols(conv[...]) + cols(qkv[0]),
        cols(proj[0]) + cols(exp[0]) + reds(red[0]) + cols(qkv[1]),
        cols(proj[1]) + cols(exp[1]) + reds(red[1]) + cols(head[:, :896]) + [tail],
    )
    begin = 0
    for index, (group, values) in enumerate(zip(groups, blocks)):
        for k, value in enumerate(values):
            group[k * sh : (k + 1) * sh, :] = value.astype(bf16)
        empty = group.shape[0] - len(values) * sh
        if empty:
            group[len(values) * sh :, :] = jnp.zeros((empty, 128), bf16)
        result = outs[min(index, 1)]
        begin = begin if index == 2 else 0
        part = group.shape[0] // across
        mine = group[pl.ds(pl.multiple_of(col[0] * part, 16), part), :]
        for row in range(result.shape[0]):
            result[row, begin : begin + part, :] = mine
        begin += part


def weight_of(blocks, first, count):
    sh = D // blocks.shape[1]
    per = blocks.shape[2] // sh
    parts = [
        blocks[k // per, :, (k % per) * sh : (k % per + 1) * sh, :].reshape(D, 128)
        for k in range(first, first + count)
    ]
    return jnp.concatenate(parts, 1)


def weight_red(blocks, first):
    rows = blocks.shape[1]
    parts = [weight_of(blocks, first + 2 * k, 2).reshape(rows, 1, D // rows, D) for k in range(3)]
    return jnp.concatenate(parts, 1).reshape(FF, D)


def table_kernel(bias, first_one, first_two):
    position_table(One, bias[0:8, :], first_one)
    position_table(Two, bias[8:16, :], first_two)


def patch_kernel(place, stem, above, left, lay, patches, stem_f, above_f):
    stem_f[...] = stem[...].astype(f32)
    above_f[...] = above[...].astype(f32)
    left_f = left[...].astype(f32)
    tiles = left_f[:384].reshape(24, 2, 8, 128)
    left_odd = tiles[:, 0]
    beside = [left_odd, tiles[:, 1], jnp.concatenate([left_odd[1:], left_f[384:392][None]], 0)]
    phases = []
    for m in range(4):
        part = stem_f[pl.ds(m, 384, stride=4), :].reshape(24, 2, 8, 128)
        even, odd = part[:, 0], part[:, 1]
        top = above_f[pl.ds(m, 8, stride=4), :]
        phases.append([jnp.concatenate([top[None], odd[:-1]], 0), even, odd])
    token = lax.broadcasted_iota(i32, (384, 1), 0)
    row_pos = place[0] + (token >> 4)
    col_pos = place[1] + One.query_col(token & 15)
    inner_row = jnp.where(row_pos == lay[:, 0:1], 0.0, 1.0)
    inner_col = jnp.where(col_pos == lay[:, 2:3], 0.0, 1.0)
    half = lax.broadcasted_iota(i32, (24, 8, 128), 1)
    for a in range(3):
        shifted = jnp.where(half == 0, beside[a], pltpu.roll(phases[3][a], 1, 1))
        taps = (
            (shifted, phases[1][a]),
            (phases[0][a], phases[2][a]),
            (phases[1][a], phases[3][a]),
        )
        for b in range(3):
            value = jnp.stack(taps[b], 1).reshape(384, 128)
            if a == 0:
                value = value * inner_row
            if b == 0:
                value = value * inner_col
            lanes = slice((3 * a + b) * 128, (3 * a + b + 1) * 128)
            patches[:, lanes] = value.astype(bf16)


def front_kernel(place, patches, early, norms, conv_out, hidden, query, keyval, first, second):
    conv = nt(patches[...], weight_of(early, 0, 9))
    conv_out[...] = conv
    h = norm(conv, norms[0:2, :])
    hidden[...] = h
    low = norm(h, norms[2:4, :]).astype(bf16)
    mixed = nn(low, weight_of(early, 9, 6))
    query[...] = mixed[:, :D].astype(bf16)
    both = mixed[:, D:].reshape(24, 2, 8, 2 * D)
    zero, one = both[:, 0], both[:, 1]
    keyval[0] = zero.reshape(192, 2 * D).astype(bf16)
    keyval[1] = one.reshape(192, 2 * D).astype(bf16)
    sub = lax.broadcasted_iota(i32, zero.shape, 1)
    left = jnp.where(sub < 4, zero, pltpu.roll(one, 4, 1))
    right = jnp.where(sub < 4, pltpu.roll(zero, 4, 1), one)
    send(
        place, EVEN_COL, first, second,
        lambda: right.reshape(192, 2 * D).astype(bf16), lambda: left.reshape(192, 2 * D).astype(bf16),
    )


def ring_kernel(place, keyval, first, second, row_first, row_second):
    def put(ref, begin):
        rows = slice(begin, begin + 48)
        ref[0] = keyval[0, rows, :]
        ref[1] = keyval[1, rows, :]

        def left(source):
            ref[2] = source[rows, :]

        def right(source):
            ref[3] = source[rows, :]

        store_received(place, EVEN_COL, first, second, left, right)

    @pl.when(place[EVEN_ROW] == 1)
    def _():
        put(row_first, 144)
        put(row_second, 0)

    @pl.when(place[EVEN_ROW] == 0)
    def _():
        put(row_first, 0)
        put(row_second, 144)


def gather_keys_one(place, keyval, col_first, col_second, row_first, row_second, pieces):
    pieces[0, 48:240, :] = keyval[0]
    pieces[1, 48:240, :] = keyval[1]

    def into(index, rows):
        def put(source):
            pieces[index, rows, :] = source[...]

        return put

    every = slice(None)
    middle = slice(48, 240)
    store_received(place, EVEN_COL, col_first, col_second, into(2, middle), into(3, middle))
    store_received(
        place, EVEN_ROW, row_first, row_second, into(every, slice(0, 48)), into(every, slice(240, 288))
    )


def gather_keys_two(place, own, first, second, pieces):
    pieces[0] = own[...]

    def into(index):
        def put(source):
            pieces[index] = source[...]

        return put

    store_received(place, EVEN_COL, first, second, into(1), into(2))


def extend_kernel(place, keyval, first, second, result):
    result[:, 48:144, :] = keyval[...]

    def above(source):
        result[:, 0:48, :] = source[...]

    def below(source):
        result[:, 144:192, :] = source[...]

    store_received(place, EVEN_ROW, first, second, above, below)


def rim_kernel(place, own, first, second, row_first, row_second):
    def total(begin):
        rows = slice(begin, begin + 48)
        value = own[:, rows, :] + first[:, rows, :].astype(f32) + second[:, rows, :].astype(f32)
        return value.astype(bf16)

    send(place, EVEN_ROW, row_first, row_second, lambda: total(144), lambda: total(0))


def sides_kernel(place, inner, first, second, col_first, col_second):
    def total(p):
        above, below = received(place, EVEN_ROW, first[p], second[p])
        rows = [inner[p, 0:48, :] + above, inner[p, 48:144, :], inner[p, 144:192, :] + below]
        return jnp.concatenate(rows, 0).astype(bf16)

    send(place, EVEN_COL, col_first, col_second, lambda: total(3), lambda: total(2))


def feed_forward(hidden, norms, w_exp, w_red, bias):
    low = norm(hidden, norms).astype(bf16)
    upper = nn(low, w_exp) + bias
    gelu = upper * normal_cdf(upper)
    return hidden + nn(gelu.astype(bf16), w_red)


PROJ, EXP, RED, QKV, HEAD = 0, 2, 8, 14, 14


def fetch(source, buffer, sem):
    copy = pltpu.make_async_copy(source, buffer, sem.at[0])
    copy.start()
    return copy.wait


def first_block_kernel(
    place, lay, hidden, query, keyval, cola, colb, rowa, rowb, first_table, late, norms, ebias,
    att, middle, last, query2, keyval2, first, second,
    pieces, table, score, prob, group, sem,
):
    arrived = fetch(late, group, sem)
    gather_keys_one(place, keyval, cola, colb, rowa, rowb, pieces)
    spread_table(One, first_table, table)
    attend(One, place, lay, query, pieces, table, att, score, prob)
    arrived()
    mid = hidden[...] + nn(att[...], weight_of(group, PROJ, 2))
    middle[...] = mid
    end = feed_forward(mid, norms[4:6, :], weight_of(group, EXP, 6), weight_red(group, RED), ebias[0:1, :])
    last[...] = end
    low = norm(end, norms[6:8, :]).astype(bf16)
    mixed = nn(low, weight_of(group, QKV, 6))
    for g, part in enumerate(grouped(mixed)):
        query2[g * 96 : (g + 1) * 96, :] = part[:, :D].astype(bf16)
        keyval2[g] = part[:, D:].astype(bf16)
    send(
        place, EVEN_ROW, first, second, lambda: keyval2[:, 48:, :], lambda: keyval2[:, :48, :]
    )


def slot_onehot(slots, images):
    entry = lax.broadcasted_iota(i32, (384, images), 1)
    return jnp.where(slots[:, 4:5] == entry, 1.0, 0.0).astype(bf16)


def ungroup(value, ref):
    for g in range(4):
        ref[:, g >> 1, g & 1] = value[g * 96 : (g + 1) * 96].reshape(12, 8, value.shape[-1])


def second_block_kernel(
    place, lay, slots, hidden, query, own, cola, colb, first_table, late, norms, ebias,
    att, middle, last, sums,
    pieces, table, score, prob, att_group, att_token, group, sem,
):
    arrived = fetch(late, group, sem)
    gather_keys_two(place, own, cola, colb, pieces)
    spread_table(Two, first_table, table)
    attend(Two, place, lay, query, pieces, table, att_group, score, prob)
    ungroup(att_group[...], att_token)
    low = att_token[...].reshape(384, D).astype(bf16)
    att[...] = low
    arrived()
    mid = hidden[...] + nn(low, weight_of(group, PROJ, 2))
    middle[...] = mid
    end = feed_forward(mid, norms[8:10, :], weight_of(group, EXP, 6), weight_red(group, RED), ebias[1:2, :])
    last[...] = end
    final = norm(end, norms[10:12, :])
    images = sums.shape[0] - 8
    where = slot_onehot(slots, images)
    high, low = two_parts(final)
    sums[...] = jnp.zeros_like(sums)
    sums[:images, :D] = tn(where, high) + tn(where, low)
    sums[images:, :images] = tn(jnp.ones((384, 8), bf16), where)


def feed_forward_back(dhid, mid, gain_bias, w_exp, w_red, bias):
    low = norm(mid, gain_bias).astype(bf16)
    upper = nn(low, w_exp) + bias
    cdf = normal_cdf(upper)
    dz = dhid.astype(bf16)
    grad_red = tn((upper * cdf).astype(bf16), dz)
    slope = cdf + upper * (jnp.exp(-0.5 * upper * upper) * 0.3989422804014327)
    dupper = (nt(dz, w_red) * slope).astype(bf16)
    grad_bias = jnp.sum(dupper.astype(f32), 0, keepdims=True)
    grad_exp = tn(low, dupper)
    dx, dgain, dbias = norm_back(mid, gain_bias, nt(dupper, w_exp))
    return dhid + dx, grad_red, grad_exp, grad_bias, dgain, dbias


def put_block(grads, k, value):
    per = grads.shape[1] // D
    grads[k // per, (k % per) * D : (k % per + 1) * D, :] = value.astype(bf16)


def put_cols(grads, first, value):
    for k in range(value.shape[1] // 128):
        put_block(grads, first + k, value[:, k * 128 : (k + 1) * 128])


def put_red(grads, first, value, share):
    parts = value.reshape(D // share, 3, share, D)
    for k in range(3):
        put_cols(grads, first + 2 * k, parts[:, k].reshape(D, D))


def put_zeros(grads, first):
    per = grads.shape[1] // D
    for k in range(first, per * grads.shape[0]):
        put_block(grads, k, jnp.zeros((D, 128), f32))


def second_back_kernel(
    place, lay, slots, sums, labels, live, hbias, hidden, middle, att, query, own, cola, colb,
    first_table, late, norms, ebias,
    loss, grad_head, grad_hbias, dhidden, grads, dnorms, debias, dpos, dquery, down, first, second,
    pieces, table, dtable, score, dscore_f, prob, dscore, dpieces, datt, dq_group, dfirst, dq_token, group, sem,
):
    arrived = fetch(late, group, sem)
    gather_keys_two(place, own, cola, colb, pieces)
    spread_table(Two, first_table, table)
    images = sums.shape[0] - 8
    total = sums[:images, :D]
    diagonal = lax.broadcasted_iota(i32, (images, images), 0)
    diagonal = diagonal == lax.broadcasted_iota(i32, (images, images), 1)
    area = jnp.where(diagonal, sums[images : images + 1, :images], 0.0)
    area = jnp.sum(area, -1, keepdims=True)
    spread_area = jnp.maximum(area, 1.0)
    pooled = (total / spread_area).astype(bf16)
    arrived()
    w_head = weight_of(group, HEAD, 8)
    logits = nn(pooled, w_head) + hbias[...]
    weight = live[...] * jnp.where(area > 0.5, 1.0, 0.0)
    count = jnp.maximum(jnp.sum(weight, 0, keepdims=True), 1.0)
    cls = lax.broadcasted_iota(i32, logits.shape, 1)
    onehot = jnp.where(cls == labels[...], 1.0, 0.0)
    top = jnp.max(logits, -1, keepdims=True)
    logsum = jnp.log(jnp.sum(jnp.exp(logits - top), -1, keepdims=True)) + top
    cross = logsum - jnp.sum(onehot * logits, -1, keepdims=True)
    loss[...] = jnp.broadcast_to(jnp.sum(weight * cross, 0, keepdims=True) / count, loss.shape)
    dlogit = ((weight / count) * (jnp.exp(logits - logsum) - onehot)).astype(bf16)
    grad_hbias[...] = jnp.sum(dlogit.astype(f32), 0, keepdims=True)
    share = grad_head.shape[0]
    channel = lax.broadcasted_iota(i32, (D, share), 0)
    mine = lax.broadcasted_iota(i32, (D, share), 1) + place[2]
    own_pooled = nn(pooled, jnp.where(channel == mine, 1.0, 0.0).astype(bf16)).astype(bf16)
    grad_head[...] = tn(own_pooled, dlogit)
    high, low = two_parts(nt(dlogit, w_head) / spread_area)
    where = slot_onehot(slots, images)
    dfinal = nn(where, high) + nn(where, low)
    dhid, dgain, dbias = norm_back(hidden[...], norms[10:12, :], dfinal)
    dnorms[2:3, :] = dgain
    dnorms[3:4, :] = dbias
    dhid, grad_red, grad_exp, grad_bias, dgain, dbias = feed_forward_back(
        dhid, middle[...], norms[8:10, :], weight_of(group, EXP, 6), weight_red(group, RED), ebias[1:2, :]
    )
    put_cols(grads, 0, grad_exp)
    put_red(grads, 6, grad_red, share)
    debias[...] = grad_bias
    dnorms[0:1, :] = dgain
    dnorms[1:2, :] = dbias
    dhidden[...] = dhid
    dy = dhid.astype(bf16)
    put_cols(grads, 12, tn(att[...], dy))
    put_zeros(grads, 14)
    back = nt(dy, weight_of(group, PROJ, 2))
    for g, part in enumerate(grouped(back)):
        datt[g * 96 : (g + 1) * 96, :] = part.astype(bf16)
    attend_back(
        Two, place, lay, query, datt, pieces, table, dq_group, dpieces, dtable,
        score, dscore_f, prob, dscore,
    )
    ungroup(dq_group[...], dq_token)
    dquery[...] = dq_token[...].reshape(384, D).astype(bf16)
    down[...] = dpieces[0]
    send(
        place, EVEN_COL, first, second,
        lambda: dpieces[2].astype(bf16), lambda: dpieces[1].astype(bf16),
    )
    dpos[...] = gather_table(Two, dtable, dfirst)


def first_back_kernel(
    place, lay, dhid_in, dquery2, dkv, dcola, dcolb, drowa, drowb, hidden, middle, att, query, keyval,
    cola, colb, rowa, rowb, first_table, late, norms, ebias,
    dhidden, grads, dnorms, debias, dpos, dquery, inner, first, second,
    pieces, table, dtable, score, dscore_f, prob, dscore, dpieces, datt, dq, dfirst, dkv_token, group, sem,
):
    arrived = fetch(late, group, sem)
    gather_keys_one(place, keyval, cola, colb, rowa, rowb, pieces)
    spread_table(One, first_table, table)
    for g in range(4):
        rows = slice(48, 144)
        total = dkv[g, rows, :] + dcola[g, rows, :].astype(f32) + dcolb[g, rows, :].astype(f32)
        total += jnp.concatenate(received(place, EVEN_ROW, drowa[g], drowb[g]), 0)
        dkv_token[:, g >> 1, g & 1] = total.reshape(12, 8, 2 * D)
    dmixed = jnp.concatenate(
        [dquery2[...], dkv_token[...].reshape(384, 2 * D).astype(bf16)], 1
    )
    low = norm(hidden[...], norms[6:8, :]).astype(bf16)
    put_cols(grads, 0, tn(low, dmixed))
    arrived()
    dx, dgain, dbias = norm_back(
        hidden[...], norms[6:8, :], nt(dmixed, weight_of(group, QKV, 6))
    )
    dnorms[2:3, :] = dgain
    dnorms[3:4, :] = dbias
    dhid, grad_red, grad_exp, grad_bias, dgain, dbias = feed_forward_back(
        dhid_in[...] + dx, middle[...], norms[4:6, :], weight_of(group, EXP, 6), weight_red(group, RED), ebias[0:1, :]
    )
    put_cols(grads, 6, grad_exp)
    put_red(grads, 12, grad_red, D // late.shape[1])
    debias[...] = grad_bias
    dnorms[0:1, :] = dgain
    dnorms[1:2, :] = dbias
    dhidden[...] = dhid
    dy = dhid.astype(bf16)
    put_cols(grads, 18, tn(att[...], dy))
    put_zeros(grads, 20)
    datt[...] = nt(dy, weight_of(group, PROJ, 2)).astype(bf16)
    attend_back(
        One, place, lay, query, datt, pieces, table, dq, dpieces, dtable,
        score, dscore_f, prob, dscore,
    )
    dquery[...] = dq[...].astype(bf16)
    inner[...] = dpieces[:, 48:240, :]
    send(
        place, EVEN_ROW, first, second,
        lambda: dpieces[:, 240:288, :].astype(bf16), lambda: dpieces[:, 0:48, :].astype(bf16),
    )
    dpos[...] = gather_table(One, dtable, dfirst)


SMALL_ROWS = 80


def front_back_kernel(
    place, dhid_in, dquery, inner, drowa, drowb, dcola, dcolb, hidden, conv, patches, early,
    norms, dnorms1, dnorms2, debias1, debias2, dpos1, dpos2,
    grads, small,
):
    left, right = received(place, EVEN_COL, dcola[...], dcolb[...])
    left, right = left.reshape(24, 8, 2 * D), right.reshape(24, 8, 2 * D)
    sub = lax.broadcasted_iota(i32, left.shape, 1)

    def whole(p):
        above, below = received(place, EVEN_ROW, drowa[p], drowb[p])
        top = inner[p, 0:48, :] + above
        bottom = inner[p, 144:192, :] + below
        return jnp.concatenate([top, inner[p, 48:144, :], bottom], 0).reshape(24, 8, 2 * D)

    zero = whole(0) + jnp.where(sub < 4, left, pltpu.roll(right, 4, 1))
    one = whole(1) + jnp.where(sub < 4, pltpu.roll(left, 4, 1), right)
    dkv = jnp.stack([zero, one], 1).reshape(384, 2 * D).astype(bf16)
    dmixed = jnp.concatenate([dquery[...], dkv], 1)
    h = hidden[...]
    low = norm(h, norms[2:4, :]).astype(bf16)
    put_cols(grads, 9, tn(low, dmixed))
    w_qkv = weight_of(early, 9, 6)
    dx, dgain1, dbias1 = norm_back(h, norms[2:4, :], nt(dmixed, w_qkv))
    dconv, dgain0, dbias0 = norm_back(conv[...], norms[0:2, :], dhid_in[...] + dx)
    put_cols(grads, 0, tn(dconv.astype(bf16), patches[...]))
    put_zeros(grads, 15)

    def place_row(first, value):
        for k in range(value.shape[1] // 128):
            small[first + k : first + k + 1, :] = value[:, k * 128 : (k + 1) * 128]

    small[...] = jnp.zeros_like(small)
    for k, value in enumerate((dgain0, dbias0, dgain1, dbias1)):
        place_row(2 * k, value)
    for k in range(4):
        place_row(8 + 2 * k, dnorms1[k : k + 1, :])
        place_row(16 + 2 * k, dnorms2[k : k + 1, :])
    place_row(24, debias1[...])
    place_row(30, debias2[...])
    for first, value in ((40, dpos1), (56, dpos2)):
        small[first : first + 8, :] = value[:, :128]
        small[first + 8 : first + 16, : WIN - 128] = value[:, 128:]
    high, low = two_parts(small[...])
    begin = grads.shape[1] - 2 * SMALL_ROWS
    for col in range(grads.shape[0]):
        grads[col, begin : begin + SMALL_ROWS, :] = high
        grads[col, begin + SMALL_ROWS :, :] = low


def small_of(parts, index, begin):
    high = parts[index, begin : begin + SMALL_ROWS, :].astype(f32)
    return high + parts[index, begin + SMALL_ROWS : begin + 2 * SMALL_ROWS, :].astype(f32)


def add_up(parts, rows):
    total = parts[0, rows, :].astype(f32)
    for index in range(1, parts.shape[0]):
        total += parts[index, rows, :].astype(f32)
    return total


def between_kernel(second, first, parts, result):
    rows = result.shape[0]
    sh = D // rows
    begin = 0
    for group in (second, first):
        for k in range(group.shape[0] // D):
            result[:, begin : begin + sh, :] = group[k * D : (k + 1) * D, :].reshape(rows, sh, 128)
            begin += sh
    for k in range(parts.shape[1] // D):
        total = add_up(parts, slice(k * D, (k + 1) * D)).astype(bf16)
        result[:, begin : begin + sh, :] = total.reshape(rows, sh, 128)
        begin += sh
    low_rows = parts.shape[1] - 2 * SMALL_ROWS
    total = small_of(parts, 0, low_rows)
    for col in range(1, parts.shape[0]):
        total += small_of(parts, col, low_rows)
    high, low = two_parts(total)
    for row in range(rows):
        result[row, begin : begin + SMALL_ROWS, :] = high
        result[row, begin + SMALL_ROWS :, :] = low


def last_sum_kernel(parts, result, small):
    count = result.shape[0]
    result[...] = add_up(parts, slice(0, count)).astype(bf16)
    total = small_of(parts, 0, count)
    for row in range(1, parts.shape[0]):
        total += small_of(parts, row, count)
    small[...] = total


def adamw(weight, grad, first, second):
    first = beta_one * first + (1.0 - beta_one) * grad
    second = beta_two * second + (1.0 - beta_two) * grad * grad
    fix_one = 1.0 - beta_one**STEP
    fix_two = 1.0 - beta_two**STEP
    new = weight - learn_rate * (
        first / fix_one / (jnp.sqrt(second / fix_two) + eps_adam) + decay_rate * weight
    )
    return (first, second, new)


def adamw_kernel(grads, *refs, sh, per):
    ins = [refs[3 * n : 3 * n + 3] for n in range(5)]
    outs = [refs[15 + 3 * n : 18 + 3 * n] for n in range(5)]

    def update(n, group, k, *where):
        begin = (sum(per[:group]) + k % per[group]) * sh
        grad = grads[k // per[group], begin : begin + sh, :].astype(f32)
        weight, first, second = (ref[where] for ref in ins[n])
        for ref, value in zip(outs[n], adamw(weight, grad, first, second)):
            ref[where] = value

    every = slice(None)
    for k in range(9):
        update(0, 2, k, every, slice(k * 128, (k + 1) * 128))
    for k in range(6):
        lanes = slice(k * 128, (k + 1) * 128)
        update(1, 2, 9 + k, 0, every, lanes)
        update(1, 1, k, 1, every, lanes)
        update(3, 1, 6 + k, 0, every, lanes)
        update(3, 0, k, 1, every, lanes)
        rows, half = slice((k // 2) * sh, (k // 2 + 1) * sh), slice((k % 2) * 128, (k % 2 + 1) * 128)
        update(4, 1, 12 + k, 0, rows, half)
        update(4, 0, 6 + k, 1, rows, half)
    for k in range(2):
        lanes = slice(k * 128, (k + 1) * 128)
        update(2, 1, 18 + k, 0, every, lanes)
        update(2, 0, 12 + k, 1, every, lanes)


def onward(value, axis):
    count = lax.axis_size(axis)
    return lax.ppermute(value, axis, [(i, (i + 1) % count) for i in range(count)])


def swaps(first, second, axis):
    count = lax.axis_size(axis)
    pairs = [[(i, i + 1) for i in range(begin, count - 1, 2)] for begin in (0, 1)]
    both = [low + [(j, i) for i, j in low] for low in pairs]
    return lax.ppermute(first, axis, both[0]), lax.ppermute(second, axis, both[1])


def sum_all(value):
    for axis in ("col", "row"):
        count = lax.axis_size(axis)
        step = 1

        def other(flip):
            return lax.ppermute(value, axis, [(i, i ^ flip) for i in range(count)])

        while step < count:
            if 4 * step <= count:
                near, far, both = other(step), other(2 * step), other(3 * step)
                value = (value + near) + (far + both)
                step *= 4
            else:
                value = value + other(step)
                step *= 2
    return value


def on_device(
    stem_map, layout, labels, live,
    conv_weight, input_proj, output_proj, expand_weight, reduce_weight, head_weight, small_params,
    first_conv, first_input, first_output, first_expand, first_reduce, first_head, first_small,
    second_conv, second_input, second_output, second_expand, second_reduce, second_head, second_small,
):
    nr, nc = lax.axis_size("row"), lax.axis_size("col")
    sh = D // nr
    images = labels.shape[0]
    padded = -(-images // 8) * 8
    per = [-(-count // nc) for count in (14, 20, 15)]
    row_index, col_index = lax.axis_index("row"), lax.axis_index("col")
    parts = [-(-count // nc) * sh for count in (15, 20, 22)]
    early, late = run(
        functools.partial(pack_kernel, across=nc),
        [out((nr, parts[0], 128), bf16), out((nr, parts[1] + parts[2], 128), bf16)],
        [
            col_index.astype(i32)[None], conv_weight.T, input_proj, output_proj, expand_weight, reduce_weight,
            head_weight,
        ],
        [pltpu.VMEM((part * nc, 128), bf16) for part in parts],
        {0: SMEM},
        56,
    )
    early = lax.all_to_all(early, "row", 0, 0, tiled=True)
    norms = small_params[: 12 * D].reshape(12, D)
    start = 12 * D
    ebias = small_params[start : start + LAYERS * FF].reshape(LAYERS, FF)
    start += LAYERS * FF
    hbias = jnp.pad(small_params[start : start + CLASSES], (0, 24), constant_values=MASKED)[None]
    start += CLASSES
    pos_bias = small_params[start:].reshape(LAYERS * HEADS, 169)
    first_one, first_two = run(
        table_kernel,
        [out((geo.pieces, HEADS * geo.across, 128)) for geo in (One, Two)],
        [jnp.pad(pos_bias, ((0, 0), (0, WIN - 169)))],
    )
    place = [row_index * 24, col_index * 16, row_index * sh, (row_index + 1) % 2, (col_index + 1) % 2]
    place = jnp.stack(place).astype(i32)
    lay_one = layout.reshape(5, 24, 8, 2).transpose(1, 3, 2, 0).reshape(384, 5)
    lay_two = layout.reshape(5, 12, 2, 8, 2).transpose(2, 4, 1, 3, 0).reshape(384, 5)
    above = onward(stem_map[-1:], "row")
    rim = jnp.concatenate([above[:, -1:], stem_map[:, -1:]], 0)
    rim = jnp.broadcast_to(onward(rim, "col"), (49, 8, 128))
    patches = run(
        patch_kernel,
        [out((384, 1152), bf16)],
        [place, stem_map.reshape(1536, 128), above.reshape(32, 128), rim.reshape(392, 128), lay_one],
        [pltpu.VMEM((1536, 128), f32), pltpu.VMEM((32, 128), f32)],
        {0: SMEM},
    )[0]
    late, _, _ = lax.optimization_barrier((late, above, early))
    early = lax.all_gather(early, "col", axis=0)
    late = lax.all_to_all(late, "row", 0, 0, tiled=True)
    rows48, edge = out((4, 48, 2 * D), bf16), out((192, 2 * D), bf16)
    conv_out, hidden0, query1, keyval1, *edges = run(
        front_kernel,
        [out((384, D)), out((384, D)), out((384, D), bf16), out((2, 192, 2 * D), bf16), edge, edge],
        [place, patches, early, norms],
        specs={0: SMEM},
    )
    late, _ = lax.optimization_barrier((late, edges))
    late1 = lax.all_gather(late[:, : parts[1]], "col", axis=0)
    late2 = lax.all_gather(late[:, parts[1] :], "col", axis=0)
    cols1 = swaps(*edges, "col")
    rows1 = swaps(*run(ring_kernel, [rows48] * 2, [place, keyval1, *cols1], specs={0: SMEM}), "row")
    anywhere = pl.BlockSpec(memory_space=pl.ANY)
    block = lambda group: [pltpu.VMEM(group.shape, bf16), pltpu.SemaphoreType.DMA((1,))]

    def tiles(geo, back):
        square = (HEADS * geo.queries, geo.keys)
        shape = (4, 288, 2 * D) if geo is One else (3, 4, 192, 2 * D)
        wide, narrow = pltpu.VMEM(square, f32), pltpu.VMEM(square, bf16)
        if not back:
            return [pltpu.VMEM(shape, bf16), wide, wide, narrow]
        return [
            pltpu.VMEM(shape, bf16), wide, wide, wide, wide, narrow, narrow, pltpu.VMEM(shape, f32),
            pltpu.VMEM((384, D), bf16), pltpu.VMEM((384, D), f32),
            pltpu.VMEM((geo.pieces, HEADS * geo.across, 128), f32),
        ]

    token5 = lambda width: pltpu.VMEM((12, 2, 2, 8, width), f32)
    tokens, ext = out((384, D)), out((4, 192, 2 * D), bf16)
    tokens_low = out((384, D), bf16)
    near1 = [keyval1, *cols1, *rows1, first_one]
    att1, middle1, last1, query2, keyval2, *edges = run(
        first_block_kernel,
        [tokens_low, tokens, tokens, tokens_low, out((4, 96, 2 * D), bf16), rows48, rows48],
        [place, lay_one, hidden0, query1, *near1, late1, norms, ebias],
        tiles(One, False) + block(late1),
        {0: SMEM, 10: anywhere},
        56,
    )
    rows2 = swaps(*edges, "row")
    own2 = run(extend_kernel, [ext], [place, keyval2, *rows2], specs={0: SMEM})[0]
    near2 = [own2, *swaps(own2, own2, "col"), first_two]
    att2, middle2, last2, sums = run(
        second_block_kernel,
        [tokens_low, tokens, tokens, out((padded + 8, max(D, -(-padded // 128) * 128)))],
        [place, lay_two, lay_one, last1, query2, *near2, late2, norms, ebias],
        tiles(Two, False) + [pltpu.VMEM((384, D), f32), token5(D)] + block(late2),
        {0: SMEM, 9: anywhere},
        56,
    )
    sums = sum_all(sums)
    pad_images = lambda x: jnp.pad(x, (0, padded - images))[:, None]
    (
        loss, grad_head, grad_hbias, dhid, grads2, dnorms2, debias2, dpos2, dquery2, down2, *edges,
    ) = run(
        second_back_kernel,
        [
            out((8, 128)), out((sh, 1024)), out((1, 1024)), tokens, out((nc, per[0] * D, 128), bf16),
            out((4, D)), out((1, FF)), out((HEADS, WIN)), tokens_low,
            out((4, 192, 2 * D)), ext, ext,
        ],
        [
            place, lay_two, lay_one, sums, pad_images(labels), pad_images(live.astype(f32)), hbias,
            last2, middle2, att2, query2, *near2, late2, norms, ebias,
        ],
        tiles(Two, True) + [token5(D)] + block(late2),
        {0: SMEM, 15: anywhere},
        56,
    )
    dcols2 = swaps(*edges, "col")
    drows2 = swaps(*run(rim_kernel, [rows48] * 2, [place, down2, *dcols2], specs={0: SMEM}), "row")
    grads2 = lax.psum_scatter(grads2, "col", scatter_dimension=0, tiled=False)
    dhid, grads1, dnorms1, debias1, dpos1, dquery1, inner1, *edges = run(
        first_back_kernel,
        [
            tokens, out((nc, per[1] * D, 128), bf16), out((4, D)), out((1, FF)), out((HEADS, WIN)),
            tokens_low, out((4, 192, 2 * D)), rows48, rows48,
        ],
        [
            place, lay_one, dhid, dquery2, down2, *dcols2, *drows2, last1, middle1, att1, query1,
            *near1, late1, norms, ebias,
        ],
        tiles(One, True) + [token5(2 * D)] + block(late1),
        {0: SMEM, 19: anywhere},
        56,
    )
    drows1 = swaps(*edges, "row")
    grads1 = lax.psum_scatter(grads1, "col", scatter_dimension=0, tiled=False)
    dcols1 = swaps(*run(sides_kernel, [edge] * 2, [place, inner1, *drows1], specs={0: SMEM}), "col")
    grads0, _ = run(
        front_back_kernel,
        [out((nc, per[2] * D + 2 * SMALL_ROWS, 128), bf16), out((SMALL_ROWS, 128))],
        [
            place, dhid, dquery1, inner1, *drows1, *dcols1, hidden0, conv_out, patches,
            early, norms, dnorms1, dnorms2, debias1, debias2, dpos1, dpos2,
        ],
        specs={0: SMEM},
    )
    grads0 = lax.all_to_all(grads0, "col", 0, 0, tiled=True)
    grads0 = run(
        between_kernel,
        [out((nr, sum(per) * sh + 2 * SMALL_ROWS, 128), bf16)],
        [grads2, grads1, grads0],
    )[0]
    grads0 = lax.all_to_all(grads0, "row", 0, 0, tiled=True)
    mine, small = run(
        last_sum_kernel,
        [out((sum(per) * sh, 128), bf16), out((SMALL_ROWS, 128))],
        [grads0],
    )
    grads = lax.all_gather(mine, "col", axis=0)
    wide = [
        conv_weight.T, first_conv.T, second_conv.T, input_proj, first_input, second_input,
        output_proj, first_output, second_output, expand_weight, first_expand, second_expand,
        reduce_weight, first_reduce, second_reduce,
    ]
    new = run(
        functools.partial(adamw_kernel, sh=sh, per=per), [out(x.shape) for x in wide], [grads, *wide]
    )
    new = [x.T for x in new[:3]] + list(new[3:])
    pos = [
        jnp.concatenate([small[k : k + 8], small[k + 8 : k + 16, : 169 - 128]], 1).reshape(-1)
        for k in (40, 56)
    ]
    grad_small = jnp.concatenate([small[:36].reshape(-1), grad_hbias[0, :CLASSES], *pos])
    head = adamw(head_weight, grad_head[:, :CLASSES], first_head, second_head)
    return (loss[0, 0], *new, *head, *adamw(small_params, grad_small, first_small, second_small))


def solution(mesh):
    return jax.shard_map(
        on_device,
        mesh=mesh,
        in_specs=(
            P("row", "col", None),
            P(None, "row", "col"),
            P(),
            P(),
            P(None, "row"),
            P(None, "row", None),
            P(None, "row", None),
            P(None, "row", None),
            P(None, "row", None),
            P("row", None),
            P(),
            P(None, "row"),
            P(None, "row", None),
            P(None, "row", None),
            P(None, "row", None),
            P(None, "row", None),
            P("row", None),
            P(),
            P(None, "row"),
            P(None, "row", None),
            P(None, "row", None),
            P(None, "row", None),
            P(None, "row", None),
            P("row", None),
            P(),
        ),
        out_specs=(
            P(),
            P(None, "row"),
            P(None, "row"),
            P(None, "row"),
            P(None, "row", None),
            P(None, "row", None),
            P(None, "row", None),
            P(None, "row", None),
            P(None, "row", None),
            P(None, "row", None),
            P(None, "row", None),
            P(None, "row", None),
            P(None, "row", None),
            P(None, "row", None),
            P(None, "row", None),
            P(None, "row", None),
            P("row", None),
            P("row", None),
            P("row", None),
            P(),
            P(),
            P(),
        ),
        check_vma=False,
    )
```

```python
import functools

import jax
import jax.numpy as jnp
from jax import lax
from jax.experimental import pallas as pl
from jax.experimental.pallas import tpu as pltpu
from jax.sharding import PartitionSpec as P

D = 256
HEADS = 8
FF = 768
CLASSES = 1000
LAYERS = 2
STEP = 5
WIN = 176

eps_norm = 1e-05
beta_one = 0.9
beta_two = 0.999
learn_rate = 0.2
decay_rate = 0.05
eps_adam = 1e-08
scale = (D // HEADS) ** -0.5

bf16 = jnp.bfloat16
f32 = jnp.float32
i32 = jnp.int32
MASKED = -1e30
LOG2E = 1.4426950408889634
MIB = 1024 * 1024


def nn(a, b):
    return lax.dot_general(a, b, (((1,), (0,)), ((), ())), preferred_element_type=f32)


def nt(a, b):
    return lax.dot_general(a, b, (((1,), (1,)), ((), ())), preferred_element_type=f32)


def tn(a, b):
    return lax.dot_general(a, b, (((0,), (0,)), ((), ())), preferred_element_type=f32)


def two_parts(x):
    high = x.astype(bf16)
    return high, (x - high.astype(f32)).astype(bf16)


def norm_parts(x):
    centre = x - jnp.mean(x, -1, keepdims=True)
    rstd = lax.rsqrt(jnp.mean(centre * centre, -1, keepdims=True) + eps_norm)
    return centre * rstd, rstd


def norm(x, gain_bias):
    return norm_parts(x)[0] * gain_bias[0:1] + gain_bias[1:2]


def norm_back(x, gain_bias, dy):
    xhat, rstd = norm_parts(x)
    dxhat = dy * gain_bias[0:1]
    dx = rstd * (
        dxhat
        - jnp.mean(dxhat, -1, keepdims=True)
        - xhat * jnp.mean(dxhat * xhat, -1, keepdims=True)
    )
    return dx, jnp.sum(dy * xhat, 0, keepdims=True), jnp.sum(dy, 0, keepdims=True)


def normal_cdf(u):
    return 0.5 * (1.0 + lax.erf(u * 0.7071067811865476))


class One:
    dilation, queries, across, pieces, steps = 1, 64, 16, 4, 6
    forward, back = 3, 3
    keys = pieces * 128

    @staticmethod
    def key_col(piece, c8):
        two = 2 * (c8 & 3) + (c8 >> 2)
        return jnp.where(
            piece == 0,
            2 * c8,
            jnp.where(piece == 1, 2 * c8 + 1, jnp.where(piece == 2, two - 8, two + 16)),
        )

    @staticmethod
    def query_col(index):
        return 2 * (index & 7) + (index >> 3)


class Two:
    dilation, queries, across, pieces, steps = 2, 32, 8, 3, 12
    forward, back = 3, 3
    keys = pieces * 128

    @staticmethod
    def key_col(piece, c8):
        return jnp.where(piece == 0, c8, jnp.where(piece == 1, c8 - 8, c8 + 8))

    @staticmethod
    def query_col(index):
        return index


def key_place(geo):
    lane = lax.broadcasted_iota(i32, (1, geo.keys), 1)
    return (lane >> 3) & 15, geo.key_col(lane >> 7, lane & 7)


def window_mask(geo, lay, step, row_first, col_first):
    token = lax.broadcasted_iota(i32, (geo.queries, 1), 0)
    if geo.dilation == 1:
        block = step
        row = block * 4 + (token >> 4)
        col = geo.query_col(token & 15)
        row_pos, col_pos = row_first + row, col_first + col
    else:
        group = step // 3
        block = step - 3 * group
        row = block * 4 + (token >> 3)
        col = token & 7
        row_pos = row_first + 2 * row + (group >> 1)
        col_pos = col_first + 2 * col + (group & 1)

    def begin(place, first, end):
        local = place - first
        extent = end - first
        if geo.dilation == 1:
            index, length = local, extent
        else:
            index, length = local >> 1, (extent - (local & 1) + 1) >> 1
        return jnp.minimum(jnp.maximum(index - 3, 0), length - 7) - index

    row_start = row + begin(row_pos, lay[:, 0:1], lay[:, 1:2])
    col_start = col + begin(col_pos, lay[:, 2:3], lay[:, 3:4])
    key_row, key_col = key_place(geo)
    down = key_row + (block * 4 - 6) - row_start
    right = key_col - col_start
    inside = (down >= 0) & (down <= 6) & (right >= 0) & (right <= 6)
    return jnp.where(inside, 0.0, MASKED).astype(f32)


def position_onehot(geo, across):
    key_row, key_col = key_place(geo)
    right = key_col - geo.query_col(across) + 6
    index = jnp.where((right >= 0) & (right <= 12) & (key_row <= 12), key_row * 13 + right, -1)
    entry = lax.broadcasted_iota(i32, (WIN, geo.keys), 0)
    return jnp.where(entry == index, 1.0, 0.0).astype(bf16)


def position_table(geo, bias, first_ref):
    high = bias.astype(bf16)
    rest = bias - high.astype(f32)
    mid = rest.astype(bf16)
    low = (rest - mid.astype(f32)).astype(bf16)
    for across in range(geo.across):
        onehot = position_onehot(geo, across)
        row = nn(high, onehot) + nn(mid, onehot) + nn(low, onehot)
        for piece in range(geo.pieces):
            lanes = slice(piece * 128, piece * 128 + 128)
            first_ref[piece, pl.ds(across, HEADS, stride=geo.across), :] = row[:, lanes]


def spread_table(geo, first_ref, table_ref):
    for head in range(HEADS):
        for row in range(4):
            for piece in range(geo.pieces):
                lanes = slice(piece * 128, piece * 128 + 128)
                value = first_ref[piece, head * geo.across : (head + 1) * geo.across, :]
                value = value * LOG2E
                if row:
                    value = pltpu.roll(value, 8 * row, 1)
                begin = head * geo.queries + row * geo.across
                table_ref[begin : begin + geo.across, lanes] = value


def gather_table(geo, table_ref, first_ref):
    for head in range(HEADS):
        for piece in range(geo.pieces):
            lanes = slice(piece * 128, piece * 128 + 128)
            total = None
            for row in range(4):
                begin = head * geo.queries + row * geo.across
                value = table_ref[begin : begin + geo.across, lanes]
                if row:
                    value = pltpu.roll(value, 128 - 8 * row, 1)
                total = value if total is None else total + value
            first_ref[piece, head * geo.across : (head + 1) * geo.across, :] = total
    grad = jnp.zeros((HEADS, WIN), f32)
    for across in range(geo.across):
        onehot = position_onehot(geo, across)
        rows = pl.ds(across, HEADS, stride=geo.across)
        first = [first_ref[piece, rows, :] for piece in range(geo.pieces)]
        high, low = two_parts(jnp.concatenate(first, 1))
        grad = grad + nt(high, onehot) + nt(low, onehot)
    return grad


def head_lanes(head):
    lane = lax.broadcasted_iota(i32, (1, D), 1)
    return jnp.where((lane >> 5) == head, 1.0, 0.0)


def by_head(x):
    return jnp.concatenate([x * head_lanes(h).astype(x.dtype) for h in range(HEADS)], 0)


def from_heads(x):
    count = x.shape[0] // HEADS
    total = None
    for h in range(HEADS):
        part = x[h * count : (h + 1) * count] * head_lanes(h)
        total = part if total is None else total + part
    return total


def key_rows(geo, step):
    if geo.dilation == 1:
        return None, pl.multiple_of(step * 32, 32)
    group = step // 3
    return group, pl.multiple_of((step - 3 * group) * 32, 32)


def load_keys(geo, pieces, step, lanes):
    group, first = key_rows(geo, step)
    if geo.dilation == 1:
        parts = [pieces[p, pl.ds(first, 128), lanes] for p in range(4)]
    else:
        parts = [pieces[p, group, pl.ds(first, 128), lanes] for p in range(3)]
    return jnp.concatenate(parts, 0)


def add_keys(geo, pieces, step, lanes, value):
    group, first = key_rows(geo, step)
    for p in range(geo.pieces):
        part = value[p * 128 : (p + 1) * 128]
        if geo.dilation == 1:
            pieces[p, pl.ds(first, 128), lanes] += part
        else:
            pieces[p, group, pl.ds(first, 128), lanes] += part


KEY = slice(0, D)
VALUE = slice(D, 2 * D)


def softmax_rows(score, table, mask):
    score = score * (scale * LOG2E) + (table + mask)
    weight = jnp.exp2(score - jnp.max(score, -1, keepdims=True))
    return weight, 1.0 / jnp.sum(weight, -1, keepdims=True)


def attend(geo, place, lay_ref, query_ref, pieces, table_ref, out_ref, score_ref, prob_ref, share_ref):
    count = geo.queries
    together = score_ref.shape[0]

    def steps_of(index, carry):
        steps = [index * together + n for n in range(together)]
        rows = [pl.ds(pl.multiple_of(step * count, count), count) for step in steps]
        for n, step in enumerate(steps):
            score_ref[n] = nt(by_head(query_ref[rows[n], :]), load_keys(geo, pieces, step, KEY))
        masks = [
            window_mask(geo, lay_ref[rows[n], :], step, place[0], place[1])
            for n, step in enumerate(steps)
        ]
        for h in range(HEADS):
            span = slice(h * count, (h + 1) * count)
            for n in range(together):
                weight, share = softmax_rows(score_ref[n, span, :], table_ref[span, :], masks[n])
                prob_ref[n, span, :] = weight.astype(bf16)
                share_ref[n, span, :] = jnp.broadcast_to(share, (count, 128))
        for n, step in enumerate(steps):
            out = nn(prob_ref[n], load_keys(geo, pieces, step, VALUE))
            out = out * jnp.concatenate([share_ref[n]] * 2, 1)
            out_ref[rows[n], :] = from_heads(out).astype(out_ref.dtype)
        return carry

    lax.fori_loop(0, geo.steps // together, steps_of, 0)


def attend_back(
    geo, place, lay_ref, query_ref, dout_ref, pieces, table_ref, dquery_ref, dpieces, dtable_ref,
    score_ref, dprob_ref, prob_ref, dscore_ref,
):
    count = geo.queries
    together = score_ref.shape[0]
    dtable_ref[...] = jnp.zeros_like(dtable_ref)
    dpieces[...] = jnp.zeros_like(dpieces)

    def steps_of(index, carry):
        steps = [index * together + n for n in range(together)]
        rows = [pl.ds(pl.multiple_of(step * count, count), count) for step in steps]
        for n, step in enumerate(steps):
            score_ref[n] = nt(by_head(query_ref[rows[n], :]), load_keys(geo, pieces, step, KEY))
            dprob_ref[n] = nt(by_head(dout_ref[rows[n], :]), load_keys(geo, pieces, step, VALUE))
        masks = [
            window_mask(geo, lay_ref[rows[n], :], step, place[0], place[1])
            for n, step in enumerate(steps)
        ]
        for h in range(HEADS):
            span = slice(h * count, (h + 1) * count)
            total = dtable_ref[span, :]
            for n in range(together):
                weight, share = softmax_rows(score_ref[n, span, :], table_ref[span, :], masks[n])
                prob = weight * share
                prob_ref[n, span, :] = prob.astype(bf16)
                dprob = dprob_ref[n, span, :]
                dscore = prob * (dprob - jnp.sum(prob * dprob, -1, keepdims=True))
                total += dscore
                dscore_ref[n, span, :] = dscore.astype(bf16)
            dtable_ref[span, :] = total
        for n, step in enumerate(steps):
            wide, dwide = by_head(query_ref[rows[n], :]), by_head(dout_ref[rows[n], :])
            dscore = dscore_ref[n]
            add_keys(geo, dpieces, step, VALUE, tn(prob_ref[n], dwide))
            add_keys(geo, dpieces, step, KEY, tn(dscore, wide) * scale)
            dquery_ref[rows[n], :] = from_heads(nn(dscore, load_keys(geo, pieces, step, KEY))) * scale
        return carry

    lax.fori_loop(0, geo.steps // together, steps_of, 0)


def grouped(x):
    parts = x.reshape(12, 2, 2, 8, x.shape[-1])
    return [parts[:, g >> 1, g & 1].reshape(96, x.shape[-1]) for g in range(4)]


EVEN_ROW, EVEN_COL, COL = 3, 4, 5


def send(place, even, first, second, after, before):
    for ref, when_even, when_odd in ((first, after, before), (second, before, after)):

        @pl.when(place[even] == 1)
        def _(ref=ref, value=when_even):
            ref[...] = value()

        @pl.when(place[even] == 0)
        def _(ref=ref, value=when_odd):
            ref[...] = value()


def received(place, even, first, second):
    flag = place[even].astype(f32)
    one, two = first.astype(f32), second.astype(f32)
    return two * flag + one * (1.0 - flag), one * flag + two * (1.0 - flag)


def store_received(place, even, first, second, before, after):
    @pl.when(place[even] == 1)
    def _():
        before(second)
        after(first)

    @pl.when(place[even] == 0)
    def _():
        before(first)
        after(second)


def run(kernel, outs, ins, scratch=(), specs=None, vmem=16):
    in_specs = [pl.BlockSpec(memory_space=pltpu.VMEM)] * len(ins)
    for index, spec in (specs or {}).items():
        in_specs[index] = spec
    return pl.pallas_call(
        kernel,
        out_shape=outs,
        in_specs=in_specs,
        out_specs=[pl.BlockSpec(memory_space=pltpu.VMEM)] * len(outs),
        scratch_shapes=list(scratch),
        compiler_params=pltpu.CompilerParams(vmem_limit_bytes=vmem * MIB),
        cost_estimate=pl.CostEstimate(flops=0, bytes_accessed=4 << 20, transcendentals=0),
    )(*ins)


SMEM = pl.BlockSpec(memory_space=pltpu.SMEM)


def out(shape, dtype=f32):
    return jax.ShapeDtypeStruct(shape, dtype)


def pack_kernel(col, conv, qkv, proj, exp, red, head, *refs, across):
    sh = qkv.shape[1]
    outs, groups = refs[:2], refs[2:]

    def cols(x):
        return [x[:, k * 128 : (k + 1) * 128] for k in range(x.shape[1] // 128)]

    def reds(x):
        return [part for k in range(3) for part in cols(x[k * sh : (k + 1) * sh, :])]

    tail = jnp.concatenate([head[:, 896:], jnp.zeros((sh, 1024 - CLASSES), f32)], 1)
    blocks = (
        cols(conv[...]) + cols(qkv[0]),
        cols(proj[0]) + cols(exp[0]) + reds(red[0]) + cols(qkv[1]),
        cols(proj[1]) + cols(exp[1]) + reds(red[1]) + cols(head[:, :896]) + [tail],
    )
    begin = 0
    for index, (group, values) in enumerate(zip(groups, blocks)):
        for k, value in enumerate(values):
            group[k * sh : (k + 1) * sh, :] = value.astype(bf16)
        empty = group.shape[0] - len(values) * sh
        if empty:
            group[len(values) * sh :, :] = jnp.zeros((empty, 128), bf16)
        result = outs[min(index, 1)]
        begin = begin if index == 2 else 0
        part = group.shape[0] // across
        mine = group[pl.ds(pl.multiple_of(col[0] * part, 16), part), :]
        for row in range(result.shape[0]):
            result[row, begin : begin + part, :] = mine
        begin += part


def weight_of(blocks, first, count):
    sh = D // blocks.shape[1]
    per = blocks.shape[2] // sh
    parts = [
        blocks[k // per, :, (k % per) * sh : (k % per + 1) * sh, :].reshape(D, 128)
        for k in range(first, first + count)
    ]
    return jnp.concatenate(parts, 1)


def weight_red(blocks, first):
    rows = blocks.shape[1]
    parts = [weight_of(blocks, first + 2 * k, 2).reshape(rows, 1, D // rows, D) for k in range(3)]
    return jnp.concatenate(parts, 1).reshape(FF, D)


def table_kernel(bias, first_one, first_two):
    position_table(One, bias[0:8, :], first_one)
    position_table(Two, bias[8:16, :], first_two)


def patch_kernel(place, stem, above, left, lay, patches, stem_f, above_f):
    stem_f[...] = stem[...].astype(f32)
    above_f[...] = above[...].astype(f32)
    left_f = left[...].astype(f32)
    tiles = left_f[:384].reshape(24, 2, 8, 128)
    left_odd = tiles[:, 0]
    beside = [left_odd, tiles[:, 1], jnp.concatenate([left_odd[1:], left_f[384:392][None]], 0)]
    phases = []
    for m in range(4):
        part = stem_f[pl.ds(m, 384, stride=4), :].reshape(24, 2, 8, 128)
        even, odd = part[:, 0], part[:, 1]
        top = above_f[pl.ds(m, 8, stride=4), :]
        phases.append([jnp.concatenate([top[None], odd[:-1]], 0), even, odd])
    token = lax.broadcasted_iota(i32, (384, 1), 0)
    row_pos = place[0] + (token >> 4)
    col_pos = place[1] + One.query_col(token & 15)
    inner_row = jnp.where(row_pos == lay[:, 0:1], 0.0, 1.0)
    inner_col = jnp.where(col_pos == lay[:, 2:3], 0.0, 1.0)
    half = lax.broadcasted_iota(i32, (24, 8, 128), 1)
    for a in range(3):
        shifted = jnp.where(half == 0, beside[a], pltpu.roll(phases[3][a], 1, 1))
        taps = (
            (shifted, phases[1][a]),
            (phases[0][a], phases[2][a]),
            (phases[1][a], phases[3][a]),
        )
        for b in range(3):
            value = jnp.stack(taps[b], 1).reshape(384, 128)
            if a == 0:
                value = value * inner_row
            if b == 0:
                value = value * inner_col
            lanes = slice((3 * a + b) * 128, (3 * a + b + 1) * 128)
            patches[:, lanes] = value.astype(bf16)


def front_kernel(place, patches, early, norms, conv_out, hidden, query, keyval, first, second):
    conv = nt(patches[...], weight_of(early, 0, 9))
    conv_out[...] = conv
    h = norm(conv, norms[0:2, :])
    hidden[...] = h
    low = norm(h, norms[2:4, :]).astype(bf16)
    mixed = nn(low, weight_of(early, 9, 6))
    query[...] = mixed[:, :D].astype(bf16)
    both = mixed[:, D:].reshape(24, 2, 8, 2 * D)
    zero, one = both[:, 0], both[:, 1]
    keyval[0] = zero.reshape(192, 2 * D).astype(bf16)
    keyval[1] = one.reshape(192, 2 * D).astype(bf16)
    sub = lax.broadcasted_iota(i32, zero.shape, 1)
    left = jnp.where(sub < 4, zero, pltpu.roll(one, 4, 1))
    right = jnp.where(sub < 4, pltpu.roll(zero, 4, 1), one)
    send(
        place, EVEN_COL, first, second,
        lambda: right.reshape(192, 2 * D).astype(bf16), lambda: left.reshape(192, 2 * D).astype(bf16),
    )


def ring_kernel(place, keyval, first, second, row_first, row_second):
    def put(ref, begin):
        rows = slice(begin, begin + 48)
        ref[0] = keyval[0, rows, :]
        ref[1] = keyval[1, rows, :]

        def left(source):
            ref[2] = source[rows, :]

        def right(source):
            ref[3] = source[rows, :]

        store_received(place, EVEN_COL, first, second, left, right)

    @pl.when(place[EVEN_ROW] == 1)
    def _():
        put(row_first, 144)
        put(row_second, 0)

    @pl.when(place[EVEN_ROW] == 0)
    def _():
        put(row_first, 0)
        put(row_second, 144)


def gather_keys_one(place, keyval, col_first, col_second, row_first, row_second, pieces):
    pieces[0, 48:240, :] = keyval[0]
    pieces[1, 48:240, :] = keyval[1]

    def into(index, rows):
        def put(source):
            pieces[index, rows, :] = source[...]

        return put

    every = slice(None)
    middle = slice(48, 240)
    store_received(place, EVEN_COL, col_first, col_second, into(2, middle), into(3, middle))
    store_received(
        place, EVEN_ROW, row_first, row_second, into(every, slice(0, 48)), into(every, slice(240, 288))
    )


def gather_keys_two(place, own, first, second, pieces):
    pieces[0] = own[...]

    def into(index):
        def put(source):
            pieces[index] = source[...]

        return put

    store_received(place, EVEN_COL, first, second, into(1), into(2))


def extend_kernel(place, keyval, first, second, result):
    result[:, 48:144, :] = keyval[...]

    def above(source):
        result[:, 0:48, :] = source[...]

    def below(source):
        result[:, 144:192, :] = source[...]

    store_received(place, EVEN_ROW, first, second, above, below)


def rim_kernel(place, own, first, second, row_first, row_second):
    def total(begin):
        rows = slice(begin, begin + 48)
        value = own[:, rows, :] + first[:, rows, :].astype(f32) + second[:, rows, :].astype(f32)
        return value.astype(bf16)

    send(place, EVEN_ROW, row_first, row_second, lambda: total(144), lambda: total(0))


def sides_kernel(place, inner, first, second, col_first, col_second):
    def total(p):
        above, below = received(place, EVEN_ROW, first[p], second[p])
        rows = [inner[p, 0:48, :] + above, inner[p, 48:144, :], inner[p, 144:192, :] + below]
        return jnp.concatenate(rows, 0).astype(bf16)

    send(place, EVEN_COL, col_first, col_second, lambda: total(3), lambda: total(2))


def feed_forward(hidden, norms, w_exp, w_red, bias):
    low = norm(hidden, norms).astype(bf16)
    upper = nn(low, w_exp) + bias
    gelu = upper * normal_cdf(upper)
    return hidden + nn(gelu.astype(bf16), w_red)


PROJ, EXP, RED, QKV, HEAD = 0, 2, 8, 14, 14


def fetch(source, buffer, sem):
    copy = pltpu.make_async_copy(source, buffer, sem.at[0])
    copy.start()
    return copy.wait


def first_block_kernel(
    place, lay, hidden, query, keyval, cola, colb, rowa, rowb, first_table, late, norms, ebias,
    att, middle, last, query2, keyval2, first, second,
    pieces, table, score, prob, share, group, sem,
):
    arrived = fetch(late, group, sem)
    gather_keys_one(place, keyval, cola, colb, rowa, rowb, pieces)
    spread_table(One, first_table, table)
    attend(One, place, lay, query, pieces, table, att, score, prob, share)
    arrived()
    mid = hidden[...] + nn(att[...], weight_of(group, PROJ, 2))
    middle[...] = mid
    end = feed_forward(mid, norms[4:6, :], weight_of(group, EXP, 6), weight_red(group, RED), ebias[0:1, :])
    last[...] = end
    low = norm(end, norms[6:8, :]).astype(bf16)
    mixed = nn(low, weight_of(group, QKV, 6))
    for g, part in enumerate(grouped(mixed)):
        query2[g * 96 : (g + 1) * 96, :] = part[:, :D].astype(bf16)
        keyval2[g] = part[:, D:].astype(bf16)
    send(
        place, EVEN_ROW, first, second, lambda: keyval2[:, 48:, :], lambda: keyval2[:, :48, :]
    )


def slot_onehot(slots, images):
    entry = lax.broadcasted_iota(i32, (384, images), 1)
    return jnp.where(slots[:, 4:5] == entry, 1.0, 0.0).astype(bf16)


def ungroup(value, ref):
    for g in range(4):
        ref[:, g >> 1, g & 1] = value[g * 96 : (g + 1) * 96].reshape(12, 8, value.shape[-1])


def second_block_kernel(
    place, lay, slots, hidden, query, own, cola, colb, first_table, late, norms, ebias,
    att, middle, last, sums,
    pieces, table, score, prob, share, att_group, att_token, group, sem,
):
    arrived = fetch(late, group, sem)
    gather_keys_two(place, own, cola, colb, pieces)
    spread_table(Two, first_table, table)
    attend(Two, place, lay, query, pieces, table, att_group, score, prob, share)
    ungroup(att_group[...], att_token)
    low = att_token[...].reshape(384, D).astype(bf16)
    att[...] = low
    arrived()
    mid = hidden[...] + nn(low, weight_of(group, PROJ, 2))
    middle[...] = mid
    end = feed_forward(mid, norms[8:10, :], weight_of(group, EXP, 6), weight_red(group, RED), ebias[1:2, :])
    last[...] = end
    final = norm(end, norms[10:12, :])
    images = sums.shape[0] - 8
    where = slot_onehot(slots, images)
    high, low = two_parts(final)
    sums[...] = jnp.zeros_like(sums)
    sums[:images, :D] = tn(where, high) + tn(where, low)
    sums[images:, :images] = tn(jnp.ones((384, 8), bf16), where)


def feed_forward_back(dhid, mid, gain_bias, w_exp, w_red, bias):
    low = norm(mid, gain_bias).astype(bf16)
    upper = nn(low, w_exp) + bias
    cdf = normal_cdf(upper)
    dz = dhid.astype(bf16)
    grad_red = tn((upper * cdf).astype(bf16), dz)
    slope = cdf + upper * (jnp.exp(-0.5 * upper * upper) * 0.3989422804014327)
    dupper = (nt(dz, w_red) * slope).astype(bf16)
    grad_bias = jnp.sum(dupper.astype(f32), 0, keepdims=True)
    grad_exp = tn(low, dupper)
    dx, dgain, dbias = norm_back(mid, gain_bias, nt(dupper, w_exp))
    return dhid + dx, grad_red, grad_exp, grad_bias, dgain, dbias


def put_block(grads, k, value):
    per = grads.shape[1] // D
    grads[k // per, (k % per) * D : (k % per + 1) * D, :] = value.astype(bf16)


def put_cols(grads, first, value):
    for k in range(value.shape[1] // 128):
        put_block(grads, first + k, value[:, k * 128 : (k + 1) * 128])


def put_red(grads, first, value, share):
    parts = value.reshape(D // share, 3, share, D)
    for k in range(3):
        put_cols(grads, first + 2 * k, parts[:, k].reshape(D, D))


def put_zeros(grads, first):
    per = grads.shape[1] // D
    for k in range(first, per * grads.shape[0]):
        put_block(grads, k, jnp.zeros((D, 128), f32))


def second_back_kernel(
    place, lay, slots, sums, labels, live, hbias, hidden, middle, att, query, own, cola, colb,
    first_table, late, norms, ebias,
    loss, grad_head, grad_hbias, dhidden, grads, dnorms, debias, dpos, dquery, down, first, second,
    pieces, table, dtable, score, dscore_f, prob, dscore, dpieces, datt, dq_group, dfirst, dq_token, group, sem,
):
    arrived = fetch(late, group, sem)
    gather_keys_two(place, own, cola, colb, pieces)
    spread_table(Two, first_table, table)
    images = sums.shape[0] - 8
    total = sums[:images, :D]
    diagonal = lax.broadcasted_iota(i32, (images, images), 0)
    diagonal = diagonal == lax.broadcasted_iota(i32, (images, images), 1)
    area = jnp.where(diagonal, sums[images : images + 1, :images], 0.0)
    area = jnp.sum(area, -1, keepdims=True)
    spread_area = jnp.maximum(area, 1.0)
    pooled = (total / spread_area).astype(bf16)
    arrived()
    w_head = weight_of(group, HEAD, 8)
    logits = nn(pooled, w_head) + hbias[...]
    weight = live[...] * jnp.where(area > 0.5, 1.0, 0.0)
    count = jnp.maximum(jnp.sum(weight, 0, keepdims=True), 1.0)
    cls = lax.broadcasted_iota(i32, logits.shape, 1)
    onehot = jnp.where(cls == labels[...], 1.0, 0.0)
    top = jnp.max(logits, -1, keepdims=True)
    logsum = jnp.log(jnp.sum(jnp.exp(logits - top), -1, keepdims=True)) + top
    cross = logsum - jnp.sum(onehot * logits, -1, keepdims=True)
    loss[...] = jnp.broadcast_to(jnp.sum(weight * cross, 0, keepdims=True) / count, loss.shape)
    dlogit = ((weight / count) * (jnp.exp(logits - logsum) - onehot)).astype(bf16)
    grad_hbias[...] = jnp.sum(dlogit.astype(f32), 0, keepdims=True)
    share = grad_head.shape[0]
    channel = lax.broadcasted_iota(i32, (D, share), 0)
    mine = lax.broadcasted_iota(i32, (D, share), 1) + place[2]
    own_pooled = nn(pooled, jnp.where(channel == mine, 1.0, 0.0).astype(bf16)).astype(bf16)
    grad_head[...] = tn(own_pooled, dlogit)
    high, low = two_parts(nt(dlogit, w_head) / spread_area)
    where = slot_onehot(slots, images)
    dfinal = nn(where, high) + nn(where, low)
    dhid, dgain, dbias = norm_back(hidden[...], norms[10:12, :], dfinal)
    dnorms[2:3, :] = dgain
    dnorms[3:4, :] = dbias
    dhid, grad_red, grad_exp, grad_bias, dgain, dbias = feed_forward_back(
        dhid, middle[...], norms[8:10, :], weight_of(group, EXP, 6), weight_red(group, RED), ebias[1:2, :]
    )
    put_cols(grads, 0, grad_exp)
    put_red(grads, 6, grad_red, share)
    debias[...] = grad_bias
    dnorms[0:1, :] = dgain
    dnorms[1:2, :] = dbias
    dhidden[...] = dhid
    dy = dhid.astype(bf16)
    put_cols(grads, 12, tn(att[...], dy))
    put_zeros(grads, 14)
    back = nt(dy, weight_of(group, PROJ, 2))
    for g, part in enumerate(grouped(back)):
        datt[g * 96 : (g + 1) * 96, :] = part.astype(bf16)
    attend_back(
        Two, place, lay, query, datt, pieces, table, dq_group, dpieces, dtable,
        score, dscore_f, prob, dscore,
    )
    ungroup(dq_group[...], dq_token)
    dquery[...] = dq_token[...].reshape(384, D).astype(bf16)
    down[...] = dpieces[0]
    send(
        place, EVEN_COL, first, second,
        lambda: dpieces[2].astype(bf16), lambda: dpieces[1].astype(bf16),
    )
    dpos[...] = gather_table(Two, dtable, dfirst)


def first_back_kernel(
    place, lay, dhid_in, dquery2, dkv, dcola, dcolb, drowa, drowb, hidden, middle, att, query, keyval,
    cola, colb, rowa, rowb, first_table, late, norms, ebias,
    dhidden, grads, dnorms, debias, dpos, dquery, inner, first, second,
    pieces, table, dtable, score, dscore_f, prob, dscore, dpieces, datt, dq, dfirst, dkv_token, group, sem,
):
    arrived = fetch(late, group, sem)
    gather_keys_one(place, keyval, cola, colb, rowa, rowb, pieces)
    spread_table(One, first_table, table)
    for g in range(4):
        rows = slice(48, 144)
        total = dkv[g, rows, :] + dcola[g, rows, :].astype(f32) + dcolb[g, rows, :].astype(f32)
        total += jnp.concatenate(received(place, EVEN_ROW, drowa[g], drowb[g]), 0)
        dkv_token[:, g >> 1, g & 1] = total.reshape(12, 8, 2 * D)
    dmixed = jnp.concatenate(
        [dquery2[...], dkv_token[...].reshape(384, 2 * D).astype(bf16)], 1
    )
    low = norm(hidden[...], norms[6:8, :]).astype(bf16)
    put_cols(grads, 0, tn(low, dmixed))
    arrived()
    dx, dgain, dbias = norm_back(
        hidden[...], norms[6:8, :], nt(dmixed, weight_of(group, QKV, 6))
    )
    dnorms[2:3, :] = dgain
    dnorms[3:4, :] = dbias
    dhid, grad_red, grad_exp, grad_bias, dgain, dbias = feed_forward_back(
        dhid_in[...] + dx, middle[...], norms[4:6, :], weight_of(group, EXP, 6), weight_red(group, RED), ebias[0:1, :]
    )
    put_cols(grads, 6, grad_exp)
    put_red(grads, 12, grad_red, D // late.shape[1])
    debias[...] = grad_bias
    dnorms[0:1, :] = dgain
    dnorms[1:2, :] = dbias
    dhidden[...] = dhid
    dy = dhid.astype(bf16)
    put_cols(grads, 18, tn(att[...], dy))
    put_zeros(grads, 20)
    datt[...] = nt(dy, weight_of(group, PROJ, 2)).astype(bf16)
    attend_back(
        One, place, lay, query, datt, pieces, table, dq, dpieces, dtable,
        score, dscore_f, prob, dscore,
    )
    dquery[...] = dq[...].astype(bf16)
    inner[...] = dpieces[:, 48:240, :]
    send(
        place, EVEN_ROW, first, second,
        lambda: dpieces[:, 240:288, :].astype(bf16), lambda: dpieces[:, 0:48, :].astype(bf16),
    )
    dpos[...] = gather_table(One, dtable, dfirst)


SMALL_ROWS = 80


def front_back_kernel(
    place, dhid_in, dquery, inner, drowa, drowb, dcola, dcolb, hidden, conv, patches, early,
    norms, dnorms1, dnorms2, debias1, debias2, dpos1, dpos2,
    keep, give,
    grads, small,
):
    left, right = received(place, EVEN_COL, dcola[...], dcolb[...])
    left, right = left.reshape(24, 8, 2 * D), right.reshape(24, 8, 2 * D)
    sub = lax.broadcasted_iota(i32, left.shape, 1)

    def whole(p):
        above, below = received(place, EVEN_ROW, drowa[p], drowb[p])
        top = inner[p, 0:48, :] + above
        bottom = inner[p, 144:192, :] + below
        return jnp.concatenate([top, inner[p, 48:144, :], bottom], 0).reshape(24, 8, 2 * D)

    zero = whole(0) + jnp.where(sub < 4, left, pltpu.roll(right, 4, 1))
    one = whole(1) + jnp.where(sub < 4, pltpu.roll(left, 4, 1), right)
    dkv = jnp.stack([zero, one], 1).reshape(384, 2 * D).astype(bf16)
    dmixed = jnp.concatenate([dquery[...], dkv], 1)
    h = hidden[...]
    low = norm(h, norms[2:4, :]).astype(bf16)
    put_cols(grads, 9, tn(low, dmixed))
    w_qkv = weight_of(early, 9, 6)
    dx, dgain1, dbias1 = norm_back(h, norms[2:4, :], nt(dmixed, w_qkv))
    dconv, dgain0, dbias0 = norm_back(conv[...], norms[0:2, :], dhid_in[...] + dx)
    put_cols(grads, 0, tn(dconv.astype(bf16), patches[...]))
    put_zeros(grads, 15)

    def place_row(first, value):
        for k in range(value.shape[1] // 128):
            small[first + k : first + k + 1, :] = value[:, k * 128 : (k + 1) * 128]

    small[...] = jnp.zeros_like(small)
    for k, value in enumerate((dgain0, dbias0, dgain1, dbias1)):
        place_row(2 * k, value)
    for k in range(4):
        place_row(8 + 2 * k, dnorms1[k : k + 1, :])
        place_row(16 + 2 * k, dnorms2[k : k + 1, :])
    place_row(24, debias1[...])
    place_row(30, debias2[...])
    for first, value in ((40, dpos1), (56, dpos2)):
        small[first : first + 8, :] = value[:, :128]
        small[first + 8 : first + 16, : WIN - 128] = value[:, 128:]
    begin = grads.shape[1] - SMALL_ROWS
    for col in range(grads.shape[0]):
        grads[col, begin:, :] = small[...].astype(bf16)
    halve(place, 0, grads, keep, give)


def halve(place, stage, parts, keep, give):
    bit = (place[COL] >> stage) & 1
    for k in range(keep.shape[0]):
        keep[k] = parts[2 * k + bit]
        give[k] = parts[2 * k + 1 - bit]


def halve_kernel(place, kept, given, keep, give, total, *, stage):
    total[...] = (kept[...].astype(f32) + given[...].astype(f32)).astype(bf16)
    halve(place, stage, total, keep, give)


def between_kernel(second, first, kept, given, result):
    rows = result.shape[0]
    sh = D // rows
    begin = 0
    for group in (second, first):
        for k in range(group.shape[0] // D):
            result[:, begin : begin + sh, :] = group[k * D : (k + 1) * D, :].reshape(rows, sh, 128)
            begin += sh
    for k in range(kept.shape[1] // D):
        span = slice(k * D, (k + 1) * D)
        total = kept[0, span, :].astype(f32) + given[0, span, :].astype(f32)
        result[:, begin : begin + sh, :] = total.astype(bf16).reshape(rows, sh, 128)
        begin += sh
    span = slice(kept.shape[1] - SMALL_ROWS, kept.shape[1])
    small = (kept[0, span, :].astype(f32) + given[0, span, :].astype(f32)).astype(bf16)
    for row in range(rows):
        result[row, begin:, :] = small


def last_sum_kernel(parts, result, small):
    total = parts[0].astype(f32)
    for row in range(1, parts.shape[0]):
        total += parts[row].astype(f32)
    count = result.shape[0]
    result[...] = total[:count].astype(bf16)
    small[...] = total[count:]


def adamw(weight, grad, first, second):
    first = beta_one * first + (1.0 - beta_one) * grad
    second = beta_two * second + (1.0 - beta_two) * grad * grad
    fix_one = 1.0 - beta_one**STEP
    fix_two = 1.0 - beta_two**STEP
    new = weight - learn_rate * (
        first / fix_one / (jnp.sqrt(second / fix_two) + eps_adam) + decay_rate * weight
    )
    return (first, second, new)


def adamw_kernel(grads, *refs, sh, per):
    ins = [refs[3 * n : 3 * n + 3] for n in range(5)]
    outs = [refs[15 + 3 * n : 18 + 3 * n] for n in range(5)]

    def update(n, group, k, *where):
        begin = (sum(per[:group]) + k % per[group]) * sh
        grad = grads[k // per[group], begin : begin + sh, :].astype(f32)
        weight, first, second = (ref[where] for ref in ins[n])
        for ref, value in zip(outs[n], adamw(weight, grad, first, second)):
            ref[where] = value

    every = slice(None)
    for k in range(9):
        update(0, 2, k, every, slice(k * 128, (k + 1) * 128))
    for k in range(6):
        lanes = slice(k * 128, (k + 1) * 128)
        update(1, 2, 9 + k, 0, every, lanes)
        update(1, 1, k, 1, every, lanes)
        update(3, 1, 6 + k, 0, every, lanes)
        update(3, 0, k, 1, every, lanes)
        rows, half = slice((k // 2) * sh, (k // 2 + 1) * sh), slice((k % 2) * 128, (k % 2 + 1) * 128)
        update(4, 1, 12 + k, 0, rows, half)
        update(4, 0, 6 + k, 1, rows, half)
    for k in range(2):
        lanes = slice(k * 128, (k + 1) * 128)
        update(2, 1, 18 + k, 0, every, lanes)
        update(2, 0, 12 + k, 1, every, lanes)


def onward(value, axis):
    count = lax.axis_size(axis)
    return lax.ppermute(value, axis, [(i, (i + 1) % count) for i in range(count)])


def swaps(first, second, axis):
    count = lax.axis_size(axis)
    pairs = [[(i, i + 1) for i in range(begin, count - 1, 2)] for begin in (0, 1)]
    both = [low + [(j, i) for i, j in low] for low in pairs]
    return lax.ppermute(first, axis, both[0]), lax.ppermute(second, axis, both[1])


def sum_all(value):
    for axis in ("col", "row"):
        count = lax.axis_size(axis)
        step = 1

        def other(flip):
            return lax.ppermute(value, axis, [(i, i ^ flip) for i in range(count)])

        while step < count:
            if 4 * step <= count:
                near, far, both = other(step), other(2 * step), other(3 * step)
                value = (value + near) + (far + both)
                step *= 4
            else:
                value = value + other(step)
                step *= 2
    return value


def on_device(
    stem_map, layout, labels, live,
    conv_weight, input_proj, output_proj, expand_weight, reduce_weight, head_weight, small_params,
    first_conv, first_input, first_output, first_expand, first_reduce, first_head, first_small,
    second_conv, second_input, second_output, second_expand, second_reduce, second_head, second_small,
):
    nr, nc = lax.axis_size("row"), lax.axis_size("col")
    sh = D // nr
    images = labels.shape[0]
    padded = -(-images // 8) * 8
    per = [-(-count // nc) for count in (14, 20, 15)]
    row_index, col_index = lax.axis_index("row"), lax.axis_index("col")
    parts = [-(-count // nc) * sh for count in (15, 20, 22)]
    early, late = run(
        functools.partial(pack_kernel, across=nc),
        [out((nr, parts[0], 128), bf16), out((nr, parts[1] + parts[2], 128), bf16)],
        [
            col_index.astype(i32)[None], conv_weight.T, input_proj, output_proj, expand_weight, reduce_weight,
            head_weight,
        ],
        [pltpu.VMEM((part * nc, 128), bf16) for part in parts],
        {0: SMEM},
        56,
    )
    early = lax.all_to_all(early, "row", 0, 0, tiled=True)
    norms = small_params[: 12 * D].reshape(12, D)
    start = 12 * D
    ebias = small_params[start : start + LAYERS * FF].reshape(LAYERS, FF)
    start += LAYERS * FF
    hbias = jnp.pad(small_params[start : start + CLASSES], (0, 24), constant_values=MASKED)[None]
    start += CLASSES
    pos_bias = small_params[start:].reshape(LAYERS * HEADS, 169)
    first_one, first_two = run(
        table_kernel,
        [out((geo.pieces, HEADS * geo.across, 128)) for geo in (One, Two)],
        [jnp.pad(pos_bias, ((0, 0), (0, WIN - 169)))],
    )
    place = [row_index * 24, col_index * 16, row_index * sh, (row_index + 1) % 2, (col_index + 1) % 2, col_index]
    place = jnp.stack(place).astype(i32)
    lay_one = layout.reshape(5, 24, 8, 2).transpose(1, 3, 2, 0).reshape(384, 5)
    lay_two = layout.reshape(5, 12, 2, 8, 2).transpose(2, 4, 1, 3, 0).reshape(384, 5)
    above = onward(stem_map[-1:], "row")
    rim = jnp.concatenate([above[:, -1:], stem_map[:, -1:]], 0)
    rim = jnp.broadcast_to(onward(rim, "col"), (49, 8, 128))
    patches = run(
        patch_kernel,
        [out((384, 1152), bf16)],
        [place, stem_map.reshape(1536, 128), above.reshape(32, 128), rim.reshape(392, 128), lay_one],
        [pltpu.VMEM((1536, 128), f32), pltpu.VMEM((32, 128), f32)],
        {0: SMEM},
    )[0]
    late, _, _ = lax.optimization_barrier((late, above, early))
    early = lax.all_gather(early, "col", axis=0)
    late = lax.all_to_all(late, "row", 0, 0, tiled=True)
    rows48, edge = out((4, 48, 2 * D), bf16), out((192, 2 * D), bf16)
    conv_out, hidden0, query1, keyval1, *edges = run(
        front_kernel,
        [out((384, D)), out((384, D)), out((384, D), bf16), out((2, 192, 2 * D), bf16), edge, edge],
        [place, patches, early, norms],
        specs={0: SMEM},
    )
    late, _ = lax.optimization_barrier((late, edges))
    late1 = lax.all_gather(late[:, : parts[1]], "col", axis=0)
    late2 = lax.all_gather(late[:, parts[1] :], "col", axis=0)
    cols1 = swaps(*edges, "col")
    rows1 = swaps(*run(ring_kernel, [rows48] * 2, [place, keyval1, *cols1], specs={0: SMEM}), "row")
    anywhere = pl.BlockSpec(memory_space=pl.ANY)
    block = lambda group: [pltpu.VMEM(group.shape, bf16), pltpu.SemaphoreType.DMA((1,))]

    def tiles(geo, back):
        square = (HEADS * geo.queries, geo.keys)
        shape = (4, 288, 2 * D) if geo is One else (3, 4, 192, 2 * D)
        table, many = pltpu.VMEM(square, f32), (geo.back if back else geo.forward, *square)
        wide, narrow = pltpu.VMEM(many, f32), pltpu.VMEM(many, bf16)
        if not back:
            return [pltpu.VMEM(shape, bf16), table, wide, narrow, pltpu.VMEM((*many[:2], 128), f32)]
        return [
            pltpu.VMEM(shape, bf16), table, table, wide, wide, narrow, narrow, pltpu.VMEM(shape, f32),
            pltpu.VMEM((384, D), bf16), pltpu.VMEM((384, D), f32),
            pltpu.VMEM((geo.pieces, HEADS * geo.across, 128), f32),
        ]

    token5 = lambda width: pltpu.VMEM((12, 2, 2, 8, width), f32)
    tokens, ext = out((384, D)), out((4, 192, 2 * D), bf16)
    tokens_low = out((384, D), bf16)
    near1 = [keyval1, *cols1, *rows1, first_one]
    att1, middle1, last1, query2, keyval2, *edges = run(
        first_block_kernel,
        [tokens_low, tokens, tokens, tokens_low, out((4, 96, 2 * D), bf16), rows48, rows48],
        [place, lay_one, hidden0, query1, *near1, late1, norms, ebias],
        tiles(One, False) + block(late1),
        {0: SMEM, 10: anywhere},
        56,
    )
    rows2 = swaps(*edges, "row")
    own2 = run(extend_kernel, [ext], [place, keyval2, *rows2], specs={0: SMEM})[0]
    near2 = [own2, *swaps(own2, own2, "col"), first_two]
    att2, middle2, last2, sums = run(
        second_block_kernel,
        [tokens_low, tokens, tokens, out((padded + 8, max(D, -(-padded // 128) * 128)))],
        [place, lay_two, lay_one, last1, query2, *near2, late2, norms, ebias],
        tiles(Two, False) + [pltpu.VMEM((384, D), f32), token5(D)] + block(late2),
        {0: SMEM, 9: anywhere},
        56,
    )
    sums = sum_all(sums)
    pad_images = lambda x: jnp.pad(x, (0, padded - images))[:, None]
    (
        loss, grad_head, grad_hbias, dhid, grads2, dnorms2, debias2, dpos2, dquery2, down2, *edges,
    ) = run(
        second_back_kernel,
        [
            out((8, 128)), out((sh, 1024)), out((1, 1024)), tokens, out((nc, per[0] * D, 128), bf16),
            out((4, D)), out((1, FF)), out((HEADS, WIN)), tokens_low,
            out((4, 192, 2 * D)), ext, ext,
        ],
        [
            place, lay_two, lay_one, sums, pad_images(labels), pad_images(live.astype(f32)), hbias,
            last2, middle2, att2, query2, *near2, late2, norms, ebias,
        ],
        tiles(Two, True) + [token5(D)] + block(late2),
        {0: SMEM, 15: anywhere},
        56,
    )
    dcols2 = swaps(*edges, "col")
    drows2 = swaps(*run(rim_kernel, [rows48] * 2, [place, down2, *dcols2], specs={0: SMEM}), "row")
    grads2 = lax.psum_scatter(grads2, "col", scatter_dimension=0, tiled=False)
    dhid, grads1, dnorms1, debias1, dpos1, dquery1, inner1, *edges = run(
        first_back_kernel,
        [
            tokens, out((nc, per[1] * D, 128), bf16), out((4, D)), out((1, FF)), out((HEADS, WIN)),
            tokens_low, out((4, 192, 2 * D)), rows48, rows48,
        ],
        [
            place, lay_one, dhid, dquery2, down2, *dcols2, *drows2, last1, middle1, att1, query1,
            *near1, late1, norms, ebias,
        ],
        tiles(One, True) + [token5(2 * D)] + block(late1),
        {0: SMEM, 19: anywhere},
        56,
    )
    drows1 = swaps(*edges, "row")
    grads1 = lax.psum_scatter(grads1, "col", scatter_dimension=0, tiled=False)
    dcols1 = swaps(*run(sides_kernel, [edge] * 2, [place, inner1, *drows1], specs={0: SMEM}), "col")
    part = per[2] * D + SMALL_ROWS
    half = lambda count: out((count, part, 128), bf16)
    kept, given = run(
        front_back_kernel,
        [half(nc // 2), half(nc // 2)],
        [
            place, dhid, dquery1, inner1, *drows1, *dcols1, hidden0, conv_out, patches,
            early, norms, dnorms1, dnorms2, debias1, debias2, dpos1, dpos2,
        ],
        [pltpu.VMEM((nc, part, 128), bf16), pltpu.VMEM((SMALL_ROWS, 128), f32)],
        {0: SMEM},
    )
    stage = 0
    while True:
        given = lax.ppermute(given, "col", [(i, i ^ (1 << stage)) for i in range(nc)])
        stage += 1
        if 1 << stage == nc:
            break
        count = nc >> (stage + 1)
        kept, given = run(
            functools.partial(halve_kernel, stage=stage),
            [half(count), half(count)],
            [place, kept, given],
            [pltpu.VMEM((2 * count, part, 128), bf16)],
            {0: SMEM},
        )
    mine = run(
        between_kernel,
        [out((nr, sum(per) * sh + SMALL_ROWS, 128), bf16)],
        [grads2, grads1, kept, given],
    )[0]
    mine = lax.all_to_all(mine, "row", 0, 0, tiled=True)
    mine, small = run(
        last_sum_kernel, [out((sum(per) * sh, 128), bf16), out((SMALL_ROWS, 128))], [mine]
    )
    grads = lax.all_gather(mine, "col", axis=0)
    wide = [
        conv_weight.T, first_conv.T, second_conv.T, input_proj, first_input, second_input,
        output_proj, first_output, second_output, expand_weight, first_expand, second_expand,
        reduce_weight, first_reduce, second_reduce,
    ]
    new = run(
        functools.partial(adamw_kernel, sh=sh, per=per), [out(x.shape) for x in wide], [grads, *wide]
    )
    new = [x.T for x in new[:3]] + list(new[3:])
    pos = [
        jnp.concatenate([small[k : k + 8], small[k + 8 : k + 16, : 169 - 128]], 1).reshape(-1)
        for k in (40, 56)
    ]
    grad_small = jnp.concatenate([small[:36].reshape(-1), grad_hbias[0, :CLASSES], *pos])
    head = adamw(head_weight, grad_head[:, :CLASSES], first_head, second_head)
    return (loss[0, 0], *new, *head, *adamw(small_params, grad_small, first_small, second_small))


def solution(mesh):
    return jax.shard_map(
        on_device,
        mesh=mesh,
        in_specs=(
            P("row", "col", None),
            P(None, "row", "col"),
            P(),
            P(),
            P(None, "row"),
            P(None, "row", None),
            P(None, "row", None),
            P(None, "row", None),
            P(None, "row", None),
            P("row", None),
            P(),
            P(None, "row"),
            P(None, "row", None),
            P(None, "row", None),
            P(None, "row", None),
            P(None, "row", None),
            P("row", None),
            P(),
            P(None, "row"),
            P(None, "row", None),
            P(None, "row", None),
            P(None, "row", None),
            P(None, "row", None),
            P("row", None),
            P(),
        ),
        out_specs=(
            P(),
            P(None, "row"),
            P(None, "row"),
            P(None, "row"),
            P(None, "row", None),
            P(None, "row", None),
            P(None, "row", None),
            P(None, "row", None),
            P(None, "row", None),
            P(None, "row", None),
            P(None, "row", None),
            P(None, "row", None),
            P(None, "row", None),
            P(None, "row", None),
            P(None, "row", None),
            P(None, "row", None),
            P("row", None),
            P("row", None),
            P("row", None),
            P(),
            P(),
            P(),
        ),
        check_vma=False,
    )
```

```python
import functools

import jax
import jax.numpy as jnp
from jax import lax
from jax.experimental import pallas as pl
from jax.experimental.pallas import tpu as pltpu
from jax.sharding import PartitionSpec as P

D = 256
HEADS = 8
FF = 768
CLASSES = 1000
LAYERS = 2
STEP = 5
WIN = 176

eps_norm = 1e-05
beta_one = 0.9
beta_two = 0.999
learn_rate = 0.2
decay_rate = 0.05
eps_adam = 1e-08
scale = (D // HEADS) ** -0.5

bf16 = jnp.bfloat16
f32 = jnp.float32
i32 = jnp.int32
MASKED = -1e30
LOG2E = 1.4426950408889634
MIB = 1024 * 1024


def nn(a, b):
    return lax.dot_general(a, b, (((1,), (0,)), ((), ())), preferred_element_type=f32)


def nt(a, b):
    return lax.dot_general(a, b, (((1,), (1,)), ((), ())), preferred_element_type=f32)


def tn(a, b):
    return lax.dot_general(a, b, (((0,), (0,)), ((), ())), preferred_element_type=f32)


def two_parts(x):
    high = x.astype(bf16)
    return high, (x - high.astype(f32)).astype(bf16)


def norm_parts(x):
    centre = x - jnp.mean(x, -1, keepdims=True)
    rstd = lax.rsqrt(jnp.mean(centre * centre, -1, keepdims=True) + eps_norm)
    return centre * rstd, rstd


def norm(x, gain_bias):
    return norm_parts(x)[0] * gain_bias[0:1] + gain_bias[1:2]


def norm_back(x, gain_bias, dy):
    xhat, rstd = norm_parts(x)
    dxhat = dy * gain_bias[0:1]
    dx = rstd * (
        dxhat
        - jnp.mean(dxhat, -1, keepdims=True)
        - xhat * jnp.mean(dxhat * xhat, -1, keepdims=True)
    )
    return dx, jnp.sum(dy * xhat, 0, keepdims=True), jnp.sum(dy, 0, keepdims=True)


def normal_cdf(u):
    return 0.5 * (1.0 + lax.erf(u * 0.7071067811865476))


class One:
    dilation, queries, across, pieces, steps = 1, 64, 16, 4, 6
    together = 3
    keys = pieces * 128

    @staticmethod
    def key_col(piece, c8):
        two = 2 * (c8 & 3) + (c8 >> 2)
        return jnp.where(
            piece == 0,
            2 * c8,
            jnp.where(piece == 1, 2 * c8 + 1, jnp.where(piece == 2, two - 8, two + 16)),
        )

    @staticmethod
    def query_col(index):
        return 2 * (index & 7) + (index >> 3)


class Two:
    dilation, queries, across, pieces, steps = 2, 32, 8, 3, 12
    together = 3
    keys = pieces * 128

    @staticmethod
    def key_col(piece, c8):
        return jnp.where(piece == 0, c8, jnp.where(piece == 1, c8 - 8, c8 + 8))

    @staticmethod
    def query_col(index):
        return index


def key_place(geo):
    lane = lax.broadcasted_iota(i32, (1, geo.keys), 1)
    return (lane >> 3) & 15, geo.key_col(lane >> 7, lane & 7)


def window_mask(geo, lay, step, row_first, col_first):
    token = lax.broadcasted_iota(i32, (geo.queries, 1), 0)
    if geo.dilation == 1:
        block = step
        row = block * 4 + (token >> 4)
        col = geo.query_col(token & 15)
        row_pos, col_pos = row_first + row, col_first + col
    else:
        group = step // 3
        block = step - 3 * group
        row = block * 4 + (token >> 3)
        col = token & 7
        row_pos = row_first + 2 * row + (group >> 1)
        col_pos = col_first + 2 * col + (group & 1)

    def begin(place, first, end):
        local = place - first
        extent = end - first
        if geo.dilation == 1:
            index, length = local, extent
        else:
            index, length = local >> 1, (extent - (local & 1) + 1) >> 1
        return jnp.minimum(jnp.maximum(index - 3, 0), length - 7) - index

    row_start = row + begin(row_pos, lay[:, 0:1], lay[:, 1:2])
    col_start = col + begin(col_pos, lay[:, 2:3], lay[:, 3:4])
    key_row, key_col = key_place(geo)
    down = key_row + (block * 4 - 6) - row_start
    right = key_col - col_start
    inside = (down >= 0) & (down <= 6) & (right >= 0) & (right <= 6)
    return jnp.where(inside, 0.0, MASKED).astype(f32)


def position_onehot(geo, across):
    key_row, key_col = key_place(geo)
    right = key_col - geo.query_col(across) + 6
    index = jnp.where((right >= 0) & (right <= 12) & (key_row <= 12), key_row * 13 + right, -1)
    entry = lax.broadcasted_iota(i32, (WIN, geo.keys), 0)
    return jnp.where(entry == index, 1.0, 0.0).astype(bf16)


def position_table(geo, bias, first_ref):
    high = bias.astype(bf16)
    rest = bias - high.astype(f32)
    mid = rest.astype(bf16)
    low = (rest - mid.astype(f32)).astype(bf16)
    for across in range(geo.across):
        onehot = position_onehot(geo, across)
        row = nn(high, onehot) + nn(mid, onehot) + nn(low, onehot)
        for piece in range(geo.pieces):
            lanes = slice(piece * 128, piece * 128 + 128)
            first_ref[piece, pl.ds(across, HEADS, stride=geo.across), :] = row[:, lanes]


def spread_table(geo, first_ref, table_ref):
    for head in range(HEADS):
        for row in range(4):
            for piece in range(geo.pieces):
                lanes = slice(piece * 128, piece * 128 + 128)
                value = first_ref[piece, head * geo.across : (head + 1) * geo.across, :]
                value = value * LOG2E
                if row:
                    value = pltpu.roll(value, 8 * row, 1)
                begin = head * geo.queries + row * geo.across
                table_ref[begin : begin + geo.across, lanes] = value


def gather_table(geo, table_ref, first_ref):
    for head in range(HEADS):
        for piece in range(geo.pieces):
            lanes = slice(piece * 128, piece * 128 + 128)
            total = None
            for row in range(4):
                begin = head * geo.queries + row * geo.across
                value = table_ref[begin : begin + geo.across, lanes]
                if row:
                    value = pltpu.roll(value, 128 - 8 * row, 1)
                total = value if total is None else total + value
            first_ref[piece, head * geo.across : (head + 1) * geo.across, :] = total
    grad = jnp.zeros((HEADS, WIN), f32)
    for across in range(geo.across):
        onehot = position_onehot(geo, across)
        rows = pl.ds(across, HEADS, stride=geo.across)
        first = [first_ref[piece, rows, :] for piece in range(geo.pieces)]
        high, low = two_parts(jnp.concatenate(first, 1))
        grad = grad + nt(high, onehot) + nt(low, onehot)
    return grad


def head_lanes(head):
    lane = lax.broadcasted_iota(i32, (1, D), 1)
    return jnp.where((lane >> 5) == head, 1.0, 0.0)


def by_head(x):
    return jnp.concatenate([x * head_lanes(h).astype(x.dtype) for h in range(HEADS)], 0)


def from_heads(x):
    count = x.shape[0] // HEADS
    total = None
    for h in range(HEADS):
        part = x[h * count : (h + 1) * count] * head_lanes(h)
        total = part if total is None else total + part
    return total


def key_rows(geo, step):
    if geo.dilation == 1:
        return None, pl.multiple_of(step * 32, 32)
    group = step // 3
    return group, pl.multiple_of((step - 3 * group) * 32, 32)


def load_keys(geo, pieces, step, lanes):
    group, first = key_rows(geo, step)
    if geo.dilation == 1:
        parts = [pieces[p, pl.ds(first, 128), lanes] for p in range(4)]
    else:
        parts = [pieces[p, group, pl.ds(first, 128), lanes] for p in range(3)]
    return jnp.concatenate(parts, 0)


def add_keys(geo, pieces, step, lanes, value):
    group, first = key_rows(geo, step)
    for p in range(geo.pieces):
        part = value[p * 128 : (p + 1) * 128]
        if geo.dilation == 1:
            pieces[p, pl.ds(first, 128), lanes] += part
        else:
            pieces[p, group, pl.ds(first, 128), lanes] += part


KEY = slice(0, D)
VALUE = slice(D, 2 * D)


def softmax_rows(score, table, mask):
    score = score * (scale * LOG2E) + (table + mask)
    weight = jnp.exp2(score - jnp.max(score, -1, keepdims=True))
    return weight * (1.0 / jnp.sum(weight, -1, keepdims=True))


def attend(geo, place, lay_ref, query_ref, pieces, table_ref, out_ref, score_ref, prob_ref, kept, sems):
    count = geo.queries
    together = score_ref.shape[0]

    def keep(index):
        span = pl.ds(index * together, together)
        return pltpu.make_async_copy(prob_ref.at[span], kept.at[span], sems.at[index])

    def steps_of(index, carry):
        steps = [index * together + n for n in range(together)]
        rows = [pl.ds(pl.multiple_of(step * count, count), count) for step in steps]
        for n, step in enumerate(steps):
            score_ref[n] = nt(by_head(query_ref[rows[n], :]), load_keys(geo, pieces, step, KEY))
        masks = [
            window_mask(geo, lay_ref[rows[n], :], step, place[0], place[1])
            for n, step in enumerate(steps)
        ]
        for h in range(HEADS):
            span = slice(h * count, (h + 1) * count)
            for n, step in enumerate(steps):
                prob = softmax_rows(score_ref[n, span, :], table_ref[span, :], masks[n])
                prob_ref[step, span, :] = prob.astype(bf16)
        keep(index).start()
        for n, step in enumerate(steps):
            out = nn(prob_ref[step], load_keys(geo, pieces, step, VALUE))
            out_ref[rows[n], :] = from_heads(out).astype(out_ref.dtype)
        return carry

    lax.fori_loop(0, geo.steps // together, steps_of, 0)
    return [keep(index) for index in range(geo.steps // together)]


def attend_back(
    geo, query_ref, dout_ref, pieces, prob_ref, dquery_ref, dpieces, dtable_ref, dprob_ref, dscore_ref,
):
    count = geo.queries
    together = dprob_ref.shape[0]
    dtable_ref[...] = jnp.zeros_like(dtable_ref)
    dpieces[...] = jnp.zeros_like(dpieces)

    def steps_of(index, carry):
        steps = [index * together + n for n in range(together)]
        rows = [pl.ds(pl.multiple_of(step * count, count), count) for step in steps]
        for n, step in enumerate(steps):
            dprob_ref[n] = nt(by_head(dout_ref[rows[n], :]), load_keys(geo, pieces, step, VALUE))
        for h in range(HEADS):
            span = slice(h * count, (h + 1) * count)
            total = dtable_ref[span, :]
            for n, step in enumerate(steps):
                prob = prob_ref[step, span, :].astype(f32)
                dprob = dprob_ref[n, span, :]
                dscore = prob * (dprob - jnp.sum(prob * dprob, -1, keepdims=True))
                total += dscore
                dscore_ref[n, span, :] = dscore.astype(bf16)
            dtable_ref[span, :] = total
        for n, step in enumerate(steps):
            wide, dwide = by_head(query_ref[rows[n], :]), by_head(dout_ref[rows[n], :])
            dscore = dscore_ref[n]
            add_keys(geo, dpieces, step, VALUE, tn(prob_ref[step], dwide))
            add_keys(geo, dpieces, step, KEY, tn(dscore, wide) * scale)
            dquery_ref[rows[n], :] = from_heads(nn(dscore, load_keys(geo, pieces, step, KEY))) * scale
        return carry

    lax.fori_loop(0, geo.steps // together, steps_of, 0)


def grouped(x):
    parts = x.reshape(12, 2, 2, 8, x.shape[-1])
    return [parts[:, g >> 1, g & 1].reshape(96, x.shape[-1]) for g in range(4)]


EVEN_ROW, EVEN_COL, COL = 3, 4, 5


def send(place, even, first, second, after, before):
    for ref, when_even, when_odd in ((first, after, before), (second, before, after)):

        @pl.when(place[even] == 1)
        def _(ref=ref, value=when_even):
            ref[...] = value()

        @pl.when(place[even] == 0)
        def _(ref=ref, value=when_odd):
            ref[...] = value()


def received(place, even, first, second):
    flag = place[even].astype(f32)
    one, two = first.astype(f32), second.astype(f32)
    return two * flag + one * (1.0 - flag), one * flag + two * (1.0 - flag)


def store_received(place, even, first, second, before, after):
    @pl.when(place[even] == 1)
    def _():
        before(second)
        after(first)

    @pl.when(place[even] == 0)
    def _():
        before(first)
        after(second)


def run(kernel, outs, ins, scratch=(), specs=None, vmem=16, out_specs=None):
    in_specs = [pl.BlockSpec(memory_space=pltpu.VMEM)] * len(ins)
    for index, spec in (specs or {}).items():
        in_specs[index] = spec
    results = [pl.BlockSpec(memory_space=pltpu.VMEM)] * len(outs)
    for index, spec in (out_specs or {}).items():
        results[index] = spec
    return pl.pallas_call(
        kernel,
        out_shape=outs,
        in_specs=in_specs,
        out_specs=results,
        scratch_shapes=list(scratch),
        compiler_params=pltpu.CompilerParams(vmem_limit_bytes=vmem * MIB),
        cost_estimate=pl.CostEstimate(flops=0, bytes_accessed=4 << 20, transcendentals=0),
    )(*ins)


SMEM = pl.BlockSpec(memory_space=pltpu.SMEM)


def out(shape, dtype=f32):
    return jax.ShapeDtypeStruct(shape, dtype)


def pack_kernel(col, conv, qkv, proj, exp, red, head, *refs, across):
    sh = qkv.shape[1]
    outs, groups = refs[:2], refs[2:]

    def cols(x):
        return [x[:, k * 128 : (k + 1) * 128] for k in range(x.shape[1] // 128)]

    def reds(x):
        return [part for k in range(3) for part in cols(x[k * sh : (k + 1) * sh, :])]

    tail = jnp.concatenate([head[:, 896:], jnp.zeros((sh, 1024 - CLASSES), f32)], 1)
    blocks = (
        cols(conv[...]) + cols(qkv[0]),
        cols(proj[0]) + cols(exp[0]) + reds(red[0]) + cols(qkv[1]),
        cols(proj[1]) + cols(exp[1]) + reds(red[1]) + cols(head[:, :896]) + [tail],
    )
    begin = 0
    for index, (group, values) in enumerate(zip(groups, blocks)):
        for k, value in enumerate(values):
            group[k * sh : (k + 1) * sh, :] = value.astype(bf16)
        empty = group.shape[0] - len(values) * sh
        if empty:
            group[len(values) * sh :, :] = jnp.zeros((empty, 128), bf16)
        result = outs[min(index, 1)]
        begin = begin if index == 2 else 0
        part = group.shape[0] // across
        mine = group[pl.ds(pl.multiple_of(col[0] * part, 16), part), :]
        for row in range(result.shape[0]):
            result[row, begin : begin + part, :] = mine
        begin += part


def weight_of(blocks, first, count):
    sh = D // blocks.shape[1]
    per = blocks.shape[2] // sh
    parts = [
        blocks[k // per, :, (k % per) * sh : (k % per + 1) * sh, :].reshape(D, 128)
        for k in range(first, first + count)
    ]
    return jnp.concatenate(parts, 1)


def weight_red(blocks, first):
    rows = blocks.shape[1]
    parts = [weight_of(blocks, first + 2 * k, 2).reshape(rows, 1, D // rows, D) for k in range(3)]
    return jnp.concatenate(parts, 1).reshape(FF, D)


def table_kernel(bias, first_one, first_two):
    position_table(One, bias[0:8, :], first_one)
    position_table(Two, bias[8:16, :], first_two)


def patch_kernel(place, stem, above, left, lay, patches, stem_f, above_f):
    stem_f[...] = stem[...].astype(f32)
    above_f[...] = above[...].astype(f32)
    left_f = left[...].astype(f32)
    tiles = left_f[:384].reshape(24, 2, 8, 128)
    left_odd = tiles[:, 0]
    beside = [left_odd, tiles[:, 1], jnp.concatenate([left_odd[1:], left_f[384:392][None]], 0)]
    phases = []
    for m in range(4):
        part = stem_f[pl.ds(m, 384, stride=4), :].reshape(24, 2, 8, 128)
        even, odd = part[:, 0], part[:, 1]
        top = above_f[pl.ds(m, 8, stride=4), :]
        phases.append([jnp.concatenate([top[None], odd[:-1]], 0), even, odd])
    token = lax.broadcasted_iota(i32, (384, 1), 0)
    row_pos = place[0] + (token >> 4)
    col_pos = place[1] + One.query_col(token & 15)
    inner_row = jnp.where(row_pos == lay[:, 0:1], 0.0, 1.0)
    inner_col = jnp.where(col_pos == lay[:, 2:3], 0.0, 1.0)
    half = lax.broadcasted_iota(i32, (24, 8, 128), 1)
    for a in range(3):
        shifted = jnp.where(half == 0, beside[a], pltpu.roll(phases[3][a], 1, 1))
        taps = (
            (shifted, phases[1][a]),
            (phases[0][a], phases[2][a]),
            (phases[1][a], phases[3][a]),
        )
        for b in range(3):
            value = jnp.stack(taps[b], 1).reshape(384, 128)
            if a == 0:
                value = value * inner_row
            if b == 0:
                value = value * inner_col
            lanes = slice((3 * a + b) * 128, (3 * a + b + 1) * 128)
            patches[:, lanes] = value.astype(bf16)


def front_kernel(place, patches, early, norms, conv_out, hidden, query, keyval, first, second):
    conv = nt(patches[...], weight_of(early, 0, 9))
    conv_out[...] = conv
    h = norm(conv, norms[0:2, :])
    hidden[...] = h
    low = norm(h, norms[2:4, :]).astype(bf16)
    mixed = nn(low, weight_of(early, 9, 6))
    query[...] = mixed[:, :D].astype(bf16)
    both = mixed[:, D:].reshape(24, 2, 8, 2 * D)
    zero, one = both[:, 0], both[:, 1]
    keyval[0] = zero.reshape(192, 2 * D).astype(bf16)
    keyval[1] = one.reshape(192, 2 * D).astype(bf16)
    sub = lax.broadcasted_iota(i32, zero.shape, 1)
    left = jnp.where(sub < 4, zero, pltpu.roll(one, 4, 1))
    right = jnp.where(sub < 4, pltpu.roll(zero, 4, 1), one)
    send(
        place, EVEN_COL, first, second,
        lambda: right.reshape(192, 2 * D).astype(bf16), lambda: left.reshape(192, 2 * D).astype(bf16),
    )


def ring_kernel(place, keyval, first, second, row_first, row_second):
    def put(ref, begin):
        rows = slice(begin, begin + 48)
        ref[0] = keyval[0, rows, :]
        ref[1] = keyval[1, rows, :]

        def left(source):
            ref[2] = source[rows, :]

        def right(source):
            ref[3] = source[rows, :]

        store_received(place, EVEN_COL, first, second, left, right)

    @pl.when(place[EVEN_ROW] == 1)
    def _():
        put(row_first, 144)
        put(row_second, 0)

    @pl.when(place[EVEN_ROW] == 0)
    def _():
        put(row_first, 0)
        put(row_second, 144)


class Copies:
    def __init__(self, sems):
        self.sems, self.used = sems, 0

    def semaphore(self):
        self.used += 1
        return self.sems.at[self.used - 1]

    def start(self, source, target):
        copy = pltpu.make_async_copy(source, target, self.semaphore())
        copy.start()
        return [copy]

    def start_received(self, place, even, first, second, before, after):
        one, two = self.semaphore(), self.semaphore()

        @pl.when(place[even] == 1)
        def _():
            pltpu.make_async_copy(second, before, one).start()
            pltpu.make_async_copy(first, after, two).start()

        @pl.when(place[even] == 0)
        def _():
            pltpu.make_async_copy(first, before, one).start()
            pltpu.make_async_copy(second, after, two).start()

        return [pltpu.make_async_copy(first, before, one), pltpu.make_async_copy(first, after, two)]


def wait_for(copies):
    for copy in copies:
        copy.wait()


def gather_keys_one(copies, place, keyval, col_first, col_second, row_first, row_second, pieces):
    inner = pl.ds(48, 192)
    return (
        copies.start(keyval, pieces.at[pl.ds(0, 2), inner, :])
        + copies.start_received(
            place, EVEN_COL, col_first, col_second, pieces.at[2, inner, :], pieces.at[3, inner, :]
        )
        + copies.start_received(
            place, EVEN_ROW, row_first, row_second,
            pieces.at[:, pl.ds(0, 48), :], pieces.at[:, pl.ds(240, 48), :],
        )
    )


def gather_keys_two(copies, place, own, first, second, pieces):
    return copies.start(own, pieces.at[0]) + copies.start_received(
        place, EVEN_COL, first, second, pieces.at[1], pieces.at[2]
    )


def extend_kernel(place, keyval, first, second, result):
    result[:, 48:144, :] = keyval[...]

    def above(source):
        result[:, 0:48, :] = source[...]

    def below(source):
        result[:, 144:192, :] = source[...]

    store_received(place, EVEN_ROW, first, second, above, below)


def rim_kernel(place, rims, first, second, row_first, row_second):
    def total(part):
        rows = slice(144 * part, 144 * part + 48)
        value = rims[:, 48 * part : 48 * part + 48, :].astype(f32)
        value += first[:, rows, :].astype(f32) + second[:, rows, :].astype(f32)
        return value.astype(bf16)

    send(place, EVEN_ROW, row_first, row_second, lambda: total(1), lambda: total(0))


def sides_kernel(place, sides, first, second, col_first, col_second):
    def total(p):
        above, below = received(place, EVEN_ROW, first[2 + p], second[2 + p])
        own = sides[p].astype(f32)
        rows = [own[0:48] + above, own[48:144], own[144:192] + below]
        return jnp.concatenate(rows, 0).astype(bf16)

    send(place, EVEN_COL, col_first, col_second, lambda: total(1), lambda: total(0))


def feed_forward(hidden, norms, w_exp, w_red, bias):
    low = norm(hidden, norms).astype(bf16)
    upper = nn(low, w_exp) + bias
    gelu = upper * normal_cdf(upper)
    return hidden + nn(gelu.astype(bf16), w_red)


PROJ, EXP, RED, QKV, HEAD = 0, 2, 8, 14, 14


def first_block_kernel(
    place, lay, hidden, query, keyval, cola, colb, rowa, rowb, first_table, late, norms, ebias,
    kept, att, middle, last, query2, keyval2, first, second,
    pieces, table, score, prob, group, before, sems, keep_sems,
):
    copies = Copies(sems)
    near = gather_keys_one(copies, place, keyval, cola, colb, rowa, rowb, pieces)
    arrived = copies.start(late, group) + copies.start(hidden, before)
    spread_table(One, first_table, table)
    wait_for(near)
    leaving = attend(One, place, lay, query, pieces, table, att, score, prob, kept, keep_sems)
    wait_for(arrived)
    mid = before[...] + nn(att[...], weight_of(group, PROJ, 2))
    middle[...] = mid
    end = feed_forward(mid, norms[4:6, :], weight_of(group, EXP, 6), weight_red(group, RED), ebias[0:1, :])
    last[...] = end
    low = norm(end, norms[6:8, :]).astype(bf16)
    mixed = nn(low, weight_of(group, QKV, 6))
    for g, part in enumerate(grouped(mixed)):
        query2[g * 96 : (g + 1) * 96, :] = part[:, :D].astype(bf16)
        keyval2[g] = part[:, D:].astype(bf16)
    send(
        place, EVEN_ROW, first, second, lambda: keyval2[:, 48:, :], lambda: keyval2[:, :48, :]
    )
    wait_for(leaving)


def slot_onehot(slots, images):
    entry = lax.broadcasted_iota(i32, (384, images), 1)
    return jnp.where(slots[:, 4:5] == entry, 1.0, 0.0).astype(bf16)


def ungroup(value, ref):
    for g in range(4):
        ref[:, g >> 1, g & 1] = value[g * 96 : (g + 1) * 96].reshape(12, 8, value.shape[-1])


def second_block_kernel(
    place, lay, slots, hidden, query, own, cola, colb, first_table, late, norms, ebias,
    kept, att, middle, last, sums,
    pieces, table, score, prob, group, before, att_group, att_token, sems, keep_sems,
):
    copies = Copies(sems)
    near = gather_keys_two(copies, place, own, cola, colb, pieces)
    arrived = copies.start(late, group) + copies.start(hidden, before)
    spread_table(Two, first_table, table)
    wait_for(near)
    leaving = attend(Two, place, lay, query, pieces, table, att_group, score, prob, kept, keep_sems)
    ungroup(att_group[...], att_token)
    low = att_token[...].reshape(384, D).astype(bf16)
    att[...] = low
    wait_for(arrived)
    mid = before[...] + nn(low, weight_of(group, PROJ, 2))
    middle[...] = mid
    end = feed_forward(mid, norms[8:10, :], weight_of(group, EXP, 6), weight_red(group, RED), ebias[1:2, :])
    last[...] = end
    final = norm(end, norms[10:12, :])
    images = sums.shape[0] - 8
    where = slot_onehot(slots, images)
    high, low = two_parts(final)
    sums[...] = jnp.zeros_like(sums)
    sums[:images, :D] = tn(where, high) + tn(where, low)
    sums[images:, :images] = tn(jnp.ones((384, 8), bf16), where)
    wait_for(leaving)


def feed_forward_back(dhid, mid, gain_bias, w_exp, w_red, bias):
    low = norm(mid, gain_bias).astype(bf16)
    upper = nn(low, w_exp) + bias
    cdf = normal_cdf(upper)
    dz = dhid.astype(bf16)
    grad_red = tn((upper * cdf).astype(bf16), dz)
    slope = cdf + upper * (jnp.exp(-0.5 * upper * upper) * 0.3989422804014327)
    dupper = (nt(dz, w_red) * slope).astype(bf16)
    grad_bias = jnp.sum(dupper.astype(f32), 0, keepdims=True)
    grad_exp = tn(low, dupper)
    dx, dgain, dbias = norm_back(mid, gain_bias, nt(dupper, w_exp))
    return dhid + dx, grad_red, grad_exp, grad_bias, dgain, dbias


def put_block(grads, k, value):
    per = grads.shape[1] // D
    grads[k // per, (k % per) * D : (k % per + 1) * D, :] = value.astype(bf16)


def put_cols(grads, first, value):
    for k in range(value.shape[1] // 128):
        put_block(grads, first + k, value[:, k * 128 : (k + 1) * 128])


def put_red(grads, first, value, share):
    parts = value.reshape(D // share, 3, share, D)
    for k in range(3):
        put_cols(grads, first + 2 * k, parts[:, k].reshape(D, D))


def put_zeros(grads, first):
    per = grads.shape[1] // D
    for k in range(first, per * grads.shape[0]):
        put_block(grads, k, jnp.zeros((D, 128), f32))


def second_back_kernel(
    place, slots, sums, labels, live, hbias, hidden, middle, att, query, own, cola, colb, kept, late,
    norms, ebias,
    loss, grad_head, grad_hbias, dhidden, grads, dnorms, debias, dtable, dquery, inner, rims, first, second,
    pieces, prob, dprob, dscore, dpieces, datt, dq_group, group, grads_out, dq_token, sems,
):
    copies = Copies(sems)
    weights = copies.start(late, group)
    near = gather_keys_two(copies, place, own, cola, colb, pieces) + copies.start(kept, prob)
    images = sums.shape[0] - 8
    total = sums[:images, :D]
    diagonal = lax.broadcasted_iota(i32, (images, images), 0)
    diagonal = diagonal == lax.broadcasted_iota(i32, (images, images), 1)
    area = jnp.where(diagonal, sums[images : images + 1, :images], 0.0)
    area = jnp.sum(area, -1, keepdims=True)
    spread_area = jnp.maximum(area, 1.0)
    pooled = (total / spread_area).astype(bf16)
    wait_for(weights)
    w_head = weight_of(group, HEAD, 8)
    logits = nn(pooled, w_head) + hbias[...]
    weight = live[...] * jnp.where(area > 0.5, 1.0, 0.0)
    count = jnp.maximum(jnp.sum(weight, 0, keepdims=True), 1.0)
    cls = lax.broadcasted_iota(i32, logits.shape, 1)
    onehot = jnp.where(cls == labels[...], 1.0, 0.0)
    top = jnp.max(logits, -1, keepdims=True)
    logsum = jnp.log(jnp.sum(jnp.exp(logits - top), -1, keepdims=True)) + top
    cross = logsum - jnp.sum(onehot * logits, -1, keepdims=True)
    loss[...] = jnp.broadcast_to(jnp.sum(weight * cross, 0, keepdims=True) / count, loss.shape)
    dlogit = ((weight / count) * (jnp.exp(logits - logsum) - onehot)).astype(bf16)
    grad_hbias[...] = jnp.sum(dlogit.astype(f32), 0, keepdims=True)
    share = grad_head.shape[0]
    channel = lax.broadcasted_iota(i32, (D, share), 0)
    mine = lax.broadcasted_iota(i32, (D, share), 1) + place[2]
    own_pooled = nn(pooled, jnp.where(channel == mine, 1.0, 0.0).astype(bf16)).astype(bf16)
    grad_head[...] = tn(own_pooled, dlogit)
    high, low = two_parts(nt(dlogit, w_head) / spread_area)
    where = slot_onehot(slots, images)
    dfinal = nn(where, high) + nn(where, low)
    dhid, dgain, dbias = norm_back(hidden[...], norms[10:12, :], dfinal)
    dnorms[2:3, :] = dgain
    dnorms[3:4, :] = dbias
    dhid, grad_red, grad_exp, grad_bias, dgain, dbias = feed_forward_back(
        dhid, middle[...], norms[8:10, :], weight_of(group, EXP, 6), weight_red(group, RED), ebias[1:2, :]
    )
    put_cols(grads_out, 0, grad_exp)
    put_red(grads_out, 6, grad_red, share)
    debias[...] = grad_bias
    dnorms[0:1, :] = dgain
    dnorms[1:2, :] = dbias
    dhidden[...] = dhid
    dy = dhid.astype(bf16)
    put_cols(grads_out, 12, tn(att[...], dy))
    put_zeros(grads_out, 14)
    leaving = copies.start(grads_out, grads)
    back = nt(dy, weight_of(group, PROJ, 2))
    for g, part in enumerate(grouped(back)):
        datt[g * 96 : (g + 1) * 96, :] = part.astype(bf16)
    wait_for(near)
    attend_back(Two, query, datt, pieces, prob, dq_group, dpieces, dtable, dprob, dscore)
    ungroup(dq_group[...], dq_token)
    dquery[...] = dq_token[...].reshape(384, D).astype(bf16)
    inner[...] = dpieces[0, :, 48:144, :]
    rims[:, 0:48, :] = dpieces[0, :, 0:48, :].astype(bf16)
    rims[:, 48:96, :] = dpieces[0, :, 144:192, :].astype(bf16)
    send(
        place, EVEN_COL, first, second,
        lambda: dpieces[2].astype(bf16), lambda: dpieces[1].astype(bf16),
    )
    wait_for(leaving)


def position_kernel(dtable, dpos, dfirst, *, geo):
    dpos[...] = gather_table(geo, dtable, dfirst)


def first_back_kernel(
    place, dhid_in, dquery2, dkv, dcola, dcolb, drowa, drowb, hidden, middle, att, query,
    keyval, cola, colb, rowa, rowb, kept, late, norms, ebias,
    dhidden, grads, dnorms, debias, dtable, dquery, inner, sides, first, second,
    pieces, prob, dprob, dscore, dpieces, datt, dq, group, grads_out, parta, partb, dkv_token, sems,
):
    copies = Copies(sems)
    rows = pl.ds(48, 96)
    parts = copies.start(dcola.at[:, rows, :], parta) + copies.start(dcolb.at[:, rows, :], partb)
    weights = copies.start(late, group)
    near = gather_keys_one(copies, place, keyval, cola, colb, rowa, rowb, pieces)
    near += copies.start(kept, prob)
    wait_for(parts)
    for g in range(4):
        total = dkv[g] + parta[g].astype(f32) + partb[g].astype(f32)
        total += jnp.concatenate(received(place, EVEN_ROW, drowa[g], drowb[g]), 0)
        dkv_token[:, g >> 1, g & 1] = total.reshape(12, 8, 2 * D)
    dmixed = jnp.concatenate(
        [dquery2[...], dkv_token[...].reshape(384, 2 * D).astype(bf16)], 1
    )
    low = norm(hidden[...], norms[6:8, :]).astype(bf16)
    put_cols(grads_out, 0, tn(low, dmixed))
    wait_for(weights)
    dx, dgain, dbias = norm_back(
        hidden[...], norms[6:8, :], nt(dmixed, weight_of(group, QKV, 6))
    )
    dnorms[2:3, :] = dgain
    dnorms[3:4, :] = dbias
    dhid, grad_red, grad_exp, grad_bias, dgain, dbias = feed_forward_back(
        dhid_in[...] + dx, middle[...], norms[4:6, :], weight_of(group, EXP, 6), weight_red(group, RED),
        ebias[0:1, :],
    )
    put_cols(grads_out, 6, grad_exp)
    put_red(grads_out, 12, grad_red, D // late.shape[1])
    debias[...] = grad_bias
    dnorms[0:1, :] = dgain
    dnorms[1:2, :] = dbias
    dhidden[...] = dhid
    dy = dhid.astype(bf16)
    put_cols(grads_out, 18, tn(att[...], dy))
    put_zeros(grads_out, 20)
    leaving = copies.start(grads_out, grads)
    datt[...] = nt(dy, weight_of(group, PROJ, 2)).astype(bf16)
    wait_for(near)
    attend_back(One, query, datt, pieces, prob, dq, dpieces, dtable, dprob, dscore)
    dquery[...] = dq[...].astype(bf16)
    inner[...] = dpieces[0:2, 48:240, :]
    sides[...] = dpieces[2:4, 48:240, :].astype(bf16)
    send(
        place, EVEN_ROW, first, second,
        lambda: dpieces[:, 240:288, :].astype(bf16), lambda: dpieces[:, 0:48, :].astype(bf16),
    )
    wait_for(leaving)


SMALL_ROWS = 80


def front_back_kernel(
    place, dhid_in, dquery, inner, drowa, drowb, dcola, dcolb, hidden, conv, patches, early,
    norms, dnorms1, dnorms2, debias1, debias2, dpos1, dpos2,
    keep, give,
    grads, small,
):
    left, right = received(place, EVEN_COL, dcola[...], dcolb[...])
    left, right = left.reshape(24, 8, 2 * D), right.reshape(24, 8, 2 * D)
    sub = lax.broadcasted_iota(i32, left.shape, 1)

    def whole(p):
        above, below = received(place, EVEN_ROW, drowa[p], drowb[p])
        top = inner[p, 0:48, :] + above
        bottom = inner[p, 144:192, :] + below
        return jnp.concatenate([top, inner[p, 48:144, :], bottom], 0).reshape(24, 8, 2 * D)

    zero = whole(0) + jnp.where(sub < 4, left, pltpu.roll(right, 4, 1))
    one = whole(1) + jnp.where(sub < 4, pltpu.roll(left, 4, 1), right)
    dkv = jnp.stack([zero, one], 1).reshape(384, 2 * D).astype(bf16)
    dmixed = jnp.concatenate([dquery[...], dkv], 1)
    h = hidden[...]
    low = norm(h, norms[2:4, :]).astype(bf16)
    put_cols(grads, 9, tn(low, dmixed))
    w_qkv = weight_of(early, 9, 6)
    dx, dgain1, dbias1 = norm_back(h, norms[2:4, :], nt(dmixed, w_qkv))
    dconv, dgain0, dbias0 = norm_back(conv[...], norms[0:2, :], dhid_in[...] + dx)
    put_cols(grads, 0, tn(dconv.astype(bf16), patches[...]))
    put_zeros(grads, 15)

    def place_row(first, value):
        for k in range(value.shape[1] // 128):
            small[first + k : first + k + 1, :] = value[:, k * 128 : (k + 1) * 128]

    small[...] = jnp.zeros_like(small)
    for k, value in enumerate((dgain0, dbias0, dgain1, dbias1)):
        place_row(2 * k, value)
    for k in range(4):
        place_row(8 + 2 * k, dnorms1[k : k + 1, :])
        place_row(16 + 2 * k, dnorms2[k : k + 1, :])
    place_row(24, debias1[...])
    place_row(30, debias2[...])
    for first, value in ((40, dpos1), (56, dpos2)):
        small[first : first + 8, :] = value[:, :128]
        small[first + 8 : first + 16, : WIN - 128] = value[:, 128:]
    begin = grads.shape[1] - SMALL_ROWS
    for col in range(grads.shape[0]):
        grads[col, begin:, :] = small[...].astype(bf16)
    halve(place, 0, grads, keep, give)


def halve(place, stage, parts, keep, give):
    bit = (place[COL] >> stage) & 1
    for k in range(keep.shape[0]):
        keep[k] = parts[2 * k + bit]
        give[k] = parts[2 * k + 1 - bit]


def halve_kernel(place, kept, given, keep, give, total, *, stage):
    total[...] = (kept[...].astype(f32) + given[...].astype(f32)).astype(bf16)
    halve(place, stage, total, keep, give)


def between_kernel(second, first, kept, given, result):
    rows = result.shape[0]
    sh = D // rows
    begin = 0
    for group in (second, first):
        for k in range(group.shape[0] // D):
            result[:, begin : begin + sh, :] = group[k * D : (k + 1) * D, :].reshape(rows, sh, 128)
            begin += sh
    for k in range(kept.shape[1] // D):
        span = slice(k * D, (k + 1) * D)
        total = kept[0, span, :].astype(f32) + given[0, span, :].astype(f32)
        result[:, begin : begin + sh, :] = total.astype(bf16).reshape(rows, sh, 128)
        begin += sh
    span = slice(kept.shape[1] - SMALL_ROWS, kept.shape[1])
    small = (kept[0, span, :].astype(f32) + given[0, span, :].astype(f32)).astype(bf16)
    for row in range(rows):
        result[row, begin:, :] = small


def last_sum_kernel(parts, result, small):
    total = parts[0].astype(f32)
    for row in range(1, parts.shape[0]):
        total += parts[row].astype(f32)
    count = result.shape[0]
    result[...] = total[:count].astype(bf16)
    small[...] = total[count:]


def adamw(weight, grad, first, second):
    first = beta_one * first + (1.0 - beta_one) * grad
    second = beta_two * second + (1.0 - beta_two) * grad * grad
    fix_one = 1.0 - beta_one**STEP
    fix_two = 1.0 - beta_two**STEP
    new = weight - learn_rate * (
        first / fix_one / (jnp.sqrt(second / fix_two) + eps_adam) + decay_rate * weight
    )
    return (first, second, new)


def adamw_kernel(grads, *refs, sh, per):
    ins = [refs[3 * n : 3 * n + 3] for n in range(5)]
    outs = [refs[15 + 3 * n : 18 + 3 * n] for n in range(5)]

    def update(n, group, k, *where):
        begin = (sum(per[:group]) + k % per[group]) * sh
        grad = grads[k // per[group], begin : begin + sh, :].astype(f32)
        weight, first, second = (ref[where] for ref in ins[n])
        for ref, value in zip(outs[n], adamw(weight, grad, first, second)):
            ref[where] = value

    every = slice(None)
    for k in range(9):
        update(0, 2, k, every, slice(k * 128, (k + 1) * 128))
    for k in range(6):
        lanes = slice(k * 128, (k + 1) * 128)
        update(1, 2, 9 + k, 0, every, lanes)
        update(1, 1, k, 1, every, lanes)
        update(3, 1, 6 + k, 0, every, lanes)
        update(3, 0, k, 1, every, lanes)
        rows, half = slice((k // 2) * sh, (k // 2 + 1) * sh), slice((k % 2) * 128, (k % 2 + 1) * 128)
        update(4, 1, 12 + k, 0, rows, half)
        update(4, 0, 6 + k, 1, rows, half)
    for k in range(2):
        lanes = slice(k * 128, (k + 1) * 128)
        update(2, 1, 18 + k, 0, every, lanes)
        update(2, 0, 12 + k, 1, every, lanes)


def onward(value, axis):
    count = lax.axis_size(axis)
    return lax.ppermute(value, axis, [(i, (i + 1) % count) for i in range(count)])


def swaps(first, second, axis):
    count = lax.axis_size(axis)
    pairs = [[(i, i + 1) for i in range(begin, count - 1, 2)] for begin in (0, 1)]
    both = [low + [(j, i) for i, j in low] for low in pairs]
    return lax.ppermute(first, axis, both[0]), lax.ppermute(second, axis, both[1])


def sum_all(value):
    for axis in ("col", "row"):
        count = lax.axis_size(axis)
        step = 1

        def other(flip):
            return lax.ppermute(value, axis, [(i, i ^ flip) for i in range(count)])

        while step < count:
            if 4 * step <= count:
                near, far, both = other(step), other(2 * step), other(3 * step)
                value = (value + near) + (far + both)
                step *= 4
            else:
                value = value + other(step)
                step *= 2
    return value


def on_device(
    stem_map, layout, labels, live,
    conv_weight, input_proj, output_proj, expand_weight, reduce_weight, head_weight, small_params,
    first_conv, first_input, first_output, first_expand, first_reduce, first_head, first_small,
    second_conv, second_input, second_output, second_expand, second_reduce, second_head, second_small,
):
    nr, nc = lax.axis_size("row"), lax.axis_size("col")
    sh = D // nr
    images = labels.shape[0]
    padded = -(-images // 8) * 8
    per = [-(-count // nc) for count in (14, 20, 15)]
    row_index, col_index = lax.axis_index("row"), lax.axis_index("col")
    parts = [-(-count // nc) * sh for count in (15, 20, 22)]
    early, late = run(
        functools.partial(pack_kernel, across=nc),
        [out((nr, parts[0], 128), bf16), out((nr, parts[1] + parts[2], 128), bf16)],
        [
            col_index.astype(i32)[None], conv_weight.T, input_proj, output_proj, expand_weight, reduce_weight,
            head_weight,
        ],
        [pltpu.VMEM((part * nc, 128), bf16) for part in parts],
        {0: SMEM},
        56,
    )
    early = lax.all_to_all(early, "row", 0, 0, tiled=True)
    norms = small_params[: 12 * D].reshape(12, D)
    start = 12 * D
    ebias = small_params[start : start + LAYERS * FF].reshape(LAYERS, FF)
    start += LAYERS * FF
    hbias = jnp.pad(small_params[start : start + CLASSES], (0, 24), constant_values=MASKED)[None]
    start += CLASSES
    pos_bias = small_params[start:].reshape(LAYERS * HEADS, 169)
    first_one, first_two = run(
        table_kernel,
        [out((geo.pieces, HEADS * geo.across, 128)) for geo in (One, Two)],
        [jnp.pad(pos_bias, ((0, 0), (0, WIN - 169)))],
    )
    place = [row_index * 24, col_index * 16, row_index * sh, (row_index + 1) % 2, (col_index + 1) % 2, col_index]
    place = jnp.stack(place).astype(i32)
    lay_one = layout.reshape(5, 24, 8, 2).transpose(1, 3, 2, 0).reshape(384, 5)
    lay_two = layout.reshape(5, 12, 2, 8, 2).transpose(2, 4, 1, 3, 0).reshape(384, 5)
    above = onward(stem_map[-1:], "row")
    rim = jnp.concatenate([above[:, -1:], stem_map[:, -1:]], 0)
    rim = jnp.broadcast_to(onward(rim, "col"), (49, 8, 128))
    patches = run(
        patch_kernel,
        [out((384, 1152), bf16)],
        [place, stem_map.reshape(1536, 128), above.reshape(32, 128), rim.reshape(392, 128), lay_one],
        [pltpu.VMEM((1536, 128), f32), pltpu.VMEM((32, 128), f32)],
        {0: SMEM},
    )[0]
    late, _, _ = lax.optimization_barrier((late, above, early))
    early = lax.all_gather(early, "col", axis=0)
    late = lax.all_to_all(late, "row", 0, 0, tiled=True)
    rows48, edge = out((4, 48, 2 * D), bf16), out((192, 2 * D), bf16)
    conv_out, hidden0, query1, keyval1, *edges = run(
        front_kernel,
        [out((384, D)), out((384, D)), out((384, D), bf16), out((2, 192, 2 * D), bf16), edge, edge],
        [place, patches, early, norms],
        specs={0: SMEM},
    )
    late, _ = lax.optimization_barrier((late, edges))
    late1 = lax.all_gather(late[:, : parts[1]], "col", axis=0)
    late2 = lax.all_gather(late[:, parts[1] :], "col", axis=0)
    cols1 = swaps(*edges, "col")
    rows1 = swaps(*run(ring_kernel, [rows48] * 2, [place, keyval1, *cols1], specs={0: SMEM}), "row")
    hbm = pl.BlockSpec(memory_space=pl.ANY)
    tokens, tokens_low, ext = out((384, D)), out((384, D), bf16), out((4, 192, 2 * D), bf16)
    token5 = lambda width: pltpu.VMEM((12, 2, 2, 8, width), f32)
    like = lambda x: pltpu.VMEM(x.shape, x.dtype)
    copy_sems = lambda count: pltpu.SemaphoreType.DMA((count,))

    def tiles(geo, back):
        square = (HEADS * geo.queries, geo.keys)
        shape = (4, 288, 2 * D) if geo is One else (3, 4, 192, 2 * D)
        pieces, prob = pltpu.VMEM(shape, bf16), pltpu.VMEM((geo.steps, *square), bf16)
        many = (geo.together, *square)
        if not back:
            return [pieces, pltpu.VMEM(square, f32), pltpu.VMEM(many, f32), prob]
        return [
            pieces, prob, pltpu.VMEM(many, f32), pltpu.VMEM(many, bf16), pltpu.VMEM(shape, f32),
            pltpu.VMEM((384, D), bf16), pltpu.VMEM((384, D), f32),
        ]

    probs = lambda geo: out((geo.steps, HEADS * geo.queries, geo.keys), bf16)
    dtable = lambda geo: out((HEADS * geo.queries, geo.keys))
    turns = lambda geo: copy_sems(geo.steps // geo.together)
    near1 = [keyval1, *cols1, *rows1]
    kept1, att1, middle1, last1, query2, keyval2, *edges = run(
        first_block_kernel,
        [probs(One), tokens_low, tokens, tokens, tokens_low, out((4, 96, 2 * D), bf16), rows48, rows48],
        [place, lay_one, hidden0, query1, *near1, first_one, late1, norms, ebias],
        tiles(One, False) + [like(late1), like(hidden0), copy_sems(7), turns(One)],
        {0: SMEM, **dict.fromkeys((2, 4, 5, 6, 7, 8, 10), hbm)},
        56,
        {0: hbm},
    )
    rows2 = swaps(*edges, "row")
    own2 = run(extend_kernel, [ext], [place, keyval2, *rows2], specs={0: SMEM})[0]
    near2 = [own2, *swaps(own2, own2, "col")]
    kept2, att2, middle2, last2, sums = run(
        second_block_kernel,
        [probs(Two), tokens_low, tokens, tokens, out((padded + 8, max(D, -(-padded // 128) * 128)))],
        [place, lay_two, lay_one, last1, query2, *near2, first_two, late2, norms, ebias],
        tiles(Two, False)
        + [like(late2), like(last1), pltpu.VMEM((384, D), f32), token5(D), copy_sems(5), turns(Two)],
        {0: SMEM, **dict.fromkeys((3, 5, 6, 7, 9), hbm)},
        56,
        {0: hbm},
    )
    sums = sum_all(sums)
    pad_images = lambda x: jnp.pad(x, (0, padded - images))[:, None]
    grads_of = lambda group: out((nc, per[group] * D, 128), bf16)
    (
        loss, grad_head, grad_hbias, dhid, grads2, dnorms2, debias2, dtable2, dquery2, inner2, rims2, *edges,
    ) = run(
        second_back_kernel,
        [
            out((8, 128)), out((sh, 1024)), out((1, 1024)), tokens, grads_of(0),
            out((4, D)), out((1, FF)), dtable(Two), tokens_low,
            out((4, 96, 2 * D)), out((4, 96, 2 * D), bf16), ext, ext,
        ],
        [
            place, lay_one, sums, pad_images(labels), pad_images(live.astype(f32)), hbias,
            last2, middle2, att2, query2, *near2, kept2, late2, norms, ebias,
        ],
        tiles(Two, True) + [like(late2), like(grads_of(0)), token5(D), copy_sems(6)],
        {0: SMEM, **dict.fromkeys((10, 11, 12, 13, 14), hbm)},
        56,
        {4: hbm},
    )
    dcols2 = swaps(*edges, "col")
    drows2 = swaps(*run(rim_kernel, [rows48] * 2, [place, rims2, *dcols2], specs={0: SMEM}), "row")
    grads2 = lax.psum_scatter(grads2, "col", scatter_dimension=0, tiled=False)

    def position(geo, table):
        scratch = [pltpu.VMEM((geo.pieces, HEADS * geo.across, 128), f32)]
        return run(functools.partial(position_kernel, geo=geo), [out((HEADS, WIN))], [table], scratch)[0]

    dpos2 = position(Two, dtable2)
    part2 = pltpu.VMEM((4, 96, 2 * D), bf16)
    dhid, grads1, dnorms1, debias1, dtable1, dquery1, inner1, sides1, *edges = run(
        first_back_kernel,
        [
            tokens, grads_of(1), out((4, D)), out((1, FF)), dtable(One),
            tokens_low, out((2, 192, 2 * D)), out((2, 192, 2 * D), bf16), rows48, rows48,
        ],
        [
            place, dhid, dquery2, inner2, *dcols2, *drows2, last1, middle1, att1, query1,
            *near1, kept1, late1, norms, ebias,
        ],
        tiles(One, True) + [like(late1), like(grads_of(1)), part2, part2, token5(2 * D), copy_sems(10)],
        {0: SMEM, **dict.fromkeys((4, 5, 12, 13, 14, 15, 16, 17, 18), hbm)},
        56,
        {1: hbm},
    )
    drows1 = swaps(*edges, "row")
    grads1 = lax.psum_scatter(grads1, "col", scatter_dimension=0, tiled=False)
    dpos1 = position(One, dtable1)
    dcols1 = swaps(*run(sides_kernel, [edge] * 2, [place, sides1, *drows1], specs={0: SMEM}), "col")
    part = per[2] * D + SMALL_ROWS
    half = lambda count: out((count, part, 128), bf16)
    kept, given = run(
        front_back_kernel,
        [half(nc // 2), half(nc // 2)],
        [
            place, dhid, dquery1, inner1, *drows1, *dcols1, hidden0, conv_out, patches,
            early, norms, dnorms1, dnorms2, debias1, debias2, dpos1, dpos2,
        ],
        [pltpu.VMEM((nc, part, 128), bf16), pltpu.VMEM((SMALL_ROWS, 128), f32)],
        {0: SMEM},
    )
    stage = 0
    while True:
        given = lax.ppermute(given, "col", [(i, i ^ (1 << stage)) for i in range(nc)])
        stage += 1
        if 1 << stage == nc:
            break
        count = nc >> (stage + 1)
        kept, given = run(
            functools.partial(halve_kernel, stage=stage),
            [half(count), half(count)],
            [place, kept, given],
            [pltpu.VMEM((2 * count, part, 128), bf16)],
            {0: SMEM},
        )
    mine = run(
        between_kernel,
        [out((nr, sum(per) * sh + SMALL_ROWS, 128), bf16)],
        [grads2, grads1, kept, given],
        vmem=56,
    )[0]
    mine = lax.all_to_all(mine, "row", 0, 0, tiled=True)
    mine, small = run(
        last_sum_kernel, [out((sum(per) * sh, 128), bf16), out((SMALL_ROWS, 128))], [mine]
    )
    grads = lax.all_gather(mine, "col", axis=0)
    wide = [
        conv_weight.T, first_conv.T, second_conv.T, input_proj, first_input, second_input,
        output_proj, first_output, second_output, expand_weight, first_expand, second_expand,
        reduce_weight, first_reduce, second_reduce,
    ]
    new = run(
        functools.partial(adamw_kernel, sh=sh, per=per), [out(x.shape) for x in wide], [grads, *wide]
    )
    new = [x.T for x in new[:3]] + list(new[3:])
    pos = [
        jnp.concatenate([small[k : k + 8], small[k + 8 : k + 16, : 169 - 128]], 1).reshape(-1)
        for k in (40, 56)
    ]
    grad_small = jnp.concatenate([small[:36].reshape(-1), grad_hbias[0, :CLASSES], *pos])
    head = adamw(head_weight, grad_head[:, :CLASSES], first_head, second_head)
    return (loss[0, 0], *new, *head, *adamw(small_params, grad_small, first_small, second_small))


def solution(mesh):
    return jax.shard_map(
        on_device,
        mesh=mesh,
        in_specs=(
            P("row", "col", None),
            P(None, "row", "col"),
            P(),
            P(),
            P(None, "row"),
            P(None, "row", None),
            P(None, "row", None),
            P(None, "row", None),
            P(None, "row", None),
            P("row", None),
            P(),
            P(None, "row"),
            P(None, "row", None),
            P(None, "row", None),
            P(None, "row", None),
            P(None, "row", None),
            P("row", None),
            P(),
            P(None, "row"),
            P(None, "row", None),
            P(None, "row", None),
            P(None, "row", None),
            P(None, "row", None),
            P("row", None),
            P(),
        ),
        out_specs=(
            P(),
            P(None, "row"),
            P(None, "row"),
            P(None, "row"),
            P(None, "row", None),
            P(None, "row", None),
            P(None, "row", None),
            P(None, "row", None),
            P(None, "row", None),
            P(None, "row", None),
            P(None, "row", None),
            P(None, "row", None),
            P(None, "row", None),
            P(None, "row", None),
            P(None, "row", None),
            P(None, "row", None),
            P("row", None),
            P("row", None),
            P("row", None),
            P(),
            P(),
            P(),
        ),
        check_vma=False,
    )
```

```python
import functools

import jax
import jax.numpy as jnp
from jax import lax
from jax.experimental import pallas as pl
from jax.experimental.pallas import tpu as pltpu
from jax.sharding import PartitionSpec as P

D = 256
HEADS = 8
FF = 768
CLASSES = 1000
LAYERS = 2
STEP = 5
WIN = 176

eps_norm = 1e-05
beta_one = 0.9
beta_two = 0.999
learn_rate = 0.2
decay_rate = 0.05
eps_adam = 1e-08
scale = (D // HEADS) ** -0.5

bf16 = jnp.bfloat16
f32 = jnp.float32
i32 = jnp.int32
MASKED = -1e30
LOG2E = 1.4426950408889634
MIB = 1024 * 1024


def nn(a, b):
    return lax.dot_general(a, b, (((1,), (0,)), ((), ())), preferred_element_type=f32)


def nt(a, b):
    return lax.dot_general(a, b, (((1,), (1,)), ((), ())), preferred_element_type=f32)


def tn(a, b):
    return lax.dot_general(a, b, (((0,), (0,)), ((), ())), preferred_element_type=f32)


def two_parts(x):
    high = x.astype(bf16)
    return high, (x - high.astype(f32)).astype(bf16)


def norm_parts(x):
    centre = x - jnp.mean(x, -1, keepdims=True)
    rstd = lax.rsqrt(jnp.mean(centre * centre, -1, keepdims=True) + eps_norm)
    return centre * rstd, rstd


def norm(x, gain_bias):
    return norm_parts(x)[0] * gain_bias[0:1] + gain_bias[1:2]


def norm_back(x, gain_bias, dy):
    xhat, rstd = norm_parts(x)
    dxhat = dy * gain_bias[0:1]
    dx = rstd * (
        dxhat
        - jnp.mean(dxhat, -1, keepdims=True)
        - xhat * jnp.mean(dxhat * xhat, -1, keepdims=True)
    )
    return dx, jnp.sum(dy * xhat, 0, keepdims=True), jnp.sum(dy, 0, keepdims=True)


def normal_cdf(u):
    return 0.5 * (1.0 + lax.erf(u * 0.7071067811865476))


class One:
    dilation, queries, across, pieces, steps = 1, 64, 16, 4, 6
    together = 3
    keys = pieces * 128

    @staticmethod
    def key_col(piece, c8):
        two = 2 * (c8 & 3) + (c8 >> 2)
        return jnp.where(
            piece == 0,
            2 * c8,
            jnp.where(piece == 1, 2 * c8 + 1, jnp.where(piece == 2, two - 8, two + 16)),
        )

    @staticmethod
    def query_col(index):
        return 2 * (index & 7) + (index >> 3)


class Two:
    dilation, queries, across, pieces, steps = 2, 32, 8, 3, 12
    together = 3
    keys = pieces * 128

    @staticmethod
    def key_col(piece, c8):
        return jnp.where(piece == 0, c8, jnp.where(piece == 1, c8 - 8, c8 + 8))

    @staticmethod
    def query_col(index):
        return index


def key_place(geo):
    lane = lax.broadcasted_iota(i32, (1, geo.keys), 1)
    return (lane >> 3) & 15, geo.key_col(lane >> 7, lane & 7)


def window_mask(geo, lay, step, row_first, col_first):
    token = lax.broadcasted_iota(i32, (geo.queries, 1), 0)
    if geo.dilation == 1:
        block = step
        row = block * 4 + (token >> 4)
        col = geo.query_col(token & 15)
        row_pos, col_pos = row_first + row, col_first + col
    else:
        group = step // 3
        block = step - 3 * group
        row = block * 4 + (token >> 3)
        col = token & 7
        row_pos = row_first + 2 * row + (group >> 1)
        col_pos = col_first + 2 * col + (group & 1)

    def begin(place, first, end):
        local = place - first
        extent = end - first
        if geo.dilation == 1:
            index, length = local, extent
        else:
            index, length = local >> 1, (extent - (local & 1) + 1) >> 1
        return jnp.minimum(jnp.maximum(index - 3, 0), length - 7) - index

    row_start = row + begin(row_pos, lay[:, 0:1], lay[:, 1:2])
    col_start = col + begin(col_pos, lay[:, 2:3], lay[:, 3:4])
    key_row, key_col = key_place(geo)
    down = key_row + (block * 4 - 6) - row_start
    right = key_col - col_start
    inside = (down >= 0) & (down <= 6) & (right >= 0) & (right <= 6)
    return jnp.where(inside, 0.0, MASKED).astype(f32)


def position_onehot(geo, across):
    key_row, key_col = key_place(geo)
    right = key_col - geo.query_col(across) + 6
    index = jnp.where((right >= 0) & (right <= 12) & (key_row <= 12), key_row * 13 + right, -1)
    entry = lax.broadcasted_iota(i32, (WIN, geo.keys), 0)
    return jnp.where(entry == index, 1.0, 0.0).astype(bf16)


def position_table(geo, bias, first_ref):
    high = bias.astype(bf16)
    rest = bias - high.astype(f32)
    mid = rest.astype(bf16)
    low = (rest - mid.astype(f32)).astype(bf16)
    for across in range(geo.across):
        onehot = position_onehot(geo, across)
        row = nn(high, onehot) + nn(mid, onehot) + nn(low, onehot)
        for piece in range(geo.pieces):
            lanes = slice(piece * 128, piece * 128 + 128)
            first_ref[piece, pl.ds(across, HEADS, stride=geo.across), :] = row[:, lanes]


def spread_table(geo, first_ref, table_ref):
    for head in range(HEADS):
        for row in range(4):
            for piece in range(geo.pieces):
                lanes = slice(piece * 128, piece * 128 + 128)
                value = first_ref[piece, head * geo.across : (head + 1) * geo.across, :]
                value = value * LOG2E
                if row:
                    value = pltpu.roll(value, 8 * row, 1)
                begin = head * geo.queries + row * geo.across
                table_ref[begin : begin + geo.across, lanes] = value


def gather_table(geo, table_ref, first_ref):
    for head in range(HEADS):
        for piece in range(geo.pieces):
            lanes = slice(piece * 128, piece * 128 + 128)
            total = None
            for row in range(4):
                begin = head * geo.queries + row * geo.across
                value = table_ref[begin : begin + geo.across, lanes]
                if row:
                    value = pltpu.roll(value, 128 - 8 * row, 1)
                total = value if total is None else total + value
            first_ref[piece, head * geo.across : (head + 1) * geo.across, :] = total
    grad = jnp.zeros((HEADS, WIN), f32)
    for across in range(geo.across):
        onehot = position_onehot(geo, across)
        rows = pl.ds(across, HEADS, stride=geo.across)
        first = [first_ref[piece, rows, :] for piece in range(geo.pieces)]
        high, low = two_parts(jnp.concatenate(first, 1))
        grad = grad + nt(high, onehot) + nt(low, onehot)
    return grad


def head_lanes(head):
    lane = lax.broadcasted_iota(i32, (1, D), 1)
    return jnp.where((lane >> 5) == head, 1.0, 0.0)


def by_head(x):
    return jnp.concatenate([x * head_lanes(h).astype(x.dtype) for h in range(HEADS)], 0)


def from_heads(x):
    count = x.shape[0] // HEADS
    total = None
    for h in range(HEADS):
        part = x[h * count : (h + 1) * count] * head_lanes(h)
        total = part if total is None else total + part
    return total


def key_rows(geo, step):
    if geo.dilation == 1:
        return None, pl.multiple_of(step * 32, 32)
    group = step // 3
    return group, pl.multiple_of((step - 3 * group) * 32, 32)


def load_keys(geo, pieces, step, lanes):
    group, first = key_rows(geo, step)
    if geo.dilation == 1:
        parts = [pieces[p, pl.ds(first, 128), lanes] for p in range(4)]
    else:
        parts = [pieces[p, group, pl.ds(first, 128), lanes] for p in range(3)]
    return jnp.concatenate(parts, 0)


def add_keys(geo, pieces, step, lanes, value):
    group, first = key_rows(geo, step)
    for p in range(geo.pieces):
        part = value[p * 128 : (p + 1) * 128]
        if geo.dilation == 1:
            pieces[p, pl.ds(first, 128), lanes] += part
        else:
            pieces[p, group, pl.ds(first, 128), lanes] += part


KEY = slice(0, D)
VALUE = slice(D, 2 * D)


def softmax_rows(score, table, mask):
    score = score * (scale * LOG2E) + (table + mask)
    weight = jnp.exp2(score - jnp.max(score, -1, keepdims=True))
    return weight * (1.0 / jnp.sum(weight, -1, keepdims=True))


def attend(geo, place, lay_ref, query_ref, pieces, table_ref, out_ref, score_ref, prob_ref, kept, sems):
    count = geo.queries
    together = score_ref.shape[0]

    def keep(index):
        span = pl.ds(index * together, together)
        return pltpu.make_async_copy(prob_ref.at[span], kept.at[span], sems.at[index])

    def steps_of(index, carry):
        steps = [index * together + n for n in range(together)]
        rows = [pl.ds(pl.multiple_of(step * count, count), count) for step in steps]
        for n, step in enumerate(steps):
            score_ref[n] = nt(by_head(query_ref[rows[n], :]), load_keys(geo, pieces, step, KEY))
        masks = [
            window_mask(geo, lay_ref[rows[n], :], step, place[0], place[1])
            for n, step in enumerate(steps)
        ]
        for h in range(HEADS):
            span = slice(h * count, (h + 1) * count)
            for n, step in enumerate(steps):
                prob = softmax_rows(score_ref[n, span, :], table_ref[span, :], masks[n])
                prob_ref[step, span, :] = prob.astype(bf16)
        keep(index).start()
        for n, step in enumerate(steps):
            out = nn(prob_ref[step], load_keys(geo, pieces, step, VALUE))
            out_ref[rows[n], :] = from_heads(out).astype(out_ref.dtype)
        return carry

    lax.fori_loop(0, geo.steps // together, steps_of, 0)
    return [keep(index) for index in range(geo.steps // together)]


def attend_back(
    geo, query_ref, dout_ref, pieces, prob_ref, dquery_ref, dpieces, dtable_ref, dprob_ref, dscore_ref,
):
    count = geo.queries
    together = dprob_ref.shape[0]
    dtable_ref[...] = jnp.zeros_like(dtable_ref)
    dpieces[...] = jnp.zeros_like(dpieces)

    def steps_of(index, carry):
        steps = [index * together + n for n in range(together)]
        rows = [pl.ds(pl.multiple_of(step * count, count), count) for step in steps]
        for n, step in enumerate(steps):
            dprob_ref[n] = nt(by_head(dout_ref[rows[n], :]), load_keys(geo, pieces, step, VALUE))
        for h in range(HEADS):
            span = slice(h * count, (h + 1) * count)
            total = dtable_ref[span, :]
            for n, step in enumerate(steps):
                prob = prob_ref[step, span, :].astype(f32)
                dprob = dprob_ref[n, span, :]
                dscore = prob * (dprob - jnp.sum(prob * dprob, -1, keepdims=True))
                total += dscore
                dscore_ref[n, span, :] = dscore.astype(bf16)
            dtable_ref[span, :] = total
        for n, step in enumerate(steps):
            wide, dwide = by_head(query_ref[rows[n], :]), by_head(dout_ref[rows[n], :])
            dscore = dscore_ref[n]
            add_keys(geo, dpieces, step, VALUE, tn(prob_ref[step], dwide))
            add_keys(geo, dpieces, step, KEY, tn(dscore, wide) * scale)
            dquery_ref[rows[n], :] = from_heads(nn(dscore, load_keys(geo, pieces, step, KEY))) * scale
        return carry

    lax.fori_loop(0, geo.steps // together, steps_of, 0)


def grouped(x):
    parts = x.reshape(12, 2, 2, 8, x.shape[-1])
    return [parts[:, g >> 1, g & 1].reshape(96, x.shape[-1]) for g in range(4)]


EVEN_ROW, EVEN_COL, COL = 3, 4, 5


def send(place, even, first, second, after, before):
    for ref, when_even, when_odd in ((first, after, before), (second, before, after)):

        @pl.when(place[even] == 1)
        def _(ref=ref, value=when_even):
            ref[...] = value()

        @pl.when(place[even] == 0)
        def _(ref=ref, value=when_odd):
            ref[...] = value()


def received(place, even, first, second):
    flag = place[even].astype(f32)
    one, two = first.astype(f32), second.astype(f32)
    return two * flag + one * (1.0 - flag), one * flag + two * (1.0 - flag)


def store_received(place, even, first, second, before, after):
    @pl.when(place[even] == 1)
    def _():
        before(second)
        after(first)

    @pl.when(place[even] == 0)
    def _():
        before(first)
        after(second)


def run(kernel, outs, ins, scratch=(), specs=None, vmem=16, out_specs=None):
    in_specs = [pl.BlockSpec(memory_space=pltpu.VMEM)] * len(ins)
    for index, spec in (specs or {}).items():
        in_specs[index] = spec
    results = [pl.BlockSpec(memory_space=pltpu.VMEM)] * len(outs)
    for index, spec in (out_specs or {}).items():
        results[index] = spec
    return pl.pallas_call(
        kernel,
        out_shape=outs,
        in_specs=in_specs,
        out_specs=results,
        scratch_shapes=list(scratch),
        compiler_params=pltpu.CompilerParams(vmem_limit_bytes=vmem * MIB),
        cost_estimate=pl.CostEstimate(flops=0, bytes_accessed=4 << 20, transcendentals=0),
    )(*ins)


SMEM = pl.BlockSpec(memory_space=pltpu.SMEM)


def out(shape, dtype=f32):
    return jax.ShapeDtypeStruct(shape, dtype)


def pack_kernel(col, conv, qkv, proj, exp, red, head, *refs, across):
    sh = qkv.shape[1]
    outs, groups = refs[:2], refs[2:]

    def cols(x):
        return [x[:, k * 128 : (k + 1) * 128] for k in range(x.shape[1] // 128)]

    def reds(x):
        return [part for k in range(3) for part in cols(x[k * sh : (k + 1) * sh, :])]

    tail = jnp.concatenate([head[:, 896:], jnp.zeros((sh, 1024 - CLASSES), f32)], 1)
    blocks = (
        cols(conv[...]) + cols(qkv[0]),
        cols(proj[0]) + cols(exp[0]) + reds(red[0]) + cols(qkv[1]),
        cols(proj[1]) + cols(exp[1]) + reds(red[1]) + cols(head[:, :896]) + [tail],
    )
    begin = 0
    for index, (group, values) in enumerate(zip(groups, blocks)):
        for k, value in enumerate(values):
            group[k * sh : (k + 1) * sh, :] = value.astype(bf16)
        empty = group.shape[0] - len(values) * sh
        if empty:
            group[len(values) * sh :, :] = jnp.zeros((empty, 128), bf16)
        result = outs[min(index, 1)]
        begin = begin if index == 2 else 0
        part = group.shape[0] // across
        mine = group[pl.ds(pl.multiple_of(col[0] * part, 16), part), :]
        for row in range(result.shape[0]):
            result[row, begin : begin + part, :] = mine
        begin += part


def weight_of(blocks, first, count):
    sh = D // blocks.shape[1]
    per = blocks.shape[2] // sh
    parts = [
        blocks[k // per, :, (k % per) * sh : (k % per + 1) * sh, :].reshape(D, 128)
        for k in range(first, first + count)
    ]
    return jnp.concatenate(parts, 1)


def weight_red(blocks, first):
    rows = blocks.shape[1]
    parts = [weight_of(blocks, first + 2 * k, 2).reshape(rows, 1, D // rows, D) for k in range(3)]
    return jnp.concatenate(parts, 1).reshape(FF, D)


def table_kernel(bias, first_one, first_two):
    position_table(One, bias[0:8, :], first_one)
    position_table(Two, bias[8:16, :], first_two)


def patch_kernel(place, stem, above, left, lay, patches, stem_f, above_f):
    stem_f[...] = stem[...].astype(f32)
    above_f[...] = above[...].astype(f32)
    left_f = left[...].astype(f32)
    tiles = left_f[:384].reshape(24, 2, 8, 128)
    left_odd = tiles[:, 0]
    beside = [left_odd, tiles[:, 1], jnp.concatenate([left_odd[1:], left_f[384:392][None]], 0)]
    phases = []
    for m in range(4):
        part = stem_f[pl.ds(m, 384, stride=4), :].reshape(24, 2, 8, 128)
        even, odd = part[:, 0], part[:, 1]
        top = above_f[pl.ds(m, 8, stride=4), :]
        phases.append([jnp.concatenate([top[None], odd[:-1]], 0), even, odd])
    token = lax.broadcasted_iota(i32, (384, 1), 0)
    row_pos = place[0] + (token >> 4)
    col_pos = place[1] + One.query_col(token & 15)
    inner_row = jnp.where(row_pos == lay[:, 0:1], 0.0, 1.0)
    inner_col = jnp.where(col_pos == lay[:, 2:3], 0.0, 1.0)
    half = lax.broadcasted_iota(i32, (24, 8, 128), 1)
    for a in range(3):
        shifted = jnp.where(half == 0, beside[a], pltpu.roll(phases[3][a], 1, 1))
        taps = (
            (shifted, phases[1][a]),
            (phases[0][a], phases[2][a]),
            (phases[1][a], phases[3][a]),
        )
        for b in range(3):
            value = jnp.stack(taps[b], 1).reshape(384, 128)
            if a == 0:
                value = value * inner_row
            if b == 0:
                value = value * inner_col
            lanes = slice((3 * a + b) * 128, (3 * a + b + 1) * 128)
            patches[:, lanes] = value.astype(bf16)


def front_kernel(place, patches, early, norms, hidden, query, keyval, first, second):
    conv = nt(patches[...], weight_of(early, 0, 9))
    h = norm(conv, norms[0:2, :])
    hidden[...] = h
    low = norm(h, norms[2:4, :]).astype(bf16)
    mixed = nn(low, weight_of(early, 9, 6))
    query[...] = mixed[:, :D].astype(bf16)
    both = mixed[:, D:].reshape(24, 2, 8, 2 * D)
    zero, one = both[:, 0], both[:, 1]
    keyval[0] = zero.reshape(192, 2 * D).astype(bf16)
    keyval[1] = one.reshape(192, 2 * D).astype(bf16)
    sub = lax.broadcasted_iota(i32, zero.shape, 1)
    left = jnp.where(sub < 4, zero, pltpu.roll(one, 4, 1))
    right = jnp.where(sub < 4, pltpu.roll(zero, 4, 1), one)
    send(
        place, EVEN_COL, first, second,
        lambda: right.reshape(192, 2 * D).astype(bf16), lambda: left.reshape(192, 2 * D).astype(bf16),
    )


def ring_kernel(place, keyval, first, second, row_first, row_second):
    def put(ref, begin):
        rows = slice(begin, begin + 48)
        ref[0] = keyval[0, rows, :]
        ref[1] = keyval[1, rows, :]

        def left(source):
            ref[2] = source[rows, :]

        def right(source):
            ref[3] = source[rows, :]

        store_received(place, EVEN_COL, first, second, left, right)

    @pl.when(place[EVEN_ROW] == 1)
    def _():
        put(row_first, 144)
        put(row_second, 0)

    @pl.when(place[EVEN_ROW] == 0)
    def _():
        put(row_first, 0)
        put(row_second, 144)


class Copies:
    def __init__(self, sems):
        self.sems, self.used = sems, 0

    def semaphore(self):
        self.used += 1
        return self.sems.at[self.used - 1]

    def start(self, source, target):
        copy = pltpu.make_async_copy(source, target, self.semaphore())
        copy.start()
        return [copy]

    def start_received(self, place, even, first, second, before, after):
        one, two = self.semaphore(), self.semaphore()

        @pl.when(place[even] == 1)
        def _():
            pltpu.make_async_copy(second, before, one).start()
            pltpu.make_async_copy(first, after, two).start()

        @pl.when(place[even] == 0)
        def _():
            pltpu.make_async_copy(first, before, one).start()
            pltpu.make_async_copy(second, after, two).start()

        return [pltpu.make_async_copy(first, before, one), pltpu.make_async_copy(first, after, two)]


def wait_for(copies):
    for copy in copies:
        copy.wait()


def gather_keys_one(copies, place, keyval, col_first, col_second, row_first, row_second, pieces):
    inner = pl.ds(48, 192)
    return (
        copies.start(keyval, pieces.at[pl.ds(0, 2), inner, :])
        + copies.start_received(
            place, EVEN_COL, col_first, col_second, pieces.at[2, inner, :], pieces.at[3, inner, :]
        )
        + copies.start_received(
            place, EVEN_ROW, row_first, row_second,
            pieces.at[:, pl.ds(0, 48), :], pieces.at[:, pl.ds(240, 48), :],
        )
    )


def gather_keys_two(copies, place, own, first, second, pieces):
    return copies.start(own, pieces.at[0]) + copies.start_received(
        place, EVEN_COL, first, second, pieces.at[1], pieces.at[2]
    )


def extend_kernel(place, keyval, first, second, result):
    result[:, 48:144, :] = keyval[...]

    def above(source):
        result[:, 0:48, :] = source[...]

    def below(source):
        result[:, 144:192, :] = source[...]

    store_received(place, EVEN_ROW, first, second, above, below)


def rim_kernel(place, rims, first, second, row_first, row_second):
    def total(part):
        rows = slice(144 * part, 144 * part + 48)
        value = rims[:, 48 * part : 48 * part + 48, :].astype(f32)
        value += first[:, rows, :].astype(f32) + second[:, rows, :].astype(f32)
        return value.astype(bf16)

    send(place, EVEN_ROW, row_first, row_second, lambda: total(1), lambda: total(0))


def sides_kernel(place, sides, first, second, col_first, col_second):
    def total(p):
        above, below = received(place, EVEN_ROW, first[2 + p], second[2 + p])
        own = sides[p].astype(f32)
        rows = [own[0:48] + above, own[48:144], own[144:192] + below]
        return jnp.concatenate(rows, 0).astype(bf16)

    send(place, EVEN_COL, col_first, col_second, lambda: total(1), lambda: total(0))


def feed_forward(hidden, norms, w_exp, w_red, bias):
    low = norm(hidden, norms).astype(bf16)
    upper = nn(low, w_exp) + bias
    gelu = upper * normal_cdf(upper)
    return hidden + nn(gelu.astype(bf16), w_red)


PROJ, EXP, RED, QKV, HEAD = 0, 2, 8, 14, 14


def first_block_kernel(
    place, lay, hidden, query, keyval, cola, colb, rowa, rowb, first_table, late, norms, ebias,
    kept, att, middle, last, query2, keyval2, first, second,
    pieces, table, score, prob, group, before, sems, keep_sems,
):
    copies = Copies(sems)
    near = gather_keys_one(copies, place, keyval, cola, colb, rowa, rowb, pieces)
    arrived = copies.start(late, group) + copies.start(hidden, before)
    spread_table(One, first_table, table)
    wait_for(near)
    leaving = attend(One, place, lay, query, pieces, table, att, score, prob, kept, keep_sems)
    wait_for(arrived)
    mid = before[...] + nn(att[...], weight_of(group, PROJ, 2))
    middle[...] = mid
    end = feed_forward(mid, norms[4:6, :], weight_of(group, EXP, 6), weight_red(group, RED), ebias[0:1, :])
    last[...] = end
    low = norm(end, norms[6:8, :]).astype(bf16)
    mixed = nn(low, weight_of(group, QKV, 6))
    for g, part in enumerate(grouped(mixed)):
        query2[g * 96 : (g + 1) * 96, :] = part[:, :D].astype(bf16)
        keyval2[g] = part[:, D:].astype(bf16)
    send(
        place, EVEN_ROW, first, second, lambda: keyval2[:, 48:, :], lambda: keyval2[:, :48, :]
    )
    wait_for(leaving)


def slot_onehot(slots, images):
    entry = lax.broadcasted_iota(i32, (384, images), 1)
    return jnp.where(slots[:, 4:5] == entry, 1.0, 0.0).astype(bf16)


def ungroup(value, ref):
    for g in range(4):
        ref[:, g >> 1, g & 1] = value[g * 96 : (g + 1) * 96].reshape(12, 8, value.shape[-1])


def second_block_kernel(
    place, lay, slots, hidden, query, own, cola, colb, first_table, late, norms, ebias,
    kept, att, middle, last, sums,
    pieces, table, score, prob, group, before, att_group, att_token, sems, keep_sems,
):
    copies = Copies(sems)
    near = gather_keys_two(copies, place, own, cola, colb, pieces)
    arrived = copies.start(late, group) + copies.start(hidden, before)
    spread_table(Two, first_table, table)
    wait_for(near)
    leaving = attend(Two, place, lay, query, pieces, table, att_group, score, prob, kept, keep_sems)
    ungroup(att_group[...], att_token)
    low = att_token[...].reshape(384, D).astype(bf16)
    att[...] = low
    wait_for(arrived)
    mid = before[...] + nn(low, weight_of(group, PROJ, 2))
    middle[...] = mid
    end = feed_forward(mid, norms[8:10, :], weight_of(group, EXP, 6), weight_red(group, RED), ebias[1:2, :])
    last[...] = end
    final = norm(end, norms[10:12, :])
    images = sums.shape[0] - 8
    where = slot_onehot(slots, images)
    high, low = two_parts(final)
    sums[...] = jnp.zeros_like(sums)
    sums[:images, :D] = tn(where, high) + tn(where, low)
    sums[images:, :images] = tn(jnp.ones((384, 8), bf16), where)
    wait_for(leaving)


def feed_forward_back(dhid, mid, gain_bias, w_exp, w_red, bias):
    low = norm(mid, gain_bias).astype(bf16)
    upper = nn(low, w_exp) + bias
    cdf = normal_cdf(upper)
    dz = dhid.astype(bf16)
    grad_red = tn((upper * cdf).astype(bf16), dz)
    slope = cdf + upper * (jnp.exp(-0.5 * upper * upper) * 0.3989422804014327)
    dupper = (nt(dz, w_red) * slope).astype(bf16)
    grad_bias = jnp.sum(dupper.astype(f32), 0, keepdims=True)
    grad_exp = tn(low, dupper)
    dx, dgain, dbias = norm_back(mid, gain_bias, nt(dupper, w_exp))
    return dhid + dx, grad_red, grad_exp, grad_bias, dgain, dbias


def put_block(grads, k, value):
    per = grads.shape[1] // D
    grads[k // per, (k % per) * D : (k % per + 1) * D, :] = value.astype(bf16)


def put_cols(grads, first, value):
    for k in range(value.shape[1] // 128):
        put_block(grads, first + k, value[:, k * 128 : (k + 1) * 128])


def put_red(grads, first, value, share):
    parts = value.reshape(D // share, 3, share, D)
    for k in range(3):
        put_cols(grads, first + 2 * k, parts[:, k].reshape(D, D))


def put_zeros(grads, first):
    per = grads.shape[1] // D
    for k in range(first, per * grads.shape[0]):
        put_block(grads, k, jnp.zeros((D, 128), f32))


def put_bias(dsmall, value):
    for k in range(3):
        dsmall[4 + k : 5 + k, :] = value[:, k * D : (k + 1) * D]
    dsmall[7:8, :] = jnp.zeros((1, D), f32)


def second_back_kernel(
    place, slots, sums_a, sums_b, labels, live, hbias, hidden, middle, att, query, own, cola, colb, kept, late,
    norms, ebias,
    loss, grad_head, grad_hbias, dhidden, grads, dsmall, dtable, dquery, inner, rims, first, second,
    pieces, prob, dprob, dscore, dpieces, datt, dq_group, group, grads_out, dq_token, sems,
):
    copies = Copies(sems)
    weights = copies.start(late, group)
    near = gather_keys_two(copies, place, own, cola, colb, pieces) + copies.start(kept, prob)
    sums = sums_a[...] + sums_b[...]
    images = sums.shape[0] - 8
    total = sums[:images, :D]
    diagonal = lax.broadcasted_iota(i32, (images, images), 0)
    diagonal = diagonal == lax.broadcasted_iota(i32, (images, images), 1)
    area = jnp.where(diagonal, sums[images : images + 1, :images], 0.0)
    area = jnp.sum(area, -1, keepdims=True)
    spread_area = jnp.maximum(area, 1.0)
    pooled = (total / spread_area).astype(bf16)
    wait_for(weights)
    w_head = weight_of(group, HEAD, 8)
    logits = nn(pooled, w_head) + hbias[...]
    weight = live[...] * jnp.where(area > 0.5, 1.0, 0.0)
    count = jnp.maximum(jnp.sum(weight, 0, keepdims=True), 1.0)
    cls = lax.broadcasted_iota(i32, logits.shape, 1)
    onehot = jnp.where(cls == labels[...], 1.0, 0.0)
    top = jnp.max(logits, -1, keepdims=True)
    logsum = jnp.log(jnp.sum(jnp.exp(logits - top), -1, keepdims=True)) + top
    cross = logsum - jnp.sum(onehot * logits, -1, keepdims=True)
    loss[...] = jnp.broadcast_to(jnp.sum(weight * cross, 0, keepdims=True) / count, loss.shape)
    dlogit = ((weight / count) * (jnp.exp(logits - logsum) - onehot)).astype(bf16)
    grad_hbias[...] = jnp.sum(dlogit.astype(f32), 0, keepdims=True)
    share = grad_head.shape[0]
    channel = lax.broadcasted_iota(i32, (D, share), 0)
    mine = lax.broadcasted_iota(i32, (D, share), 1) + place[2]
    own_pooled = nn(pooled, jnp.where(channel == mine, 1.0, 0.0).astype(bf16)).astype(bf16)
    grad_head[...] = tn(own_pooled, dlogit)
    high, low = two_parts(nt(dlogit, w_head) / spread_area)
    where = slot_onehot(slots, images)
    dfinal = nn(where, high) + nn(where, low)
    dhid, dgain, dbias = norm_back(hidden[...], norms[10:12, :], dfinal)
    dsmall[2:3, :] = dgain
    dsmall[3:4, :] = dbias
    dhid, grad_red, grad_exp, grad_bias, dgain, dbias = feed_forward_back(
        dhid, middle[...], norms[8:10, :], weight_of(group, EXP, 6), weight_red(group, RED), ebias[1:2, :]
    )
    put_cols(grads_out, 0, grad_exp)
    put_red(grads_out, 6, grad_red, share)
    put_bias(dsmall, grad_bias)
    dsmall[0:1, :] = dgain
    dsmall[1:2, :] = dbias
    dhidden[...] = dhid
    dy = dhid.astype(bf16)
    put_cols(grads_out, 12, tn(att[...], dy))
    put_zeros(grads_out, 14)
    leaving = copies.start(grads_out, grads)
    back = nt(dy, weight_of(group, PROJ, 2))
    for g, part in enumerate(grouped(back)):
        datt[g * 96 : (g + 1) * 96, :] = part.astype(bf16)
    wait_for(near)
    attend_back(Two, query, datt, pieces, prob, dq_group, dpieces, dtable, dprob, dscore)
    ungroup(dq_group[...], dq_token)
    dquery[...] = dq_token[...].reshape(384, D).astype(bf16)
    inner[...] = dpieces[0, :, 48:144, :]
    rims[:, 0:48, :] = dpieces[0, :, 0:48, :].astype(bf16)
    rims[:, 48:96, :] = dpieces[0, :, 144:192, :].astype(bf16)
    send(
        place, EVEN_COL, first, second,
        lambda: dpieces[2].astype(bf16), lambda: dpieces[1].astype(bf16),
    )
    wait_for(leaving)


def position_kernel(dtable, dpos, dfirst, *, geo):
    dpos[...] = gather_table(geo, dtable, dfirst)


def first_back_kernel(
    place, dhid_in, dquery2, dkv, dcola, dcolb, drowa, drowb, hidden, middle, att, query,
    keyval, cola, colb, rowa, rowb, kept, late, norms, ebias,
    dhidden, grads, dsmall, dtable, dquery, inner, sides, first, second,
    pieces, prob, dprob, dscore, dpieces, datt, dq, group, grads_out, parta, partb, dkv_token, sems,
):
    copies = Copies(sems)
    rows = pl.ds(48, 96)
    parts = copies.start(dcola.at[:, rows, :], parta) + copies.start(dcolb.at[:, rows, :], partb)
    weights = copies.start(late, group)
    near = gather_keys_one(copies, place, keyval, cola, colb, rowa, rowb, pieces)
    near += copies.start(kept, prob)
    wait_for(parts)
    for g in range(4):
        total = dkv[g] + parta[g].astype(f32) + partb[g].astype(f32)
        total += jnp.concatenate(received(place, EVEN_ROW, drowa[g], drowb[g]), 0)
        dkv_token[:, g >> 1, g & 1] = total.reshape(12, 8, 2 * D)
    dmixed = jnp.concatenate(
        [dquery2[...], dkv_token[...].reshape(384, 2 * D).astype(bf16)], 1
    )
    low = norm(hidden[...], norms[6:8, :]).astype(bf16)
    put_cols(grads_out, 0, tn(low, dmixed))
    wait_for(weights)
    dx, dgain, dbias = norm_back(
        hidden[...], norms[6:8, :], nt(dmixed, weight_of(group, QKV, 6))
    )
    dsmall[2:3, :] = dgain
    dsmall[3:4, :] = dbias
    dhid, grad_red, grad_exp, grad_bias, dgain, dbias = feed_forward_back(
        dhid_in[...] + dx, middle[...], norms[4:6, :], weight_of(group, EXP, 6), weight_red(group, RED),
        ebias[0:1, :],
    )
    put_cols(grads_out, 6, grad_exp)
    put_red(grads_out, 12, grad_red, D // late.shape[1])
    put_bias(dsmall, grad_bias)
    dsmall[0:1, :] = dgain
    dsmall[1:2, :] = dbias
    dhidden[...] = dhid
    dy = dhid.astype(bf16)
    put_cols(grads_out, 18, tn(att[...], dy))
    put_zeros(grads_out, 20)
    leaving = copies.start(grads_out, grads)
    datt[...] = nt(dy, weight_of(group, PROJ, 2)).astype(bf16)
    wait_for(near)
    attend_back(One, query, datt, pieces, prob, dq, dpieces, dtable, dprob, dscore)
    dquery[...] = dq[...].astype(bf16)
    inner[...] = dpieces[0:2, 48:240, :]
    sides[...] = dpieces[2:4, 48:240, :].astype(bf16)
    send(
        place, EVEN_ROW, first, second,
        lambda: dpieces[:, 240:288, :].astype(bf16), lambda: dpieces[:, 0:48, :].astype(bf16),
    )
    wait_for(leaving)


SMALL_ROWS = 64


def front_back_kernel(
    place, dhid_in, dquery, inner, drowa, drowb, dcola, dcolb, patches, early,
    norms, dsmall1, dsmall2, dpos1, dpos2,
    keep, give,
    grads, small,
):
    left, right = received(place, EVEN_COL, dcola[...], dcolb[...])
    left, right = left.reshape(24, 8, 2 * D), right.reshape(24, 8, 2 * D)
    sub = lax.broadcasted_iota(i32, left.shape, 1)

    def whole(p):
        above, below = received(place, EVEN_ROW, drowa[p], drowb[p])
        top = inner[p, 0:48, :] + above
        bottom = inner[p, 144:192, :] + below
        return jnp.concatenate([top, inner[p, 48:144, :], bottom], 0).reshape(24, 8, 2 * D)

    zero = whole(0) + jnp.where(sub < 4, left, pltpu.roll(right, 4, 1))
    one = whole(1) + jnp.where(sub < 4, pltpu.roll(left, 4, 1), right)
    dkv = jnp.stack([zero, one], 1).reshape(384, 2 * D).astype(bf16)
    dmixed = jnp.concatenate([dquery[...], dkv], 1)
    conv = nt(patches[...], weight_of(early, 0, 9))
    h = norm(conv, norms[0:2, :])
    low = norm(h, norms[2:4, :]).astype(bf16)
    put_cols(grads, 9, tn(low, dmixed))
    w_qkv = weight_of(early, 9, 6)
    dx, dgain1, dbias1 = norm_back(h, norms[2:4, :], nt(dmixed, w_qkv))
    dconv, dgain0, dbias0 = norm_back(conv, norms[0:2, :], dhid_in[...] + dx)
    put_cols(grads, 0, tn(dconv.astype(bf16), patches[...]))
    put_zeros(grads, 15)

    def place_row(first, value):
        for k in range(value.shape[1] // 128):
            small[first + k : first + k + 1, :] = value[:, k * 128 : (k + 1) * 128]

    small[...] = jnp.zeros_like(small)
    for k, value in enumerate((dgain0, dbias0, dgain1, dbias1)):
        place_row(2 * k, value)
    for k in range(4):
        place_row(8 + 2 * k, dsmall1[k : k + 1, :])
        place_row(16 + 2 * k, dsmall2[k : k + 1, :])
    for k in range(3):
        place_row(24 + 2 * k, dsmall1[4 + k : 5 + k, :])
        place_row(30 + 2 * k, dsmall2[4 + k : 5 + k, :])
    for layer, value in enumerate((dpos1, dpos2)):
        small[40 + 8 * layer : 48 + 8 * layer, :] = value[:, :128]
        small[56:64, 64 * layer : 64 * layer + WIN - 128] = value[:, 128:]
    begin = grads.shape[1] - SMALL_ROWS
    for col in range(grads.shape[0]):
        grads[col, begin:, :] = small[...].astype(bf16)
    halve(place, 0, grads, keep, give)


def halve(place, stage, parts, keep, give):
    bit = (place[COL] >> stage) & 1
    for k in range(keep.shape[0]):
        keep[k] = parts[2 * k + bit]
        give[k] = parts[2 * k + 1 - bit]


def halve_kernel(place, kept, given, keep, give, total, *, stage):
    total[...] = (kept[...].astype(f32) + given[...].astype(f32)).astype(bf16)
    halve(place, stage, total, keep, give)


def between_kernel(second, first, kept, given, result):
    rows = result.shape[0]
    sh = D // rows
    begin = 0
    for group in (second, first):
        for k in range(group.shape[0] // D):
            result[:, begin : begin + sh, :] = group[k * D : (k + 1) * D, :].reshape(rows, sh, 128)
            begin += sh
    for k in range(kept.shape[1] // D):
        span = slice(k * D, (k + 1) * D)
        total = kept[0, span, :].astype(f32) + given[0, span, :].astype(f32)
        result[:, begin : begin + sh, :] = total.astype(bf16).reshape(rows, sh, 128)
        begin += sh
    span = slice(kept.shape[1] - SMALL_ROWS, kept.shape[1])
    small = (kept[0, span, :].astype(f32) + given[0, span, :].astype(f32)).astype(bf16)
    for row in range(rows):
        result[row, begin:, :] = small


def last_sum_kernel(parts, result, small):
    total = parts[0].astype(f32)
    for row in range(1, parts.shape[0]):
        total += parts[row].astype(f32)
    count = result.shape[0]
    result[...] = total[:count].astype(bf16)
    small[...] = total[count:]


def adamw(weight, grad, first, second):
    first = beta_one * first + (1.0 - beta_one) * grad
    second = beta_two * second + (1.0 - beta_two) * grad * grad
    fix_one = 1.0 - beta_one**STEP
    fix_two = 1.0 - beta_two**STEP
    new = weight - learn_rate * (
        first / fix_one / (jnp.sqrt(second / fix_two) + eps_adam) + decay_rate * weight
    )
    return (first, second, new)


def adamw_kernel(grads, *refs, sh, per):
    ins = [refs[3 * n : 3 * n + 3] for n in range(5)]
    outs = [refs[15 + 3 * n : 18 + 3 * n] for n in range(5)]

    def update(n, group, k, *where):
        begin = (sum(per[:group]) + k % per[group]) * sh
        grad = grads[k // per[group], begin : begin + sh, :].astype(f32)
        weight, first, second = (ref[where] for ref in ins[n])
        for ref, value in zip(outs[n], adamw(weight, grad, first, second)):
            ref[where] = value

    every = slice(None)
    for k in range(9):
        update(0, 2, k, every, slice(k * 128, (k + 1) * 128))
    for k in range(6):
        lanes = slice(k * 128, (k + 1) * 128)
        update(1, 2, 9 + k, 0, every, lanes)
        update(1, 1, k, 1, every, lanes)
        update(3, 1, 6 + k, 0, every, lanes)
        update(3, 0, k, 1, every, lanes)
        rows, half = slice((k // 2) * sh, (k // 2 + 1) * sh), slice((k % 2) * 128, (k % 2 + 1) * 128)
        update(4, 1, 12 + k, 0, rows, half)
        update(4, 0, 6 + k, 1, rows, half)
    for k in range(2):
        lanes = slice(k * 128, (k + 1) * 128)
        update(2, 1, 18 + k, 0, every, lanes)
        update(2, 0, 12 + k, 1, every, lanes)


def onward(value, axis):
    count = lax.axis_size(axis)
    return lax.ppermute(value, axis, [(i, (i + 1) % count) for i in range(count)])


def swaps(first, second, axis):
    count = lax.axis_size(axis)
    pairs = [[(i, i + 1) for i in range(begin, count - 1, 2)] for begin in (0, 1)]
    both = [low + [(j, i) for i, j in low] for low in pairs]
    return lax.ppermute(first, axis, both[0]), lax.ppermute(second, axis, both[1])


def sum_all(value):
    axes = [axis for axis in ("col", "row") if lax.axis_size(axis) > 1]
    terms = [value, jnp.zeros_like(value)]
    for axis in axes:
        count = lax.axis_size(axis)
        first = 1
        while first < count:
            group = min(4, count // first)

            def other(flip):
                return lax.ppermute(value, axis, [(i, i ^ (flip * first)) for i in range(count)])

            terms = [value, *(other(flip) for flip in range(1, group))]
            while len(terms) > 2:
                terms = [a + b for a, b in zip(terms[::2], terms[1::2])]
            first *= group
            if axis != axes[-1] or first < count:
                value = terms[0] + terms[1]
    return terms


def on_device(
    stem_map, layout, labels, live,
    conv_weight, input_proj, output_proj, expand_weight, reduce_weight, head_weight, small_params,
    first_conv, first_input, first_output, first_expand, first_reduce, first_head, first_small,
    second_conv, second_input, second_output, second_expand, second_reduce, second_head, second_small,
):
    nr, nc = lax.axis_size("row"), lax.axis_size("col")
    sh = D // nr
    images = labels.shape[0]
    padded = -(-images // 8) * 8
    per = [-(-count // nc) for count in (14, 20, 15)]
    row_index, col_index = lax.axis_index("row"), lax.axis_index("col")
    parts = [-(-count // nc) * sh for count in (15, 20, 22)]
    early, late = run(
        functools.partial(pack_kernel, across=nc),
        [out((nr, parts[0], 128), bf16), out((nr, parts[1] + parts[2], 128), bf16)],
        [
            col_index.astype(i32)[None], conv_weight.T, input_proj, output_proj, expand_weight, reduce_weight,
            head_weight,
        ],
        [pltpu.VMEM((part * nc, 128), bf16) for part in parts],
        {0: SMEM},
        56,
    )
    early = lax.all_to_all(early, "row", 0, 0, tiled=True)
    norms = small_params[: 12 * D].reshape(12, D)
    start = 12 * D
    ebias = small_params[start : start + LAYERS * FF].reshape(LAYERS, FF)
    start += LAYERS * FF
    hbias = jnp.pad(small_params[start : start + CLASSES], (0, 24), constant_values=MASKED)[None]
    start += CLASSES
    pos_bias = small_params[start:].reshape(LAYERS * HEADS, 169)
    first_one, first_two = run(
        table_kernel,
        [out((geo.pieces, HEADS * geo.across, 128)) for geo in (One, Two)],
        [jnp.pad(pos_bias, ((0, 0), (0, WIN - 169)))],
    )
    place = [row_index * 24, col_index * 16, row_index * sh, (row_index + 1) % 2, (col_index + 1) % 2, col_index]
    place = jnp.stack(place).astype(i32)
    lay_one = layout.reshape(5, 24, 8, 2).transpose(1, 3, 2, 0).reshape(384, 5)
    lay_two = layout.reshape(5, 12, 2, 8, 2).transpose(2, 4, 1, 3, 0).reshape(384, 5)
    early, above = lax.optimization_barrier((early, onward(stem_map[-1:], "row")))
    rim = jnp.concatenate([above[:, -1:], stem_map[:, -1:]], 0)
    rim = jnp.broadcast_to(onward(rim, "col"), (49, 8, 128))
    patches = run(
        patch_kernel,
        [out((384, 1152), bf16)],
        [place, stem_map.reshape(1536, 128), above.reshape(32, 128), rim.reshape(392, 128), lay_one],
        [pltpu.VMEM((1536, 128), f32), pltpu.VMEM((32, 128), f32)],
        {0: SMEM},
    )[0]
    late, _ = lax.optimization_barrier((late, early))
    early = lax.all_gather(early, "col", axis=0)
    late = lax.all_to_all(late, "row", 0, 0, tiled=True)
    rows48, edge = out((4, 48, 2 * D), bf16), out((192, 2 * D), bf16)
    hidden0, query1, keyval1, *edges = run(
        front_kernel,
        [out((384, D)), out((384, D), bf16), out((2, 192, 2 * D), bf16), edge, edge],
        [place, patches, early, norms],
        specs={0: SMEM},
    )
    late, _ = lax.optimization_barrier((late, edges))
    late1 = lax.all_gather(late[:, : parts[1]], "col", axis=0)
    late2 = lax.all_gather(late[:, parts[1] :], "col", axis=0)
    cols1 = swaps(*edges, "col")
    rows1 = swaps(*run(ring_kernel, [rows48] * 2, [place, keyval1, *cols1], specs={0: SMEM}), "row")
    hbm = pl.BlockSpec(memory_space=pl.ANY)
    tokens, tokens_low, ext = out((384, D)), out((384, D), bf16), out((4, 192, 2 * D), bf16)
    token5 = lambda width: pltpu.VMEM((12, 2, 2, 8, width), f32)
    like = lambda x: pltpu.VMEM(x.shape, x.dtype)
    copy_sems = lambda count: pltpu.SemaphoreType.DMA((count,))

    def tiles(geo, back):
        square = (HEADS * geo.queries, geo.keys)
        shape = (4, 288, 2 * D) if geo is One else (3, 4, 192, 2 * D)
        pieces, prob = pltpu.VMEM(shape, bf16), pltpu.VMEM((geo.steps, *square), bf16)
        many = (geo.together, *square)
        if not back:
            return [pieces, pltpu.VMEM(square, f32), pltpu.VMEM(many, f32), prob]
        return [
            pieces, prob, pltpu.VMEM(many, f32), pltpu.VMEM(many, bf16), pltpu.VMEM(shape, f32),
            pltpu.VMEM((384, D), bf16), pltpu.VMEM((384, D), f32),
        ]

    probs = lambda geo: out((geo.steps, HEADS * geo.queries, geo.keys), bf16)
    dtable = lambda geo: out((HEADS * geo.queries, geo.keys))
    turns = lambda geo: copy_sems(geo.steps // geo.together)
    near1 = [keyval1, *cols1, *rows1]
    kept1, att1, middle1, last1, query2, keyval2, *edges = run(
        first_block_kernel,
        [probs(One), tokens_low, tokens, tokens, tokens_low, out((4, 96, 2 * D), bf16), rows48, rows48],
        [place, lay_one, hidden0, query1, *near1, first_one, late1, norms, ebias],
        tiles(One, False) + [like(late1), like(hidden0), copy_sems(7), turns(One)],
        {0: SMEM, **dict.fromkeys((2, 4, 5, 6, 7, 8, 10), hbm)},
        56,
        {0: hbm},
    )
    rows2 = swaps(*edges, "row")
    own2 = run(extend_kernel, [ext], [place, keyval2, *rows2], specs={0: SMEM})[0]
    near2 = [own2, *swaps(own2, own2, "col")]
    kept2, att2, middle2, last2, sums = run(
        second_block_kernel,
        [probs(Two), tokens_low, tokens, tokens, out((padded + 8, max(D, -(-padded // 128) * 128)))],
        [place, lay_two, lay_one, last1, query2, *near2, first_two, late2, norms, ebias],
        tiles(Two, False)
        + [like(late2), like(last1), pltpu.VMEM((384, D), f32), token5(D), copy_sems(5), turns(Two)],
        {0: SMEM, **dict.fromkeys((3, 5, 6, 7, 9), hbm)},
        56,
        {0: hbm},
    )
    sums_a, sums_b = sum_all(sums)
    pad_images = lambda x: jnp.pad(x, (0, padded - images))[:, None]
    grads_of = lambda group: out((nc, per[group] * D, 128), bf16)
    (
        loss, grad_head, grad_hbias, dhid, grads2, dsmall2, dtable2, dquery2, inner2, rims2, *edges,
    ) = run(
        second_back_kernel,
        [
            out((8, 128)), out((sh, 1024)), out((1, 1024)), tokens, grads_of(0),
            out((8, D)), dtable(Two), tokens_low,
            out((4, 96, 2 * D)), out((4, 96, 2 * D), bf16), ext, ext,
        ],
        [
            place, lay_one, sums_a, sums_b, pad_images(labels), pad_images(live.astype(f32)), hbias,
            last2, middle2, att2, query2, *near2, kept2, late2, norms, ebias,
        ],
        tiles(Two, True) + [like(late2), like(grads_of(0)), token5(D), copy_sems(6)],
        {0: SMEM, **dict.fromkeys((11, 12, 13, 14, 15), hbm)},
        56,
        {4: hbm},
    )
    dcols2 = swaps(*edges, "col")
    drows2 = swaps(*run(rim_kernel, [rows48] * 2, [place, rims2, *dcols2], specs={0: SMEM}), "row")
    grads2 = lax.psum_scatter(grads2, "col", scatter_dimension=0, tiled=False)

    def position(geo, table):
        scratch = [pltpu.VMEM((geo.pieces, HEADS * geo.across, 128), f32)]
        return run(functools.partial(position_kernel, geo=geo), [out((HEADS, WIN))], [table], scratch)[0]

    dpos2 = position(Two, dtable2)
    part2 = pltpu.VMEM((4, 96, 2 * D), bf16)
    dhid, grads1, dsmall1, dtable1, dquery1, inner1, sides1, *edges = run(
        first_back_kernel,
        [
            tokens, grads_of(1), out((8, D)), dtable(One),
            tokens_low, out((2, 192, 2 * D)), out((2, 192, 2 * D), bf16), rows48, rows48,
        ],
        [
            place, dhid, dquery2, inner2, *dcols2, *drows2, last1, middle1, att1, query1,
            *near1, kept1, late1, norms, ebias,
        ],
        tiles(One, True) + [like(late1), like(grads_of(1)), part2, part2, token5(2 * D), copy_sems(10)],
        {0: SMEM, **dict.fromkeys((4, 5, 12, 13, 14, 15, 16, 17, 18), hbm)},
        56,
        {1: hbm},
    )
    drows1 = swaps(*edges, "row")
    grads1 = lax.psum_scatter(grads1, "col", scatter_dimension=0, tiled=False)
    dpos1 = position(One, dtable1)
    dcols1 = swaps(*run(sides_kernel, [edge] * 2, [place, sides1, *drows1], specs={0: SMEM}), "col")
    part = per[2] * D + SMALL_ROWS
    half = lambda count: out((count, part, 128), bf16)
    kept, given = run(
        front_back_kernel,
        [half(nc // 2), half(nc // 2)],
        [
            place, dhid, dquery1, inner1, *drows1, *dcols1, patches,
            early, norms, dsmall1, dsmall2, dpos1, dpos2,
        ],
        [pltpu.VMEM((nc, part, 128), bf16), pltpu.VMEM((SMALL_ROWS, 128), f32)],
        {0: SMEM},
    )
    stage = 0
    while True:
        given = lax.ppermute(given, "col", [(i, i ^ (1 << stage)) for i in range(nc)])
        stage += 1
        if 1 << stage == nc:
            break
        count = nc >> (stage + 1)
        kept, given = run(
            functools.partial(halve_kernel, stage=stage),
            [half(count), half(count)],
            [place, kept, given],
            [pltpu.VMEM((2 * count, part, 128), bf16)],
            {0: SMEM},
        )
    mine = run(
        between_kernel,
        [out((nr, sum(per) * sh + SMALL_ROWS, 128), bf16)],
        [grads2, grads1, kept, given],
        vmem=56,
    )[0]
    mine = lax.all_to_all(mine, "row", 0, 0, tiled=True)
    mine, small = run(
        last_sum_kernel, [out((sum(per) * sh, 128), bf16), out((SMALL_ROWS, 128))], [mine]
    )
    grads = lax.all_gather(mine, "col", axis=0)
    wide = [
        conv_weight.T, first_conv.T, second_conv.T, input_proj, first_input, second_input,
        output_proj, first_output, second_output, expand_weight, first_expand, second_expand,
        reduce_weight, first_reduce, second_reduce,
    ]
    new = run(
        functools.partial(adamw_kernel, sh=sh, per=per), [out(x.shape) for x in wide], [grads, *wide]
    )
    new = [x.T for x in new[:3]] + list(new[3:])
    pos = [
        jnp.concatenate([small[40 + 8 * k : 48 + 8 * k], small[56:64, 64 * k : 64 * k + 41]], 1).reshape(-1)
        for k in range(2)
    ]
    grad_small = jnp.concatenate([small[:36].reshape(-1), grad_hbias[0, :CLASSES], *pos])
    head = adamw(head_weight, grad_head[:, :CLASSES], first_head, second_head)
    return (loss[0, 0], *new, *head, *adamw(small_params, grad_small, first_small, second_small))


def solution(mesh):
    return jax.shard_map(
        on_device,
        mesh=mesh,
        in_specs=(
            P("row", "col", None),
            P(None, "row", "col"),
            P(),
            P(),
            P(None, "row"),
            P(None, "row", None),
            P(None, "row", None),
            P(None, "row", None),
            P(None, "row", None),
            P("row", None),
            P(),
            P(None, "row"),
            P(None, "row", None),
            P(None, "row", None),
            P(None, "row", None),
            P(None, "row", None),
            P("row", None),
            P(),
            P(None, "row"),
            P(None, "row", None),
            P(None, "row", None),
            P(None, "row", None),
            P(None, "row", None),
            P("row", None),
            P(),
        ),
        out_specs=(
            P(),
            P(None, "row"),
            P(None, "row"),
            P(None, "row"),
            P(None, "row", None),
            P(None, "row", None),
            P(None, "row", None),
            P(None, "row", None),
            P(None, "row", None),
            P(None, "row", None),
            P(None, "row", None),
            P(None, "row", None),
            P(None, "row", None),
            P(None, "row", None),
            P(None, "row", None),
            P(None, "row", None),
            P("row", None),
            P("row", None),
            P("row", None),
            P(),
            P(),
            P(),
        ),
        check_vma=False,
    )
```

```python
import functools

import jax
import jax.numpy as jnp
from jax import lax
from jax.experimental import pallas as pl
from jax.experimental.pallas import tpu as pltpu
from jax.sharding import PartitionSpec as P

D = 256
HEADS = 8
FF = 768
CLASSES = 1000
LAYERS = 2
STEP = 5
WIN = 176

eps_norm = 1e-05
beta_one = 0.9
beta_two = 0.999
learn_rate = 0.2
decay_rate = 0.05
eps_adam = 1e-08
scale = (D // HEADS) ** -0.5

bf16 = jnp.bfloat16
f32 = jnp.float32
i32 = jnp.int32
MASKED = -1e30
LOG2E = 1.4426950408889634
MIB = 1024 * 1024


def nn(a, b):
    return lax.dot_general(a, b, (((1,), (0,)), ((), ())), preferred_element_type=f32)


def nt(a, b):
    return lax.dot_general(a, b, (((1,), (1,)), ((), ())), preferred_element_type=f32)


def tn(a, b):
    return lax.dot_general(a, b, (((0,), (0,)), ((), ())), preferred_element_type=f32)


def two_parts(x):
    high = x.astype(bf16)
    return high, (x - high.astype(f32)).astype(bf16)


def norm_parts(x):
    centre = x - jnp.mean(x, -1, keepdims=True)
    rstd = lax.rsqrt(jnp.mean(centre * centre, -1, keepdims=True) + eps_norm)
    return centre * rstd, rstd


def norm(x, gain_bias):
    return norm_parts(x)[0] * gain_bias[0:1] + gain_bias[1:2]


def norm_back(x, gain_bias, dy):
    xhat, rstd = norm_parts(x)
    dxhat = dy * gain_bias[0:1]
    dx = rstd * (
        dxhat
        - jnp.mean(dxhat, -1, keepdims=True)
        - xhat * jnp.mean(dxhat * xhat, -1, keepdims=True)
    )
    return dx, jnp.sum(dy * xhat, 0, keepdims=True), jnp.sum(dy, 0, keepdims=True)


def normal_cdf(u):
    return 0.5 * (1.0 + lax.erf(u * 0.7071067811865476))


class One:
    dilation, queries, across, pieces, steps = 1, 64, 16, 4, 6
    together = 3
    keys = pieces * 128

    @staticmethod
    def key_col(piece, c8):
        two = 2 * (c8 & 3) + (c8 >> 2)
        return jnp.where(
            piece == 0,
            2 * c8,
            jnp.where(piece == 1, 2 * c8 + 1, jnp.where(piece == 2, two - 8, two + 16)),
        )

    @staticmethod
    def query_col(index):
        return 2 * (index & 7) + (index >> 3)


class Two:
    dilation, queries, across, pieces, steps = 2, 32, 8, 3, 12
    together = 3
    keys = pieces * 128

    @staticmethod
    def key_col(piece, c8):
        return jnp.where(piece == 0, c8, jnp.where(piece == 1, c8 - 8, c8 + 8))

    @staticmethod
    def query_col(index):
        return index


def key_place(geo):
    lane = lax.broadcasted_iota(i32, (1, geo.keys), 1)
    return (lane >> 3) & 15, geo.key_col(lane >> 7, lane & 7)


def window_mask(geo, lay, step, row_first, col_first):
    token = lax.broadcasted_iota(i32, (geo.queries, 1), 0)
    if geo.dilation == 1:
        block = step
        row = block * 4 + (token >> 4)
        col = geo.query_col(token & 15)
        row_pos, col_pos = row_first + row, col_first + col
    else:
        group = step // 3
        block = step - 3 * group
        row = block * 4 + (token >> 3)
        col = token & 7
        row_pos = row_first + 2 * row + (group >> 1)
        col_pos = col_first + 2 * col + (group & 1)

    def begin(place, first, end):
        local = place - first
        extent = end - first
        if geo.dilation == 1:
            index, length = local, extent
        else:
            index, length = local >> 1, (extent - (local & 1) + 1) >> 1
        return jnp.minimum(jnp.maximum(index - 3, 0), length - 7) - index

    row_start = row + begin(row_pos, lay[:, 0:1], lay[:, 1:2])
    col_start = col + begin(col_pos, lay[:, 2:3], lay[:, 3:4])
    key_row, key_col = key_place(geo)
    down = key_row + (block * 4 - 6) - row_start
    right = key_col - col_start
    inside = (down >= 0) & (down <= 6) & (right >= 0) & (right <= 6)
    return jnp.where(inside, 0.0, MASKED).astype(f32)


def position_onehot(geo, across):
    key_row, key_col = key_place(geo)
    right = key_col - geo.query_col(across) + 6
    index = jnp.where((right >= 0) & (right <= 12) & (key_row <= 12), key_row * 13 + right, -1)
    entry = lax.broadcasted_iota(i32, (WIN, geo.keys), 0)
    return jnp.where(entry == index, 1.0, 0.0).astype(bf16)


def position_table(geo, bias, first_ref):
    high = bias.astype(bf16)
    rest = bias - high.astype(f32)
    mid = rest.astype(bf16)
    low = (rest - mid.astype(f32)).astype(bf16)
    for across in range(geo.across):
        onehot = position_onehot(geo, across)
        row = nn(high, onehot) + nn(mid, onehot) + nn(low, onehot)
        for piece in range(geo.pieces):
            lanes = slice(piece * 128, piece * 128 + 128)
            first_ref[piece, pl.ds(across, HEADS, stride=geo.across), :] = row[:, lanes]


def spread_table(geo, first_ref, table_ref):
    for head in range(HEADS):
        for row in range(4):
            for piece in range(geo.pieces):
                lanes = slice(piece * 128, piece * 128 + 128)
                value = first_ref[piece, head * geo.across : (head + 1) * geo.across, :]
                value = value * LOG2E
                if row:
                    value = pltpu.roll(value, 8 * row, 1)
                begin = head * geo.queries + row * geo.across
                table_ref[begin : begin + geo.across, lanes] = value


def gather_table(geo, table_ref, first_ref):
    for head in range(HEADS):
        for piece in range(geo.pieces):
            lanes = slice(piece * 128, piece * 128 + 128)
            total = None
            for row in range(4):
                begin = head * geo.queries + row * geo.across
                value = table_ref[begin : begin + geo.across, lanes]
                if row:
                    value = pltpu.roll(value, 128 - 8 * row, 1)
                total = value if total is None else total + value
            first_ref[piece, head * geo.across : (head + 1) * geo.across, :] = total
    grad = jnp.zeros((HEADS, WIN), f32)
    for across in range(geo.across):
        onehot = position_onehot(geo, across)
        rows = pl.ds(across, HEADS, stride=geo.across)
        first = [first_ref[piece, rows, :] for piece in range(geo.pieces)]
        high, low = two_parts(jnp.concatenate(first, 1))
        grad = grad + nt(high, onehot) + nt(low, onehot)
    return grad


def head_lanes(head):
    lane = lax.broadcasted_iota(i32, (1, D), 1)
    return jnp.where((lane >> 5) == head, 1.0, 0.0)


def by_head(x):
    return jnp.concatenate([x * head_lanes(h).astype(x.dtype) for h in range(HEADS)], 0)


def from_heads(x):
    count = x.shape[0] // HEADS
    total = None
    for h in range(HEADS):
        part = x[h * count : (h + 1) * count] * head_lanes(h)
        total = part if total is None else total + part
    return total


def key_rows(geo, step):
    if geo.dilation == 1:
        return None, pl.multiple_of(step * 32, 32)
    group = step // 3
    return group, pl.multiple_of((step - 3 * group) * 32, 32)


def load_keys(geo, pieces, step, lanes):
    group, first = key_rows(geo, step)
    if geo.dilation == 1:
        parts = [pieces[p, pl.ds(first, 128), lanes] for p in range(4)]
    else:
        parts = [pieces[p, group, pl.ds(first, 128), lanes] for p in range(3)]
    return jnp.concatenate(parts, 0)


def add_keys(geo, pieces, step, lanes, value):
    group, first = key_rows(geo, step)
    for p in range(geo.pieces):
        part = value[p * 128 : (p + 1) * 128]
        if geo.dilation == 1:
            pieces[p, pl.ds(first, 128), lanes] += part
        else:
            pieces[p, group, pl.ds(first, 128), lanes] += part


KEY = slice(0, D)
VALUE = slice(D, 2 * D)


def softmax_rows(score, table, mask):
    score = score * (scale * LOG2E) + (table + mask)
    weight = jnp.exp2(score - jnp.max(score, -1, keepdims=True))
    return weight * (1.0 / jnp.sum(weight, -1, keepdims=True))


def attend(geo, place, lay_ref, query_ref, pieces, table_ref, out_ref, score_ref, prob_ref, kept, sems):
    count = geo.queries
    together = score_ref.shape[0]

    def keep(index):
        span = pl.ds(index * together, together)
        return pltpu.make_async_copy(prob_ref.at[span], kept.at[span], sems.at[index])

    def steps_of(index, carry):
        steps = [index * together + n for n in range(together)]
        rows = [pl.ds(pl.multiple_of(step * count, count), count) for step in steps]
        for n, step in enumerate(steps):
            score_ref[n] = nt(by_head(query_ref[rows[n], :]), load_keys(geo, pieces, step, KEY))
        masks = [
            window_mask(geo, lay_ref[rows[n], :], step, place[0], place[1])
            for n, step in enumerate(steps)
        ]
        for h in range(HEADS):
            span = slice(h * count, (h + 1) * count)
            for n, step in enumerate(steps):
                prob = softmax_rows(score_ref[n, span, :], table_ref[span, :], masks[n])
                prob_ref[step, span, :] = prob.astype(bf16)
        keep(index).start()
        for n, step in enumerate(steps):
            out = nn(prob_ref[step], load_keys(geo, pieces, step, VALUE))
            out_ref[rows[n], :] = from_heads(out).astype(out_ref.dtype)
        return carry

    lax.fori_loop(0, geo.steps // together, steps_of, 0)
    return [keep(index) for index in range(geo.steps // together)]


def attend_back(
    geo, query_ref, dout_ref, pieces, prob_ref, dquery_ref, dpieces, dtable_ref, dprob_ref, dscore_ref,
):
    count = geo.queries
    together = dprob_ref.shape[0]
    dtable_ref[...] = jnp.zeros_like(dtable_ref)
    dpieces[...] = jnp.zeros_like(dpieces)

    def steps_of(index, carry):
        steps = [index * together + n for n in range(together)]
        rows = [pl.ds(pl.multiple_of(step * count, count), count) for step in steps]
        for n, step in enumerate(steps):
            dprob_ref[n] = nt(by_head(dout_ref[rows[n], :]), load_keys(geo, pieces, step, VALUE))
        for h in range(HEADS):
            span = slice(h * count, (h + 1) * count)
            total = dtable_ref[span, :]
            for n, step in enumerate(steps):
                prob = prob_ref[step, span, :].astype(f32)
                dprob = dprob_ref[n, span, :]
                dscore = prob * (dprob - jnp.sum(prob * dprob, -1, keepdims=True))
                total += dscore
                dscore_ref[n, span, :] = dscore.astype(bf16)
            dtable_ref[span, :] = total
        for n, step in enumerate(steps):
            wide, dwide = by_head(query_ref[rows[n], :]), by_head(dout_ref[rows[n], :])
            dscore = dscore_ref[n]
            add_keys(geo, dpieces, step, VALUE, tn(prob_ref[step], dwide))
            add_keys(geo, dpieces, step, KEY, tn(dscore, wide) * scale)
            dquery_ref[rows[n], :] = from_heads(nn(dscore, load_keys(geo, pieces, step, KEY))) * scale
        return carry

    lax.fori_loop(0, geo.steps // together, steps_of, 0)


def grouped(x):
    parts = x.reshape(12, 2, 2, 8, x.shape[-1])
    return [parts[:, g >> 1, g & 1].reshape(96, x.shape[-1]) for g in range(4)]


EVEN_ROW, EVEN_COL, COL = 3, 4, 5


def send(place, even, first, second, after, before):
    for ref, when_even, when_odd in ((first, after, before), (second, before, after)):

        @pl.when(place[even] == 1)
        def _(ref=ref, value=when_even):
            ref[...] = value()

        @pl.when(place[even] == 0)
        def _(ref=ref, value=when_odd):
            ref[...] = value()


def received(place, even, first, second):
    flag = place[even].astype(f32)
    one, two = first.astype(f32), second.astype(f32)
    return two * flag + one * (1.0 - flag), one * flag + two * (1.0 - flag)


def store_received(place, even, first, second, before, after):
    @pl.when(place[even] == 1)
    def _():
        before(second)
        after(first)

    @pl.when(place[even] == 0)
    def _():
        before(first)
        after(second)


def run(kernel, outs, ins, scratch=(), specs=None, vmem=16, out_specs=None):
    in_specs = [pl.BlockSpec(memory_space=pltpu.VMEM)] * len(ins)
    for index, spec in (specs or {}).items():
        in_specs[index] = spec
    results = [pl.BlockSpec(memory_space=pltpu.VMEM)] * len(outs)
    for index, spec in (out_specs or {}).items():
        results[index] = spec
    return pl.pallas_call(
        kernel,
        out_shape=outs,
        in_specs=in_specs,
        out_specs=results,
        scratch_shapes=list(scratch),
        compiler_params=pltpu.CompilerParams(vmem_limit_bytes=vmem * MIB),
        cost_estimate=pl.CostEstimate(flops=0, bytes_accessed=4 << 20, transcendentals=0),
    )(*ins)


SMEM = pl.BlockSpec(memory_space=pltpu.SMEM)


def out(shape, dtype=f32):
    return jax.ShapeDtypeStruct(shape, dtype)


def pack_kernel(col, conv, qkv, proj, exp, red, head, *refs, across):
    sh = qkv.shape[1]
    outs, groups = refs[:2], refs[2:]

    def cols(x):
        return [x[:, k * 128 : (k + 1) * 128] for k in range(x.shape[1] // 128)]

    def reds(x):
        return [part for k in range(3) for part in cols(x[k * sh : (k + 1) * sh, :])]

    tail = jnp.concatenate([head[:, 896:], jnp.zeros((sh, 1024 - CLASSES), f32)], 1)
    blocks = (
        cols(conv[...]) + cols(qkv[0]),
        cols(proj[0]) + cols(exp[0]) + reds(red[0]) + cols(qkv[1]),
        cols(proj[1]) + cols(exp[1]) + reds(red[1]) + cols(head[:, :896]) + [tail],
    )
    begin = 0
    for index, (group, values) in enumerate(zip(groups, blocks)):
        for k, value in enumerate(values):
            group[k * sh : (k + 1) * sh, :] = value.astype(bf16)
        empty = group.shape[0] - len(values) * sh
        if empty:
            group[len(values) * sh :, :] = jnp.zeros((empty, 128), bf16)
        result = outs[min(index, 1)]
        begin = begin if index == 2 else 0
        part = group.shape[0] // across
        mine = group[pl.ds(pl.multiple_of(col[0] * part, 16), part), :]
        for row in range(result.shape[0]):
            result[row, begin : begin + part, :] = mine
        begin += part


def weight_of(blocks, first, count):
    sh = D // blocks.shape[1]
    per = blocks.shape[2] // sh
    parts = [
        blocks[k // per, :, (k % per) * sh : (k % per + 1) * sh, :].reshape(D, 128)
        for k in range(first, first + count)
    ]
    return jnp.concatenate(parts, 1)


def weight_red(blocks, first):
    rows = blocks.shape[1]
    parts = [weight_of(blocks, first + 2 * k, 2).reshape(rows, 1, D // rows, D) for k in range(3)]
    return jnp.concatenate(parts, 1).reshape(FF, D)


def table_kernel(bias, first_one, first_two):
    position_table(One, bias[0:8, :], first_one)
    position_table(Two, bias[8:16, :], first_two)


def patch_kernel(place, stem, above, left, lay, patches, stem_f, above_f):
    stem_f[...] = stem[...].astype(f32)
    above_f[...] = above[...].astype(f32)
    left_f = left[...].astype(f32)
    tiles = left_f[:384].reshape(24, 2, 8, 128)
    left_odd = tiles[:, 0]
    beside = [left_odd, tiles[:, 1], jnp.concatenate([left_odd[1:], left_f[384:392][None]], 0)]
    phases = []
    for m in range(4):
        part = stem_f[pl.ds(m, 384, stride=4), :].reshape(24, 2, 8, 128)
        even, odd = part[:, 0], part[:, 1]
        top = above_f[pl.ds(m, 8, stride=4), :]
        phases.append([jnp.concatenate([top[None], odd[:-1]], 0), even, odd])
    token = lax.broadcasted_iota(i32, (384, 1), 0)
    row_pos = place[0] + (token >> 4)
    col_pos = place[1] + One.query_col(token & 15)
    inner_row = jnp.where(row_pos == lay[:, 0:1], 0.0, 1.0)
    inner_col = jnp.where(col_pos == lay[:, 2:3], 0.0, 1.0)
    half = lax.broadcasted_iota(i32, (24, 8, 128), 1)
    for a in range(3):
        shifted = jnp.where(half == 0, beside[a], pltpu.roll(phases[3][a], 1, 1))
        taps = (
            (shifted, phases[1][a]),
            (phases[0][a], phases[2][a]),
            (phases[1][a], phases[3][a]),
        )
        for b in range(3):
            value = jnp.stack(taps[b], 1).reshape(384, 128)
            if a == 0:
                value = value * inner_row
            if b == 0:
                value = value * inner_col
            lanes = slice((3 * a + b) * 128, (3 * a + b + 1) * 128)
            patches[:, lanes] = value.astype(bf16)


def front_kernel(place, patches, early, norms, hidden, query, keyval, first, second):
    conv = nt(patches[...], weight_of(early, 0, 9))
    h = norm(conv, norms[0:2, :])
    hidden[...] = h
    low = norm(h, norms[2:4, :]).astype(bf16)
    mixed = nn(low, weight_of(early, 9, 6))
    query[...] = mixed[:, :D].astype(bf16)
    both = mixed[:, D:].reshape(24, 2, 8, 2 * D)
    zero, one = both[:, 0], both[:, 1]
    keyval[0] = zero.reshape(192, 2 * D).astype(bf16)
    keyval[1] = one.reshape(192, 2 * D).astype(bf16)
    sub = lax.broadcasted_iota(i32, zero.shape, 1)
    left = jnp.where(sub < 4, zero, pltpu.roll(one, 4, 1))
    right = jnp.where(sub < 4, pltpu.roll(zero, 4, 1), one)
    send(
        place, EVEN_COL, first, second,
        lambda: right.reshape(192, 2 * D).astype(bf16), lambda: left.reshape(192, 2 * D).astype(bf16),
    )


def ring_kernel(place, keyval, first, second, row_first, row_second):
    def put(ref, begin):
        rows = slice(begin, begin + 48)
        ref[0] = keyval[0, rows, :]
        ref[1] = keyval[1, rows, :]

        def left(source):
            ref[2] = source[rows, :]

        def right(source):
            ref[3] = source[rows, :]

        store_received(place, EVEN_COL, first, second, left, right)

    @pl.when(place[EVEN_ROW] == 1)
    def _():
        put(row_first, 144)
        put(row_second, 0)

    @pl.when(place[EVEN_ROW] == 0)
    def _():
        put(row_first, 0)
        put(row_second, 144)


class Copies:
    def __init__(self, sems):
        self.sems, self.used = sems, 0

    def semaphore(self):
        self.used += 1
        return self.sems.at[self.used - 1]

    def start(self, source, target):
        copy = pltpu.make_async_copy(source, target, self.semaphore())
        copy.start()
        return [copy]

    def start_received(self, place, even, first, second, before, after):
        one, two = self.semaphore(), self.semaphore()

        @pl.when(place[even] == 1)
        def _():
            pltpu.make_async_copy(second, before, one).start()
            pltpu.make_async_copy(first, after, two).start()

        @pl.when(place[even] == 0)
        def _():
            pltpu.make_async_copy(first, before, one).start()
            pltpu.make_async_copy(second, after, two).start()

        return [pltpu.make_async_copy(first, before, one), pltpu.make_async_copy(first, after, two)]


def wait_for(copies):
    for copy in copies:
        copy.wait()


def gather_keys_one(copies, place, keyval, col_first, col_second, row_first, row_second, pieces):
    inner = pl.ds(48, 192)
    return (
        copies.start(keyval, pieces.at[pl.ds(0, 2), inner, :])
        + copies.start_received(
            place, EVEN_COL, col_first, col_second, pieces.at[2, inner, :], pieces.at[3, inner, :]
        )
        + copies.start_received(
            place, EVEN_ROW, row_first, row_second,
            pieces.at[:, pl.ds(0, 48), :], pieces.at[:, pl.ds(240, 48), :],
        )
    )


def gather_keys_two(copies, place, own, first, second, pieces):
    return copies.start(own, pieces.at[0]) + copies.start_received(
        place, EVEN_COL, first, second, pieces.at[1], pieces.at[2]
    )


def extend_kernel(place, keyval, first, second, result):
    result[:, 48:144, :] = keyval[...]

    def above(source):
        result[:, 0:48, :] = source[...]

    def below(source):
        result[:, 144:192, :] = source[...]

    store_received(place, EVEN_ROW, first, second, above, below)


def rim_kernel(place, rims, first, second, row_first, row_second):
    def total(part):
        rows = slice(144 * part, 144 * part + 48)
        value = rims[:, 48 * part : 48 * part + 48, :].astype(f32)
        value += first[:, rows, :].astype(f32) + second[:, rows, :].astype(f32)
        return value.astype(bf16)

    send(place, EVEN_ROW, row_first, row_second, lambda: total(1), lambda: total(0))


def sides_kernel(place, sides, first, second, col_first, col_second):
    def total(p):
        above, below = received(place, EVEN_ROW, first[2 + p], second[2 + p])
        own = sides[p].astype(f32)
        rows = [own[0:48] + above, own[48:144], own[144:192] + below]
        return jnp.concatenate(rows, 0).astype(bf16)

    send(place, EVEN_COL, col_first, col_second, lambda: total(1), lambda: total(0))


def feed_forward(hidden, norms, w_exp, w_red, bias):
    low = norm(hidden, norms).astype(bf16)
    upper = nn(low, w_exp) + bias
    gelu = upper * normal_cdf(upper)
    return hidden + nn(gelu.astype(bf16), w_red)


PROJ, EXP, RED, QKV, HEAD = 0, 2, 8, 14, 14


def first_block_kernel(
    place, lay, hidden, query, keyval, cola, colb, rowa, rowb, first_table, late, norms, ebias,
    kept, att, middle, last, query2, keyval2, first, second,
    pieces, table, score, prob, group, before, sems, keep_sems,
):
    copies = Copies(sems)
    near = gather_keys_one(copies, place, keyval, cola, colb, rowa, rowb, pieces)
    arrived = copies.start(late, group) + copies.start(hidden, before)
    spread_table(One, first_table, table)
    wait_for(near)
    leaving = attend(One, place, lay, query, pieces, table, att, score, prob, kept, keep_sems)
    wait_for(arrived)
    mid = before[...] + nn(att[...], weight_of(group, PROJ, 2))
    middle[...] = mid
    end = feed_forward(mid, norms[4:6, :], weight_of(group, EXP, 6), weight_red(group, RED), ebias[0:1, :])
    last[...] = end
    low = norm(end, norms[6:8, :]).astype(bf16)
    mixed = nn(low, weight_of(group, QKV, 6))
    for g, part in enumerate(grouped(mixed)):
        query2[g * 96 : (g + 1) * 96, :] = part[:, :D].astype(bf16)
        keyval2[g] = part[:, D:].astype(bf16)
    send(
        place, EVEN_ROW, first, second, lambda: keyval2[:, 48:, :], lambda: keyval2[:, :48, :]
    )
    wait_for(leaving)


def slot_onehot(slots, images):
    entry = lax.broadcasted_iota(i32, (384, images), 1)
    return jnp.where(slots[:, 4:5] == entry, 1.0, 0.0).astype(bf16)


def ungroup(value, ref):
    for g in range(4):
        ref[:, g >> 1, g & 1] = value[g * 96 : (g + 1) * 96].reshape(12, 8, value.shape[-1])


def second_block_kernel(
    place, lay, slots, hidden, query, own, cola, colb, first_table, late, norms, ebias,
    kept, att, middle, last, sums,
    pieces, table, score, prob, group, before, att_group, att_token, sems, keep_sems,
):
    copies = Copies(sems)
    near = gather_keys_two(copies, place, own, cola, colb, pieces)
    arrived = copies.start(late, group) + copies.start(hidden, before)
    spread_table(Two, first_table, table)
    wait_for(near)
    leaving = attend(Two, place, lay, query, pieces, table, att_group, score, prob, kept, keep_sems)
    ungroup(att_group[...], att_token)
    low = att_token[...].reshape(384, D).astype(bf16)
    att[...] = low
    wait_for(arrived)
    mid = before[...] + nn(low, weight_of(group, PROJ, 2))
    middle[...] = mid
    end = feed_forward(mid, norms[8:10, :], weight_of(group, EXP, 6), weight_red(group, RED), ebias[1:2, :])
    last[...] = end
    final = norm(end, norms[10:12, :])
    images = sums.shape[0] - 8
    where = slot_onehot(slots, images)
    high, low = two_parts(final)
    sums[...] = jnp.zeros_like(sums)
    sums[:images, :D] = tn(where, high) + tn(where, low)
    sums[images:, :images] = tn(jnp.ones((384, 8), bf16), where)
    wait_for(leaving)


def feed_forward_back(dhid, mid, gain_bias, w_exp, w_red, bias):
    low = norm(mid, gain_bias).astype(bf16)
    upper = nn(low, w_exp) + bias
    cdf = normal_cdf(upper)
    dz = dhid.astype(bf16)
    grad_red = tn((upper * cdf).astype(bf16), dz)
    slope = cdf + upper * (jnp.exp(-0.5 * upper * upper) * 0.3989422804014327)
    dupper = (nt(dz, w_red) * slope).astype(bf16)
    grad_bias = jnp.sum(dupper.astype(f32), 0, keepdims=True)
    grad_exp = tn(low, dupper)
    dx, dgain, dbias = norm_back(mid, gain_bias, nt(dupper, w_exp))
    return dhid + dx, grad_red, grad_exp, grad_bias, dgain, dbias


def put_block(grads, k, value):
    per = grads.shape[1] // D
    grads[k // per, (k % per) * D : (k % per + 1) * D, :] = value.astype(bf16)


def put_cols(grads, first, value):
    for k in range(value.shape[1] // 128):
        put_block(grads, first + k, value[:, k * 128 : (k + 1) * 128])


def put_red(grads, first, value, share):
    parts = value.reshape(D // share, 3, share, D)
    for k in range(3):
        put_cols(grads, first + 2 * k, parts[:, k].reshape(D, D))


def put_zeros(grads, first):
    per = grads.shape[1] // D
    for k in range(first, per * grads.shape[0]):
        put_block(grads, k, jnp.zeros((D, 128), f32))


def put_bias(dsmall, value):
    for k in range(3):
        dsmall[4 + k : 5 + k, :] = value[:, k * D : (k + 1) * D]
    dsmall[7:8, :] = jnp.zeros((1, D), f32)


def second_back_kernel(
    place, slots, sums_a, sums_b, labels, live, hbias, hidden, middle, att, query, own, cola, colb, kept, late,
    norms, ebias,
    loss, grad_head, grad_hbias, dhidden, grads, dsmall, dtable, dquery, inner, rims, first, second,
    pieces, prob, dprob, dscore, dpieces, datt, dq_group, group, grads_out, dq_token, sems,
):
    copies = Copies(sems)
    weights = copies.start(late, group)
    near = gather_keys_two(copies, place, own, cola, colb, pieces) + copies.start(kept, prob)
    sums = sums_a[...] + sums_b[...]
    images = sums.shape[0] - 8
    total = sums[:images, :D]
    diagonal = lax.broadcasted_iota(i32, (images, images), 0)
    diagonal = diagonal == lax.broadcasted_iota(i32, (images, images), 1)
    area = jnp.where(diagonal, sums[images : images + 1, :images], 0.0)
    area = jnp.sum(area, -1, keepdims=True)
    spread_area = jnp.maximum(area, 1.0)
    pooled = (total / spread_area).astype(bf16)
    wait_for(weights)
    w_head = weight_of(group, HEAD, 8)
    logits = nn(pooled, w_head) + hbias[...]
    weight = live[...] * jnp.where(area > 0.5, 1.0, 0.0)
    count = jnp.maximum(jnp.sum(weight, 0, keepdims=True), 1.0)
    cls = lax.broadcasted_iota(i32, logits.shape, 1)
    onehot = jnp.where(cls == labels[...], 1.0, 0.0)
    top = jnp.max(logits, -1, keepdims=True)
    logsum = jnp.log(jnp.sum(jnp.exp(logits - top), -1, keepdims=True)) + top
    cross = logsum - jnp.sum(onehot * logits, -1, keepdims=True)
    loss[...] = jnp.broadcast_to(jnp.sum(weight * cross, 0, keepdims=True) / count, loss.shape)
    dlogit = ((weight / count) * (jnp.exp(logits - logsum) - onehot)).astype(bf16)
    grad_hbias[...] = jnp.sum(dlogit.astype(f32), 0, keepdims=True)
    share = grad_head.shape[0]
    channel = lax.broadcasted_iota(i32, (D, share), 0)
    mine = lax.broadcasted_iota(i32, (D, share), 1) + place[2]
    own_pooled = nn(pooled, jnp.where(channel == mine, 1.0, 0.0).astype(bf16)).astype(bf16)
    grad_head[...] = tn(own_pooled, dlogit)
    high, low = two_parts(nt(dlogit, w_head) / spread_area)
    where = slot_onehot(slots, images)
    dfinal = nn(where, high) + nn(where, low)
    dhid, dgain, dbias = norm_back(hidden[...], norms[10:12, :], dfinal)
    dsmall[2:3, :] = dgain
    dsmall[3:4, :] = dbias
    dhid, grad_red, grad_exp, grad_bias, dgain, dbias = feed_forward_back(
        dhid, middle[...], norms[8:10, :], weight_of(group, EXP, 6), weight_red(group, RED), ebias[1:2, :]
    )
    put_cols(grads_out, 0, grad_exp)
    put_red(grads_out, 6, grad_red, share)
    put_bias(dsmall, grad_bias)
    dsmall[0:1, :] = dgain
    dsmall[1:2, :] = dbias
    dhidden[...] = dhid
    dy = dhid.astype(bf16)
    put_cols(grads_out, 12, tn(att[...], dy))
    put_zeros(grads_out, 14)
    leaving = copies.start(grads_out, grads)
    back = nt(dy, weight_of(group, PROJ, 2))
    for g, part in enumerate(grouped(back)):
        datt[g * 96 : (g + 1) * 96, :] = part.astype(bf16)
    wait_for(near)
    attend_back(Two, query, datt, pieces, prob, dq_group, dpieces, dtable, dprob, dscore)
    ungroup(dq_group[...], dq_token)
    dquery[...] = dq_token[...].reshape(384, D).astype(bf16)
    inner[...] = dpieces[0, :, 48:144, :]
    rims[:, 0:48, :] = dpieces[0, :, 0:48, :].astype(bf16)
    rims[:, 48:96, :] = dpieces[0, :, 144:192, :].astype(bf16)
    send(
        place, EVEN_COL, first, second,
        lambda: dpieces[2].astype(bf16), lambda: dpieces[1].astype(bf16),
    )
    wait_for(leaving)


def position_kernel(dtable, rims, dpos, near, dfirst, *, geo):
    near[...] = rims[...]
    dpos[...] = gather_table(geo, dtable, dfirst)


def first_back_kernel(
    place, dhid_in, dquery2, dkv, dcola, dcolb, drowa, drowb, hidden, middle, att, query,
    keyval, cola, colb, rowa, rowb, kept, late, norms, ebias,
    dhidden, grads, dsmall, dtable, dquery, inner, sides, first, second,
    pieces, prob, dprob, dscore, dpieces, datt, dq, group, grads_out, parta, partb, dkv_token, sems,
):
    copies = Copies(sems)
    rows = pl.ds(48, 96)
    parts = copies.start(dcola.at[:, rows, :], parta) + copies.start(dcolb.at[:, rows, :], partb)
    weights = copies.start(late, group)
    near = gather_keys_one(copies, place, keyval, cola, colb, rowa, rowb, pieces)
    near += copies.start(kept, prob)
    wait_for(parts)
    for g in range(4):
        total = dkv[g] + parta[g].astype(f32) + partb[g].astype(f32)
        total += jnp.concatenate(received(place, EVEN_ROW, drowa[g], drowb[g]), 0)
        dkv_token[:, g >> 1, g & 1] = total.reshape(12, 8, 2 * D)
    dmixed = jnp.concatenate(
        [dquery2[...], dkv_token[...].reshape(384, 2 * D).astype(bf16)], 1
    )
    low = norm(hidden[...], norms[6:8, :]).astype(bf16)
    put_cols(grads_out, 0, tn(low, dmixed))
    wait_for(weights)
    dx, dgain, dbias = norm_back(
        hidden[...], norms[6:8, :], nt(dmixed, weight_of(group, QKV, 6))
    )
    dsmall[2:3, :] = dgain
    dsmall[3:4, :] = dbias
    dhid, grad_red, grad_exp, grad_bias, dgain, dbias = feed_forward_back(
        dhid_in[...] + dx, middle[...], norms[4:6, :], weight_of(group, EXP, 6), weight_red(group, RED),
        ebias[0:1, :],
    )
    put_cols(grads_out, 6, grad_exp)
    put_red(grads_out, 12, grad_red, D // late.shape[1])
    put_bias(dsmall, grad_bias)
    dsmall[0:1, :] = dgain
    dsmall[1:2, :] = dbias
    dhidden[...] = dhid
    dy = dhid.astype(bf16)
    put_cols(grads_out, 18, tn(att[...], dy))
    put_zeros(grads_out, 20)
    leaving = copies.start(grads_out, grads)
    datt[...] = nt(dy, weight_of(group, PROJ, 2)).astype(bf16)
    wait_for(near)
    attend_back(One, query, datt, pieces, prob, dq, dpieces, dtable, dprob, dscore)
    dquery[...] = dq[...].astype(bf16)
    inner[...] = dpieces[0:2, 48:240, :]
    sides[...] = dpieces[2:4, 48:240, :].astype(bf16)
    send(
        place, EVEN_ROW, first, second,
        lambda: dpieces[:, 240:288, :].astype(bf16), lambda: dpieces[:, 0:48, :].astype(bf16),
    )
    wait_for(leaving)


SMALL_ROWS = 64


def front_back_kernel(
    place, dhid_in, dquery, inner, drowa, drowb, dcolb, dcola, patches, early,
    norms, dsmall1, dsmall2, dpos1, dpos2,
    keep, give,
    grads, small,
):
    left, right = received(place, EVEN_COL, dcola[...], dcolb[...])
    left, right = left.reshape(24, 8, 2 * D), right.reshape(24, 8, 2 * D)
    sub = lax.broadcasted_iota(i32, left.shape, 1)

    def whole(p):
        above, below = received(place, EVEN_ROW, drowa[p], drowb[p])
        top = inner[p, 0:48, :] + above
        bottom = inner[p, 144:192, :] + below
        return jnp.concatenate([top, inner[p, 48:144, :], bottom], 0).reshape(24, 8, 2 * D)

    zero = whole(0) + jnp.where(sub < 4, left, pltpu.roll(right, 4, 1))
    one = whole(1) + jnp.where(sub < 4, pltpu.roll(left, 4, 1), right)
    dkv = jnp.stack([zero, one], 1).reshape(384, 2 * D).astype(bf16)
    dmixed = jnp.concatenate([dquery[...], dkv], 1)
    conv = nt(patches[...], weight_of(early, 0, 9))
    h = norm(conv, norms[0:2, :])
    low = norm(h, norms[2:4, :]).astype(bf16)
    put_cols(grads, 9, tn(low, dmixed))
    w_qkv = weight_of(early, 9, 6)
    dx, dgain1, dbias1 = norm_back(h, norms[2:4, :], nt(dmixed, w_qkv))
    dconv, dgain0, dbias0 = norm_back(conv, norms[0:2, :], dhid_in[...] + dx)
    put_cols(grads, 0, tn(dconv.astype(bf16), patches[...]))
    put_zeros(grads, 15)

    def place_row(first, value):
        for k in range(value.shape[1] // 128):
            small[first + k : first + k + 1, :] = value[:, k * 128 : (k + 1) * 128]

    small[...] = jnp.zeros_like(small)
    for k, value in enumerate((dgain0, dbias0, dgain1, dbias1)):
        place_row(2 * k, value)
    for k in range(4):
        place_row(8 + 2 * k, dsmall1[k : k + 1, :])
        place_row(16 + 2 * k, dsmall2[k : k + 1, :])
    for k in range(3):
        place_row(24 + 2 * k, dsmall1[4 + k : 5 + k, :])
        place_row(30 + 2 * k, dsmall2[4 + k : 5 + k, :])
    for layer, value in enumerate((dpos1, dpos2)):
        small[40 + 8 * layer : 48 + 8 * layer, :] = value[:, :128]
        small[56:64, 64 * layer : 64 * layer + WIN - 128] = value[:, 128:]
    begin = grads.shape[1] - SMALL_ROWS
    for col in range(grads.shape[0]):
        grads[col, begin:, :] = small[...].astype(bf16)
    halve(place, 0, grads, keep, give)


def halve(place, stage, parts, keep, give):
    bit = (place[COL] >> stage) & 1
    for k in range(keep.shape[0]):
        keep[k] = parts[2 * k + bit]
        give[k] = parts[2 * k + 1 - bit]


def halve_kernel(place, kept, given, keep, give, total, *, stage):
    total[...] = (kept[...].astype(f32) + given[...].astype(f32)).astype(bf16)
    halve(place, stage, total, keep, give)


def between_kernel(second, first, kept, given, result):
    rows = result.shape[0]
    sh = D // rows
    begin = 0
    for group in (second, first):
        for k in range(group.shape[0] // D):
            result[:, begin : begin + sh, :] = group[k * D : (k + 1) * D, :].reshape(rows, sh, 128)
            begin += sh
    for k in range(kept.shape[1] // D):
        span = slice(k * D, (k + 1) * D)
        total = kept[0, span, :].astype(f32) + given[0, span, :].astype(f32)
        result[:, begin : begin + sh, :] = total.astype(bf16).reshape(rows, sh, 128)
        begin += sh
    span = slice(kept.shape[1] - SMALL_ROWS, kept.shape[1])
    small = (kept[0, span, :].astype(f32) + given[0, span, :].astype(f32)).astype(bf16)
    for row in range(rows):
        result[row, begin:, :] = small


def last_sum_kernel(parts, result, small):
    total = parts[0].astype(f32)
    for row in range(1, parts.shape[0]):
        total += parts[row].astype(f32)
    count = result.shape[0]
    result[...] = total[:count].astype(bf16)
    small[...] = total[count:]


def adamw(weight, grad, first, second):
    first = beta_one * first + (1.0 - beta_one) * grad
    second = beta_two * second + (1.0 - beta_two) * grad * grad
    fix_one = 1.0 - beta_one**STEP
    fix_two = 1.0 - beta_two**STEP
    new = weight - learn_rate * (
        first / fix_one / (jnp.sqrt(second / fix_two) + eps_adam) + decay_rate * weight
    )
    return (first, second, new)


def adamw_kernel(grads, *refs, sh, per):
    ins = [refs[3 * n : 3 * n + 3] for n in range(5)]
    outs = [refs[15 + 3 * n : 18 + 3 * n] for n in range(5)]

    def update(n, group, k, *where):
        begin = (sum(per[:group]) + k % per[group]) * sh
        grad = grads[k // per[group], begin : begin + sh, :].astype(f32)
        weight, first, second = (ref[where] for ref in ins[n])
        for ref, value in zip(outs[n], adamw(weight, grad, first, second)):
            ref[where] = value

    every = slice(None)
    for k in range(9):
        update(0, 2, k, every, slice(k * 128, (k + 1) * 128))
    for k in range(6):
        lanes = slice(k * 128, (k + 1) * 128)
        update(1, 2, 9 + k, 0, every, lanes)
        update(1, 1, k, 1, every, lanes)
        update(3, 1, 6 + k, 0, every, lanes)
        update(3, 0, k, 1, every, lanes)
        rows, half = slice((k // 2) * sh, (k // 2 + 1) * sh), slice((k % 2) * 128, (k % 2 + 1) * 128)
        update(4, 1, 12 + k, 0, rows, half)
        update(4, 0, 6 + k, 1, rows, half)
    for k in range(2):
        lanes = slice(k * 128, (k + 1) * 128)
        update(2, 1, 18 + k, 0, every, lanes)
        update(2, 0, 12 + k, 1, every, lanes)


def onward(value, axis):
    count = lax.axis_size(axis)
    return lax.ppermute(value, axis, [(i, (i + 1) % count) for i in range(count)])


def swaps(first, second, axis):
    count = lax.axis_size(axis)
    pairs = [[(i, i + 1) for i in range(begin, count - 1, 2)] for begin in (0, 1)]
    both = [low + [(j, i) for i, j in low] for low in pairs]
    return lax.ppermute(first, axis, both[0]), lax.ppermute(second, axis, both[1])


def sum_all(value):
    axes = [axis for axis in ("col", "row") if lax.axis_size(axis) > 1]
    terms = [value, jnp.zeros_like(value)]
    for axis in axes:
        count = lax.axis_size(axis)
        first = 1
        while first < count:
            group = min(4, count // first)

            def other(flip):
                return lax.ppermute(value, axis, [(i, i ^ (flip * first)) for i in range(count)])

            terms = [value, *(other(flip) for flip in range(1, group))]
            while len(terms) > 2:
                terms = [a + b for a, b in zip(terms[::2], terms[1::2])]
            first *= group
            if axis != axes[-1] or first < count:
                value = terms[0] + terms[1]
    return terms


def on_device(
    stem_map, layout, labels, live,
    conv_weight, input_proj, output_proj, expand_weight, reduce_weight, head_weight, small_params,
    first_conv, first_input, first_output, first_expand, first_reduce, first_head, first_small,
    second_conv, second_input, second_output, second_expand, second_reduce, second_head, second_small,
):
    nr, nc = lax.axis_size("row"), lax.axis_size("col")
    sh = D // nr
    images = labels.shape[0]
    padded = -(-images // 8) * 8
    per = [-(-count // nc) for count in (14, 20, 15)]
    row_index, col_index = lax.axis_index("row"), lax.axis_index("col")
    parts = [-(-count // nc) * sh for count in (15, 20, 22)]
    early, late = run(
        functools.partial(pack_kernel, across=nc),
        [out((nr, parts[0], 128), bf16), out((nr, parts[1] + parts[2], 128), bf16)],
        [
            col_index.astype(i32)[None], conv_weight.T, input_proj, output_proj, expand_weight, reduce_weight,
            head_weight,
        ],
        [pltpu.VMEM((part * nc, 128), bf16) for part in parts],
        {0: SMEM},
        56,
    )
    early = lax.all_to_all(early, "row", 0, 0, tiled=True)
    norms = small_params[: 12 * D].reshape(12, D)
    start = 12 * D
    ebias = small_params[start : start + LAYERS * FF].reshape(LAYERS, FF)
    start += LAYERS * FF
    hbias = jnp.pad(small_params[start : start + CLASSES], (0, 24), constant_values=MASKED)[None]
    start += CLASSES
    pos_bias = small_params[start:].reshape(LAYERS * HEADS, 169)
    first_one, first_two = run(
        table_kernel,
        [out((geo.pieces, HEADS * geo.across, 128)) for geo in (One, Two)],
        [jnp.pad(pos_bias, ((0, 0), (0, WIN - 169)))],
    )
    place = [row_index * 24, col_index * 16, row_index * sh, (row_index + 1) % 2, (col_index + 1) % 2, col_index]
    place = jnp.stack(place).astype(i32)
    lay_one = layout.reshape(5, 24, 8, 2).transpose(1, 3, 2, 0).reshape(384, 5)
    lay_two = layout.reshape(5, 12, 2, 8, 2).transpose(2, 4, 1, 3, 0).reshape(384, 5)
    early, above = lax.optimization_barrier((early, onward(stem_map[-1:], "row")))
    rim = jnp.concatenate([above[:, -1:], stem_map[:, -1:]], 0)
    rim = jnp.broadcast_to(onward(rim, "col"), (49, 8, 128))
    patches = run(
        patch_kernel,
        [out((384, 1152), bf16)],
        [place, stem_map.reshape(1536, 128), above.reshape(32, 128), rim.reshape(392, 128), lay_one],
        [pltpu.VMEM((1536, 128), f32), pltpu.VMEM((32, 128), f32)],
        {0: SMEM},
    )[0]
    late, _ = lax.optimization_barrier((late, early))
    early = lax.all_gather(early, "col", axis=0)
    late = lax.all_to_all(late, "row", 0, 0, tiled=True)
    rows48, edge = out((4, 48, 2 * D), bf16), out((192, 2 * D), bf16)
    hidden0, query1, keyval1, *edges = run(
        front_kernel,
        [out((384, D)), out((384, D), bf16), out((2, 192, 2 * D), bf16), edge, edge],
        [place, patches, early, norms],
        specs={0: SMEM},
    )
    late, _ = lax.optimization_barrier((late, edges))
    late1 = lax.all_gather(late[:, : parts[1]], "col", axis=0)
    late2 = lax.all_gather(late[:, parts[1] :], "col", axis=0)
    cols1 = swaps(*edges, "col")
    rows1 = swaps(*run(ring_kernel, [rows48] * 2, [place, keyval1, *cols1], specs={0: SMEM}), "row")
    hbm = pl.BlockSpec(memory_space=pl.ANY)
    tokens, tokens_low, ext = out((384, D)), out((384, D), bf16), out((4, 192, 2 * D), bf16)
    token5 = lambda width: pltpu.VMEM((12, 2, 2, 8, width), f32)
    like = lambda x: pltpu.VMEM(x.shape, x.dtype)
    copy_sems = lambda count: pltpu.SemaphoreType.DMA((count,))

    def tiles(geo, back):
        square = (HEADS * geo.queries, geo.keys)
        shape = (4, 288, 2 * D) if geo is One else (3, 4, 192, 2 * D)
        pieces, prob = pltpu.VMEM(shape, bf16), pltpu.VMEM((geo.steps, *square), bf16)
        many = (geo.together, *square)
        if not back:
            return [pieces, pltpu.VMEM(square, f32), pltpu.VMEM(many, f32), prob]
        return [
            pieces, prob, pltpu.VMEM(many, f32), pltpu.VMEM(many, bf16), pltpu.VMEM(shape, f32),
            pltpu.VMEM((384, D), bf16), pltpu.VMEM((384, D), f32),
        ]

    probs = lambda geo: out((geo.steps, HEADS * geo.queries, geo.keys), bf16)
    dtable = lambda geo: out((HEADS * geo.queries, geo.keys))
    turns = lambda geo: copy_sems(geo.steps // geo.together)
    near1 = [keyval1, *cols1, *rows1]
    kept1, att1, middle1, last1, query2, keyval2, *edges = run(
        first_block_kernel,
        [probs(One), tokens_low, tokens, tokens, tokens_low, out((4, 96, 2 * D), bf16), rows48, rows48],
        [place, lay_one, hidden0, query1, *near1, first_one, late1, norms, ebias],
        tiles(One, False) + [like(late1), like(hidden0), copy_sems(7), turns(One)],
        {0: SMEM, **dict.fromkeys((2, 4, 5, 6, 7, 8, 10), hbm)},
        56,
        {0: hbm},
    )
    rows2 = swaps(*edges, "row")
    own2 = run(extend_kernel, [ext], [place, keyval2, *rows2], specs={0: SMEM})[0]
    near2 = [own2, *swaps(own2, own2, "col")]
    kept2, att2, middle2, last2, sums = run(
        second_block_kernel,
        [probs(Two), tokens_low, tokens, tokens, out((padded + 8, max(D, -(-padded // 128) * 128)))],
        [place, lay_two, lay_one, last1, query2, *near2, first_two, late2, norms, ebias],
        tiles(Two, False)
        + [like(late2), like(last1), pltpu.VMEM((384, D), f32), token5(D), copy_sems(5), turns(Two)],
        {0: SMEM, **dict.fromkeys((3, 5, 6, 7, 9), hbm)},
        56,
        {0: hbm},
    )
    sums_a, sums_b = sum_all(sums)
    pad_images = lambda x: jnp.pad(x, (0, padded - images))[:, None]
    grads_of = lambda group: out((nc, per[group] * D, 128), bf16)
    (
        loss, grad_head, grad_hbias, dhid, grads2, dsmall2, dtable2, dquery2, inner2, rims2, *edges,
    ) = run(
        second_back_kernel,
        [
            out((8, 128)), out((sh, 1024)), out((1, 1024)), tokens, grads_of(0),
            out((8, D)), dtable(Two), tokens_low,
            out((4, 96, 2 * D)), out((4, 96, 2 * D), bf16), ext, ext,
        ],
        [
            place, lay_one, sums_a, sums_b, pad_images(labels), pad_images(live.astype(f32)), hbias,
            last2, middle2, att2, query2, *near2, kept2, late2, norms, ebias,
        ],
        tiles(Two, True) + [like(late2), like(grads_of(0)), token5(D), copy_sems(6)],
        {0: SMEM, **dict.fromkeys((11, 12, 13, 14, 15), hbm)},
        56,
        {4: hbm},
    )
    def position(geo, table, rims):
        scratch = [pltpu.VMEM((geo.pieces, HEADS * geo.across, 128), f32)]
        return run(
            functools.partial(position_kernel, geo=geo),
            [out((HEADS, WIN)), out(rims.shape, bf16)],
            [table, rims],
            scratch,
        )

    dpos2, rims2 = position(Two, dtable2, rims2)
    dcols2 = swaps(*edges, "col")[::-1]
    drows2 = swaps(*run(rim_kernel, [rows48] * 2, [place, rims2, *dcols2], specs={0: SMEM}), "row")
    grads2 = lax.psum_scatter(grads2, "col", scatter_dimension=0, tiled=False)

    part2 = pltpu.VMEM((4, 96, 2 * D), bf16)
    dhid, grads1, dsmall1, dtable1, dquery1, inner1, sides1, *edges = run(
        first_back_kernel,
        [
            tokens, grads_of(1), out((8, D)), dtable(One),
            tokens_low, out((2, 192, 2 * D)), out((2, 192, 2 * D), bf16), rows48, rows48,
        ],
        [
            place, dhid, dquery2, inner2, *dcols2, *drows2, last1, middle1, att1, query1,
            *near1, kept1, late1, norms, ebias,
        ],
        tiles(One, True) + [like(late1), like(grads_of(1)), part2, part2, token5(2 * D), copy_sems(10)],
        {0: SMEM, **dict.fromkeys((4, 5, 12, 13, 14, 15, 16, 17, 18), hbm)},
        56,
        {1: hbm},
    )
    drows1 = swaps(*edges, "row")
    grads1 = lax.psum_scatter(grads1, "col", scatter_dimension=0, tiled=False)
    dpos1, sides1 = position(One, dtable1, sides1)
    dcols1 = swaps(*run(sides_kernel, [edge] * 2, [place, sides1, *drows1], specs={0: SMEM}), "col")
    part = per[2] * D + SMALL_ROWS
    half = lambda count: out((count, part, 128), bf16)
    kept, given = run(
        front_back_kernel,
        [half(nc // 2), half(nc // 2)],
        [
            place, dhid, dquery1, inner1, *drows1, *dcols1[::-1], patches,
            early, norms, dsmall1, dsmall2, dpos1, dpos2,
        ],
        [pltpu.VMEM((nc, part, 128), bf16), pltpu.VMEM((SMALL_ROWS, 128), f32)],
        {0: SMEM},
    )
    stage = 0
    while True:
        given = lax.ppermute(given, "col", [(i, i ^ (1 << stage)) for i in range(nc)])
        stage += 1
        if 1 << stage == nc:
            break
        count = nc >> (stage + 1)
        kept, given = run(
            functools.partial(halve_kernel, stage=stage),
            [half(count), half(count)],
            [place, kept, given],
            [pltpu.VMEM((2 * count, part, 128), bf16)],
            {0: SMEM},
        )
    mine = run(
        between_kernel,
        [out((nr, sum(per) * sh + SMALL_ROWS, 128), bf16)],
        [grads2, grads1, kept, given],
        vmem=56,
    )[0]
    mine = lax.all_to_all(mine, "row", 0, 0, tiled=True)
    mine, small = run(
        last_sum_kernel, [out((sum(per) * sh, 128), bf16), out((SMALL_ROWS, 128))], [mine]
    )
    grads = lax.all_gather(mine, "col", axis=0)
    wide = [
        conv_weight.T, first_conv.T, second_conv.T, input_proj, first_input, second_input,
        output_proj, first_output, second_output, expand_weight, first_expand, second_expand,
        reduce_weight, first_reduce, second_reduce,
    ]
    new = run(
        functools.partial(adamw_kernel, sh=sh, per=per), [out(x.shape) for x in wide], [grads, *wide]
    )
    new = [x.T for x in new[:3]] + list(new[3:])
    pos = [
        jnp.concatenate([small[40 + 8 * k : 48 + 8 * k], small[56:64, 64 * k : 64 * k + 41]], 1).reshape(-1)
        for k in range(2)
    ]
    grad_small = jnp.concatenate([small[:36].reshape(-1), grad_hbias[0, :CLASSES], *pos])
    head = adamw(head_weight, grad_head[:, :CLASSES], first_head, second_head)
    return (loss[0, 0], *new, *head, *adamw(small_params, grad_small, first_small, second_small))


def solution(mesh):
    return jax.shard_map(
        on_device,
        mesh=mesh,
        in_specs=(
            P("row", "col", None),
            P(None, "row", "col"),
            P(),
            P(),
            P(None, "row"),
            P(None, "row", None),
            P(None, "row", None),
            P(None, "row", None),
            P(None, "row", None),
            P("row", None),
            P(),
            P(None, "row"),
            P(None, "row", None),
            P(None, "row", None),
            P(None, "row", None),
            P(None, "row", None),
            P("row", None),
            P(),
            P(None, "row"),
            P(None, "row", None),
            P(None, "row", None),
            P(None, "row", None),
            P(None, "row", None),
            P("row", None),
            P(),
        ),
        out_specs=(
            P(),
            P(None, "row"),
            P(None, "row"),
            P(None, "row"),
            P(None, "row", None),
            P(None, "row", None),
            P(None, "row", None),
            P(None, "row", None),
            P(None, "row", None),
            P(None, "row", None),
            P(None, "row", None),
            P(None, "row", None),
            P(None, "row", None),
            P(None, "row", None),
            P(None, "row", None),
            P(None, "row", None),
            P("row", None),
            P("row", None),
            P("row", None),
            P(),
            P(),
            P(),
        ),
        check_vma=False,
    )
```

```python
import functools

import jax
import jax.numpy as jnp
from jax import lax
from jax.experimental import pallas as pl
from jax.experimental.pallas import tpu as pltpu
from jax.sharding import PartitionSpec as P

D = 256
HEADS = 8
FF = 768
CLASSES = 1000
LAYERS = 2
STEP = 5
WIN = 176

eps_norm = 1e-05
beta_one = 0.9
beta_two = 0.999
learn_rate = 0.2
decay_rate = 0.05
eps_adam = 1e-08
scale = (D // HEADS) ** -0.5

bf16 = jnp.bfloat16
f32 = jnp.float32
i32 = jnp.int32
MASKED = -1e30
LOG2E = 1.4426950408889634
MIB = 1024 * 1024


def nn(a, b):
    return lax.dot_general(a, b, (((1,), (0,)), ((), ())), preferred_element_type=f32)


def nt(a, b):
    return lax.dot_general(a, b, (((1,), (1,)), ((), ())), preferred_element_type=f32)


def tn(a, b):
    return lax.dot_general(a, b, (((0,), (0,)), ((), ())), preferred_element_type=f32)


def two_parts(x):
    high = x.astype(bf16)
    return high, (x - high.astype(f32)).astype(bf16)


def norm_parts(x):
    centre = x - jnp.mean(x, -1, keepdims=True)
    rstd = lax.rsqrt(jnp.mean(centre * centre, -1, keepdims=True) + eps_norm)
    return centre * rstd, rstd


def norm(x, gain_bias):
    return norm_parts(x)[0] * gain_bias[0:1] + gain_bias[1:2]


def norm_back(x, gain_bias, dy):
    xhat, rstd = norm_parts(x)
    dxhat = dy * gain_bias[0:1]
    dx = rstd * (
        dxhat
        - jnp.mean(dxhat, -1, keepdims=True)
        - xhat * jnp.mean(dxhat * xhat, -1, keepdims=True)
    )
    return dx, jnp.sum(dy * xhat, 0, keepdims=True), jnp.sum(dy, 0, keepdims=True)


def normal_cdf(u):
    return 0.5 * (1.0 + lax.erf(u * 0.7071067811865476))


class One:
    dilation, queries, across, pieces, steps = 1, 64, 16, 4, 6
    together = 3
    keys = pieces * 128

    @staticmethod
    def key_col(piece, c8):
        two = 2 * (c8 & 3) + (c8 >> 2)
        return jnp.where(
            piece == 0,
            2 * c8,
            jnp.where(piece == 1, 2 * c8 + 1, jnp.where(piece == 2, two - 8, two + 16)),
        )

    @staticmethod
    def query_col(index):
        return 2 * (index & 7) + (index >> 3)


class Two:
    dilation, queries, across, pieces, steps = 2, 32, 8, 3, 12
    together = 3
    keys = pieces * 128

    @staticmethod
    def key_col(piece, c8):
        return jnp.where(piece == 0, c8, jnp.where(piece == 1, c8 - 8, c8 + 8))

    @staticmethod
    def query_col(index):
        return index


def key_place(geo):
    lane = lax.broadcasted_iota(i32, (1, geo.keys), 1)
    return (lane >> 3) & 15, geo.key_col(lane >> 7, lane & 7)


def window_mask(geo, lay, step, row_first, col_first):
    token = lax.broadcasted_iota(i32, (geo.queries, 1), 0)
    if geo.dilation == 1:
        block = step
        row = block * 4 + (token >> 4)
        col = geo.query_col(token & 15)
        row_pos, col_pos = row_first + row, col_first + col
    else:
        group = step // 3
        block = step - 3 * group
        row = block * 4 + (token >> 3)
        col = token & 7
        row_pos = row_first + 2 * row + (group >> 1)
        col_pos = col_first + 2 * col + (group & 1)

    def begin(place, first, end):
        local = place - first
        extent = end - first
        if geo.dilation == 1:
            index, length = local, extent
        else:
            index, length = local >> 1, (extent - (local & 1) + 1) >> 1
        return jnp.minimum(jnp.maximum(index - 3, 0), length - 7) - index

    row_start = row + begin(row_pos, lay[:, 0:1], lay[:, 1:2])
    col_start = col + begin(col_pos, lay[:, 2:3], lay[:, 3:4])
    key_row, key_col = key_place(geo)
    down = key_row + (block * 4 - 6) - row_start
    right = key_col - col_start
    inside = (down >= 0) & (down <= 6) & (right >= 0) & (right <= 6)
    return jnp.where(inside, 0.0, MASKED).astype(f32)


def position_onehot(geo, across):
    key_row, key_col = key_place(geo)
    right = key_col - geo.query_col(across) + 6
    index = jnp.where((right >= 0) & (right <= 12) & (key_row <= 12), key_row * 13 + right, -1)
    entry = lax.broadcasted_iota(i32, (WIN, geo.keys), 0)
    return jnp.where(entry == index, 1.0, 0.0).astype(bf16)


def position_table(geo, bias, first_ref):
    high = bias.astype(bf16)
    rest = bias - high.astype(f32)
    mid = rest.astype(bf16)
    low = (rest - mid.astype(f32)).astype(bf16)
    for across in range(geo.across):
        onehot = position_onehot(geo, across)
        row = nn(high, onehot) + nn(mid, onehot) + nn(low, onehot)
        for piece in range(geo.pieces):
            lanes = slice(piece * 128, piece * 128 + 128)
            first_ref[piece, pl.ds(across, HEADS, stride=geo.across), :] = row[:, lanes]


def spread_table(geo, first_ref, table_ref):
    for head in range(HEADS):
        for row in range(4):
            for piece in range(geo.pieces):
                lanes = slice(piece * 128, piece * 128 + 128)
                value = first_ref[piece, head * geo.across : (head + 1) * geo.across, :]
                value = value * LOG2E
                if row:
                    value = pltpu.roll(value, 8 * row, 1)
                begin = head * geo.queries + row * geo.across
                table_ref[begin : begin + geo.across, lanes] = value


def gather_table(geo, table_ref, first_ref):
    for head in range(HEADS):
        for piece in range(geo.pieces):
            lanes = slice(piece * 128, piece * 128 + 128)
            total = None
            for row in range(4):
                begin = head * geo.queries + row * geo.across
                value = table_ref[begin : begin + geo.across, lanes]
                if row:
                    value = pltpu.roll(value, 128 - 8 * row, 1)
                total = value if total is None else total + value
            first_ref[piece, head * geo.across : (head + 1) * geo.across, :] = total
    grad = jnp.zeros((HEADS, WIN), f32)
    for across in range(geo.across):
        onehot = position_onehot(geo, across)
        rows = pl.ds(across, HEADS, stride=geo.across)
        first = [first_ref[piece, rows, :] for piece in range(geo.pieces)]
        high, low = two_parts(jnp.concatenate(first, 1))
        grad = grad + nt(high, onehot) + nt(low, onehot)
    return grad


def head_lanes(head):
    lane = lax.broadcasted_iota(i32, (1, D), 1)
    return jnp.where((lane >> 5) == head, 1.0, 0.0)


def by_head(x):
    return jnp.concatenate([x * head_lanes(h).astype(x.dtype) for h in range(HEADS)], 0)


def from_heads(x):
    count = x.shape[0] // HEADS
    total = None
    for h in range(HEADS):
        part = x[h * count : (h + 1) * count] * head_lanes(h)
        total = part if total is None else total + part
    return total


def key_rows(geo, step):
    if geo.dilation == 1:
        return None, pl.multiple_of(step * 32, 32)
    group = step // 3
    return group, pl.multiple_of((step - 3 * group) * 32, 32)


def load_keys(geo, pieces, step, lanes):
    group, first = key_rows(geo, step)
    if geo.dilation == 1:
        parts = [pieces[p, pl.ds(first, 128), lanes] for p in range(4)]
    else:
        parts = [pieces[p, group, pl.ds(first, 128), lanes] for p in range(3)]
    return jnp.concatenate(parts, 0)


def add_keys(geo, pieces, step, lanes, value):
    group, first = key_rows(geo, step)
    for p in range(geo.pieces):
        part = value[p * 128 : (p + 1) * 128]
        if geo.dilation == 1:
            pieces[p, pl.ds(first, 128), lanes] += part
        else:
            pieces[p, group, pl.ds(first, 128), lanes] += part


KEY = slice(0, D)
VALUE = slice(D, 2 * D)


def softmax_rows(score, table, mask):
    score = score * (scale * LOG2E) + (table + mask)
    weight = jnp.exp2(score - jnp.max(score, -1, keepdims=True))
    return weight * (1.0 / jnp.sum(weight, -1, keepdims=True))


def attend(geo, place, lay_ref, query_ref, pieces, table_ref, out_ref, score_ref, prob_ref, kept, sems):
    count = geo.queries
    together = score_ref.shape[0]

    def keep(index):
        span = pl.ds(index * together, together)
        return pltpu.make_async_copy(prob_ref.at[span], kept.at[span], sems.at[index])

    def steps_of(index, carry):
        steps = [index * together + n for n in range(together)]
        rows = [pl.ds(pl.multiple_of(step * count, count), count) for step in steps]
        for n, step in enumerate(steps):
            score_ref[n] = nt(by_head(query_ref[rows[n], :]), load_keys(geo, pieces, step, KEY))
        masks = [
            window_mask(geo, lay_ref[rows[n], :], step, place[0], place[1])
            for n, step in enumerate(steps)
        ]
        for h in range(HEADS):
            span = slice(h * count, (h + 1) * count)
            for n, step in enumerate(steps):
                prob = softmax_rows(score_ref[n, span, :], table_ref[span, :], masks[n])
                prob_ref[step, span, :] = prob.astype(bf16)
        keep(index).start()
        for n, step in enumerate(steps):
            out = nn(prob_ref[step], load_keys(geo, pieces, step, VALUE))
            out_ref[rows[n], :] = from_heads(out).astype(out_ref.dtype)
        return carry

    lax.fori_loop(0, geo.steps // together, steps_of, 0)
    return [keep(index) for index in range(geo.steps // together)]


def attend_back(
    geo, query_ref, dout_ref, pieces, prob_ref, dquery_ref, dpieces, dtable_ref, dprob_ref, dscore_ref,
):
    count = geo.queries
    together = dprob_ref.shape[0]
    dtable_ref[...] = jnp.zeros_like(dtable_ref)
    dpieces[...] = jnp.zeros_like(dpieces)

    def steps_of(index, carry):
        steps = [index * together + n for n in range(together)]
        rows = [pl.ds(pl.multiple_of(step * count, count), count) for step in steps]
        for n, step in enumerate(steps):
            dprob_ref[n] = nt(by_head(dout_ref[rows[n], :]), load_keys(geo, pieces, step, VALUE))
        for h in range(HEADS):
            span = slice(h * count, (h + 1) * count)
            total = dtable_ref[span, :]
            for n, step in enumerate(steps):
                prob = prob_ref[step, span, :].astype(f32)
                dprob = dprob_ref[n, span, :]
                dscore = prob * (dprob - jnp.sum(prob * dprob, -1, keepdims=True))
                total += dscore
                dscore_ref[n, span, :] = dscore.astype(bf16)
            dtable_ref[span, :] = total
        for n, step in enumerate(steps):
            wide, dwide = by_head(query_ref[rows[n], :]), by_head(dout_ref[rows[n], :])
            dscore = dscore_ref[n]
            add_keys(geo, dpieces, step, VALUE, tn(prob_ref[step], dwide))
            add_keys(geo, dpieces, step, KEY, tn(dscore, wide) * scale)
            dquery_ref[rows[n], :] = from_heads(nn(dscore, load_keys(geo, pieces, step, KEY))) * scale
        return carry

    lax.fori_loop(0, geo.steps // together, steps_of, 0)


def grouped(x):
    parts = x.reshape(12, 2, 2, 8, x.shape[-1])
    return [parts[:, g >> 1, g & 1].reshape(96, x.shape[-1]) for g in range(4)]


EVEN_ROW, EVEN_COL, COL = 3, 4, 5


def send(place, even, first, second, after, before):
    for ref, when_even, when_odd in ((first, after, before), (second, before, after)):

        @pl.when(place[even] == 1)
        def _(ref=ref, value=when_even):
            ref[...] = value()

        @pl.when(place[even] == 0)
        def _(ref=ref, value=when_odd):
            ref[...] = value()


def received(place, even, first, second):
    flag = place[even].astype(f32)
    one, two = first.astype(f32), second.astype(f32)
    return two * flag + one * (1.0 - flag), one * flag + two * (1.0 - flag)


def store_received(place, even, first, second, before, after):
    @pl.when(place[even] == 1)
    def _():
        before(second)
        after(first)

    @pl.when(place[even] == 0)
    def _():
        before(first)
        after(second)


def run(kernel, outs, ins, scratch=(), specs=None, vmem=16, out_specs=None):
    in_specs = [pl.BlockSpec(memory_space=pltpu.VMEM)] * len(ins)
    for index, spec in (specs or {}).items():
        in_specs[index] = spec
    results = [pl.BlockSpec(memory_space=pltpu.VMEM)] * len(outs)
    for index, spec in (out_specs or {}).items():
        results[index] = spec
    return pl.pallas_call(
        kernel,
        out_shape=outs,
        in_specs=in_specs,
        out_specs=results,
        scratch_shapes=list(scratch),
        compiler_params=pltpu.CompilerParams(vmem_limit_bytes=vmem * MIB),
        cost_estimate=pl.CostEstimate(flops=0, bytes_accessed=4 << 20, transcendentals=0),
    )(*ins)


SMEM = pl.BlockSpec(memory_space=pltpu.SMEM)


def out(shape, dtype=f32):
    return jax.ShapeDtypeStruct(shape, dtype)


def pack_kernel(col, conv, qkv, proj, exp, red, head, *refs, across):
    sh = qkv.shape[1]
    outs, groups = refs[:2], refs[2:]

    def cols(x):
        return [x[:, k * 128 : (k + 1) * 128] for k in range(x.shape[1] // 128)]

    def reds(x):
        return [part for k in range(3) for part in cols(x[k * sh : (k + 1) * sh, :])]

    tail = jnp.concatenate([head[:, 896:], jnp.zeros((sh, 1024 - CLASSES), f32)], 1)
    blocks = (
        cols(conv[...]) + cols(qkv[0]),
        cols(proj[0]) + cols(exp[0]) + reds(red[0]) + cols(qkv[1]),
        cols(proj[1]) + cols(exp[1]) + reds(red[1]) + cols(head[:, :896]) + [tail],
    )
    begin = 0
    for index, (group, values) in enumerate(zip(groups, blocks)):
        for k, value in enumerate(values):
            group[k * sh : (k + 1) * sh, :] = value.astype(bf16)
        empty = group.shape[0] - len(values) * sh
        if empty:
            group[len(values) * sh :, :] = jnp.zeros((empty, 128), bf16)
        result = outs[min(index, 1)]
        begin = begin if index == 2 else 0
        part = group.shape[0] // across
        mine = group[pl.ds(pl.multiple_of(col[0] * part, 16), part), :]
        for row in range(result.shape[0]):
            result[row, begin : begin + part, :] = mine
        begin += part


def weight_of(blocks, first, count):
    sh = D // blocks.shape[1]
    per = blocks.shape[2] // sh
    parts = [
        blocks[k // per, :, (k % per) * sh : (k % per + 1) * sh, :].reshape(D, 128)
        for k in range(first, first + count)
    ]
    return jnp.concatenate(parts, 1)


def weight_red(blocks, first):
    rows = blocks.shape[1]
    parts = [weight_of(blocks, first + 2 * k, 2).reshape(rows, 1, D // rows, D) for k in range(3)]
    return jnp.concatenate(parts, 1).reshape(FF, D)


def table_kernel(bias, first_one, first_two):
    position_table(One, bias[0:8, :], first_one)
    position_table(Two, bias[8:16, :], first_two)


def patch_kernel(place, stem, above, left, lay, patches, stem_f, above_f):
    stem_f[...] = stem[...].astype(f32)
    above_f[...] = above[...].astype(f32)
    left_f = left[...].astype(f32)
    tiles = left_f[:384].reshape(24, 2, 8, 128)
    left_odd = tiles[:, 0]
    beside = [left_odd, tiles[:, 1], jnp.concatenate([left_odd[1:], left_f[384:392][None]], 0)]
    phases = []
    for m in range(4):
        part = stem_f[pl.ds(m, 384, stride=4), :].reshape(24, 2, 8, 128)
        even, odd = part[:, 0], part[:, 1]
        top = above_f[pl.ds(m, 8, stride=4), :]
        phases.append([jnp.concatenate([top[None], odd[:-1]], 0), even, odd])
    token = lax.broadcasted_iota(i32, (384, 1), 0)
    row_pos = place[0] + (token >> 4)
    col_pos = place[1] + One.query_col(token & 15)
    inner_row = jnp.where(row_pos == lay[:, 0:1], 0.0, 1.0)
    inner_col = jnp.where(col_pos == lay[:, 2:3], 0.0, 1.0)
    half = lax.broadcasted_iota(i32, (24, 8, 128), 1)
    for a in range(3):
        shifted = jnp.where(half == 0, beside[a], pltpu.roll(phases[3][a], 1, 1))
        taps = (
            (shifted, phases[1][a]),
            (phases[0][a], phases[2][a]),
            (phases[1][a], phases[3][a]),
        )
        for b in range(3):
            value = jnp.stack(taps[b], 1).reshape(384, 128)
            if a == 0:
                value = value * inner_row
            if b == 0:
                value = value * inner_col
            lanes = slice((3 * a + b) * 128, (3 * a + b + 1) * 128)
            patches[:, lanes] = value.astype(bf16)


def front_kernel(place, patches, early, norms, hidden, query, keyval, first, second):
    conv = nt(patches[...], weight_of(early, 0, 9))
    h = norm(conv, norms[0:2, :])
    hidden[...] = h
    low = norm(h, norms[2:4, :]).astype(bf16)
    mixed = nn(low, weight_of(early, 9, 6))
    query[...] = mixed[:, :D].astype(bf16)
    both = mixed[:, D:].reshape(24, 2, 8, 2 * D)
    zero, one = both[:, 0], both[:, 1]
    keyval[0] = zero.reshape(192, 2 * D).astype(bf16)
    keyval[1] = one.reshape(192, 2 * D).astype(bf16)
    sub = lax.broadcasted_iota(i32, zero.shape, 1)
    left = jnp.where(sub < 4, zero, pltpu.roll(one, 4, 1))
    right = jnp.where(sub < 4, pltpu.roll(zero, 4, 1), one)
    send(
        place, EVEN_COL, first, second,
        lambda: right.reshape(192, 2 * D).astype(bf16), lambda: left.reshape(192, 2 * D).astype(bf16),
    )


def ring_kernel(place, keyval, first, second, row_first, row_second):
    def put(ref, begin):
        rows = slice(begin, begin + 48)
        ref[0] = keyval[0, rows, :]
        ref[1] = keyval[1, rows, :]

        def left(source):
            ref[2] = source[rows, :]

        def right(source):
            ref[3] = source[rows, :]

        store_received(place, EVEN_COL, first, second, left, right)

    @pl.when(place[EVEN_ROW] == 1)
    def _():
        put(row_first, 144)
        put(row_second, 0)

    @pl.when(place[EVEN_ROW] == 0)
    def _():
        put(row_first, 0)
        put(row_second, 144)


class Copies:
    def __init__(self, sems):
        self.sems, self.used = sems, 0

    def semaphore(self):
        self.used += 1
        return self.sems.at[self.used - 1]

    def start(self, source, target):
        copy = pltpu.make_async_copy(source, target, self.semaphore())
        copy.start()
        return [copy]

    def start_received(self, place, even, first, second, before, after):
        one, two = self.semaphore(), self.semaphore()

        @pl.when(place[even] == 1)
        def _():
            pltpu.make_async_copy(second, before, one).start()
            pltpu.make_async_copy(first, after, two).start()

        @pl.when(place[even] == 0)
        def _():
            pltpu.make_async_copy(first, before, one).start()
            pltpu.make_async_copy(second, after, two).start()

        return [pltpu.make_async_copy(first, before, one), pltpu.make_async_copy(first, after, two)]


def wait_for(copies):
    for copy in copies:
        copy.wait()


def gather_keys_one(copies, place, keyval, col_first, col_second, row_first, row_second, pieces):
    inner = pl.ds(48, 192)
    return (
        copies.start(keyval, pieces.at[pl.ds(0, 2), inner, :])
        + copies.start_received(
            place, EVEN_COL, col_first, col_second, pieces.at[2, inner, :], pieces.at[3, inner, :]
        )
        + copies.start_received(
            place, EVEN_ROW, row_first, row_second,
            pieces.at[:, pl.ds(0, 48), :], pieces.at[:, pl.ds(240, 48), :],
        )
    )


def gather_keys_two(copies, place, own, first, second, pieces):
    return copies.start(own, pieces.at[0]) + copies.start_received(
        place, EVEN_COL, first, second, pieces.at[1], pieces.at[2]
    )


def bring_kernel(source, near):
    near[...] = source[...]


def extend_kernel(place, keyval, first, second, result):
    result[:, 48:144, :] = keyval[...]

    def above(source):
        result[:, 0:48, :] = source[...]

    def below(source):
        result[:, 144:192, :] = source[...]

    store_received(place, EVEN_ROW, first, second, above, below)


def rim_kernel(place, rims, first, second, row_first, row_second):
    def total(part):
        rows = slice(144 * part, 144 * part + 48)
        value = rims[:, 48 * part : 48 * part + 48, :].astype(f32)
        value += first[:, rows, :].astype(f32) + second[:, rows, :].astype(f32)
        return value.astype(bf16)

    send(place, EVEN_ROW, row_first, row_second, lambda: total(1), lambda: total(0))


def sides_kernel(place, sides, first, second, col_first, col_second):
    def total(p):
        above, below = received(place, EVEN_ROW, first[2 + p], second[2 + p])
        own = sides[p].astype(f32)
        rows = [own[0:48] + above, own[48:144], own[144:192] + below]
        return jnp.concatenate(rows, 0).astype(bf16)

    send(place, EVEN_COL, col_first, col_second, lambda: total(1), lambda: total(0))


def feed_forward(hidden, norms, w_exp, w_red, bias):
    low = norm(hidden, norms).astype(bf16)
    upper = nn(low, w_exp) + bias
    gelu = upper * normal_cdf(upper)
    return hidden + nn(gelu.astype(bf16), w_red)


PROJ, EXP, RED, QKV, HEAD = 0, 2, 8, 14, 14


def first_block_kernel(
    place, lay, hidden, query, keyval, cola, colb, rowa, rowb, first_table, late, norms, ebias,
    kept, att, middle, last, query2, keyval2, first, second,
    pieces, table, score, prob, group, before, sems, keep_sems,
):
    copies = Copies(sems)
    near = gather_keys_one(copies, place, keyval, cola, colb, rowa, rowb, pieces)
    arrived = copies.start(late, group) + copies.start(hidden, before)
    spread_table(One, first_table, table)
    wait_for(near)
    leaving = attend(One, place, lay, query, pieces, table, att, score, prob, kept, keep_sems)
    wait_for(arrived)
    mid = before[...] + nn(att[...], weight_of(group, PROJ, 2))
    middle[...] = mid
    end = feed_forward(mid, norms[4:6, :], weight_of(group, EXP, 6), weight_red(group, RED), ebias[0:1, :])
    last[...] = end
    low = norm(end, norms[6:8, :]).astype(bf16)
    mixed = nn(low, weight_of(group, QKV, 6))
    for g, part in enumerate(grouped(mixed)):
        query2[g * 96 : (g + 1) * 96, :] = part[:, :D].astype(bf16)
        keyval2[g] = part[:, D:].astype(bf16)
    send(
        place, EVEN_ROW, first, second, lambda: keyval2[:, 48:, :], lambda: keyval2[:, :48, :]
    )
    wait_for(leaving)


def slot_onehot(slots, images):
    entry = lax.broadcasted_iota(i32, (384, images), 1)
    return jnp.where(slots[:, 4:5] == entry, 1.0, 0.0).astype(bf16)


def ungroup(value, ref):
    for g in range(4):
        ref[:, g >> 1, g & 1] = value[g * 96 : (g + 1) * 96].reshape(12, 8, value.shape[-1])


def second_block_kernel(
    place, lay, slots, hidden, query, own, cola, colb, first_table, late, norms, ebias,
    kept, att, middle, last, sums,
    pieces, table, score, prob, group, before, att_group, att_token, sems, keep_sems,
):
    copies = Copies(sems)
    near = gather_keys_two(copies, place, own, cola, colb, pieces)
    arrived = copies.start(late, group) + copies.start(hidden, before)
    spread_table(Two, first_table, table)
    wait_for(near)
    leaving = attend(Two, place, lay, query, pieces, table, att_group, score, prob, kept, keep_sems)
    ungroup(att_group[...], att_token)
    low = att_token[...].reshape(384, D).astype(bf16)
    att[...] = low
    wait_for(arrived)
    mid = before[...] + nn(low, weight_of(group, PROJ, 2))
    middle[...] = mid
    end = feed_forward(mid, norms[8:10, :], weight_of(group, EXP, 6), weight_red(group, RED), ebias[1:2, :])
    last[...] = end
    final = norm(end, norms[10:12, :])
    images = sums.shape[0] - 8
    where = slot_onehot(slots, images)
    high, low = two_parts(final)
    sums[...] = jnp.zeros_like(sums)
    sums[:images, :D] = tn(where, high) + tn(where, low)
    sums[images:, :images] = tn(jnp.ones((384, 8), bf16), where)
    wait_for(leaving)


def feed_forward_back(dhid, mid, gain_bias, w_exp, w_red, bias):
    low = norm(mid, gain_bias).astype(bf16)
    upper = nn(low, w_exp) + bias
    cdf = normal_cdf(upper)
    dz = dhid.astype(bf16)
    grad_red = tn((upper * cdf).astype(bf16), dz)
    slope = cdf + upper * (jnp.exp(-0.5 * upper * upper) * 0.3989422804014327)
    dupper = (nt(dz, w_red) * slope).astype(bf16)
    grad_bias = jnp.sum(dupper.astype(f32), 0, keepdims=True)
    grad_exp = tn(low, dupper)
    dx, dgain, dbias = norm_back(mid, gain_bias, nt(dupper, w_exp))
    return dhid + dx, grad_red, grad_exp, grad_bias, dgain, dbias


def put_block(grads, k, value):
    per = grads.shape[1] // D
    grads[k // per, (k % per) * D : (k % per + 1) * D, :] = value.astype(bf16)


def put_cols(grads, first, value):
    for k in range(value.shape[1] // 128):
        put_block(grads, first + k, value[:, k * 128 : (k + 1) * 128])


def put_red(grads, first, value, share):
    parts = value.reshape(D // share, 3, share, D)
    for k in range(3):
        put_cols(grads, first + 2 * k, parts[:, k].reshape(D, D))


def put_zeros(grads, first):
    per = grads.shape[1] // D
    for k in range(first, per * grads.shape[0]):
        put_block(grads, k, jnp.zeros((D, 128), f32))


def put_bias(dsmall, value):
    for k in range(3):
        dsmall[4 + k : 5 + k, :] = value[:, k * D : (k + 1) * D]
    dsmall[7:8, :] = jnp.zeros((1, D), f32)


def second_back_kernel(
    place, slots, sums_a, sums_b, labels, live, hbias, hidden, middle, att, query, own, cola, colb, kept, late,
    norms, ebias,
    loss, grad_head, grad_hbias, dhidden, grads, dsmall, dtable, dquery, inner, rims, first, second,
    pieces, prob, dprob, dscore, dpieces, datt, dq_group, group, grads_out, dq_token, sems,
):
    copies = Copies(sems)
    weights = copies.start(late, group)
    near = gather_keys_two(copies, place, own, cola, colb, pieces) + copies.start(kept, prob)
    sums = sums_a[...] + sums_b[...]
    images = sums.shape[0] - 8
    total = sums[:images, :D]
    diagonal = lax.broadcasted_iota(i32, (images, images), 0)
    diagonal = diagonal == lax.broadcasted_iota(i32, (images, images), 1)
    area = jnp.where(diagonal, sums[images : images + 1, :images], 0.0)
    area = jnp.sum(area, -1, keepdims=True)
    spread_area = jnp.maximum(area, 1.0)
    pooled = (total / spread_area).astype(bf16)
    wait_for(weights)
    w_head = weight_of(group, HEAD, 8)
    logits = nn(pooled, w_head) + hbias[...]
    weight = live[...] * jnp.where(area > 0.5, 1.0, 0.0)
    count = jnp.maximum(jnp.sum(weight, 0, keepdims=True), 1.0)
    cls = lax.broadcasted_iota(i32, logits.shape, 1)
    onehot = jnp.where(cls == labels[...], 1.0, 0.0)
    top = jnp.max(logits, -1, keepdims=True)
    logsum = jnp.log(jnp.sum(jnp.exp(logits - top), -1, keepdims=True)) + top
    cross = logsum - jnp.sum(onehot * logits, -1, keepdims=True)
    loss[...] = jnp.broadcast_to(jnp.sum(weight * cross, 0, keepdims=True) / count, loss.shape)
    dlogit = ((weight / count) * (jnp.exp(logits - logsum) - onehot)).astype(bf16)
    grad_hbias[...] = jnp.sum(dlogit.astype(f32), 0, keepdims=True)
    share = grad_head.shape[0]
    channel = lax.broadcasted_iota(i32, (D, share), 0)
    mine = lax.broadcasted_iota(i32, (D, share), 1) + place[2]
    own_pooled = nn(pooled, jnp.where(channel == mine, 1.0, 0.0).astype(bf16)).astype(bf16)
    grad_head[...] = tn(own_pooled, dlogit)
    high, low = two_parts(nt(dlogit, w_head) / spread_area)
    where = slot_onehot(slots, images)
    dfinal = nn(where, high) + nn(where, low)
    dhid, dgain, dbias = norm_back(hidden[...], norms[10:12, :], dfinal)
    dsmall[2:3, :] = dgain
    dsmall[3:4, :] = dbias
    dhid, grad_red, grad_exp, grad_bias, dgain, dbias = feed_forward_back(
        dhid, middle[...], norms[8:10, :], weight_of(group, EXP, 6), weight_red(group, RED), ebias[1:2, :]
    )
    put_cols(grads_out, 0, grad_exp)
    put_red(grads_out, 6, grad_red, share)
    put_bias(dsmall, grad_bias)
    dsmall[0:1, :] = dgain
    dsmall[1:2, :] = dbias
    dhidden[...] = dhid
    dy = dhid.astype(bf16)
    put_cols(grads_out, 12, tn(att[...], dy))
    put_zeros(grads_out, 14)
    leaving = copies.start(grads_out, grads)
    back = nt(dy, weight_of(group, PROJ, 2))
    for g, part in enumerate(grouped(back)):
        datt[g * 96 : (g + 1) * 96, :] = part.astype(bf16)
    wait_for(near)
    attend_back(Two, query, datt, pieces, prob, dq_group, dpieces, dtable, dprob, dscore)
    ungroup(dq_group[...], dq_token)
    dquery[...] = dq_token[...].reshape(384, D).astype(bf16)
    inner[...] = dpieces[0, :, 48:144, :]
    rims[:, 0:48, :] = dpieces[0, :, 0:48, :].astype(bf16)
    rims[:, 48:96, :] = dpieces[0, :, 144:192, :].astype(bf16)
    send(
        place, EVEN_COL, first, second,
        lambda: dpieces[2].astype(bf16), lambda: dpieces[1].astype(bf16),
    )
    wait_for(leaving)


def position_kernel(dtable, rims, dpos, near, dfirst, *, geo):
    near[...] = rims[...]
    dpos[...] = gather_table(geo, dtable, dfirst)


def first_back_kernel(
    place, dhid_in, dquery2, dkv, dcola, dcolb, drowa, drowb, hidden, middle, att, query,
    keyval, cola, colb, rowa, rowb, kept, late, norms, ebias,
    dhidden, grads, dsmall, dtable, dquery, inner, sides, first, second,
    pieces, prob, dprob, dscore, dpieces, datt, dq, group, grads_out, parta, partb, dkv_token, sems,
):
    copies = Copies(sems)
    rows = pl.ds(48, 96)
    parts = copies.start(dcola.at[:, rows, :], parta) + copies.start(dcolb.at[:, rows, :], partb)
    weights = copies.start(late, group)
    near = gather_keys_one(copies, place, keyval, cola, colb, rowa, rowb, pieces)
    near += copies.start(kept, prob)
    wait_for(parts)
    for g in range(4):
        total = dkv[g] + parta[g].astype(f32) + partb[g].astype(f32)
        total += jnp.concatenate(received(place, EVEN_ROW, drowa[g], drowb[g]), 0)
        dkv_token[:, g >> 1, g & 1] = total.reshape(12, 8, 2 * D)
    dmixed = jnp.concatenate(
        [dquery2[...], dkv_token[...].reshape(384, 2 * D).astype(bf16)], 1
    )
    low = norm(hidden[...], norms[6:8, :]).astype(bf16)
    put_cols(grads_out, 0, tn(low, dmixed))
    wait_for(weights)
    dx, dgain, dbias = norm_back(
        hidden[...], norms[6:8, :], nt(dmixed, weight_of(group, QKV, 6))
    )
    dsmall[2:3, :] = dgain
    dsmall[3:4, :] = dbias
    dhid, grad_red, grad_exp, grad_bias, dgain, dbias = feed_forward_back(
        dhid_in[...] + dx, middle[...], norms[4:6, :], weight_of(group, EXP, 6), weight_red(group, RED),
        ebias[0:1, :],
    )
    put_cols(grads_out, 6, grad_exp)
    put_red(grads_out, 12, grad_red, D // late.shape[1])
    put_bias(dsmall, grad_bias)
    dsmall[0:1, :] = dgain
    dsmall[1:2, :] = dbias
    dhidden[...] = dhid
    dy = dhid.astype(bf16)
    put_cols(grads_out, 18, tn(att[...], dy))
    put_zeros(grads_out, 20)
    leaving = copies.start(grads_out, grads)
    datt[...] = nt(dy, weight_of(group, PROJ, 2)).astype(bf16)
    wait_for(near)
    attend_back(One, query, datt, pieces, prob, dq, dpieces, dtable, dprob, dscore)
    dquery[...] = dq[...].astype(bf16)
    inner[...] = dpieces[0:2, 48:240, :]
    sides[...] = dpieces[2:4, 48:240, :].astype(bf16)
    send(
        place, EVEN_ROW, first, second,
        lambda: dpieces[:, 240:288, :].astype(bf16), lambda: dpieces[:, 0:48, :].astype(bf16),
    )
    wait_for(leaving)


SMALL_ROWS = 64


def front_back_kernel(
    place, dhid_in, dquery, inner, drowa, drowb, dcolb, dcola, patches, early,
    norms, dsmall1, dsmall2, dpos1, dpos2,
    keep, give,
    grads, small,
):
    left, right = received(place, EVEN_COL, dcola[...], dcolb[...])
    left, right = left.reshape(24, 8, 2 * D), right.reshape(24, 8, 2 * D)
    sub = lax.broadcasted_iota(i32, left.shape, 1)

    def whole(p):
        above, below = received(place, EVEN_ROW, drowa[p], drowb[p])
        top = inner[p, 0:48, :] + above
        bottom = inner[p, 144:192, :] + below
        return jnp.concatenate([top, inner[p, 48:144, :], bottom], 0).reshape(24, 8, 2 * D)

    zero = whole(0) + jnp.where(sub < 4, left, pltpu.roll(right, 4, 1))
    one = whole(1) + jnp.where(sub < 4, pltpu.roll(left, 4, 1), right)
    dkv = jnp.stack([zero, one], 1).reshape(384, 2 * D).astype(bf16)
    dmixed = jnp.concatenate([dquery[...], dkv], 1)
    conv = nt(patches[...], weight_of(early, 0, 9))
    h = norm(conv, norms[0:2, :])
    low = norm(h, norms[2:4, :]).astype(bf16)
    put_cols(grads, 9, tn(low, dmixed))
    w_qkv = weight_of(early, 9, 6)
    dx, dgain1, dbias1 = norm_back(h, norms[2:4, :], nt(dmixed, w_qkv))
    dconv, dgain0, dbias0 = norm_back(conv, norms[0:2, :], dhid_in[...] + dx)
    put_cols(grads, 0, tn(dconv.astype(bf16), patches[...]))
    put_zeros(grads, 15)

    def place_row(first, value):
        for k in range(value.shape[1] // 128):
            small[first + k : first + k + 1, :] = value[:, k * 128 : (k + 1) * 128]

    small[...] = jnp.zeros_like(small)
    for k, value in enumerate((dgain0, dbias0, dgain1, dbias1)):
        place_row(2 * k, value)
    for k in range(4):
        place_row(8 + 2 * k, dsmall1[k : k + 1, :])
        place_row(16 + 2 * k, dsmall2[k : k + 1, :])
    for k in range(3):
        place_row(24 + 2 * k, dsmall1[4 + k : 5 + k, :])
        place_row(30 + 2 * k, dsmall2[4 + k : 5 + k, :])
    for layer, value in enumerate((dpos1, dpos2)):
        small[40 + 8 * layer : 48 + 8 * layer, :] = value[:, :128]
        small[56:64, 64 * layer : 64 * layer + WIN - 128] = value[:, 128:]
    begin = grads.shape[1] - SMALL_ROWS
    for col in range(grads.shape[0]):
        grads[col, begin:, :] = small[...].astype(bf16)
    halve(place, 0, grads, keep, give)


def halve(place, stage, parts, keep, give):
    bit = (place[COL] >> stage) & 1
    for k in range(keep.shape[0]):
        keep[k] = parts[2 * k + bit]
        give[k] = parts[2 * k + 1 - bit]


def halve_kernel(place, kept, given, keep, give, total, *, stage):
    total[...] = (kept[...].astype(f32) + given[...].astype(f32)).astype(bf16)
    halve(place, stage, total, keep, give)


def lay_out_kernel(second, first, result):
    rows = result.shape[0]
    sh = D // rows
    begin = 0
    for group in (second, first):
        for k in range(group.shape[0] // D):
            result[:, begin : begin + sh, :] = group[k * D : (k + 1) * D, :].reshape(rows, sh, 128)
            begin += sh


def between_kernel(ready, kept, given, result):
    rows = result.shape[0]
    sh = D // rows
    begin = ready.shape[1]
    result[:, :begin, :] = ready[...]
    for k in range(kept.shape[1] // D):
        span = slice(k * D, (k + 1) * D)
        total = kept[0, span, :].astype(f32) + given[0, span, :].astype(f32)
        result[:, begin : begin + sh, :] = total.astype(bf16).reshape(rows, sh, 128)
        begin += sh
    span = slice(kept.shape[1] - SMALL_ROWS, kept.shape[1])
    small = (kept[0, span, :].astype(f32) + given[0, span, :].astype(f32)).astype(bf16)
    for row in range(rows):
        result[row, begin:, :] = small


def last_sum_kernel(parts, result, small):
    total = parts[0].astype(f32)
    for row in range(1, parts.shape[0]):
        total += parts[row].astype(f32)
    count = result.shape[0]
    result[...] = total[:count].astype(bf16)
    small[...] = total[count:]


def adamw(weight, grad, first, second):
    first = beta_one * first + (1.0 - beta_one) * grad
    second = beta_two * second + (1.0 - beta_two) * grad * grad
    fix_one = 1.0 - beta_one**STEP
    fix_two = 1.0 - beta_two**STEP
    new = weight - learn_rate * (
        first / fix_one / (jnp.sqrt(second / fix_two) + eps_adam) + decay_rate * weight
    )
    return (first, second, new)


def adamw_kernel(grads, *refs, sh, per):
    ins = [refs[3 * n : 3 * n + 3] for n in range(5)]
    outs = [refs[15 + 3 * n : 18 + 3 * n] for n in range(5)]

    def update(n, group, k, *where):
        begin = (sum(per[:group]) + k % per[group]) * sh
        grad = grads[k // per[group], begin : begin + sh, :].astype(f32)
        weight, first, second = (ref[where] for ref in ins[n])
        for ref, value in zip(outs[n], adamw(weight, grad, first, second)):
            ref[where] = value

    every = slice(None)
    for k in range(9):
        update(0, 2, k, every, slice(k * 128, (k + 1) * 128))
    for k in range(6):
        lanes = slice(k * 128, (k + 1) * 128)
        update(1, 2, 9 + k, 0, every, lanes)
        update(1, 1, k, 1, every, lanes)
        update(3, 1, 6 + k, 0, every, lanes)
        update(3, 0, k, 1, every, lanes)
        rows, half = slice((k // 2) * sh, (k // 2 + 1) * sh), slice((k % 2) * 128, (k % 2 + 1) * 128)
        update(4, 1, 12 + k, 0, rows, half)
        update(4, 0, 6 + k, 1, rows, half)
    for k in range(2):
        lanes = slice(k * 128, (k + 1) * 128)
        update(2, 1, 18 + k, 0, every, lanes)
        update(2, 0, 12 + k, 1, every, lanes)


def onward(value, axis):
    count = lax.axis_size(axis)
    return lax.ppermute(value, axis, [(i, (i + 1) % count) for i in range(count)])


def swaps(first, second, axis):
    count = lax.axis_size(axis)
    pairs = [[(i, i + 1) for i in range(begin, count - 1, 2)] for begin in (0, 1)]
    both = [low + [(j, i) for i, j in low] for low in pairs]
    return lax.ppermute(first, axis, both[0]), lax.ppermute(second, axis, both[1])


def sum_all(value):
    axes = [axis for axis in ("col", "row") if lax.axis_size(axis) > 1]
    terms = [value, jnp.zeros_like(value)]
    for axis in axes:
        count = lax.axis_size(axis)
        first = 1
        while first < count:
            group = min(4, count // first)

            def other(flip):
                return lax.ppermute(value, axis, [(i, i ^ (flip * first)) for i in range(count)])

            terms = [value, *(other(flip) for flip in range(1, group))]
            while len(terms) > 2:
                terms = [a + b for a, b in zip(terms[::2], terms[1::2])]
            first *= group
            if axis != axes[-1] or first < count:
                value = terms[0] + terms[1]
    return terms


def on_device(
    stem_map, layout, labels, live,
    conv_weight, input_proj, output_proj, expand_weight, reduce_weight, head_weight, small_params,
    first_conv, first_input, first_output, first_expand, first_reduce, first_head, first_small,
    second_conv, second_input, second_output, second_expand, second_reduce, second_head, second_small,
):
    nr, nc = lax.axis_size("row"), lax.axis_size("col")
    sh = D // nr
    images = labels.shape[0]
    padded = -(-images // 8) * 8
    per = [-(-count // nc) for count in (14, 20, 15)]
    row_index, col_index = lax.axis_index("row"), lax.axis_index("col")
    parts = [-(-count // nc) * sh for count in (15, 20, 22)]
    early, late = run(
        functools.partial(pack_kernel, across=nc),
        [out((nr, parts[0], 128), bf16), out((nr, parts[1] + parts[2], 128), bf16)],
        [
            col_index.astype(i32)[None], conv_weight.T, input_proj, output_proj, expand_weight, reduce_weight,
            head_weight,
        ],
        [pltpu.VMEM((part * nc, 128), bf16) for part in parts],
        {0: SMEM},
        56,
    )
    early = lax.all_to_all(early, "row", 0, 0, tiled=True)
    norms = small_params[: 12 * D].reshape(12, D)
    start = 12 * D
    ebias = small_params[start : start + LAYERS * FF].reshape(LAYERS, FF)
    start += LAYERS * FF
    hbias = jnp.pad(small_params[start : start + CLASSES], (0, 24), constant_values=MASKED)[None]
    start += CLASSES
    pos_bias = small_params[start:].reshape(LAYERS * HEADS, 169)
    first_one, first_two = run(
        table_kernel,
        [out((geo.pieces, HEADS * geo.across, 128)) for geo in (One, Two)],
        [jnp.pad(pos_bias, ((0, 0), (0, WIN - 169)))],
    )
    place = [row_index * 24, col_index * 16, row_index * sh, (row_index + 1) % 2, (col_index + 1) % 2, col_index]
    place = jnp.stack(place).astype(i32)
    lay_one = layout.reshape(5, 24, 8, 2).transpose(1, 3, 2, 0).reshape(384, 5)
    lay_two = layout.reshape(5, 12, 2, 8, 2).transpose(2, 4, 1, 3, 0).reshape(384, 5)
    early, above = lax.optimization_barrier((early, onward(stem_map[-1:], "row")))
    rim = jnp.concatenate([above[:, -1:], stem_map[:, -1:]], 0)
    rim = jnp.broadcast_to(onward(rim, "col"), (49, 8, 128))
    patches = run(
        patch_kernel,
        [out((384, 1152), bf16)],
        [place, stem_map.reshape(1536, 128), above.reshape(32, 128), rim.reshape(392, 128), lay_one],
        [pltpu.VMEM((1536, 128), f32), pltpu.VMEM((32, 128), f32)],
        {0: SMEM},
    )[0]
    late, _ = lax.optimization_barrier((late, early))
    early = lax.all_gather(early, "col", axis=0)
    late = lax.all_to_all(late, "row", 0, 0, tiled=True)
    rows48, edge = out((4, 48, 2 * D), bf16), out((192, 2 * D), bf16)
    hidden0, query1, keyval1, *edges = run(
        front_kernel,
        [out((384, D)), out((384, D), bf16), out((2, 192, 2 * D), bf16), edge, edge],
        [place, patches, early, norms],
        specs={0: SMEM},
    )
    late, _ = lax.optimization_barrier((late, edges))
    late1 = lax.all_gather(late[:, : parts[1]], "col", axis=0)
    late2 = lax.all_gather(late[:, parts[1] :], "col", axis=0)
    cols1 = swaps(*edges, "col")
    rows1 = swaps(*run(ring_kernel, [rows48] * 2, [place, keyval1, *cols1], specs={0: SMEM}), "row")
    hbm = pl.BlockSpec(memory_space=pl.ANY)
    tokens, tokens_low, ext = out((384, D)), out((384, D), bf16), out((4, 192, 2 * D), bf16)
    token5 = lambda width: pltpu.VMEM((12, 2, 2, 8, width), f32)
    like = lambda x: pltpu.VMEM(x.shape, x.dtype)
    copy_sems = lambda count: pltpu.SemaphoreType.DMA((count,))

    def tiles(geo, back):
        square = (HEADS * geo.queries, geo.keys)
        shape = (4, 288, 2 * D) if geo is One else (3, 4, 192, 2 * D)
        pieces, prob = pltpu.VMEM(shape, bf16), pltpu.VMEM((geo.steps, *square), bf16)
        many = (geo.together, *square)
        if not back:
            return [pieces, pltpu.VMEM(square, f32), pltpu.VMEM(many, f32), prob]
        return [
            pieces, prob, pltpu.VMEM(many, f32), pltpu.VMEM(many, bf16), pltpu.VMEM(shape, f32),
            pltpu.VMEM((384, D), bf16), pltpu.VMEM((384, D), f32),
        ]

    probs = lambda geo: out((geo.steps, HEADS * geo.queries, geo.keys), bf16)
    dtable = lambda geo: out((HEADS * geo.queries, geo.keys))
    turns = lambda geo: copy_sems(geo.steps // geo.together)
    near1 = [keyval1, *cols1, *rows1]
    kept1, att1, middle1, last1, query2, keyval2, *edges = run(
        first_block_kernel,
        [probs(One), tokens_low, tokens, tokens, tokens_low, out((4, 96, 2 * D), bf16), rows48, rows48],
        [place, lay_one, hidden0, query1, *near1, first_one, late1, norms, ebias],
        tiles(One, False) + [like(late1), like(hidden0), copy_sems(7), turns(One)],
        {0: SMEM, **dict.fromkeys((2, 4, 5, 6, 7, 8, 10), hbm)},
        56,
        {0: hbm},
    )
    rows2 = swaps(*edges, "row")
    near_keyval2 = run(bring_kernel, [out(keyval2.shape, bf16)], [keyval2])[0]
    own2 = run(extend_kernel, [ext], [place, near_keyval2, *rows2], specs={0: SMEM})[0]
    near2 = [own2, *swaps(own2, own2, "col")]
    kept2, att2, middle2, last2, sums = run(
        second_block_kernel,
        [probs(Two), tokens_low, tokens, tokens, out((padded + 8, max(D, -(-padded // 128) * 128)))],
        [place, lay_two, lay_one, last1, query2, *near2, first_two, late2, norms, ebias],
        tiles(Two, False)
        + [like(late2), like(last1), pltpu.VMEM((384, D), f32), token5(D), copy_sems(5), turns(Two)],
        {0: SMEM, **dict.fromkeys((3, 5, 6, 7, 9), hbm)},
        56,
        {0: hbm},
    )
    sums_a, sums_b = sum_all(sums)
    pad_images = lambda x: jnp.pad(x, (0, padded - images))[:, None]
    grads_of = lambda group: out((nc, per[group] * D, 128), bf16)
    (
        loss, grad_head, grad_hbias, dhid, grads2, dsmall2, dtable2, dquery2, inner2, rims2, *edges,
    ) = run(
        second_back_kernel,
        [
            out((8, 128)), out((sh, 1024)), out((1, 1024)), tokens, grads_of(0),
            out((8, D)), dtable(Two), tokens_low,
            out((4, 96, 2 * D)), out((4, 96, 2 * D), bf16), ext, ext,
        ],
        [
            place, lay_one, sums_a, sums_b, pad_images(labels), pad_images(live.astype(f32)), hbias,
            last2, middle2, att2, query2, *near2, kept2, late2, norms, ebias,
        ],
        tiles(Two, True) + [like(late2), like(grads_of(0)), token5(D), copy_sems(6)],
        {0: SMEM, **dict.fromkeys((11, 12, 13, 14, 15), hbm)},
        56,
        {4: hbm},
    )
    def position(geo, table, rims):
        scratch = [pltpu.VMEM((geo.pieces, HEADS * geo.across, 128), f32)]
        return run(
            functools.partial(position_kernel, geo=geo),
            [out((HEADS, WIN)), out(rims.shape, bf16)],
            [table, rims],
            scratch,
        )

    dpos2, rims2 = position(Two, dtable2, rims2)
    dcols2 = swaps(*edges, "col")[::-1]
    drows2 = swaps(*run(rim_kernel, [rows48] * 2, [place, rims2, *dcols2], specs={0: SMEM}), "row")
    grads2 = lax.psum_scatter(grads2, "col", scatter_dimension=0, tiled=False)

    part2 = pltpu.VMEM((4, 96, 2 * D), bf16)
    dhid, grads1, dsmall1, dtable1, dquery1, inner1, sides1, *edges = run(
        first_back_kernel,
        [
            tokens, grads_of(1), out((8, D)), dtable(One),
            tokens_low, out((2, 192, 2 * D)), out((2, 192, 2 * D), bf16), rows48, rows48,
        ],
        [
            place, dhid, dquery2, inner2, *dcols2, *drows2, last1, middle1, att1, query1,
            *near1, kept1, late1, norms, ebias,
        ],
        tiles(One, True) + [like(late1), like(grads_of(1)), part2, part2, token5(2 * D), copy_sems(10)],
        {0: SMEM, **dict.fromkeys((4, 5, 12, 13, 14, 15, 16, 17, 18), hbm)},
        56,
        {1: hbm},
    )
    drows1 = swaps(*edges, "row")
    grads1 = lax.psum_scatter(grads1, "col", scatter_dimension=0, tiled=False)
    dpos1, sides1 = position(One, dtable1, sides1)
    dcols1 = swaps(*run(sides_kernel, [edge] * 2, [place, sides1, *drows1], specs={0: SMEM}), "col")
    part = per[2] * D + SMALL_ROWS
    half = lambda count: out((count, part, 128), bf16)
    kept, given = run(
        front_back_kernel,
        [half(nc // 2), half(nc // 2)],
        [
            place, dhid, dquery1, inner1, *drows1, *dcols1[::-1], patches,
            early, norms, dsmall1, dsmall2, dpos1, dpos2,
        ],
        [pltpu.VMEM((nc, part, 128), bf16), pltpu.VMEM((SMALL_ROWS, 128), f32)],
        {0: SMEM},
    )
    stage = 0
    while True:
        given = lax.ppermute(given, "col", [(i, i ^ (1 << stage)) for i in range(nc)])
        stage += 1
        if 1 << stage == nc:
            break
        count = nc >> (stage + 1)
        kept, given = run(
            functools.partial(halve_kernel, stage=stage),
            [half(count), half(count)],
            [place, kept, given],
            [pltpu.VMEM((2 * count, part, 128), bf16)],
            {0: SMEM},
        )
    ready = run(lay_out_kernel, [out((nr, (per[0] + per[1]) * sh, 128), bf16)], [grads2, grads1])[0]
    mine = run(
        between_kernel,
        [out((nr, sum(per) * sh + SMALL_ROWS, 128), bf16)],
        [ready, kept, given],
    )[0]
    mine = lax.all_to_all(mine, "row", 0, 0, tiled=True)
    mine, small = run(
        last_sum_kernel, [out((sum(per) * sh, 128), bf16), out((SMALL_ROWS, 128))], [mine]
    )
    grads = lax.all_gather(mine, "col", axis=0)
    wide = [
        conv_weight.T, first_conv.T, second_conv.T, input_proj, first_input, second_input,
        output_proj, first_output, second_output, expand_weight, first_expand, second_expand,
        reduce_weight, first_reduce, second_reduce,
    ]
    new = run(
        functools.partial(adamw_kernel, sh=sh, per=per), [out(x.shape) for x in wide], [grads, *wide]
    )
    new = [x.T for x in new[:3]] + list(new[3:])
    pos = [
        jnp.concatenate([small[40 + 8 * k : 48 + 8 * k], small[56:64, 64 * k : 64 * k + 41]], 1).reshape(-1)
        for k in range(2)
    ]
    grad_small = jnp.concatenate([small[:36].reshape(-1), grad_hbias[0, :CLASSES], *pos])
    head = adamw(head_weight, grad_head[:, :CLASSES], first_head, second_head)
    return (loss[0, 0], *new, *head, *adamw(small_params, grad_small, first_small, second_small))


def solution(mesh):
    return jax.shard_map(
        on_device,
        mesh=mesh,
        in_specs=(
            P("row", "col", None),
            P(None, "row", "col"),
            P(),
            P(),
            P(None, "row"),
            P(None, "row", None),
            P(None, "row", None),
            P(None, "row", None),
            P(None, "row", None),
            P("row", None),
            P(),
            P(None, "row"),
            P(None, "row", None),
            P(None, "row", None),
            P(None, "row", None),
            P(None, "row", None),
            P("row", None),
            P(),
            P(None, "row"),
            P(None, "row", None),
            P(None, "row", None),
            P(None, "row", None),
            P(None, "row", None),
            P("row", None),
            P(),
        ),
        out_specs=(
            P(),
            P(None, "row"),
            P(None, "row"),
            P(None, "row"),
            P(None, "row", None),
            P(None, "row", None),
            P(None, "row", None),
            P(None, "row", None),
            P(None, "row", None),
            P(None, "row", None),
            P(None, "row", None),
            P(None, "row", None),
            P(None, "row", None),
            P(None, "row", None),
            P(None, "row", None),
            P(None, "row", None),
            P("row", None),
            P("row", None),
            P("row", None),
            P(),
            P(),
            P(),
        ),
        check_vma=False,
    )
```
